32 devices in a mesh: replica: 8 (over y, x, core), group: 4 (over z).
Axes of the slice: x: 2, y: 2, z: 4, core: 2. Of those that a mesh axis runs over, the one named last changes fastest.
Arguments:
- tokens: bfloat16 [8192, 1024], P(('replica', 'group')), may hold values from -6 to 6
- lengths: int32 [32, 4], P(('replica', 'group')), may hold values from 1 to 128, 256 in all within a row
- cotangent: bfloat16 [8192, 1024], P(('replica', 'group')), may hold values from -6 to 6
- attn_gain: bfloat16 [2, 1024], P(None, 'group'), may hold values from 0.5 to 1.5
- w_query: bfloat16 [2, 1024, 2048], P(None, 'group'), may hold values from -0.1875 to 0.1875
- w_key: bfloat16 [2, 1024, 1024], P(None, 'group'), may hold values from -0.1875 to 0.1875
- w_value: bfloat16 [2, 1024, 1024], P(None, 'group'), may hold values from -0.1875 to 0.1875
- query_gain: bfloat16 [2, 128], P(None, 'group'), may hold values from 0.5 to 1.5
- key_gain: bfloat16 [2, 128], P(None, 'group'), may hold values from 0.5 to 1.5
- w_output: bfloat16 [2, 2048, 1024], P(None, 'group'), may hold values from -0.5 to 0.5
- mlp_gain: bfloat16 [2, 1024], P(None, 'group'), may hold values from 0.5 to 1.5
- w_gate: bfloat16 [2, 1024, 3072], P(None, 'group'), may hold values from -0.1875 to 0.1875
- w_up: bfloat16 [2, 1024, 3072], P(None, 'group'), may hold values from -0.1875 to 0.1875
- w_down: bfloat16 [2, 3072, 1024], P(None, 'group'), may hold values from -0.21875 to 0.21875
Outputs:
- result_tokens: bfloat16 [8192, 1024], P(('replica', 'group'))
- grad_tokens: float32 [8192, 1024], P(('replica', 'group'))
- grad_attn_gain: float32 [2, 1024], P(None, 'group')
- grad_w_query: float32 [2, 1024, 2048], P(None, 'group')
- grad_w_key: float32 [2, 1024, 1024], P(None, 'group')
- grad_w_value: float32 [2, 1024, 1024], P(None, 'group')
- grad_query_gain: float32 [2, 128], P(None, 'group')
- grad_key_gain: float32 [2, 128], P(None, 'group')
- grad_w_output: float32 [2, 2048, 1024], P(None, 'group')
- grad_mlp_gain: float32 [2, 1024], P(None, 'group')
- grad_w_gate: float32 [2, 1024, 3072], P(None, 'group')
- grad_w_up: float32 [2, 1024, 3072], P(None, 'group')
- grad_w_down: float32 [2, 3072, 1024], P(None, 'group')
The draws below stay inside these ranges and needn't reach their ends.
Inputs may be any that keep to these rules, and one draw needn't show every extreme that they name: Each row of lengths adds up to 256, and its largest entry is exactly 128.
All inputs are finite; a program needn't handle non-finite values.
Results may differ from the reference program's by a relative error of at most 0.025.
Values may be sent and summed in bfloat16 or wider, within the bound.
No kernel may reach another device: no remote copies, remote signals or barrier semaphores. Data moves between devices by JAX's collectives and lax.ppermute only.
A program may use at most 384 MiB of HBM per device.

```python
import math
import jax
import jax.numpy as jnp
import numpy as np
from jax import lax

D = 1024
FF = 3072
HEADS = 16
KV_HEADS = 8
HEAD_DIM = 128
LAYERS = 2
TOK_DEV = 256
SEQS_DEV = 4
SEQ_MOST = 128
PACKS = 32
TOKENS = 8192


def block_scale(rng, dims, shards, least, top_value):
    def one(dim, parts):
        steps = jax.random.uniform(jax.random.fold_in(jax.random.fold_in(rng, 6), dim), (parts,), jnp.float32, least / len(shards), top_value / len(shards))
        return jnp.repeat(jnp.exp(steps), dims[dim] // parts).reshape((-1,) + (1,) * (len(dims) - dim - 1))

    factor_of = one(*shards[0])
    for cut in shards[1:]:
        factor_of = factor_of * one(*cut)
    return factor_of


def split_up(count, total, bound, skew):
    loads = [(1 << 20) // math.isqrt(grade ** skew) + 1 for grade in range(2, count + 1)]
    rest, holding = total - bound - (count - 1), [1] * (count - 1)
    while rest > 0:
        movable = [i for i in range(count - 1) if holding[i] < bound]
        whole, budget = sum([loads[i] for i in movable]), rest
        for i in movable:
            more = min(bound - holding[i], max(1, budget * loads[i] // whole), rest)
            holding[i] = holding[i] + more
            rest = rest - more
    return np.array([bound] + holding)


def uneven(stream_key, count, total, bound, skew):
    if count == 2:
        one = jax.random.randint(stream_key, (), max(1, total - bound), min(bound, total - 1) + 1)
        return jnp.stack([one, total - one])
    sizes = jnp.asarray(split_up(count, total, bound, skew), jnp.int32)
    pairs = (count - 1) // 2
    giver, sink = sizes[1:1 + 2 * pairs:2], sizes[2:2 + 2 * pairs:2]
    slack = jnp.minimum(giver - 1, bound - sink)
    passed = jax.random.randint(jax.random.fold_in(stream_key, 1), (pairs,), 0, 1 << 20) % (slack + 1)
    sizes = sizes.at[1:1 + 2 * pairs:2].set(giver - passed).at[2:2 + 2 * pairs:2].set(sink + passed)
    return sizes[jax.random.permutation(jax.random.fold_in(stream_key, 2), count)]


def normal_values(stream_key, dims, width, reach, shards=(), kind=jnp.bfloat16):
    values = width * jax.random.normal(stream_key, dims, jnp.float32)
    if shards:
        values = values * block_scale(stream_key, dims, shards, -0.22, 0.18)
    return jnp.clip(values, -reach, reach).astype(kind)


def setup_inputs(seed: int = 0) -> dict:
    key_of = jax.random.split(jax.random.key(seed), 15)
    tokens = normal_values(key_of[0], (TOKENS, D), 1.0, 6.0, ((0, 32),))
    lengths = jax.vmap(lambda own: uneven(own, SEQS_DEV, TOK_DEV, SEQ_MOST, 2))(jax.random.split(key_of[1], PACKS)).reshape((PACKS, SEQS_DEV)).astype(jnp.int32)
    cotangent = normal_values(key_of[2], (TOKENS, D), 1.0, 6.0, ((0, 32),))
    attn_gain = jnp.clip(1.0 + 0.1 * jax.random.normal(key_of[3], (LAYERS, D), jnp.float32), 0.5, 1.5).astype(jnp.bfloat16)
    w_query = normal_values(key_of[4], (LAYERS, D, HEADS * HEAD_DIM), D ** -0.5, 0.1875, ((1, 4),))
    w_key = normal_values(key_of[5], (LAYERS, D, KV_HEADS * HEAD_DIM), D ** -0.5, 0.1875, ((1, 4),))
    w_value = normal_values(key_of[6], (LAYERS, D, KV_HEADS * HEAD_DIM), D ** -0.5, 0.1875, ((1, 4),))
    query_gain = jnp.clip(1.0 + 0.1 * jax.random.normal(key_of[7], (LAYERS, HEAD_DIM), jnp.float32), 0.5, 1.5).astype(jnp.bfloat16)
    key_gain = jnp.clip(1.0 + 0.1 * jax.random.normal(key_of[8], (LAYERS, HEAD_DIM), jnp.float32), 0.5, 1.5).astype(jnp.bfloat16)
    w_output = normal_values(key_of[9], (LAYERS, HEADS * HEAD_DIM, D), (HEADS * HEAD_DIM // 16) ** -0.5, 0.5, ((1, 4),))
    mlp_gain = jnp.clip(1.0 + 0.1 * jax.random.normal(key_of[10], (LAYERS, D), jnp.float32), 0.5, 1.5).astype(jnp.bfloat16)
    w_gate = normal_values(key_of[11], (LAYERS, D, FF), D ** -0.5, 0.1875, ((1, 4),))
    w_up = normal_values(key_of[12], (LAYERS, D, FF), D ** -0.5, 0.1875, ((1, 4),))
    w_down = normal_values(key_of[13], (LAYERS, FF, D), (FF // 4) ** -0.5, 0.21875, ((1, 4),))
    return {"tokens": tokens, "lengths": lengths, "cotangent": cotangent, "attn_gain": attn_gain, "w_query": w_query, "w_key": w_key, "w_value": w_value, "query_gain": query_gain, "key_gain": key_gain, "w_output": w_output, "mlp_gain": mlp_gain, "w_gate": w_gate, "w_up": w_up, "w_down": w_down}


EPS = 1e-06
THETA = 1000000.0
MASKED = -1e+30

@jax.custom_vjp
def low(v):
    return lax.optimization_barrier(v.astype(jnp.bfloat16)).astype(jnp.float32)

@jax.custom_vjp
def low_back(v):
    return v

def low_keep(v):
    return (low(v), None)

def low_pass(kept, grad):
    return (grad,)

def back_keep(v):
    return (v, None)

def back_low(kept, grad):
    return (low(grad),)
low.defvjp(low_keep, low_pass)
low_back.defvjp(back_keep, back_low)

def product(left_mat, right_mat):
    return jnp.dot(left_mat, right_mat, precision=lax.Precision.HIGHEST)

def rmsnorm(vector, gain_vec):
    return vector * lax.rsqrt(lax.optimization_barrier(jnp.mean(vector * vector, -1, keepdims=True)) + EPS) * gain_vec

def layout(lengths):
    seq_ends = jnp.cumsum(lengths, 1).astype(jnp.int32)
    starts = (seq_ends - lengths).astype(jnp.int32)
    indices = jnp.arange(TOK_DEV, dtype=jnp.int32)
    segment = lax.optimization_barrier(jnp.sum((indices[None, :, None] >= seq_ends[:, None, :]).astype(jnp.int32), 2)).astype(jnp.int32)
    owners = segment[:, :, None] == jnp.arange(SEQS_DEV, dtype=jnp.int32)[None, None, :]
    position = indices[None, :] - lax.optimization_barrier(jnp.sum(jnp.where(owners, starts[:, None, :], 0), 2)).astype(jnp.int32)
    return (position.astype(jnp.int32), segment)

def rope_tables(position):
    half_width = HEAD_DIM // 2
    frequency = THETA ** (-jnp.arange(half_width, dtype=jnp.float32) * 2.0 / HEAD_DIM)
    angles = position.astype(jnp.float32)[:, None] * frequency[None, :]
    return (jnp.cos(angles), jnp.sin(angles))

def rotate(vector, cosine_table, rotary_sine):
    half_width = vector.shape[-1] // 2
    front_half = vector[..., :half_width]
    back_half = vector[..., half_width:]
    cosine_table = cosine_table[:, None, :]
    rotary_sine = rotary_sine[:, None, :]
    return jnp.concatenate([front_half * cosine_table - back_half * rotary_sine, back_half * cosine_table + front_half * rotary_sine], -1)

def head_norm(projected, gain_vec, cosine_table, rotary_sine, head_count):
    shaped = projected.reshape(projected.shape[0], head_count, HEAD_DIM)
    return rotate(rmsnorm(shaped, gain_vec), cosine_table, rotary_sine).reshape(projected.shape[0], head_count * HEAD_DIM)

def attend(pack_rows):
    queries, key_rows, values, segment = pack_rows
    indices = jnp.arange(TOK_DEV, dtype=jnp.int32)
    visible_mask = (segment[:, None] == segment[None, :]) & (indices[:, None] >= indices[None, :])
    query_groups = queries.reshape(TOK_DEV, KV_HEADS, HEADS // KV_HEADS, HEAD_DIM)
    key_groups = key_rows.reshape(TOK_DEV, KV_HEADS, HEAD_DIM)
    value_groups = values.reshape(TOK_DEV, KV_HEADS, HEAD_DIM)
    scores = jnp.einsum('qgrd,kgd->grqk', query_groups, key_groups, precision=lax.Precision.HIGHEST) * HEAD_DIM ** (-0.5)
    scores = low_back(scores)
    scores = jnp.where(visible_mask[None, None], scores, MASKED)
    row_peak = lax.optimization_barrier(jnp.max(scores, -1, keepdims=True))
    exponent = jnp.exp(scores - row_peak)
    soft_rows = low(exponent / lax.optimization_barrier(jnp.sum(exponent, -1, keepdims=True)))
    mixed_rows = jnp.einsum('grqk,kgd->qgrd', soft_rows, value_groups, precision=lax.Precision.HIGHEST)
    return mixed_rows.reshape(TOK_DEV, HEADS * HEAD_DIM)

def residual_block(state, weights, segment, cosine_table, rotary_sine):
    attn_gain, w_query, w_key, w_value, query_gain, key_gain, w_output, mlp_gain, w_gate, w_up, w_down = weights
    normed = low(rmsnorm(state, attn_gain))
    query_proj = low_back(product(normed, w_query))
    key_proj = low_back(product(normed, w_key))
    values = low(low_back(product(normed, w_value)))
    queries = low(head_norm(query_proj, query_gain, cosine_table, rotary_sine, HEADS))
    key_rows = low(head_norm(key_proj, key_gain, cosine_table, rotary_sine, KV_HEADS))
    mixed_rows = lax.map(jax.checkpoint(attend), (queries.reshape(PACKS, TOK_DEV, -1), key_rows.reshape(PACKS, TOK_DEV, -1), values.reshape(PACKS, TOK_DEV, -1), segment))
    mixed_rows = low(low_back(mixed_rows.reshape(TOKENS, HEADS * HEAD_DIM)))
    middle = state + low_back(product(mixed_rows, w_output))
    mlp_in = low(rmsnorm(middle, mlp_gain))
    gate_proj = low_back(product(mlp_in, w_gate))
    up_proj = low_back(product(mlp_in, w_up))
    hidden = low(jax.nn.silu(gate_proj) * up_proj)
    return middle + low_back(product(hidden, w_down))

def reference(tokens, lengths, cotangent, attn_gain, w_query, w_key, w_value, query_gain, key_gain, w_output, mlp_gain, w_gate, w_up, w_down):
    position, segment = layout(lengths)
    cosine_table, rotary_sine = rope_tables(position.reshape(-1))
    weights = tuple((member.astype(jnp.float32) for member in (attn_gain, w_query, w_key, w_value, query_gain, key_gain, w_output, mlp_gain, w_gate, w_up, w_down)))

    def forward(state, weight_set):
        for layer_number in range(LAYERS):
            state = residual_block(state, tuple((member[layer_number] for member in weight_set)), segment, cosine_table, rotary_sine)
        return state
    result, pullback = jax.vjp(forward, tokens.astype(jnp.float32), weights)
    grad_state, weight_grads = pullback(cotangent.astype(jnp.float32))
    return (result.astype(jnp.bfloat16), grad_state, weight_grads[0], weight_grads[1], weight_grads[2], weight_grads[3], weight_grads[4], weight_grads[5], weight_grads[6], weight_grads[7], weight_grads[8], weight_grads[9], weight_grads[10])
```

```python
import functools

import jax
import jax.numpy as jnp
from jax import lax
from jax.experimental import pallas as pl
from jax.experimental.pallas import tpu as pltpu
from jax.sharding import PartitionSpec as P

EPS = 1e-06
THETA = 1000000.0
MASKED = -1e30
AXES = ("replica", "group")
BF16 = jnp.bfloat16
F32 = jnp.float32
PLANE = 4


def dot(a, b):
    return jnp.dot(a, b, preferred_element_type=F32)


def dot_nt(a, b):
    return lax.dot_general(a, b, (((1,), (1,)), ((), ())), preferred_element_type=F32)


def dot_tn(a, b):
    return lax.dot_general(a, b, (((0,), (0,)), ((), ())), preferred_element_type=F32)


class Links:
    def __init__(self, replicas, groups):
        self.replicas, self.groups = replicas, groups

        def pairs(move):
            return [
                (r * groups + g, move(r, g)[0] * groups + move(r, g)[1])
                for r in range(replicas)
                for g in range(groups)
            ]

        self.pair = pairs(lambda r, g: (r ^ 1, g))
        self.first = pairs(lambda r, g: (r ^ (4 if r & 1 else 2), g))
        self.second = pairs(lambda r, g: (r ^ (2 if r & 1 else 4), g))
        self.shift = [pairs(lambda r, g, d=d: (r, (g + d) % groups)) for d in range(groups)]
        self.outer = []
        bit = 8
        while bit < replicas:
            self.outer.append(pairs(lambda r, g, b=bit: (r ^ b, g)))
            bit *= 2

    @staticmethod
    def send(x, perm):
        return lax.ppermute(x, AXES, perm)


def place_kernel(where, own, near, first, second, both, out, sems):
    width = near.shape[-1]
    copies = [pltpu.make_async_copy(own, out.at[where[0]], sems.at[0])]
    for j, source in enumerate((near, first, second, both)):
        column = pl.multiple_of(where[4 + j] * width, 128)
        for d in range(near.shape[0]):
            copies.append(
                pltpu.make_async_copy(
                    source.at[d],
                    out.at[where[1 + d], :, pl.ds(column, width)],
                    sems.at[1 + j * near.shape[0] + d],
                )
            )
    for copy in copies:
        copy.start()
    for copy in copies:
        copy.wait()


def place(where, own, near, first, second, both):
    groups = near.shape[0] + 1
    rows, columns = own.shape
    full = pl.pallas_call(
        place_kernel,
        out_shape=jax.ShapeDtypeStruct((groups, rows, columns), own.dtype),
        in_specs=[pl.BlockSpec(memory_space=pltpu.SMEM)] + [pl.BlockSpec(memory_space=pl.ANY)] * 5,
        out_specs=pl.BlockSpec(memory_space=pl.ANY),
        scratch_shapes=[pltpu.SemaphoreType.DMA((1 + PLANE * (groups - 1),))],
        cost_estimate=pl.CostEstimate(
            flops=0, bytes_accessed=4 * groups * rows * columns, transcendentals=0
        ),
        name="place",
    )(where, own, near, first, second, both)
    return full.reshape(groups * rows, columns)


def finish_kernel(spot, tiles, *refs, widths):
    outs = refs[-len(widths):]
    at = 0
    for out, width in zip(outs, widths):
        out[0] = tiles[0, 0, :, at:at + width].astype(F32)
        at += width


def finish(spot, tiles, layer, shapes, widths, row_split, previous):
    rows = tiles.shape[2]

    def out_map(width):
        if row_split:
            return pl.BlockSpec(
                (1, rows, width), lambda m, j, s: (layer, s[m], s[2 + PLANE * m + j])
            )
        return pl.BlockSpec(
            (1, rows, width), lambda m, j, s: (layer, 0, s[2 + PLANE * m + j] * 2 + s[m])
        )

    extra = [] if previous is None else list(previous)
    aliases = {2 + k: k for k in range(len(extra))}
    return pl.pallas_call(
        functools.partial(finish_kernel, widths=widths),
        grid_spec=pltpu.PrefetchScalarGridSpec(
            num_scalar_prefetch=1,
            grid=(2, PLANE),
            in_specs=[pl.BlockSpec((1, 1, rows, sum(widths)), lambda m, j, s: (m, j, 0, 0))]
            + [pl.BlockSpec(memory_space=pl.ANY)] * len(extra),
            out_specs=[out_map(w) for w in widths],
        ),
        out_shape=[jax.ShapeDtypeStruct(s, F32) for s in shapes],
        input_output_aliases=aliases,
        cost_estimate=pl.CostEstimate(
            flops=0, bytes_accessed=6 * tiles.size, transcendentals=0
        ),
        name="finish",
    )(spot, tiles, *extra)


def normalise(vector):
    return vector * lax.rsqrt(jnp.mean(vector * vector, -1, keepdims=True) + EPS)


def rmsnorm(vector, gain_vec):
    return normalise(vector) * gain_vec


def layout(lengths, row_count):
    seq_ends = jnp.cumsum(lengths, 1)
    starts = seq_ends - lengths
    indices = jnp.arange(row_count, dtype=jnp.int32)
    segment = jnp.sum((indices[None, :, None] >= seq_ends[:, None, :]).astype(jnp.int32), 2)
    owners = segment[:, :, None] == jnp.arange(lengths.shape[1], dtype=jnp.int32)[None, None, :]
    position = indices[None, :] - jnp.sum(jnp.where(owners, starts[:, None, :], 0), 2)
    visible = (segment[:, :, None] == segment[:, None, :]) & (
        indices[None, :, None] >= indices[None, None, :]
    )
    return position, visible


def rope_tables(position, head_width):
    half_width = head_width // 2
    frequency = THETA ** (-jnp.arange(half_width, dtype=F32) * 2.0 / head_width)
    angles = position.astype(F32)[..., None] * frequency
    return jnp.cos(angles), jnp.sin(angles)


def rotate(vector, cosine_table, rotary_sine):
    half = vector.shape[-1] // 2
    front, back = vector[..., :half], vector[..., half:]
    return jnp.concatenate(
        [front * cosine_table - back * rotary_sine, back * cosine_table + front * rotary_sine], -1
    )


def head_norm(projected, gain_vec, tables):
    cosine_table, rotary_sine = tables
    return rotate(
        rmsnorm(projected, gain_vec), cosine_table[:, :, None, :], rotary_sine[:, :, None, :]
    )


def score_block(queries, key_rows, visible):
    scores = jnp.einsum(
        "bqgrd,bkgd->bgrqk", queries, key_rows, preferred_element_type=F32
    ) * queries.shape[-1] ** (-0.5)
    return jnp.where(visible[:, None, None], scores, MASKED)


def attention_forward(queries, key_rows, values, visible):
    scores = score_block(queries, key_rows, visible)
    row_peak = jnp.max(scores, -1, keepdims=True)
    exponent = jnp.exp(scores - row_peak)
    row_total = jnp.sum(exponent, -1, keepdims=True)
    soft_rows = exponent / row_total
    mixed = jnp.einsum(
        "bgrqk,bkgd->bqgrd", soft_rows.astype(BF16), values, preferred_element_type=F32
    )
    return mixed.astype(BF16), row_peak + jnp.log(row_total)


def attention_back(queries, key_rows, values, visible, logsum, grad_mixed):
    scores = score_block(queries, key_rows, visible)
    soft_rows = jnp.exp(scores - logsum)
    grad_values = jnp.einsum(
        "bgrqk,bqgrd->bkgd", soft_rows.astype(BF16), grad_mixed, preferred_element_type=F32
    )
    grad_soft = jnp.einsum(
        "bqgrd,bkgd->bgrqk", grad_mixed, values, preferred_element_type=F32
    )
    grad_scores = soft_rows * (grad_soft - jnp.sum(soft_rows * grad_soft, -1, keepdims=True))
    grad_scores = grad_scores.astype(BF16)
    scale = queries.shape[-1] ** (-0.5)
    grad_queries = (
        jnp.einsum("bgrqk,bkgd->bqgrd", grad_scores, key_rows, preferred_element_type=F32) * scale
    )
    grad_keys = (
        jnp.einsum("bgrqk,bqgrd->bkgd", grad_scores, queries, preferred_element_type=F32) * scale
    )
    return grad_queries, grad_keys, grad_values.astype(BF16)


def body(
    tokens,
    lengths,
    cotangent,
    attn_gain,
    w_query,
    w_key,
    w_value,
    query_gain,
    key_gain,
    w_output,
    mlp_gain,
    w_gate,
    w_up,
    w_down,
    links=None,
):
    send = links.send
    groups = links.groups
    row_count, width = tokens.shape
    layer_count = w_query.shape[0]
    head_width = query_gain.shape[1] * groups
    kv_heads = w_key.shape[2] // head_width
    share = w_query.shape[2] // w_key.shape[2]
    hidden_units = w_gate.shape[2]
    blocks = kv_heads // 2
    unit = hidden_units // (2 * blocks)
    q_width = share * head_width

    replica = lax.axis_index("replica")
    z = lax.axis_index("group")
    core = replica % 2
    plane = (replica // 2) % PLANE
    step_first = 1 + core
    step_second = 2 - core
    planes = [plane, plane ^ step_first, plane ^ step_second, plane ^ 3]
    where = jnp.stack(
        [z] + [(z + groups - d) % groups for d in range(1, groups)] + planes
    ).astype(jnp.int32)
    partner_planes = [planes[0], planes[2], planes[1], planes[3]]
    spot = jnp.stack([core, 1 - core] + planes + partner_planes).astype(jnp.int32)

    gains_own = jnp.concatenate([attn_gain, mlp_gain, query_gain, key_gain], 1)
    gains = lax.all_gather(gains_own, "group", axis=0)
    part = attn_gain.shape[1]
    head_part = query_gain.shape[1]

    def gain_of(start, size, layer):
        return gains[:, layer, start:start + size].reshape(-1).astype(F32)

    both_lengths = jnp.concatenate([lengths, send(lengths, links.pair)], 0)
    position, visible = layout(both_lengths, row_count)
    tables = rope_tables(position, head_width)

    def half_columns(weight):
        shaped = weight.reshape(weight.shape[0], blocks, 2, -1)
        return lax.dynamic_index_in_dim(shaped, core, 2, keepdims=False)

    def half_rows(weight):
        shaped = weight.reshape(2, -1, weight.shape[1])
        return lax.dynamic_index_in_dim(shaped, core, 0, keepdims=False)

    def own_chunks(layer):
        rows = w_query.shape[1]
        qkv = jnp.concatenate(
            [half_columns(w_query[layer]), half_columns(w_key[layer]), half_columns(w_value[layer])],
            -1,
        ).reshape(rows, -1)
        gate_up = jnp.concatenate(
            [half_columns(w_gate[layer]), half_columns(w_up[layer])], -1
        ).reshape(rows, -1)
        return [qkv, half_rows(w_output[layer]), gate_up, half_rows(w_down[layer])]

    def gather(own, after):
        tile_width = own.shape[1] // PLANE
        tile = lax.dynamic_slice_in_dim(own, plane * tile_width, tile_width, 1)
        if after is not None:
            tile, after = lax.optimization_barrier((tile, after))
        arrived = [send(tile, links.shift[d]) for d in range(1, groups)]
        near = jnp.stack(arrived)
        first = send(near, links.first)
        second = send(near, links.second)
        both = send(first, links.second)
        return place(where, own, near, first, second, both), arrived

    weights = []
    after = None
    for layer in range(layer_count):
        held = []
        for own in own_chunks(layer):
            full, after = gather(own, after)
            held.append(full)
        weights.append(held)

    def pair_rows(rows):
        return jnp.concatenate([rows, send(rows, links.pair)], 0)

    def pair_sum(partial):
        return partial[:row_count] + send(partial[row_count:], links.pair)

    def split_qkv(projected):
        shaped = projected.reshape(2, row_count, blocks, q_width + 2 * head_width)
        query = shaped[..., :q_width].reshape(2, row_count, blocks * share, head_width)
        key = shaped[..., q_width:q_width + head_width]
        value = shaped[..., q_width + head_width:]
        return query, key, value

    def grouped(queries):
        return queries.reshape(2, row_count, blocks, share, head_width)

    state = tokens.astype(F32)
    kept = []
    for layer in range(layer_count):
        w_qkv, w_out, w_gu, w_dn = weights[layer]
        attn_g = gain_of(0, part, layer)
        mlp_g = gain_of(part, part, layer)
        query_g = gain_of(2 * part, head_part, layer)
        key_g = gain_of(2 * part + head_part, head_part, layer)
        normed = pair_rows(rmsnorm(state, attn_g).astype(BF16))
        query_proj, key_proj, values = split_qkv(dot(normed, w_qkv))
        values = values.astype(BF16)
        queries = grouped(head_norm(query_proj, query_g, tables).astype(BF16))
        key_rows = head_norm(key_proj, key_g, tables).astype(BF16)
        mixed, logsum = attention_forward(queries, key_rows, values, visible)
        mixed = mixed.reshape(2 * row_count, -1)
        middle = state + pair_sum(dot(mixed, w_out))
        mlp_in = pair_rows(rmsnorm(middle, mlp_g).astype(BF16))
        gate_up = dot(mlp_in, w_gu).reshape(2 * row_count, blocks, 2, unit)
        gate_proj, up_proj = gate_up[:, :, 0], gate_up[:, :, 1]
        hidden = (jax.nn.silu(gate_proj) * up_proj).astype(BF16).reshape(2 * row_count, -1)
        new_state = middle + pair_sum(dot(hidden, w_dn))
        kept.append(
            (
                state,
                normed,
                query_proj,
                key_proj,
                queries,
                key_rows,
                values,
                logsum,
                mixed,
                middle,
                mlp_in,
                gate_proj,
                up_proj,
                hidden,
                attn_g,
                mlp_g,
                query_g,
                key_g,
            )
        )
        state = new_state
    result_tokens = state.astype(BF16)

    def reduce_tiles(rows_bf, cols_bf):
        count = cols_bf.shape[1] // PLANE
        picked = [
            lax.dynamic_slice_in_dim(cols_bf, index * count, count, 1) for index in planes
        ]
        away = dot_tn(rows_bf, jnp.concatenate([picked[3], picked[1]], 1)).astype(BF16)
        came = send(away, links.first)
        mine = dot_tn(rows_bf, jnp.concatenate([picked[2], picked[0]], 1)) + came.astype(F32)
        away = mine[:, :count].astype(BF16)
        came = send(away, links.second)
        mine = mine[:, count:] + came.astype(F32)
        for perm in links.outer:
            mine = mine + send(mine.astype(BF16), perm).astype(F32)
        mine = mine.astype(BF16).reshape(groups, -1, count)
        total = lax.dynamic_index_in_dim(mine, z, 0, keepdims=False).astype(F32)
        for d in range(1, groups):
            leaving = lax.dynamic_index_in_dim(mine, (z + d) % groups, 0, keepdims=False)
            total = total + send(leaving, links.shift[d]).astype(F32)
        tile = total.astype(BF16)
        first = send(tile, links.first)
        second = send(tile, links.second)
        both = send(first, links.second)
        tiles = jnp.stack([tile, first, second, both])
        return jnp.stack([tiles, send(tiles, links.pair)])

    gate_shape, down_shape = w_gate.shape, w_down.shape
    gradient = cotangent.astype(F32)
    outs = [None] * 4
    gain_terms = [None] * layer_count
    for layer in reversed(range(layer_count)):
        w_qkv, w_out, w_gu, w_dn = weights[layer]
        (
            state,
            normed,
            query_proj,
            key_proj,
            queries,
            key_rows,
            values,
            logsum,
            mixed,
            middle,
            mlp_in,
            gate_proj,
            up_proj,
            hidden,
            attn_g,
            mlp_g,
            query_g,
            key_g,
        ) = kept[layer]
        branch = pair_rows(gradient.astype(BF16))
        outs[3] = finish(
            spot, reduce_tiles(hidden, branch), layer, [down_shape],
            [width // PLANE], True, outs[3],
        )
        grad_hidden = dot_nt(branch, w_dn).reshape(2 * row_count, blocks, unit)
        _, swiglu_back = jax.vjp(lambda a, b: jax.nn.silu(a) * b, gate_proj, up_proj)
        grad_gate, grad_up = swiglu_back(grad_hidden)
        grad_gu = jnp.stack([grad_gate.astype(BF16), grad_up.astype(BF16)], 2)
        grad_gu = grad_gu.reshape(2 * row_count, -1)
        outs[2] = finish(
            spot, reduce_tiles(mlp_in, grad_gu), layer, [gate_shape, gate_shape],
            [unit, unit], False, outs[2],
        )
        grad_mlp_in = pair_sum(dot_nt(grad_gu, w_gu))
        _, mlp_norm_back = jax.vjp(rmsnorm, middle, mlp_g)
        grad_middle, grad_mlp_gain = mlp_norm_back(grad_mlp_in)
        grad_middle = grad_middle + gradient
        grad_out = pair_rows(grad_middle.astype(BF16))
        outs[1] = finish(
            spot, reduce_tiles(mixed, grad_out), layer, [w_output.shape],
            [width // PLANE], True, outs[1],
        )
        grad_mixed = dot_nt(grad_out, w_out).astype(BF16)
        grad_mixed = grouped(grad_mixed)
        grad_queries, grad_keys, grad_values = attention_back(
            queries, key_rows, values, visible, logsum, grad_mixed
        )
        norm_of = lambda projected, gain_vec: head_norm(projected, gain_vec, tables)
        _, query_back = jax.vjp(norm_of, query_proj, query_g)
        grad_query_proj, grad_query_gain = query_back(grad_queries.reshape(query_proj.shape))
        _, key_back = jax.vjp(norm_of, key_proj, key_g)
        grad_key_proj, grad_key_gain = key_back(grad_keys)
        grad_qkv = jnp.concatenate(
            [
                grad_query_proj.astype(BF16).reshape(2, row_count, blocks, q_width),
                grad_key_proj.astype(BF16),
                grad_values,
            ],
            -1,
        ).reshape(2 * row_count, -1)
        outs[0] = finish(
            spot, reduce_tiles(normed, grad_qkv), layer,
            [w_query.shape, w_key.shape, w_value.shape],
            [q_width, head_width, head_width], False, outs[0],
        )
        grad_normed = pair_sum(dot_nt(grad_qkv, w_qkv))
        _, attn_norm_back = jax.vjp(rmsnorm, state, attn_g)
        grad_state, grad_attn_gain = attn_norm_back(grad_normed)
        gradient = grad_state + grad_middle
        gain_terms[layer] = jnp.concatenate(
            [grad_attn_gain, grad_mlp_gain, grad_query_gain, grad_key_gain]
        )
    gain_sums = lax.psum(jnp.stack(gain_terms), AXES)

    def own_gain(start, size):
        return lax.dynamic_slice_in_dim(gain_sums, start + z * size, size, 1)

    return (
        result_tokens,
        gradient,
        own_gain(0, part),
        outs[0][0],
        outs[0][1],
        outs[0][2],
        own_gain(2 * width, head_part),
        own_gain(2 * width + head_width, head_part),
        outs[1][0],
        own_gain(width, part),
        outs[2][0],
        outs[2][1],
        outs[3][0],
    )


def solution(mesh):
    links = Links(mesh.shape["replica"], mesh.shape["group"])
    return jax.shard_map(
        functools.partial(body, links=links),
        mesh=mesh,
        in_specs=(
            P(AXES, None),
            P(AXES, None),
            P(AXES, None),
            P(None, "group"),
            P(None, "group", None),
            P(None, "group", None),
            P(None, "group", None),
            P(None, "group"),
            P(None, "group"),
            P(None, "group", None),
            P(None, "group"),
            P(None, "group", None),
            P(None, "group", None),
            P(None, "group", None),
        ),
        out_specs=(
            P(AXES, None),
            P(AXES, None),
            P(None, "group"),
            P(None, "group", None),
            P(None, "group", None),
            P(None, "group", None),
            P(None, "group"),
            P(None, "group"),
            P(None, "group", None),
            P(None, "group"),
            P(None, "group", None),
            P(None, "group", None),
            P(None, "group", None),
        ),
        check_vma=False,
    )
```

```python
import functools

import jax
import jax.numpy as jnp
from jax import lax
from jax.experimental import pallas as pl
from jax.experimental.pallas import tpu as pltpu
from jax.sharding import PartitionSpec as P

EPS = 1e-06
THETA = 1000000.0
MASKED = -1e30
AXES = ("replica", "group")
BF16 = jnp.bfloat16
F32 = jnp.float32
PLANE = 4


def dot(a, b):
    return jnp.dot(a, b, preferred_element_type=F32)


def dot_nt(a, b):
    return lax.dot_general(a, b, (((1,), (1,)), ((), ())), preferred_element_type=F32)


def dot_tn(a, b):
    return lax.dot_general(a, b, (((0,), (0,)), ((), ())), preferred_element_type=F32)


class Links:
    def __init__(self, replicas, groups):
        self.replicas, self.groups = replicas, groups

        def pairs(move):
            return [
                (r * groups + g, move(r, g)[0] * groups + move(r, g)[1])
                for r in range(replicas)
                for g in range(groups)
            ]

        self.pair = pairs(lambda r, g: (r ^ 1, g))
        self.first = pairs(lambda r, g: (r ^ (4 if r & 1 else 2), g))
        self.second = pairs(lambda r, g: (r ^ (2 if r & 1 else 4), g))
        self.shift = [pairs(lambda r, g, d=d: (r, (g + d) % groups)) for d in range(groups)]
        self.turns = [pairs(lambda r, g, b=b: (r ^ b, g)) for b in (2, 4)]
        bit = 1
        while bit < groups:
            self.turns.append(pairs(lambda r, g, b=bit: (r, g ^ b)))
            bit *= 2
        self.outer = []
        bit = 8
        while bit < replicas:
            self.outer.append(pairs(lambda r, g, b=bit: (r ^ b, g)))
            bit *= 2

    @staticmethod
    def send(x, perm):
        return lax.ppermute(x, AXES, perm)


def place_kernel(where, own, near, first, second, both, out, sems):
    width = near.shape[-1]
    copies = [pltpu.make_async_copy(own, out.at[where[0]], sems.at[0])]
    for j, source in enumerate((near, first, second, both)):
        column = pl.multiple_of(where[4 + j] * width, 128)
        for d in range(near.shape[0]):
            copies.append(
                pltpu.make_async_copy(
                    source.at[d],
                    out.at[where[1 + d], :, pl.ds(column, width)],
                    sems.at[1 + j * near.shape[0] + d],
                )
            )
    for copy in copies:
        copy.start()
    for copy in copies:
        copy.wait()


def place(where, own, near, first, second, both):
    groups = near.shape[0] + 1
    rows, columns = own.shape
    full = pl.pallas_call(
        place_kernel,
        out_shape=jax.ShapeDtypeStruct((groups, rows, columns), own.dtype),
        in_specs=[pl.BlockSpec(memory_space=pltpu.SMEM)] + [pl.BlockSpec(memory_space=pl.ANY)] * 5,
        out_specs=pl.BlockSpec(memory_space=pltpu.VMEM),
        scratch_shapes=[pltpu.SemaphoreType.DMA((1 + PLANE * (groups - 1),))],
        compiler_params=pltpu.CompilerParams(
            vmem_limit_bytes=2 * groups * rows * columns + (4 << 20)
        ),
        cost_estimate=pl.CostEstimate(
            flops=0, bytes_accessed=4 * groups * rows * columns, transcendentals=0
        ),
        name="place",
    )(where, own, near, first, second, both)
    return full.reshape(groups * rows, columns)


def finish_kernel(spot, tiles, *refs, widths):
    outs = refs[-len(widths):]
    at = 0
    for out, width in zip(outs, widths):
        out[0] = tiles[0, 0, :, at:at + width].astype(F32)
        at += width


def finish(spot, tiles, layer, shapes, widths, row_split, previous):
    rows = tiles.shape[2]

    def out_map(width):
        if row_split:
            return pl.BlockSpec(
                (1, rows, width), lambda m, j, s: (layer, s[m], s[2 + PLANE * m + j])
            )
        return pl.BlockSpec(
            (1, rows, width), lambda m, j, s: (layer, 0, s[2 + PLANE * m + j] * 2 + s[m])
        )

    extra = [] if previous is None else list(previous)
    aliases = {2 + k: k for k in range(len(extra))}
    return pl.pallas_call(
        functools.partial(finish_kernel, widths=widths),
        grid_spec=pltpu.PrefetchScalarGridSpec(
            num_scalar_prefetch=1,
            grid=(2, PLANE),
            in_specs=[pl.BlockSpec((1, 1, rows, sum(widths)), lambda m, j, s: (m, j, 0, 0))]
            + [pl.BlockSpec(memory_space=pl.ANY)] * len(extra),
            out_specs=[out_map(w) for w in widths],
        ),
        out_shape=[jax.ShapeDtypeStruct(s, F32) for s in shapes],
        input_output_aliases=aliases,
        cost_estimate=pl.CostEstimate(
            flops=0, bytes_accessed=6 * tiles.size, transcendentals=0
        ),
        name="finish",
    )(spot, tiles, *extra)


def normalise(vector):
    return vector * lax.rsqrt(jnp.mean(vector * vector, -1, keepdims=True) + EPS)


def rmsnorm(vector, gain_vec):
    return normalise(vector) * gain_vec


def layout(lengths, row_count):
    seq_ends = jnp.cumsum(lengths, 1)
    starts = seq_ends - lengths
    indices = jnp.arange(row_count, dtype=jnp.int32)
    segment = jnp.sum((indices[None, :, None] >= seq_ends[:, None, :]).astype(jnp.int32), 2)
    owners = segment[:, :, None] == jnp.arange(lengths.shape[1], dtype=jnp.int32)[None, None, :]
    position = indices[None, :] - jnp.sum(jnp.where(owners, starts[:, None, :], 0), 2)
    visible = (segment[:, :, None] == segment[:, None, :]) & (
        indices[None, :, None] >= indices[None, None, :]
    )
    return position, visible


def rope_tables(position, head_width):
    half_width = head_width // 2
    frequency = THETA ** (-jnp.arange(half_width, dtype=F32) * 2.0 / head_width)
    angles = position.astype(F32)[..., None] * frequency
    return jnp.cos(angles), jnp.sin(angles)


def rotate(vector, cosine_table, rotary_sine):
    half = vector.shape[-1] // 2
    front, back = vector[..., :half], vector[..., half:]
    return jnp.concatenate(
        [front * cosine_table - back * rotary_sine, back * cosine_table + front * rotary_sine], -1
    )


def head_norm(projected, gain_vec, tables):
    cosine_table, rotary_sine = tables
    return rotate(
        rmsnorm(projected, gain_vec), cosine_table[:, :, None, :], rotary_sine[:, :, None, :]
    )


def score_block(queries, key_rows, visible):
    scores = jnp.einsum(
        "bqgrd,bkgd->bgrqk", queries, key_rows, preferred_element_type=F32
    ) * queries.shape[-1] ** (-0.5)
    return jnp.where(visible[:, None, None], scores, MASKED)


def attention_forward(queries, key_rows, values, visible):
    scores = score_block(queries, key_rows, visible)
    row_peak = jnp.max(scores, -1, keepdims=True)
    exponent = jnp.exp(scores - row_peak)
    row_total = jnp.sum(exponent, -1, keepdims=True)
    soft_rows = exponent / row_total
    mixed = jnp.einsum(
        "bgrqk,bkgd->bqgrd", soft_rows.astype(BF16), values, preferred_element_type=F32
    )
    return mixed.astype(BF16), row_peak + jnp.log(row_total)


def attention_back(queries, key_rows, values, visible, logsum, grad_mixed):
    scores = score_block(queries, key_rows, visible)
    soft_rows = jnp.exp(scores - logsum)
    grad_values = jnp.einsum(
        "bgrqk,bqgrd->bkgd", soft_rows.astype(BF16), grad_mixed, preferred_element_type=F32
    )
    grad_soft = jnp.einsum(
        "bqgrd,bkgd->bgrqk", grad_mixed, values, preferred_element_type=F32
    )
    grad_scores = soft_rows * (grad_soft - jnp.sum(soft_rows * grad_soft, -1, keepdims=True))
    grad_scores = grad_scores.astype(BF16)
    scale = queries.shape[-1] ** (-0.5)
    grad_queries = (
        jnp.einsum("bgrqk,bkgd->bqgrd", grad_scores, key_rows, preferred_element_type=F32) * scale
    )
    grad_keys = (
        jnp.einsum("bgrqk,bqgrd->bkgd", grad_scores, queries, preferred_element_type=F32) * scale
    )
    return grad_queries, grad_keys, grad_values.astype(BF16)


def body(
    tokens,
    lengths,
    cotangent,
    attn_gain,
    w_query,
    w_key,
    w_value,
    query_gain,
    key_gain,
    w_output,
    mlp_gain,
    w_gate,
    w_up,
    w_down,
    links=None,
):
    send = links.send
    groups = links.groups
    row_count, width = tokens.shape
    layer_count = w_query.shape[0]
    head_width = query_gain.shape[1] * groups
    kv_heads = w_key.shape[2] // head_width
    share = w_query.shape[2] // w_key.shape[2]
    hidden_units = w_gate.shape[2]
    blocks = kv_heads // 2
    unit = hidden_units // (2 * blocks)
    q_width = share * head_width

    replica = lax.axis_index("replica")
    z = lax.axis_index("group")
    core = replica % 2
    plane = (replica // 2) % PLANE
    step_first = 1 + core
    step_second = 2 - core
    planes = [plane, plane ^ step_first, plane ^ step_second, plane ^ 3]
    where = jnp.stack(
        [z] + [(z + groups - d) % groups for d in range(1, groups)] + planes
    ).astype(jnp.int32)
    partner_planes = [planes[0], planes[2], planes[1], planes[3]]
    spot = jnp.stack([core, 1 - core] + planes + partner_planes).astype(jnp.int32)

    gains_own = jnp.concatenate([attn_gain, mlp_gain, query_gain, key_gain], 1)
    gains = jnp.zeros((groups,) + gains_own.shape, BF16)
    gains = lax.dynamic_update_index_in_dim(gains, gains_own, z, 0)
    for d in range(1, groups):
        gains = lax.dynamic_update_index_in_dim(
            gains, send(gains_own, links.shift[d]), (z + groups - d) % groups, 0
        )
    part = attn_gain.shape[1]
    head_part = query_gain.shape[1]

    def gain_of(start, size, layer):
        return gains[:, layer, start:start + size].reshape(-1).astype(F32)

    def pair_rows(rows):
        other = send(rows, links.pair)
        return jnp.concatenate(
            [jnp.where(core == 0, rows, other), jnp.where(core == 0, other, rows)], 0
        )

    both_lengths = pair_rows(lengths)
    position, visible = layout(both_lengths, row_count)
    tables = rope_tables(position, head_width)

    def half_columns(weight):
        shaped = weight.reshape(weight.shape[0], blocks, 2, -1)
        return lax.dynamic_index_in_dim(shaped, core, 2, keepdims=False)

    def half_rows(weight):
        shaped = weight.reshape(2, -1, weight.shape[1])
        return lax.dynamic_index_in_dim(shaped, core, 0, keepdims=False)

    def own_chunks(layer):
        rows = w_query.shape[1]
        qkv = jnp.concatenate(
            [half_columns(w_query[layer]), half_columns(w_key[layer]), half_columns(w_value[layer])],
            -1,
        ).reshape(rows, -1)
        gate_up = jnp.concatenate(
            [half_columns(w_gate[layer]), half_columns(w_up[layer])], -1
        ).reshape(rows, -1)
        return [qkv, half_rows(w_output[layer]), gate_up, half_rows(w_down[layer])]

    def gather(own, after):
        tile_width = own.shape[1] // PLANE
        tile = lax.dynamic_slice_in_dim(own, plane * tile_width, tile_width, 1)
        if after is not None:
            tile, after = lax.optimization_barrier((tile, after))
        arrived = [send(tile, links.shift[d]) for d in range(1, groups)]
        near = jnp.stack(arrived)
        first = send(near, links.first)
        second = send(near, links.second)
        both = send(first, links.second)
        return place(where, own, near, first, second, both), arrived

    weights = []
    after = None
    for layer in range(layer_count):
        held = []
        for own in own_chunks(layer):
            full, after = gather(own, after)
            held.append(full)
        weights.append(held)

    def pair_sum(partial):
        return partial + send(partial, links.pair)

    def own_rows(rows):
        return lax.dynamic_slice_in_dim(rows, core * row_count, row_count, 0)

    def split_qkv(projected):
        shaped = projected.reshape(2, row_count, blocks, q_width + 2 * head_width)
        query = shaped[..., :q_width].reshape(2, row_count, blocks * share, head_width)
        key = shaped[..., q_width:q_width + head_width]
        value = shaped[..., q_width + head_width:]
        return query, key, value

    def grouped(queries):
        return queries.reshape(2, row_count, blocks, share, head_width)

    state = pair_rows(tokens).astype(F32)
    kept = []
    for layer in range(layer_count):
        w_qkv, w_out, w_gu, w_dn = weights[layer]
        attn_g = gain_of(0, part, layer)
        mlp_g = gain_of(part, part, layer)
        query_g = gain_of(2 * part, head_part, layer)
        key_g = gain_of(2 * part + head_part, head_part, layer)
        normed = rmsnorm(state, attn_g).astype(BF16)
        query_proj, key_proj, values = split_qkv(dot(normed, w_qkv))
        values = values.astype(BF16)
        queries = grouped(head_norm(query_proj, query_g, tables).astype(BF16))
        key_rows = head_norm(key_proj, key_g, tables).astype(BF16)
        mixed, logsum = attention_forward(queries, key_rows, values, visible)
        mixed = mixed.reshape(2 * row_count, -1)
        middle = state + pair_sum(dot(mixed, w_out))
        mlp_in = rmsnorm(middle, mlp_g).astype(BF16)
        gate_up = dot(mlp_in, w_gu).reshape(2 * row_count, blocks, 2, unit)
        gate_proj, up_proj = gate_up[:, :, 0], gate_up[:, :, 1]
        hidden = (jax.nn.silu(gate_proj) * up_proj).astype(BF16).reshape(2 * row_count, -1)
        new_state = middle + pair_sum(dot(hidden, w_dn))
        kept.append(
            (
                state,
                normed,
                query_proj,
                key_proj,
                queries,
                key_rows,
                values,
                logsum,
                mixed,
                middle,
                mlp_in,
                gate_proj,
                up_proj,
                hidden,
                attn_g,
                mlp_g,
                query_g,
                key_g,
            )
        )
        state = new_state
    result_tokens = own_rows(state).astype(BF16)

    def reduce_tiles(rows_bf, cols_bf):
        count = cols_bf.shape[1] // PLANE
        picked = [
            lax.dynamic_slice_in_dim(cols_bf, index * count, count, 1) for index in planes
        ]
        away = dot_tn(rows_bf, jnp.concatenate([picked[3], picked[1]], 1)).astype(BF16)
        came = send(away, links.first)
        mine = dot_tn(rows_bf, jnp.concatenate([picked[2], picked[0]], 1)) + came.astype(F32)
        away = mine[:, :count].astype(BF16)
        came = send(away, links.second)
        mine = mine[:, count:] + came.astype(F32)
        for perm in links.outer:
            mine = mine.astype(BF16)
            mine = mine.astype(F32) + send(mine, perm).astype(F32)
        mine = mine.astype(BF16).reshape(groups, -1, count)
        total = lax.dynamic_index_in_dim(mine, z, 0, keepdims=False).astype(F32)
        for d in range(1, groups):
            leaving = lax.dynamic_index_in_dim(mine, (z + d) % groups, 0, keepdims=False)
            total = total + send(leaving, links.shift[d]).astype(F32)
        tile = total.astype(BF16)
        first = send(tile, links.first)
        second = send(tile, links.second)
        both = send(first, links.second)
        tiles = jnp.stack([tile, first, second, both])
        return jnp.stack([tiles, send(tiles, links.pair)])

    gate_shape, down_shape = w_gate.shape, w_down.shape
    gradient = pair_rows(cotangent).astype(F32)
    outs = [None] * 4
    gain_terms = [None] * layer_count
    for layer in reversed(range(layer_count)):
        w_qkv, w_out, w_gu, w_dn = weights[layer]
        (
            state,
            normed,
            query_proj,
            key_proj,
            queries,
            key_rows,
            values,
            logsum,
            mixed,
            middle,
            mlp_in,
            gate_proj,
            up_proj,
            hidden,
            attn_g,
            mlp_g,
            query_g,
            key_g,
        ) = kept[layer]
        branch = gradient.astype(BF16)
        outs[3] = finish(
            spot, reduce_tiles(hidden, branch), layer, [down_shape],
            [width // PLANE], True, outs[3],
        )
        grad_hidden = dot_nt(branch, w_dn).reshape(2 * row_count, blocks, unit)
        _, swiglu_back = jax.vjp(lambda a, b: jax.nn.silu(a) * b, gate_proj, up_proj)
        grad_gate, grad_up = swiglu_back(grad_hidden)
        grad_gu = jnp.stack([grad_gate.astype(BF16), grad_up.astype(BF16)], 2)
        grad_gu = grad_gu.reshape(2 * row_count, -1)
        outs[2] = finish(
            spot, reduce_tiles(mlp_in, grad_gu), layer, [gate_shape, gate_shape],
            [unit, unit], False, outs[2],
        )
        grad_mlp_in = pair_sum(dot_nt(grad_gu, w_gu))
        _, mlp_norm_back = jax.vjp(rmsnorm, middle, mlp_g)
        grad_middle, grad_mlp_gain = mlp_norm_back(grad_mlp_in)
        grad_middle = grad_middle + gradient
        grad_out = grad_middle.astype(BF16)
        outs[1] = finish(
            spot, reduce_tiles(mixed, grad_out), layer, [w_output.shape],
            [width // PLANE], True, outs[1],
        )
        grad_mixed = dot_nt(grad_out, w_out).astype(BF16)
        grad_mixed = grouped(grad_mixed)
        grad_queries, grad_keys, grad_values = attention_back(
            queries, key_rows, values, visible, logsum, grad_mixed
        )
        norm_of = lambda projected, gain_vec: head_norm(projected, gain_vec, tables)
        _, query_back = jax.vjp(norm_of, query_proj, query_g)
        grad_query_proj, grad_query_gain = query_back(grad_queries.reshape(query_proj.shape))
        _, key_back = jax.vjp(norm_of, key_proj, key_g)
        grad_key_proj, grad_key_gain = key_back(grad_keys)
        grad_qkv = jnp.concatenate(
            [
                grad_query_proj.astype(BF16).reshape(2, row_count, blocks, q_width),
                grad_key_proj.astype(BF16),
                grad_values,
            ],
            -1,
        ).reshape(2 * row_count, -1)
        outs[0] = finish(
            spot, reduce_tiles(normed, grad_qkv), layer,
            [w_query.shape, w_key.shape, w_value.shape],
            [q_width, head_width, head_width], False, outs[0],
        )
        grad_normed = pair_sum(dot_nt(grad_qkv, w_qkv))
        _, attn_norm_back = jax.vjp(rmsnorm, state, attn_g)
        grad_state, grad_attn_gain = attn_norm_back(grad_normed)
        gradient = grad_state + grad_middle
        heads_term = pair_sum(jnp.concatenate([grad_query_gain, grad_key_gain])[None])
        terms = jnp.concatenate([grad_attn_gain[None], grad_mlp_gain[None], heads_term], 1)
        for perm in links.turns + links.outer:
            terms = terms + send(terms, perm)
        gain_terms[layer] = terms
    gain_sums = jnp.concatenate(gain_terms, 0)

    def own_gain(start, size):
        return lax.dynamic_slice_in_dim(gain_sums, start + z * size, size, 1)

    return (
        result_tokens,
        own_rows(gradient),
        own_gain(0, part),
        outs[0][0],
        outs[0][1],
        outs[0][2],
        own_gain(2 * width, head_part),
        own_gain(2 * width + head_width, head_part),
        outs[1][0],
        own_gain(width, part),
        outs[2][0],
        outs[2][1],
        outs[3][0],
    )


def solution(mesh):
    links = Links(mesh.shape["replica"], mesh.shape["group"])
    return jax.shard_map(
        functools.partial(body, links=links),
        mesh=mesh,
        in_specs=(
            P(AXES, None),
            P(AXES, None),
            P(AXES, None),
            P(None, "group"),
            P(None, "group", None),
            P(None, "group", None),
            P(None, "group", None),
            P(None, "group"),
            P(None, "group"),
            P(None, "group", None),
            P(None, "group"),
            P(None, "group", None),
            P(None, "group", None),
            P(None, "group", None),
        ),
        out_specs=(
            P(AXES, None),
            P(AXES, None),
            P(None, "group"),
            P(None, "group", None),
            P(None, "group", None),
            P(None, "group", None),
            P(None, "group"),
            P(None, "group"),
            P(None, "group", None),
            P(None, "group"),
            P(None, "group", None),
            P(None, "group", None),
            P(None, "group", None),
        ),
        check_vma=False,
    )
```

```python
import functools

import jax
import jax.numpy as jnp
from jax import lax
from jax.experimental import pallas as pl
from jax.experimental.pallas import tpu as pltpu
from jax.sharding import PartitionSpec as P

EPS = 1e-06
THETA = 1000000.0
MASKED = -1e30
AXES = ("replica", "group")
BF16 = jnp.bfloat16
F32 = jnp.float32
PLANE = 4


def dot(a, b):
    return jnp.dot(a, b, preferred_element_type=F32)


def dot_nt(a, b):
    return lax.dot_general(a, b, (((1,), (1,)), ((), ())), preferred_element_type=F32)


def dot_tn(a, b):
    return lax.dot_general(a, b, (((0,), (0,)), ((), ())), preferred_element_type=F32)


def rmsnorm(vector, gain_vec):
    return vector * lax.rsqrt(jnp.mean(vector * vector, -1, keepdims=True) + EPS) * gain_vec


class Links:
    def __init__(self, replicas, groups):
        self.replicas, self.groups = replicas, groups

        def pairs(move):
            return [
                (r * groups + g, move(r, g)[0] * groups + move(r, g)[1])
                for r in range(replicas)
                for g in range(groups)
            ]

        self.pair = pairs(lambda r, g: (r ^ 1, g))
        self.first = pairs(lambda r, g: (r ^ (4 if r & 1 else 2), g))
        self.second = pairs(lambda r, g: (r ^ (2 if r & 1 else 4), g))
        self.shift = [pairs(lambda r, g, d=d: (r, (g + d) % groups)) for d in range(groups)]
        self.turns = [pairs(lambda r, g, b=b: (r ^ b, g)) for b in (2, 4)]
        bit = 1
        while bit < groups:
            self.turns.append(pairs(lambda r, g, b=bit: (r, g ^ b)))
            bit *= 2
        self.outer = []
        bit = 8
        while bit < replicas:
            self.outer.append(pairs(lambda r, g, b=bit: (r ^ b, g)))
            bit *= 2

    @staticmethod
    def send(x, perm):
        return lax.ppermute(x, AXES, perm)


VMEM = pl.BlockSpec(memory_space=pltpu.VMEM)
SMEM = pl.BlockSpec(memory_space=pltpu.SMEM)
ANY = pl.BlockSpec(memory_space=pl.ANY)
STRIP = 64


def tile_copies(where, sources, weight, sems):
    own, rest = sources[0], sources[1:]
    rows, columns = own.shape
    width = columns // PLANE
    others = weight.shape[0] // rows - 1

    def band(z):
        return pl.ds(pl.multiple_of(z * rows, rows), rows)

    copies = [pltpu.make_async_copy(own, weight.at[band(where[0])], sems.at[0])]
    for j, source in enumerate(rest):
        column = pl.multiple_of(where[1 + others + j] * width, 128)
        for d in range(others):
            copies.append(
                pltpu.make_async_copy(
                    source.at[d],
                    weight.at[band(where[1 + d]), pl.ds(column, width)],
                    sems.at[len(copies)],
                )
            )
    return copies


def tile_scratch(tiles):
    own, near = tiles[0], tiles[1]
    groups = near.shape[0] + 1
    return [
        pltpu.VMEM((groups * own.shape[0], own.shape[1]), BF16),
        pltpu.SemaphoreType.DMA((1 + PLANE * (groups - 1),)),
    ]


def call(kernel, name, inputs, specs, outs, scratch, flops=0, vmem=52):
    moved = sum(x.size * x.dtype.itemsize for x in inputs)
    moved += sum(x.size * x.dtype.itemsize for x in outs)
    return pl.pallas_call(
        kernel,
        in_specs=specs,
        out_specs=[VMEM] * len(outs),
        out_shape=outs,
        scratch_shapes=scratch,
        compiler_params=pltpu.CompilerParams(vmem_limit_bytes=vmem << 20),
        cost_estimate=pl.CostEstimate(flops=flops, bytes_accessed=moved, transcendentals=0),
        name=name,
    )(*inputs)


def strips(rows, step):
    def run(i, carry):
        step(pl.ds(pl.multiple_of(i * STRIP, STRIP), STRIP))
        return carry

    lax.fori_loop(0, rows // STRIP, run, 0)


def head_forward(v, gain_vec, cosine, sine):
    r = lax.rsqrt(jnp.mean(v * v, -1, keepdims=True) + EPS)
    n = v * r * gain_vec
    return n * cosine + pltpu.roll(n, n.shape[-1] // 2, 1) * sine


def head_back(grad, v, gain_vec, cosine, sine):
    r = lax.rsqrt(jnp.mean(v * v, -1, keepdims=True) + EPS)
    grad = grad * cosine + pltpu.roll(grad * sine, grad.shape[-1] // 2, 1)
    unit_v = v * r
    gain_term = jnp.sum(grad * unit_v, 0, keepdims=True)
    inner = grad * gain_vec
    return r * (inner - unit_v * jnp.mean(unit_v * inner, -1, keepdims=True)), gain_term


def soft(queries, key_rows, bias):
    scores = dot_nt(queries, key_rows) * queries.shape[-1] ** (-0.5) + bias
    exponent = jnp.exp(scores - jnp.max(scores, -1, keepdims=True))
    return exponent / jnp.sum(exponent, -1, keepdims=True)


def attn_forward_kernel(count, head, share, *refs):
    where, gain, query_gain, key_gain, cosine, sine, bias = refs[:7]
    parts = refs[7:7 + count]
    qkv_tiles = refs[7 + count:12 + count]
    out_tiles = refs[12 + count:17 + count]
    state, normed, proj, mixed, partial = refs[17 + count:22 + count]
    w_qkv, sem_qkv, w_out, sem_out = refs[22 + count:]
    first_copies = tile_copies(where, qkv_tiles, w_qkv, sem_qkv)
    last_copies = tile_copies(where, out_tiles, w_out, sem_out)
    for copy in first_copies + last_copies:
        copy.start()

    def prepare(rows):
        total = parts[0][rows, :].astype(F32)
        for part in parts[1:]:
            total = total + part[rows, :]
        state[rows, :] = total
        normed[rows, :] = rmsnorm(total, gain[...]).astype(BF16)

    strips(state.shape[0], prepare)
    for copy in first_copies:
        copy.wait()
    span = (share + 2) * head
    packs, pack = bias.shape[0], bias.shape[1]

    def group(g, carry):
        columns = pl.ds(pl.multiple_of(g * span, span), span)
        proj[:, columns] = dot(normed[...], w_qkv[:, columns])
        base = g * span
        heads = [
            head_forward(
                proj[:, pl.ds(pl.multiple_of(base + h * head, head), head)],
                query_gain[...] if h < share else key_gain[...],
                cosine[...],
                sine[...],
            ).astype(BF16)
            for h in range(share + 1)
        ]
        value = proj[:, pl.ds(pl.multiple_of(base + (share + 1) * head, head), head)].astype(BF16)
        for b in range(packs):
            rows = slice(b * pack, (b + 1) * pack)
            for h in range(share):
                probs = soft(heads[h][rows], heads[share][rows], bias[b])
                at = pl.multiple_of((g * share + h) * head, head)
                mixed[rows, pl.ds(at, head)] = dot(probs.astype(BF16), value[rows]).astype(BF16)
        return carry

    lax.fori_loop(0, w_qkv.shape[1] // span, group, 0)
    for copy in last_copies:
        copy.wait()
    partial[...] = dot(mixed[...], w_out[...])


def mlp_forward_kernel(unit, *refs):
    where, gain, s_ref, p_ref, c_ref = refs[:5]
    tiles = refs[5:10]
    middle, mlp_in, gate_up, hidden = refs[10:14]
    weight, sems = refs[14:]
    copies = tile_copies(where, tiles, weight, sems)
    for copy in copies:
        copy.start()

    def prepare(rows):
        total = s_ref[rows, :] + (p_ref[rows, :] + c_ref[rows, :])
        middle[rows, :] = total
        mlp_in[rows, :] = rmsnorm(total, gain[...]).astype(BF16)

    strips(middle.shape[0], prepare)
    for copy in copies:
        copy.wait()

    def block(j, carry):
        columns = pl.ds(pl.multiple_of(j * 2 * unit, 2 * unit), 2 * unit)
        gate_up[:, columns] = dot(mlp_in[...], weight[:, columns])
        gates = gate_up[:, pl.ds(pl.multiple_of(j * 2 * unit, unit), unit)]
        ups = gate_up[:, pl.ds(pl.multiple_of(j * 2 * unit + unit, unit), unit)]
        hidden[:, pl.ds(pl.multiple_of(j * unit, unit), unit)] = (
            gates / (1.0 + jnp.exp(-gates)) * ups
        ).astype(BF16)
        return carry

    lax.fori_loop(0, weight.shape[1] // (2 * unit), block, 0)


def down_kernel(where, hidden, *refs):
    tiles, partial, weight, sems = refs[:5], refs[5], refs[6], refs[7]
    copies = tile_copies(where, tiles, weight, sems)
    for copy in copies:
        copy.start()
    for copy in copies:
        copy.wait()
    partial[...] = dot(hidden[...], weight[...])


def mlp_back_kernel(unit, *refs):
    where, branch, gate_up = refs[:3]
    down_tiles, gu_tiles = refs[3:8], refs[8:13]
    grad_gu, partial = refs[13:15]
    w_down, sem_down, w_gu, sem_gu = refs[15:]
    first_copies = tile_copies(where, down_tiles, w_down, sem_down)
    last_copies = tile_copies(where, gu_tiles, w_gu, sem_gu)
    for copy in first_copies + last_copies:
        copy.start()
    for copy in first_copies:
        copy.wait()

    def block(j, carry):
        grad = dot_nt(branch[...], w_down[pl.ds(pl.multiple_of(j * unit, unit), unit), :])
        at = pl.ds(pl.multiple_of(j * 2 * unit, unit), unit)
        past = pl.ds(pl.multiple_of(j * 2 * unit + unit, unit), unit)
        gates = gate_up[:, at]
        sigma = 1.0 / (1.0 + jnp.exp(-gates))
        silu = gates * sigma
        grad_gu[:, at] = (grad * gate_up[:, past] * (sigma + silu * (1.0 - sigma))).astype(BF16)
        grad_gu[:, past] = (grad * silu).astype(BF16)
        return carry

    lax.fori_loop(0, w_down.shape[0] // unit, block, 0)
    for copy in last_copies:
        copy.wait()
    partial[...] = dot_nt(grad_gu[...], w_gu[...])


def norm_back(rows, v_ref, gain, p_ref, c_ref, residual, grad_ref, low_ref, term):
    v = v_ref[rows, :]
    r = lax.rsqrt(jnp.mean(v * v, -1, keepdims=True) + EPS)
    grad = p_ref[rows, :] + c_ref[rows, :]
    unit_v = v * r
    term[...] += jnp.sum(grad * unit_v, 0, keepdims=True)
    inner = grad * gain[...]
    total = residual[rows, :].astype(F32) + r * (
        inner - unit_v * jnp.mean(unit_v * inner, -1, keepdims=True)
    )
    grad_ref[rows, :] = total
    low_ref[rows, :] = total.astype(BF16)


def norm_back_kernel(gain, v_ref, p_ref, c_ref, residual, grad_ref, low_ref, term):
    term[...] = jnp.zeros_like(term)
    strips(
        v_ref.shape[0],
        lambda rows: norm_back(rows, v_ref, gain, p_ref, c_ref, residual, grad_ref, low_ref, term),
    )


def attn_back_kernel(head, share, *refs):
    where, gain, query_gain, key_gain, cosine, sine, bias = refs[:7]
    v_ref, p_ref, c_ref, residual, proj = refs[7:12]
    out_tiles, qkv_tiles = refs[12:17], refs[17:22]
    grad_ref, low_ref, term, grad_qkv, query_term, key_term, partial = refs[22:29]
    w_out, sem_out, w_qkv, sem_qkv, grad_mixed = refs[29:]
    first_copies = tile_copies(where, out_tiles, w_out, sem_out)
    last_copies = tile_copies(where, qkv_tiles, w_qkv, sem_qkv)
    for copy in first_copies + last_copies:
        copy.start()
    norm_back_kernel(gain, v_ref, p_ref, c_ref, residual, grad_ref, low_ref, term)
    for copy in first_copies:
        copy.wait()
    grad_mixed[...] = dot_nt(low_ref[...], w_out[...]).astype(BF16)
    span = (share + 2) * head
    packs, pack = bias.shape[0], bias.shape[1]
    query_term[...] = jnp.zeros_like(query_term)
    key_term[...] = jnp.zeros_like(key_term)
    scale = head ** (-0.5)

    def group(g, carry):
        def part(h):
            return pl.ds(pl.multiple_of(g * span + h * head, head), head)

        for b in range(packs):
            rows = slice(b * pack, (b + 1) * pack)
            cos_b, sin_b = cosine[rows, :], sine[rows, :]
            key_raw = proj[rows, part(share)]
            key_rows = head_forward(key_raw, key_gain[...], cos_b, sin_b).astype(BF16)
            value = proj[rows, part(share + 1)].astype(BF16)
            grad_key = jnp.zeros((pack, head), F32)
            grad_value = jnp.zeros((pack, head), F32)
            for h in range(share):
                query_raw = proj[rows, part(h)]
                query = head_forward(query_raw, query_gain[...], cos_b, sin_b).astype(BF16)
                probs = soft(query, key_rows, bias[b])
                at = pl.multiple_of((g * share + h) * head, head)
                upstream = grad_mixed[rows, pl.ds(at, head)]
                grad_value += dot_tn(probs.astype(BF16), upstream)
                grad_probs = dot_nt(upstream, value)
                grad_scores = probs * (
                    grad_probs - jnp.sum(probs * grad_probs, -1, keepdims=True)
                )
                grad_scores = grad_scores.astype(BF16)
                grad_key += dot_tn(grad_scores, query)
                grad_query, extra = head_back(
                    dot(grad_scores, key_rows) * scale, query_raw, query_gain[...], cos_b, sin_b
                )
                query_term[...] += extra
                grad_qkv[rows, part(h)] = grad_query.astype(BF16)
            grad_key, extra = head_back(grad_key * scale, key_raw, key_gain[...], cos_b, sin_b)
            key_term[...] += extra
            grad_qkv[rows, part(share)] = grad_key.astype(BF16)
            grad_qkv[rows, part(share + 1)] = grad_value.astype(BF16)
        return carry

    lax.fori_loop(0, w_qkv.shape[1] // span, group, 0)
    for copy in last_copies:
        copy.wait()
    partial[...] = dot_nt(grad_qkv[...], w_qkv[...])


def finish_kernel(spot, tiles, *refs, widths):
    outs = refs[-len(widths):]
    at = 0
    for out, width in zip(outs, widths):
        out[0] = tiles[0, 0, :, at:at + width].astype(F32)
        at += width


def finish(spot, tiles, layer, shapes, widths, row_split, previous):
    rows = tiles.shape[2]

    def out_map(width):
        if row_split:
            return pl.BlockSpec(
                (1, rows, width), lambda m, j, s: (layer, s[m], s[2 + PLANE * m + j])
            )
        return pl.BlockSpec(
            (1, rows, width), lambda m, j, s: (layer, 0, s[2 + PLANE * m + j] * 2 + s[m])
        )

    extra = [] if previous is None else list(previous)
    aliases = {2 + k: k for k in range(len(extra))}
    return pl.pallas_call(
        functools.partial(finish_kernel, widths=widths),
        grid_spec=pltpu.PrefetchScalarGridSpec(
            num_scalar_prefetch=1,
            grid=(2, PLANE),
            in_specs=[pl.BlockSpec((1, 1, rows, sum(widths)), lambda m, j, s: (m, j, 0, 0))]
            + [pl.BlockSpec(memory_space=pl.ANY)] * len(extra),
            out_specs=[out_map(w) for w in widths],
        ),
        out_shape=[jax.ShapeDtypeStruct(s, F32) for s in shapes],
        input_output_aliases=aliases,
        cost_estimate=pl.CostEstimate(
            flops=0, bytes_accessed=6 * tiles.size, transcendentals=0
        ),
        name="finish",
    )(spot, tiles, *extra)


def layout(lengths, row_count):
    seq_ends = jnp.cumsum(lengths, 1)
    starts = seq_ends - lengths
    indices = jnp.arange(row_count, dtype=jnp.int32)
    segment = jnp.sum((indices[None, :, None] >= seq_ends[:, None, :]).astype(jnp.int32), 2)
    owners = segment[:, :, None] == jnp.arange(lengths.shape[1], dtype=jnp.int32)[None, None, :]
    position = indices[None, :] - jnp.sum(jnp.where(owners, starts[:, None, :], 0), 2)
    visible = (segment[:, :, None] == segment[:, None, :]) & (
        indices[None, :, None] >= indices[None, None, :]
    )
    return position, jnp.where(visible, 0.0, MASKED).astype(F32)


def rope_tables(position, head_width):
    half_width = head_width // 2
    frequency = THETA ** (-jnp.arange(half_width, dtype=F32) * 2.0 / head_width)
    angles = position.reshape(-1).astype(F32)[:, None] * frequency
    cosine, sine = jnp.cos(angles), jnp.sin(angles)
    return jnp.concatenate([cosine, cosine], 1), jnp.concatenate([-sine, sine], 1)


def body(
    tokens,
    lengths,
    cotangent,
    attn_gain,
    w_query,
    w_key,
    w_value,
    query_gain,
    key_gain,
    w_output,
    mlp_gain,
    w_gate,
    w_up,
    w_down,
    links=None,
):
    send = links.send
    groups = links.groups
    row_count, width = tokens.shape
    layer_count = w_query.shape[0]
    head_width = query_gain.shape[1] * groups
    kv_heads = w_key.shape[2] // head_width
    share = w_query.shape[2] // w_key.shape[2]
    hidden_units = w_gate.shape[2]
    blocks = kv_heads // 2
    unit = hidden_units // (2 * blocks)
    q_width = share * head_width

    replica = lax.axis_index("replica")
    z = lax.axis_index("group")
    core = replica % 2
    plane = (replica // 2) % PLANE
    step_first = 1 + core
    step_second = 2 - core
    planes = [plane, plane ^ step_first, plane ^ step_second, plane ^ 3]
    where = jnp.stack(
        [z] + [(z + groups - d) % groups for d in range(1, groups)] + planes
    ).astype(jnp.int32)
    partner_planes = [planes[0], planes[2], planes[1], planes[3]]
    spot = jnp.stack([core, 1 - core] + planes + partner_planes).astype(jnp.int32)

    gains_own = jnp.concatenate([attn_gain, mlp_gain, query_gain, key_gain], 1)
    gains = jnp.zeros((groups,) + gains_own.shape, BF16)
    gains = lax.dynamic_update_index_in_dim(gains, gains_own, z, 0)
    for d in range(1, groups):
        gains = lax.dynamic_update_index_in_dim(
            gains, send(gains_own, links.shift[d]), (z + groups - d) % groups, 0
        )
    part = attn_gain.shape[1]
    head_part = query_gain.shape[1]

    def gain_of(start, size, layer):
        return gains[:, layer, start:start + size].reshape(1, -1).astype(F32)

    def pair_rows(rows):
        other = send(rows, links.pair)
        return jnp.concatenate(
            [jnp.where(core == 0, rows, other), jnp.where(core == 0, other, rows)], 0
        )

    position, bias = layout(pair_rows(lengths), row_count)
    cosine, sine = rope_tables(position, head_width)

    def half_columns(weight):
        shaped = weight.reshape(weight.shape[0], blocks, 2, -1)
        return lax.dynamic_index_in_dim(shaped, core, 2, keepdims=False)

    def half_rows(weight):
        shaped = weight.reshape(2, -1, weight.shape[1])
        return lax.dynamic_index_in_dim(shaped, core, 0, keepdims=False)

    def own_chunks(layer):
        rows = w_query.shape[1]
        qkv = jnp.concatenate(
            [half_columns(w_query[layer]), half_columns(w_key[layer]), half_columns(w_value[layer])],
            -1,
        ).reshape(rows, -1)
        gate_up = jnp.concatenate(
            [half_columns(w_gate[layer]), half_columns(w_up[layer])], -1
        ).reshape(rows, -1)
        return [qkv, half_rows(w_output[layer]), gate_up, half_rows(w_down[layer])]

    def gather(own, after):
        tile_width = own.shape[1] // PLANE
        tile = lax.dynamic_slice_in_dim(own, plane * tile_width, tile_width, 1)
        if after is not None:
            tile, after = lax.optimization_barrier((tile, after))
        arrived = [send(tile, links.shift[d]) for d in range(1, groups)]
        near = jnp.stack(arrived)
        first = send(near, links.first)
        second = send(near, links.second)
        both = send(first, links.second)
        return (own, near, first, second, both), arrived

    weights = []
    after = None
    for layer in range(layer_count):
        held = []
        for own in own_chunks(layer):
            full, after = gather(own, after)
            held.append(full)
        weights.append(held)

    def exchange(partial):
        return send(partial, links.pair)

    def own_rows(rows):
        return lax.dynamic_slice_in_dim(rows, core * row_count, row_count, 0)

    def shape(columns, kind):
        return jax.ShapeDtypeStruct((2 * row_count, columns), kind)

    qkv_columns = blocks * (q_width + 2 * head_width)
    mixed_columns = blocks * q_width
    hidden_columns = blocks * unit
    forms = (head_width, share)

    parts = [pair_rows(tokens)]
    kept = []
    for layer in range(layer_count):
        t_qkv, t_out, t_gu, t_dn = weights[layer]
        attn_g = gain_of(0, part, layer)
        mlp_g = gain_of(part, part, layer)
        query_g = gain_of(2 * part, head_part, layer)
        key_g = gain_of(2 * part + head_part, head_part, layer)
        state, normed, proj, mixed, partial = call(
            functools.partial(attn_forward_kernel, len(parts), *forms),
            "attn_forward",
            [where, attn_g, query_g, key_g, cosine, sine, bias, *parts, *t_qkv, *t_out],
            [SMEM] + [VMEM] * (6 + len(parts)) + [ANY] * 10,
            [
                shape(width, F32),
                shape(width, BF16),
                shape(qkv_columns, F32),
                shape(mixed_columns, BF16),
                shape(width, F32),
            ],
            tile_scratch(t_qkv) + tile_scratch(t_out),
            4 * row_count * width * (qkv_columns + mixed_columns),
        )
        came = exchange(partial)
        middle, mlp_in, gate_up, hidden = call(
            functools.partial(mlp_forward_kernel, unit),
            "mlp_forward",
            [where, mlp_g, state, partial, came, *t_gu],
            [SMEM] + [VMEM] * 4 + [ANY] * 5,
            [
                shape(width, F32),
                shape(width, BF16),
                shape(2 * hidden_columns, F32),
                shape(hidden_columns, BF16),
            ],
            tile_scratch(t_gu),
            8 * row_count * width * hidden_columns,
        )
        (partial,) = call(
            down_kernel,
            "down",
            [where, hidden, *t_dn],
            [SMEM, VMEM] + [ANY] * 5,
            [shape(width, F32)],
            tile_scratch(t_dn),
            4 * row_count * width * hidden_columns,
        )
        came = exchange(partial)
        parts = [middle, partial, came]
        kept.append((state, normed, proj, mixed, middle, mlp_in, gate_up, hidden,
                     attn_g, mlp_g, query_g, key_g))
    result_tokens = own_rows(parts[0] + (parts[1] + parts[2])).astype(BF16)

    def reduce_tiles(rows_bf, cols_bf):
        count = cols_bf.shape[1] // PLANE
        picked = [
            lax.dynamic_slice_in_dim(cols_bf, index * count, count, 1) for index in planes
        ]
        away = dot_tn(rows_bf, jnp.concatenate([picked[3], picked[1]], 1)).astype(BF16)
        came = send(away, links.first)
        mine = dot_tn(rows_bf, jnp.concatenate([picked[2], picked[0]], 1)) + came.astype(F32)
        away = mine[:, :count].astype(BF16)
        came = send(away, links.second)
        mine = mine[:, count:] + came.astype(F32)
        for perm in links.outer:
            mine = mine.astype(BF16)
            mine = mine.astype(F32) + send(mine, perm).astype(F32)
        mine = mine.astype(BF16).reshape(groups, -1, count)
        total = lax.dynamic_index_in_dim(mine, z, 0, keepdims=False).astype(F32)
        for d in range(1, groups):
            leaving = lax.dynamic_index_in_dim(mine, (z + d) % groups, 0, keepdims=False)
            total = total + send(leaving, links.shift[d]).astype(F32)
        tile = total.astype(BF16)
        first = send(tile, links.first)
        second = send(tile, links.second)
        both = send(first, links.second)
        tiles = jnp.stack([tile, first, second, both])
        return jnp.stack([tiles, send(tiles, links.pair)])

    gate_shape, down_shape = w_gate.shape, w_down.shape
    row_shape = jax.ShapeDtypeStruct((1, width), F32)
    head_shape = jax.ShapeDtypeStruct((1, head_width), F32)
    branch = pair_rows(cotangent)
    gradient = branch
    outs = [None] * 4
    gain_terms = [None] * layer_count
    for layer in reversed(range(layer_count)):
        t_qkv, t_out, t_gu, t_dn = weights[layer]
        (state, normed, proj, mixed, middle, mlp_in, gate_up, hidden,
         attn_g, mlp_g, query_g, key_g) = kept[layer]
        outs[3] = finish(
            spot, reduce_tiles(hidden, branch), layer, [down_shape],
            [width // PLANE], True, outs[3],
        )
        grad_gu, partial = call(
            functools.partial(mlp_back_kernel, unit),
            "mlp_back",
            [where, branch, gate_up, *t_dn, *t_gu],
            [SMEM] + [VMEM] * 2 + [ANY] * 10,
            [shape(2 * hidden_columns, BF16), shape(width, F32)],
            tile_scratch(t_dn) + tile_scratch(t_gu),
            12 * row_count * width * hidden_columns,
        )
        came = exchange(partial)
        outs[2] = finish(
            spot, reduce_tiles(mlp_in, grad_gu), layer, [gate_shape, gate_shape],
            [unit, unit], False, outs[2],
        )
        grad_middle, grad_out, mlp_term, grad_qkv, query_term, key_term, partial = call(
            functools.partial(attn_back_kernel, *forms),
            "attn_back",
            [where, mlp_g, query_g, key_g, cosine, sine, bias,
             middle, partial, came, gradient, proj, *t_out, *t_qkv],
            [SMEM] + [VMEM] * 11 + [ANY] * 10,
            [
                shape(width, F32),
                shape(width, BF16),
                row_shape,
                shape(qkv_columns, BF16),
                head_shape,
                head_shape,
                shape(width, F32),
            ],
            tile_scratch(t_out) + tile_scratch(t_qkv)
            + [pltpu.VMEM((2 * row_count, mixed_columns), BF16)],
            4 * row_count * width * (qkv_columns + mixed_columns),
        )
        came = exchange(partial)
        outs[1] = finish(
            spot, reduce_tiles(mixed, grad_out), layer, [w_output.shape],
            [width // PLANE], True, outs[1],
        )
        outs[0] = finish(
            spot, reduce_tiles(normed, grad_qkv), layer,
            [w_query.shape, w_key.shape, w_value.shape],
            [q_width, head_width, head_width], False, outs[0],
        )
        gradient, branch, attn_term = call(
            norm_back_kernel,
            "norm_back",
            [attn_g, state, partial, came, grad_middle],
            [VMEM] * 5,
            [shape(width, F32), shape(width, BF16), row_shape],
            [],
        )
        heads_term = jnp.concatenate([query_term, key_term], 1)
        heads_term = heads_term + send(heads_term, links.pair)
        terms = jnp.concatenate([attn_term, mlp_term, heads_term], 1)
        for perm in links.turns + links.outer:
            terms = terms + send(terms, perm)
        gain_terms[layer] = terms
    gain_sums = jnp.concatenate(gain_terms, 0)

    def own_gain(start, size):
        return lax.dynamic_slice_in_dim(gain_sums, start + z * size, size, 1)

    return (
        result_tokens,
        own_rows(gradient),
        own_gain(0, part),
        outs[0][0],
        outs[0][1],
        outs[0][2],
        own_gain(2 * width, head_part),
        own_gain(2 * width + head_width, head_part),
        outs[1][0],
        own_gain(width, part),
        outs[2][0],
        outs[2][1],
        outs[3][0],
    )


def solution(mesh):
    links = Links(mesh.shape["replica"], mesh.shape["group"])
    return jax.shard_map(
        functools.partial(body, links=links),
        mesh=mesh,
        in_specs=(
            P(AXES, None),
            P(AXES, None),
            P(AXES, None),
            P(None, "group"),
            P(None, "group", None),
            P(None, "group", None),
            P(None, "group", None),
            P(None, "group"),
            P(None, "group"),
            P(None, "group", None),
            P(None, "group"),
            P(None, "group", None),
            P(None, "group", None),
            P(None, "group", None),
        ),
        out_specs=(
            P(AXES, None),
            P(AXES, None),
            P(None, "group"),
            P(None, "group", None),
            P(None, "group", None),
            P(None, "group", None),
            P(None, "group"),
            P(None, "group"),
            P(None, "group", None),
            P(None, "group"),
            P(None, "group", None),
            P(None, "group", None),
            P(None, "group", None),
        ),
        check_vma=False,
    )
```

```python
import functools

import jax
import jax.numpy as jnp
from jax import lax
from jax.experimental import pallas as pl
from jax.experimental.pallas import tpu as pltpu
from jax.sharding import PartitionSpec as P

EPS = 1e-06
THETA = 1000000.0
MASKED = -1e30
AXES = ("replica", "group")
BF16 = jnp.bfloat16
F32 = jnp.float32
PLANE = 4


def dot(a, b):
    return jnp.dot(a, b, preferred_element_type=F32)


def dot_nt(a, b):
    return lax.dot_general(a, b, (((1,), (1,)), ((), ())), preferred_element_type=F32)


def dot_tn(a, b):
    return lax.dot_general(a, b, (((0,), (0,)), ((), ())), preferred_element_type=F32)


def rmsnorm(vector, gain_vec):
    return vector * lax.rsqrt(jnp.mean(vector * vector, -1, keepdims=True) + EPS) * gain_vec


class Tiles:
    def __init__(self, refs, at):
        self.refs, self.at = refs, at


class Links:
    def __init__(self, replicas, groups):
        self.replicas, self.groups = replicas, groups

        def pairs(move):
            return [
                (r * groups + g, move(r, g)[0] * groups + move(r, g)[1])
                for r in range(replicas)
                for g in range(groups)
            ]

        self.pair = pairs(lambda r, g: (r ^ 1, g))
        self.first = pairs(lambda r, g: (r ^ (4 if r & 1 else 2), g))
        self.second = pairs(lambda r, g: (r ^ (2 if r & 1 else 4), g))
        self.turns = [pairs(lambda r, g, b=b: (r ^ b, g)) for b in (2, 4)]
        bit = 1
        while bit < groups:
            self.turns.append(pairs(lambda r, g, b=bit: (r, g ^ b)))
            bit *= 2
        self.outer = []
        bit = 8
        while bit < replicas:
            self.outer.append(pairs(lambda r, g, b=bit: (r ^ b, g)))
            bit *= 2

    @staticmethod
    def send(x, perm):
        return lax.ppermute(x, AXES, perm)


VMEM = pl.BlockSpec(memory_space=pltpu.VMEM)
SMEM = pl.BlockSpec(memory_space=pltpu.SMEM)
ANY = pl.BlockSpec(memory_space=pl.ANY)
STRIP = 64


def tile_copies(where, sources, weight, sems, offset=0):
    own, rest = sources[0], sources[1:]
    rows, columns = own.shape
    width = columns // PLANE
    others = weight.shape[0] // rows - 1

    def band(z):
        return pl.ds(pl.multiple_of(z * rows, rows), rows)

    copies = [pltpu.make_async_copy(own, weight.at[band(where[0])], sems.at[0])]
    for j, source in enumerate(rest):
        column = pl.multiple_of(where[1 + others + j] * width, 128)
        for d in range(others):
            copies.append(
                pltpu.make_async_copy(
                    source.at[d, :, pl.ds(offset, width)],
                    weight.at[band(where[1 + d]), pl.ds(column, width)],
                    sems.at[len(copies)],
                )
            )
    return copies


def tile_scratch(tiles):
    own, near = tiles.refs[0], tiles.refs[1]
    groups = near.shape[0] + 1
    return [
        pltpu.VMEM((groups * own.shape[0], own.shape[1]), BF16),
        pltpu.SemaphoreType.DMA((1 + PLANE * (groups - 1),)),
    ]


def call(kernel, name, inputs, specs, outs, scratch, flops=0, vmem=52):
    moved = sum(x.size * x.dtype.itemsize for x in inputs)
    moved += sum(x.size * x.dtype.itemsize for x in outs)
    return pl.pallas_call(
        kernel,
        in_specs=specs,
        out_specs=[VMEM] * len(outs),
        out_shape=outs,
        scratch_shapes=scratch,
        compiler_params=pltpu.CompilerParams(vmem_limit_bytes=vmem << 20),
        cost_estimate=pl.CostEstimate(flops=flops, bytes_accessed=moved, transcendentals=0),
        name=name,
    )(*inputs)


def strips(rows, step):
    def run(i, carry):
        step(pl.ds(pl.multiple_of(i * STRIP, STRIP), STRIP))
        return carry

    lax.fori_loop(0, rows // STRIP, run, 0)


def head_forward(v, gain_vec, cosine, sine):
    r = lax.rsqrt(jnp.mean(v * v, -1, keepdims=True) + EPS)
    n = v * r * gain_vec
    return n * cosine + pltpu.roll(n, n.shape[-1] // 2, 1) * sine


def head_back(grad, v, gain_vec, cosine, sine):
    r = lax.rsqrt(jnp.mean(v * v, -1, keepdims=True) + EPS)
    grad = grad * cosine + pltpu.roll(grad * sine, grad.shape[-1] // 2, 1)
    unit_v = v * r
    gain_term = jnp.sum(grad * unit_v, 0, keepdims=True)
    inner = grad * gain_vec
    return r * (inner - unit_v * jnp.mean(unit_v * inner, -1, keepdims=True)), gain_term


def soft(queries, key_rows, bias):
    scores = dot_nt(queries, key_rows) * queries.shape[-1] ** (-0.5) + bias
    exponent = jnp.exp(scores - jnp.max(scores, -1, keepdims=True))
    return exponent / jnp.sum(exponent, -1, keepdims=True)


def attn_forward_kernel(count, head, share, qkv_at, out_at, *refs):
    where, gain, query_gain, key_gain, cosine, sine, bias = refs[:7]
    parts = refs[7:7 + count]
    qkv_tiles = refs[7 + count:12 + count]
    out_tiles = refs[12 + count:17 + count]
    state, normed, proj, mixed, partial = refs[17 + count:22 + count]
    w_qkv, sem_qkv, w_out, sem_out = refs[22 + count:]
    first_copies = tile_copies(where, qkv_tiles, w_qkv, sem_qkv, qkv_at)
    last_copies = tile_copies(where, out_tiles, w_out, sem_out, out_at)
    for copy in first_copies + last_copies:
        copy.start()

    def prepare(rows):
        total = parts[0][rows, :].astype(F32)
        for part in parts[1:]:
            total = total + part[rows, :]
        state[rows, :] = total
        normed[rows, :] = rmsnorm(total, gain[...]).astype(BF16)

    strips(state.shape[0], prepare)
    for copy in first_copies:
        copy.wait()
    span = (share + 2) * head
    packs, pack = bias.shape[0], bias.shape[1]

    def group(g, carry):
        columns = pl.ds(pl.multiple_of(g * span, span), span)
        proj[:, columns] = dot(normed[...], w_qkv[:, columns])
        base = g * span
        heads = [
            head_forward(
                proj[:, pl.ds(pl.multiple_of(base + h * head, head), head)],
                query_gain[...] if h < share else key_gain[...],
                cosine[...],
                sine[...],
            ).astype(BF16)
            for h in range(share + 1)
        ]
        value = proj[:, pl.ds(pl.multiple_of(base + (share + 1) * head, head), head)].astype(BF16)
        for b in range(packs):
            rows = slice(b * pack, (b + 1) * pack)
            for h in range(share):
                probs = soft(heads[h][rows], heads[share][rows], bias[b])
                at = pl.multiple_of((g * share + h) * head, head)
                mixed[rows, pl.ds(at, head)] = dot(probs.astype(BF16), value[rows]).astype(BF16)
        return carry

    lax.fori_loop(0, w_qkv.shape[1] // span, group, 0)
    for copy in last_copies:
        copy.wait()
    partial[...] = dot(mixed[...], w_out[...])


def mlp_forward_kernel(unit, at, *refs):
    where, gain, s_ref, p_ref, c_ref = refs[:5]
    tiles = refs[5:10]
    middle, mlp_in, gate_up, hidden = refs[10:14]
    weight, sems = refs[14:]
    copies = tile_copies(where, tiles, weight, sems, at)
    for copy in copies:
        copy.start()

    def prepare(rows):
        total = s_ref[rows, :] + (p_ref[rows, :] + c_ref[rows, :])
        middle[rows, :] = total
        mlp_in[rows, :] = rmsnorm(total, gain[...]).astype(BF16)

    strips(middle.shape[0], prepare)
    for copy in copies:
        copy.wait()

    def block(j, carry):
        columns = pl.ds(pl.multiple_of(j * 2 * unit, 2 * unit), 2 * unit)
        gate_up[:, columns] = dot(mlp_in[...], weight[:, columns])
        gates = gate_up[:, pl.ds(pl.multiple_of(j * 2 * unit, unit), unit)]
        ups = gate_up[:, pl.ds(pl.multiple_of(j * 2 * unit + unit, unit), unit)]
        hidden[:, pl.ds(pl.multiple_of(j * unit, unit), unit)] = (
            gates / (1.0 + jnp.exp(-gates)) * ups
        ).astype(BF16)
        return carry

    lax.fori_loop(0, weight.shape[1] // (2 * unit), block, 0)


def down_kernel(at, where, hidden, *refs):
    tiles, partial, weight, sems = refs[:5], refs[5], refs[6], refs[7]
    copies = tile_copies(where, tiles, weight, sems, at)
    for copy in copies:
        copy.start()
    for copy in copies:
        copy.wait()
    partial[...] = dot(hidden[...], weight[...])


def mlp_back_kernel(unit, down_at, gu_at, *refs):
    where, branch, gate_up = refs[:3]
    down_tiles, gu_tiles = refs[3:8], refs[8:13]
    grad_gu, partial = refs[13:15]
    w_down, sem_down, w_gu, sem_gu = refs[15:]
    first_copies = tile_copies(where, down_tiles, w_down, sem_down, down_at)
    last_copies = tile_copies(where, gu_tiles, w_gu, sem_gu, gu_at)
    for copy in first_copies + last_copies:
        copy.start()
    for copy in first_copies:
        copy.wait()

    def block(j, carry):
        grad = dot_nt(branch[...], w_down[pl.ds(pl.multiple_of(j * unit, unit), unit), :])
        at = pl.ds(pl.multiple_of(j * 2 * unit, unit), unit)
        past = pl.ds(pl.multiple_of(j * 2 * unit + unit, unit), unit)
        gates = gate_up[:, at]
        sigma = 1.0 / (1.0 + jnp.exp(-gates))
        silu = gates * sigma
        grad_gu[:, at] = (grad * gate_up[:, past] * (sigma + silu * (1.0 - sigma))).astype(BF16)
        grad_gu[:, past] = (grad * silu).astype(BF16)
        return carry

    lax.fori_loop(0, w_down.shape[0] // unit, block, 0)
    for copy in last_copies:
        copy.wait()
    partial[...] = dot_nt(grad_gu[...], w_gu[...])


def norm_back(rows, v_ref, gain, p_ref, c_ref, residual, grad_ref, low_ref, term):
    v = v_ref[rows, :]
    r = lax.rsqrt(jnp.mean(v * v, -1, keepdims=True) + EPS)
    grad = p_ref[rows, :] + c_ref[rows, :]
    unit_v = v * r
    term[...] += jnp.sum(grad * unit_v, 0, keepdims=True)
    inner = grad * gain[...]
    total = residual[rows, :].astype(F32) + r * (
        inner - unit_v * jnp.mean(unit_v * inner, -1, keepdims=True)
    )
    grad_ref[rows, :] = total
    low_ref[rows, :] = total.astype(BF16)


def norm_back_kernel(gain, v_ref, p_ref, c_ref, residual, grad_ref, low_ref, term):
    term[...] = jnp.zeros_like(term)
    strips(
        v_ref.shape[0],
        lambda rows: norm_back(rows, v_ref, gain, p_ref, c_ref, residual, grad_ref, low_ref, term),
    )


def attn_back_kernel(head, share, out_at, qkv_at, *refs):
    where, gain, query_gain, key_gain, cosine, sine, bias = refs[:7]
    v_ref, p_ref, c_ref, residual, proj = refs[7:12]
    out_tiles, qkv_tiles = refs[12:17], refs[17:22]
    grad_ref, low_ref, term, grad_qkv, query_term, key_term, partial = refs[22:29]
    w_out, sem_out, w_qkv, sem_qkv, grad_mixed = refs[29:]
    first_copies = tile_copies(where, out_tiles, w_out, sem_out, out_at)
    last_copies = tile_copies(where, qkv_tiles, w_qkv, sem_qkv, qkv_at)
    for copy in first_copies + last_copies:
        copy.start()
    norm_back_kernel(gain, v_ref, p_ref, c_ref, residual, grad_ref, low_ref, term)
    for copy in first_copies:
        copy.wait()
    grad_mixed[...] = dot_nt(low_ref[...], w_out[...]).astype(BF16)
    span = (share + 2) * head
    packs, pack = bias.shape[0], bias.shape[1]
    query_term[...] = jnp.zeros_like(query_term)
    key_term[...] = jnp.zeros_like(key_term)
    scale = head ** (-0.5)

    def group(g, carry):
        def part(h):
            return pl.ds(pl.multiple_of(g * span + h * head, head), head)

        for b in range(packs):
            rows = slice(b * pack, (b + 1) * pack)
            cos_b, sin_b = cosine[rows, :], sine[rows, :]
            key_raw = proj[rows, part(share)]
            key_rows = head_forward(key_raw, key_gain[...], cos_b, sin_b).astype(BF16)
            value = proj[rows, part(share + 1)].astype(BF16)
            grad_key = jnp.zeros((pack, head), F32)
            grad_value = jnp.zeros((pack, head), F32)
            for h in range(share):
                query_raw = proj[rows, part(h)]
                query = head_forward(query_raw, query_gain[...], cos_b, sin_b).astype(BF16)
                probs = soft(query, key_rows, bias[b])
                at = pl.multiple_of((g * share + h) * head, head)
                upstream = grad_mixed[rows, pl.ds(at, head)]
                grad_value += dot_tn(probs.astype(BF16), upstream)
                grad_probs = dot_nt(upstream, value)
                grad_scores = probs * (
                    grad_probs - jnp.sum(probs * grad_probs, -1, keepdims=True)
                )
                grad_scores = grad_scores.astype(BF16)
                grad_key += dot_tn(grad_scores, query)
                grad_query, extra = head_back(
                    dot(grad_scores, key_rows) * scale, query_raw, query_gain[...], cos_b, sin_b
                )
                query_term[...] += extra
                grad_qkv[rows, part(h)] = grad_query.astype(BF16)
            grad_key, extra = head_back(grad_key * scale, key_raw, key_gain[...], cos_b, sin_b)
            key_term[...] += extra
            grad_qkv[rows, part(share)] = grad_key.astype(BF16)
            grad_qkv[rows, part(share + 1)] = grad_value.astype(BF16)
        return carry

    lax.fori_loop(0, w_qkv.shape[1] // span, group, 0)
    for copy in last_copies:
        copy.wait()
    partial[...] = dot_nt(grad_qkv[...], w_qkv[...])


def finish_kernel(spot, tiles, *refs, widths):
    outs = refs[-len(widths):]
    at = 0
    for out, width in zip(outs, widths):
        out[0] = tiles[0, 0, :, at:at + width].astype(F32)
        at += width


def finish(spot, tiles, layer, shapes, widths, row_split, previous):
    rows = tiles.shape[2]

    def out_map(width):
        if row_split:
            return pl.BlockSpec(
                (1, rows, width), lambda m, j, s: (layer, s[m], s[2 + PLANE * m + j])
            )
        return pl.BlockSpec(
            (1, rows, width), lambda m, j, s: (layer, 0, s[2 + PLANE * m + j] * 2 + s[m])
        )

    extra = [] if previous is None else list(previous)
    aliases = {2 + k: k for k in range(len(extra))}
    return pl.pallas_call(
        functools.partial(finish_kernel, widths=widths),
        grid_spec=pltpu.PrefetchScalarGridSpec(
            num_scalar_prefetch=1,
            grid=(2, PLANE),
            in_specs=[pl.BlockSpec((1, 1, rows, sum(widths)), lambda m, j, s: (m, j, 0, 0))]
            + [pl.BlockSpec(memory_space=pl.ANY)] * len(extra),
            out_specs=[out_map(w) for w in widths],
        ),
        out_shape=[jax.ShapeDtypeStruct(s, F32) for s in shapes],
        input_output_aliases=aliases,
        cost_estimate=pl.CostEstimate(
            flops=0, bytes_accessed=6 * tiles.size, transcendentals=0
        ),
        name="finish",
    )(spot, tiles, *extra)


def layout(lengths, row_count):
    seq_ends = jnp.cumsum(lengths, 1)
    starts = seq_ends - lengths
    indices = jnp.arange(row_count, dtype=jnp.int32)
    segment = jnp.sum((indices[None, :, None] >= seq_ends[:, None, :]).astype(jnp.int32), 2)
    owners = segment[:, :, None] == jnp.arange(lengths.shape[1], dtype=jnp.int32)[None, None, :]
    position = indices[None, :] - jnp.sum(jnp.where(owners, starts[:, None, :], 0), 2)
    visible = (segment[:, :, None] == segment[:, None, :]) & (
        indices[None, :, None] >= indices[None, None, :]
    )
    return position, jnp.where(visible, 0.0, MASKED).astype(F32)


def rope_tables(position, head_width):
    half_width = head_width // 2
    frequency = THETA ** (-jnp.arange(half_width, dtype=F32) * 2.0 / head_width)
    angles = position.reshape(-1).astype(F32)[:, None] * frequency
    cosine, sine = jnp.cos(angles), jnp.sin(angles)
    return jnp.concatenate([cosine, cosine], 1), jnp.concatenate([-sine, sine], 1)


def body(
    tokens,
    lengths,
    cotangent,
    attn_gain,
    w_query,
    w_key,
    w_value,
    query_gain,
    key_gain,
    w_output,
    mlp_gain,
    w_gate,
    w_up,
    w_down,
    links=None,
):
    send = links.send
    groups = links.groups
    row_count, width = tokens.shape
    layer_count = w_query.shape[0]
    head_width = query_gain.shape[1] * groups
    kv_heads = w_key.shape[2] // head_width
    share = w_query.shape[2] // w_key.shape[2]
    hidden_units = w_gate.shape[2]
    blocks = kv_heads // 2
    unit = hidden_units // (2 * blocks)
    q_width = share * head_width

    replica = lax.axis_index("replica")
    z = lax.axis_index("group")
    core = replica % 2
    plane = (replica // 2) % PLANE
    step_first = 1 + core
    step_second = 2 - core
    planes = [plane, plane ^ step_first, plane ^ step_second, plane ^ 3]
    where = jnp.stack(
        [z] + [(z + d) % groups for d in range(1, groups)] + planes
    ).astype(jnp.int32)
    partner_planes = [planes[0], planes[2], planes[1], planes[3]]
    spot = jnp.stack([core, 1 - core] + planes + partner_planes).astype(jnp.int32)

    part = attn_gain.shape[1]
    head_part = query_gain.shape[1]

    def pair_rows(rows):
        other = send(rows, links.pair)
        return jnp.concatenate(
            [jnp.where(core == 0, rows, other), jnp.where(core == 0, other, rows)], 0
        )

    position, bias = layout(pair_rows(lengths), row_count)
    cosine, sine = rope_tables(position, head_width)

    def half_columns(weight):
        shaped = weight.reshape(weight.shape[0], blocks, 2, -1)
        return lax.dynamic_index_in_dim(shaped, core, 2, keepdims=False)

    def half_rows(weight):
        shaped = weight.reshape(2, -1, weight.shape[1])
        return lax.dynamic_index_in_dim(shaped, core, 0, keepdims=False)

    def own_chunks(layer):
        rows = w_query.shape[1]
        qkv = jnp.concatenate(
            [half_columns(w_query[layer]), half_columns(w_key[layer]), half_columns(w_value[layer])],
            -1,
        ).reshape(rows, -1)
        gate_up = jnp.concatenate(
            [half_columns(w_gate[layer]), half_columns(w_up[layer])], -1
        ).reshape(rows, -1)
        return [qkv, half_rows(w_output[layer]), gate_up, half_rows(w_down[layer])]

    def gather(owns, after, extra=None):
        rows = owns[0].shape[0]
        tile = []
        for own in owns:
            tile_width = own.shape[1] // PLANE
            tile.append(lax.dynamic_slice_in_dim(own, plane * tile_width, tile_width, 1))
        tile = jnp.concatenate(tile, 1)
        if extra is not None:
            tile = jnp.concatenate([tile, extra], 0)
        if after is not None:
            tile, after = lax.optimization_barrier((tile, after))
        column = lax.all_gather(tile, "group", axis=0)
        near = jnp.stack(
            [
                lax.dynamic_index_in_dim(column[:, :rows], (z + d) % groups, 0, keepdims=False)
                for d in range(1, groups)
            ]
        )
        first = send(near, links.first)
        second = send(near, links.second)
        both = send(first, links.second)
        tiles, at = [], 0
        for own in owns:
            tiles.append(Tiles((own, near, first, second, both), at))
            at += own.shape[1] // PLANE
        return tiles, column

    gains_own = jnp.concatenate([attn_gain, mlp_gain, query_gain, key_gain], 1)
    gain_width = gains_own.shape[1]
    weights = []
    after = None
    for layer in range(layer_count):
        qkv, out, gate_up, down = own_chunks(layer)
        if layer == 0:
            tile_width = qkv.shape[1] // PLANE
            slots = 16 * tile_width
            extra = jnp.pad(gains_own.reshape(-1), (0, slots - gains_own.size))
            (t_qkv,), after = gather([qkv], after, extra.reshape(16, tile_width))
            gains = after[:, qkv.shape[0]:].reshape(groups, -1)[:, :gains_own.size]
            gains = gains.reshape(groups, layer_count, gain_width)
            (t_out, t_gu), after = gather([out, gate_up], after)
        else:
            (t_qkv, t_out), after = gather([qkv, out], after)
            (t_gu,), after = gather([gate_up], after)
        (t_dn,), after = gather([down], after)
        weights.append((t_qkv, t_out, t_gu, t_dn))

    def gain_of(start, size, layer):
        return gains[:, layer, start:start + size].reshape(1, -1).astype(F32)

    def exchange(partial):
        return send(partial, links.pair)

    def own_rows(rows):
        return lax.dynamic_slice_in_dim(rows, core * row_count, row_count, 0)

    def shape(columns, kind):
        return jax.ShapeDtypeStruct((2 * row_count, columns), kind)

    qkv_columns = blocks * (q_width + 2 * head_width)
    mixed_columns = blocks * q_width
    hidden_columns = blocks * unit
    forms = (head_width, share)

    parts = [pair_rows(tokens)]
    kept = []
    for layer in range(layer_count):
        t_qkv, t_out, t_gu, t_dn = weights[layer]
        attn_g = gain_of(0, part, layer)
        mlp_g = gain_of(part, part, layer)
        query_g = gain_of(2 * part, head_part, layer)
        key_g = gain_of(2 * part + head_part, head_part, layer)
        state, normed, proj, mixed, partial = call(
            functools.partial(attn_forward_kernel, len(parts), *forms, t_qkv.at, t_out.at),
            "attn_forward",
            [where, attn_g, query_g, key_g, cosine, sine, bias, *parts, *t_qkv.refs, *t_out.refs],
            [SMEM] + [VMEM] * (6 + len(parts)) + [ANY] * 10,
            [
                shape(width, F32),
                shape(width, BF16),
                shape(qkv_columns, F32),
                shape(mixed_columns, BF16),
                shape(width, F32),
            ],
            tile_scratch(t_qkv) + tile_scratch(t_out),
            4 * row_count * width * (qkv_columns + mixed_columns),
        )
        came = exchange(partial)
        middle, mlp_in, gate_up, hidden = call(
            functools.partial(mlp_forward_kernel, unit, t_gu.at),
            "mlp_forward",
            [where, mlp_g, state, partial, came, *t_gu.refs],
            [SMEM] + [VMEM] * 4 + [ANY] * 5,
            [
                shape(width, F32),
                shape(width, BF16),
                shape(2 * hidden_columns, F32),
                shape(hidden_columns, BF16),
            ],
            tile_scratch(t_gu),
            8 * row_count * width * hidden_columns,
        )
        (partial,) = call(
            functools.partial(down_kernel, t_dn.at),
            "down",
            [where, hidden, *t_dn.refs],
            [SMEM, VMEM] + [ANY] * 5,
            [shape(width, F32)],
            tile_scratch(t_dn),
            4 * row_count * width * hidden_columns,
        )
        came = exchange(partial)
        parts = [middle, partial, came]
        kept.append((state, normed, proj, mixed, middle, mlp_in, gate_up, hidden,
                     attn_g, mlp_g, query_g, key_g))
    result_tokens = own_rows(parts[0] + (parts[1] + parts[2])).astype(BF16)

    def reduce_tiles(rows_bf, cols_bf):
        count = cols_bf.shape[1] // PLANE
        picked = [
            lax.dynamic_slice_in_dim(cols_bf, index * count, count, 1) for index in planes
        ]
        away = dot_tn(rows_bf, jnp.concatenate([picked[3], picked[1]], 1)).astype(BF16)
        came = send(away, links.first)
        mine = dot_tn(rows_bf, jnp.concatenate([picked[2], picked[0]], 1)) + came.astype(F32)
        away = mine[:, :count].astype(BF16)
        came = send(away, links.second)
        mine = mine[:, count:] + came.astype(F32)
        for perm in links.outer:
            mine = mine.astype(BF16)
            mine = mine.astype(F32) + send(mine, perm).astype(F32)
        tile = lax.psum_scatter(mine.astype(BF16), "group", scatter_dimension=0, tiled=True)
        first = send(tile, links.first)
        second = send(tile, links.second)
        both = send(first, links.second)
        tiles = jnp.stack([tile, first, second, both])
        return jnp.stack([tiles, send(tiles, links.pair)])

    gate_shape, down_shape = w_gate.shape, w_down.shape
    row_shape = jax.ShapeDtypeStruct((1, width), F32)
    head_shape = jax.ShapeDtypeStruct((1, head_width), F32)
    branch = pair_rows(cotangent)
    gradient = branch
    outs = [None] * 4
    gain_terms = [None] * layer_count
    for layer in reversed(range(layer_count)):
        t_qkv, t_out, t_gu, t_dn = weights[layer]
        (state, normed, proj, mixed, middle, mlp_in, gate_up, hidden,
         attn_g, mlp_g, query_g, key_g) = kept[layer]
        outs[3] = finish(
            spot, reduce_tiles(hidden, branch), layer, [down_shape],
            [width // PLANE], True, outs[3],
        )
        grad_gu, partial = call(
            functools.partial(mlp_back_kernel, unit, t_dn.at, t_gu.at),
            "mlp_back",
            [where, branch, gate_up, *t_dn.refs, *t_gu.refs],
            [SMEM] + [VMEM] * 2 + [ANY] * 10,
            [shape(2 * hidden_columns, BF16), shape(width, F32)],
            tile_scratch(t_dn) + tile_scratch(t_gu),
            12 * row_count * width * hidden_columns,
        )
        came = exchange(partial)
        outs[2] = finish(
            spot, reduce_tiles(mlp_in, grad_gu), layer, [gate_shape, gate_shape],
            [unit, unit], False, outs[2],
        )
        grad_middle, grad_out, mlp_term, grad_qkv, query_term, key_term, partial = call(
            functools.partial(attn_back_kernel, *forms, t_out.at, t_qkv.at),
            "attn_back",
            [where, mlp_g, query_g, key_g, cosine, sine, bias,
             middle, partial, came, gradient, proj, *t_out.refs, *t_qkv.refs],
            [SMEM] + [VMEM] * 11 + [ANY] * 10,
            [
                shape(width, F32),
                shape(width, BF16),
                row_shape,
                shape(qkv_columns, BF16),
                head_shape,
                head_shape,
                shape(width, F32),
            ],
            tile_scratch(t_out) + tile_scratch(t_qkv)
            + [pltpu.VMEM((2 * row_count, mixed_columns), BF16)],
            4 * row_count * width * (qkv_columns + mixed_columns),
        )
        came = exchange(partial)
        outs[1] = finish(
            spot, reduce_tiles(mixed, grad_out), layer, [w_output.shape],
            [width // PLANE], True, outs[1],
        )
        outs[0] = finish(
            spot, reduce_tiles(normed, grad_qkv), layer,
            [w_query.shape, w_key.shape, w_value.shape],
            [q_width, head_width, head_width], False, outs[0],
        )
        gradient, branch, attn_term = call(
            norm_back_kernel,
            "norm_back",
            [attn_g, state, partial, came, grad_middle],
            [VMEM] * 5,
            [shape(width, F32), shape(width, BF16), row_shape],
            [],
        )
        gain_terms[layer] = jnp.concatenate([attn_term, mlp_term, query_term, key_term], 1)
    gain_sums = jnp.concatenate(gain_terms, 0)
    heads_term = gain_sums[:, 2 * width:]
    heads_term = heads_term + send(heads_term, links.pair)
    gain_sums = jnp.concatenate([gain_sums[:, :2 * width], heads_term], 1)
    for perm in links.turns + links.outer:
        gain_sums = gain_sums + send(gain_sums, perm)

    def own_gain(start, size):
        return lax.dynamic_slice_in_dim(gain_sums, start + z * size, size, 1)

    return (
        result_tokens,
        own_rows(gradient),
        own_gain(0, part),
        outs[0][0],
        outs[0][1],
        outs[0][2],
        own_gain(2 * width, head_part),
        own_gain(2 * width + head_width, head_part),
        outs[1][0],
        own_gain(width, part),
        outs[2][0],
        outs[2][1],
        outs[3][0],
    )


def solution(mesh):
    links = Links(mesh.shape["replica"], mesh.shape["group"])
    return jax.shard_map(
        functools.partial(body, links=links),
        mesh=mesh,
        in_specs=(
            P(AXES, None),
            P(AXES, None),
            P(AXES, None),
            P(None, "group"),
            P(None, "group", None),
            P(None, "group", None),
            P(None, "group", None),
            P(None, "group"),
            P(None, "group"),
            P(None, "group", None),
            P(None, "group"),
            P(None, "group", None),
            P(None, "group", None),
            P(None, "group", None),
        ),
        out_specs=(
            P(AXES, None),
            P(AXES, None),
            P(None, "group"),
            P(None, "group", None),
            P(None, "group", None),
            P(None, "group", None),
            P(None, "group"),
            P(None, "group"),
            P(None, "group", None),
            P(None, "group"),
            P(None, "group", None),
            P(None, "group", None),
            P(None, "group", None),
        ),
        check_vma=False,
    )
```

```python
import functools

import jax
import jax.numpy as jnp
from jax import lax
from jax.experimental import pallas as pl
from jax.experimental.pallas import tpu as pltpu
from jax.sharding import PartitionSpec as P

EPS = 1e-06
THETA = 1000000.0
MASKED = -1e30
AXES = ("replica", "group")
BF16 = jnp.bfloat16
F32 = jnp.float32
PLANE = 4
UNIT = 256


def dot(a, b):
    return jnp.dot(a, b, preferred_element_type=F32)


def dot_nt(a, b):
    return lax.dot_general(a, b, (((1,), (1,)), ((), ())), preferred_element_type=F32)


def dot_tn(a, b):
    return lax.dot_general(a, b, (((0,), (0,)), ((), ())), preferred_element_type=F32)


def rmsnorm(vector, gain_vec):
    return vector * lax.rsqrt(jnp.mean(vector * vector, -1, keepdims=True) + EPS) * gain_vec


class Queue:
    def __init__(self, depth):
        self.sent, self.depth = [], depth

    def send(self, x, perm):
        if len(self.sent) >= self.depth:
            x, _ = lax.optimization_barrier((x, self.sent[-self.depth]))
        x = Links.send(x, perm)
        self.sent.append(x)
        return x


class Tiles:
    def __init__(self, refs, at):
        self.refs, self.at = refs, at


class Links:
    def __init__(self, replicas, groups):
        self.replicas, self.groups = replicas, groups

        def pairs(move):
            return [
                (r * groups + g, move(r, g)[0] * groups + move(r, g)[1])
                for r in range(replicas)
                for g in range(groups)
            ]

        self.pair = pairs(lambda r, g: (r ^ 1, g))
        self.first = pairs(lambda r, g: (r ^ (4 if r & 1 else 2), g))
        self.second = pairs(lambda r, g: (r ^ (2 if r & 1 else 4), g))
        self.turns = [pairs(lambda r, g, b=b: (r ^ b, g)) for b in (2, 4)]
        bit = 1
        while bit < groups:
            self.turns.append(pairs(lambda r, g, b=bit: (r, g ^ b)))
            bit *= 2
        self.outer = []
        bit = 8
        while bit < replicas:
            self.outer.append(pairs(lambda r, g, b=bit: (r ^ b, g)))
            bit *= 2

    @staticmethod
    def send(x, perm):
        return lax.ppermute(x, AXES, perm)


VMEM = pl.BlockSpec(memory_space=pltpu.VMEM)
SMEM = pl.BlockSpec(memory_space=pltpu.SMEM)
ANY = pl.BlockSpec(memory_space=pl.ANY)
STRIP = 64


def tile_copies(where, sources, weight, sems, offset=0):
    own, rest = sources[0], sources[1:]
    rows, columns = own.shape
    width = columns // PLANE
    others = weight.shape[0] // rows - 1

    def band(z):
        return pl.ds(pl.multiple_of(z * rows, rows), rows)

    copies = [pltpu.make_async_copy(own, weight.at[band(where[0])], sems.at[0])]
    for j, source in enumerate(rest):
        column = pl.multiple_of(where[1 + others + j] * width, 128)
        for d in range(others):
            for at_row, at_column, tall, wide, to_row, to_column in pieces(rows, width):
                top = pl.multiple_of(where[1 + d] * rows + to_row, 128)
                copies.append(
                    pltpu.make_async_copy(
                        source.at[d, pl.ds(at_row, tall), pl.ds(offset + at_column, wide)],
                        weight.at[pl.ds(top, tall), pl.ds(column + to_column, wide)],
                        sems.at[len(copies)],
                    )
                )
    return copies


def pieces(rows, width):
    if rows == UNIT:
        return [(0, 0, UNIT, width, 0, 0)]
    half, extra = width // 2, UNIT // 2
    return [
        (0, 0, UNIT, width, 0, 0),
        (0, width, extra, half, UNIT, 0),
        (extra, width, extra, half, UNIT, half),
    ]


def pack(tile):
    if tile.shape[0] == UNIT:
        return tile
    half = tile.shape[1] // 2
    return jnp.concatenate(
        [tile[:UNIT], jnp.concatenate([tile[UNIT:, :half], tile[UNIT:, half:]], 0)], 1
    )


def tile_scratch(tiles):
    own, near = tiles.refs[0], tiles.refs[1]
    groups = near.shape[0] + 1
    return [
        pltpu.VMEM((groups * own.shape[0], own.shape[1]), BF16),
        pltpu.SemaphoreType.DMA(
            (1 + PLANE * (groups - 1) * len(pieces(own.shape[0], own.shape[1] // PLANE)),)
        ),
    ]


def call(kernel, name, inputs, specs, outs, scratch, flops=0, vmem=52):
    moved = sum(x.size * x.dtype.itemsize for x in inputs)
    moved += sum(x.size * x.dtype.itemsize for x in outs)
    return pl.pallas_call(
        kernel,
        in_specs=specs,
        out_specs=[VMEM] * len(outs),
        out_shape=outs,
        scratch_shapes=scratch,
        compiler_params=pltpu.CompilerParams(vmem_limit_bytes=vmem << 20),
        cost_estimate=pl.CostEstimate(flops=flops, bytes_accessed=moved, transcendentals=0),
        name=name,
    )(*inputs)


def strips(rows, step):
    def run(i, carry):
        step(pl.ds(pl.multiple_of(i * STRIP, STRIP), STRIP))
        return carry

    lax.fori_loop(0, rows // STRIP, run, 0)


def head_forward(v, gain_vec, cosine, sine):
    r = lax.rsqrt(jnp.mean(v * v, -1, keepdims=True) + EPS)
    n = v * r * gain_vec
    return n * cosine + pltpu.roll(n, n.shape[-1] // 2, 1) * sine


def head_back(grad, v, gain_vec, cosine, sine):
    r = lax.rsqrt(jnp.mean(v * v, -1, keepdims=True) + EPS)
    grad = grad * cosine + pltpu.roll(grad * sine, grad.shape[-1] // 2, 1)
    unit_v = v * r
    gain_term = jnp.sum(grad * unit_v, 0, keepdims=True)
    inner = grad * gain_vec
    return r * (inner - unit_v * jnp.mean(unit_v * inner, -1, keepdims=True)), gain_term


def soft(queries, key_rows, bias):
    scores = dot_nt(queries, key_rows) * queries.shape[-1] ** (-0.5) + bias
    exponent = jnp.exp(scores - jnp.max(scores, -1, keepdims=True))
    return exponent / jnp.sum(exponent, -1, keepdims=True)


def attn_forward_kernel(count, head, share, qkv_at, out_at, *refs):
    where, gain, query_gain, key_gain, cosine, sine, bias = refs[:7]
    parts = refs[7:7 + count]
    qkv_tiles = refs[7 + count:12 + count]
    out_tiles = refs[12 + count:17 + count]
    state, normed, proj, mixed, partial = refs[17 + count:22 + count]
    w_qkv, sem_qkv, w_out, sem_out = refs[22 + count:]
    first_copies = tile_copies(where, qkv_tiles, w_qkv, sem_qkv, qkv_at)
    last_copies = tile_copies(where, out_tiles, w_out, sem_out, out_at)
    for copy in first_copies + last_copies:
        copy.start()

    def prepare(rows):
        total = parts[0][rows, :].astype(F32)
        for part in parts[1:]:
            total = total + part[rows, :].astype(F32)
        state[rows, :] = total
        normed[rows, :] = rmsnorm(total, gain[...]).astype(BF16)

    strips(state.shape[0], prepare)
    for copy in first_copies:
        copy.wait()
    span = (share + 2) * head
    packs, pack = bias.shape[0], bias.shape[1]

    def group(g, carry):
        columns = pl.ds(pl.multiple_of(g * span, span), span)
        proj[:, columns] = dot(normed[...], w_qkv[:, columns])
        base = g * span
        heads = [
            head_forward(
                proj[:, pl.ds(pl.multiple_of(base + h * head, head), head)],
                query_gain[...] if h < share else key_gain[...],
                cosine[...],
                sine[...],
            ).astype(BF16)
            for h in range(share + 1)
        ]
        value = proj[:, pl.ds(pl.multiple_of(base + (share + 1) * head, head), head)].astype(BF16)
        for b in range(packs):
            rows = slice(b * pack, (b + 1) * pack)
            for h in range(share):
                probs = soft(heads[h][rows], heads[share][rows], bias[b])
                at = pl.multiple_of((g * share + h) * head, head)
                mixed[rows, pl.ds(at, head)] = dot(probs.astype(BF16), value[rows]).astype(BF16)
        return carry

    lax.fori_loop(0, w_qkv.shape[1] // span, group, 0)
    for copy in last_copies:
        copy.wait()
    partial[...] = dot(mixed[...], w_out[...]).astype(BF16)


def mlp_forward_kernel(unit, at, *refs):
    where, gain, s_ref, p_ref, c_ref = refs[:5]
    tiles = refs[5:10]
    middle, mlp_in, gate_up, hidden = refs[10:14]
    weight, sems = refs[14:]
    copies = tile_copies(where, tiles, weight, sems, at)
    for copy in copies:
        copy.start()

    def prepare(rows):
        total = s_ref[rows, :] + p_ref[rows, :].astype(F32) + c_ref[rows, :].astype(F32)
        middle[rows, :] = total
        mlp_in[rows, :] = rmsnorm(total, gain[...]).astype(BF16)

    strips(middle.shape[0], prepare)
    for copy in copies:
        copy.wait()

    def block(j, carry):
        columns = pl.ds(pl.multiple_of(j * 2 * unit, 2 * unit), 2 * unit)
        gate_up[:, columns] = dot(mlp_in[...], weight[:, columns])
        gates = gate_up[:, pl.ds(pl.multiple_of(j * 2 * unit, unit), unit)]
        ups = gate_up[:, pl.ds(pl.multiple_of(j * 2 * unit + unit, unit), unit)]
        hidden[:, pl.ds(pl.multiple_of(j * unit, unit), unit)] = (
            gates / (1.0 + jnp.exp(-gates)) * ups
        ).astype(BF16)
        return carry

    lax.fori_loop(0, weight.shape[1] // (2 * unit), block, 0)


def down_kernel(at, where, hidden, *refs):
    tiles, partial, weight, sems = refs[:5], refs[5], refs[6], refs[7]
    copies = tile_copies(where, tiles, weight, sems, at)
    for copy in copies:
        copy.start()
    for copy in copies:
        copy.wait()
    partial[...] = dot(hidden[...], weight[...]).astype(BF16)


def mlp_back_kernel(unit, down_at, gu_at, *refs):
    where, branch, gate_up = refs[:3]
    down_tiles, gu_tiles = refs[3:8], refs[8:13]
    grad_gu, partial = refs[13:15]
    w_down, sem_down, w_gu, sem_gu = refs[15:]
    first_copies = tile_copies(where, down_tiles, w_down, sem_down, down_at)
    last_copies = tile_copies(where, gu_tiles, w_gu, sem_gu, gu_at)
    for copy in first_copies + last_copies:
        copy.start()
    for copy in first_copies:
        copy.wait()

    def block(j, carry):
        grad = dot_nt(branch[...], w_down[pl.ds(pl.multiple_of(j * unit, unit), unit), :])
        at = pl.ds(pl.multiple_of(j * 2 * unit, unit), unit)
        past = pl.ds(pl.multiple_of(j * 2 * unit + unit, unit), unit)
        gates = gate_up[:, at]
        sigma = 1.0 / (1.0 + jnp.exp(-gates))
        silu = gates * sigma
        grad_gu[:, at] = (grad * gate_up[:, past] * (sigma + silu * (1.0 - sigma))).astype(BF16)
        grad_gu[:, past] = (grad * silu).astype(BF16)
        return carry

    lax.fori_loop(0, w_down.shape[0] // unit, block, 0)
    for copy in last_copies:
        copy.wait()
    partial[...] = dot_nt(grad_gu[...], w_gu[...]).astype(BF16)


def norm_back(rows, v_ref, gain, p_ref, c_ref, residual, grad_ref, low_ref, term):
    v = v_ref[rows, :]
    r = lax.rsqrt(jnp.mean(v * v, -1, keepdims=True) + EPS)
    grad = p_ref[rows, :].astype(F32) + c_ref[rows, :].astype(F32)
    unit_v = v * r
    term[...] += jnp.sum(grad * unit_v, 0, keepdims=True)
    inner = grad * gain[...]
    total = residual[rows, :].astype(F32) + r * (
        inner - unit_v * jnp.mean(unit_v * inner, -1, keepdims=True)
    )
    grad_ref[rows, :] = total
    low_ref[rows, :] = total.astype(BF16)


def norm_back_kernel(gain, v_ref, p_ref, c_ref, residual, grad_ref, low_ref, term):
    term[...] = jnp.zeros_like(term)
    strips(
        v_ref.shape[0],
        lambda rows: norm_back(rows, v_ref, gain, p_ref, c_ref, residual, grad_ref, low_ref, term),
    )


def attn_back_kernel(head, share, out_at, qkv_at, *refs):
    where, gain, query_gain, key_gain, cosine, sine, bias = refs[:7]
    v_ref, p_ref, c_ref, residual, proj = refs[7:12]
    out_tiles, qkv_tiles = refs[12:17], refs[17:22]
    grad_ref, low_ref, term, grad_qkv, query_term, key_term, partial = refs[22:29]
    w_out, sem_out, w_qkv, sem_qkv, grad_mixed = refs[29:]
    first_copies = tile_copies(where, out_tiles, w_out, sem_out, out_at)
    last_copies = tile_copies(where, qkv_tiles, w_qkv, sem_qkv, qkv_at)
    for copy in first_copies + last_copies:
        copy.start()
    norm_back_kernel(gain, v_ref, p_ref, c_ref, residual, grad_ref, low_ref, term)
    for copy in first_copies:
        copy.wait()
    grad_mixed[...] = dot_nt(low_ref[...], w_out[...]).astype(BF16)
    span = (share + 2) * head
    packs, pack = bias.shape[0], bias.shape[1]
    query_term[...] = jnp.zeros_like(query_term)
    key_term[...] = jnp.zeros_like(key_term)
    scale = head ** (-0.5)

    def group(g, carry):
        def part(h):
            return pl.ds(pl.multiple_of(g * span + h * head, head), head)

        for b in range(packs):
            rows = slice(b * pack, (b + 1) * pack)
            cos_b, sin_b = cosine[rows, :], sine[rows, :]
            key_raw = proj[rows, part(share)]
            key_rows = head_forward(key_raw, key_gain[...], cos_b, sin_b).astype(BF16)
            value = proj[rows, part(share + 1)].astype(BF16)
            grad_key = jnp.zeros((pack, head), F32)
            grad_value = jnp.zeros((pack, head), F32)
            for h in range(share):
                query_raw = proj[rows, part(h)]
                query = head_forward(query_raw, query_gain[...], cos_b, sin_b).astype(BF16)
                probs = soft(query, key_rows, bias[b])
                at = pl.multiple_of((g * share + h) * head, head)
                upstream = grad_mixed[rows, pl.ds(at, head)]
                grad_value += dot_tn(probs.astype(BF16), upstream)
                grad_probs = dot_nt(upstream, value)
                grad_scores = probs * (
                    grad_probs - jnp.sum(probs * grad_probs, -1, keepdims=True)
                )
                grad_scores = grad_scores.astype(BF16)
                grad_key += dot_tn(grad_scores, query)
                grad_query, extra = head_back(
                    dot(grad_scores, key_rows) * scale, query_raw, query_gain[...], cos_b, sin_b
                )
                query_term[...] += extra
                grad_qkv[rows, part(h)] = grad_query.astype(BF16)
            grad_key, extra = head_back(grad_key * scale, key_raw, key_gain[...], cos_b, sin_b)
            key_term[...] += extra
            grad_qkv[rows, part(share)] = grad_key.astype(BF16)
            grad_qkv[rows, part(share + 1)] = grad_value.astype(BF16)
        return carry

    lax.fori_loop(0, w_qkv.shape[1] // span, group, 0)
    for copy in last_copies:
        copy.wait()
    partial[...] = dot_nt(grad_qkv[...], w_qkv[...]).astype(BF16)


def finish_kernel(layer, widths, row_split, spot, mine, other, *refs):
    outs, wides, sems = refs[-2 - len(widths):-2], refs[-2], refs[-1]
    rows = mine.shape[1]
    copies = []
    for m, tiles in enumerate((mine, other)):
        for j in range(PLANE):
            at = 0
            for out, width in zip(outs, widths):
                n = len(copies)
                wides[m * PLANE + j, :, at:at + width] = tiles[j, :, at:at + width].astype(F32)
                if row_split:
                    row, column = spot[m] * rows, spot[2 + PLANE * m + j] * width
                else:
                    row, column = 0, (spot[2 + PLANE * m + j] * 2 + spot[m]) * width
                copies.append(
                    pltpu.make_async_copy(
                        wides.at[m * PLANE + j, :, pl.ds(at, width)],
                        out.at[
                            layer,
                            pl.ds(pl.multiple_of(row, 128), rows),
                            pl.ds(pl.multiple_of(column, 128), width),
                        ],
                        sems.at[n],
                    )
                )
                copies[n].start()
                at += width
    for copy in copies:
        copy.wait()


def finish(spot, mine, other, layer, shapes, widths, row_split, previous):
    extra = [] if previous is None else list(previous)
    return pl.pallas_call(
        functools.partial(finish_kernel, layer, widths, row_split),
        in_specs=[SMEM, VMEM, VMEM] + [ANY] * len(extra),
        out_specs=[ANY] * len(shapes),
        out_shape=[jax.ShapeDtypeStruct(s, F32) for s in shapes],
        scratch_shapes=[
            pltpu.VMEM((2 * PLANE,) + mine.shape[1:], F32),
            pltpu.SemaphoreType.DMA((2 * PLANE * len(widths),)),
        ],
        input_output_aliases={3 + k: k for k in range(len(extra))},
        compiler_params=pltpu.CompilerParams(vmem_limit_bytes=24 << 20),
        cost_estimate=pl.CostEstimate(flops=0, bytes_accessed=12 * mine.size, transcendentals=0),
        name="finish",
    )(spot, mine, other, *extra)


def layout(lengths, row_count):
    seq_ends = jnp.cumsum(lengths, 1)
    starts = seq_ends - lengths
    indices = jnp.arange(row_count, dtype=jnp.int32)
    segment = jnp.sum((indices[None, :, None] >= seq_ends[:, None, :]).astype(jnp.int32), 2)
    owners = segment[:, :, None] == jnp.arange(lengths.shape[1], dtype=jnp.int32)[None, None, :]
    position = indices[None, :] - jnp.sum(jnp.where(owners, starts[:, None, :], 0), 2)
    visible = (segment[:, :, None] == segment[:, None, :]) & (
        indices[None, :, None] >= indices[None, None, :]
    )
    return position, jnp.where(visible, 0.0, MASKED).astype(F32)


def rope_tables(position, head_width):
    half_width = head_width // 2
    frequency = THETA ** (-jnp.arange(half_width, dtype=F32) * 2.0 / head_width)
    angles = position.reshape(-1).astype(F32)[:, None] * frequency
    cosine, sine = jnp.cos(angles), jnp.sin(angles)
    return jnp.concatenate([cosine, cosine], 1), jnp.concatenate([-sine, sine], 1)


def body(
    tokens,
    lengths,
    cotangent,
    attn_gain,
    w_query,
    w_key,
    w_value,
    query_gain,
    key_gain,
    w_output,
    mlp_gain,
    w_gate,
    w_up,
    w_down,
    links=None,
):
    send = links.send
    groups = links.groups
    row_count, width = tokens.shape
    layer_count = w_query.shape[0]
    head_width = query_gain.shape[1] * groups
    kv_heads = w_key.shape[2] // head_width
    share = w_query.shape[2] // w_key.shape[2]
    hidden_units = w_gate.shape[2]
    blocks = kv_heads // 2
    unit = hidden_units // (2 * blocks)
    q_width = share * head_width

    replica = lax.axis_index("replica")
    z = lax.axis_index("group")
    core = replica % 2
    plane = (replica // 2) % PLANE
    step_first = 1 + core
    step_second = 2 - core
    planes = [plane, plane ^ step_first, plane ^ step_second, plane ^ 3]
    where = jnp.stack(
        [z] + [(z + d) % groups for d in range(1, groups)] + planes
    ).astype(jnp.int32)
    partner_planes = [planes[0], planes[2], planes[1], planes[3]]
    spot = jnp.stack([core, 1 - core] + planes + partner_planes).astype(jnp.int32)

    part = attn_gain.shape[1]
    head_part = query_gain.shape[1]

    def pair_rows(rows):
        other = send(rows, links.pair)
        return jnp.concatenate(
            [jnp.where(core == 0, rows, other), jnp.where(core == 0, other, rows)], 0
        )

    position, bias = layout(pair_rows(lengths), row_count)
    cosine, sine = rope_tables(position, head_width)

    def half_columns(weight):
        shaped = weight.reshape(weight.shape[0], blocks, 2, -1)
        return lax.dynamic_index_in_dim(shaped, core, 2, keepdims=False)

    def half_rows(weight):
        shaped = weight.reshape(2, -1, weight.shape[1])
        return lax.dynamic_index_in_dim(shaped, core, 0, keepdims=False)

    def own_chunks(layer):
        rows = w_query.shape[1]
        qkv = jnp.concatenate(
            [half_columns(w_query[layer]), half_columns(w_key[layer]), half_columns(w_value[layer])],
            -1,
        ).reshape(rows, -1)
        gate_up = jnp.concatenate(
            [half_columns(w_gate[layer]), half_columns(w_up[layer])], -1
        ).reshape(rows, -1)
        return [qkv, half_rows(w_output[layer]), gate_up, half_rows(w_down[layer])]

    queue = Queue(3)

    nears = []

    def gather(owns, extra=None):
        tile = []
        for own in owns:
            tile_width = own.shape[1] // PLANE
            tile.append(pack(lax.dynamic_slice_in_dim(own, plane * tile_width, tile_width, 1)))
        widths = [x.shape[1] for x in tile]
        least = max(0, 2 * UNIT - sum(widths))
        if least:
            tile.append(jnp.zeros((UNIT, least), BF16))
        tile = jnp.concatenate(tile, 1)
        if extra is not None:
            tile = jnp.concatenate([tile, extra], 0)
        column = lax.all_gather(tile, "group", axis=0)
        if nears:
            column, _ = lax.optimization_barrier((column, queue.sent[-3]))
        near = jnp.stack(
            [
                lax.dynamic_index_in_dim(
                    column[:, :UNIT, :sum(widths)], (z + d) % groups, 0, keepdims=False
                )
                for d in range(1, groups)
            ]
        )
        nears.append(near)
        first = queue.send(near, links.first)
        second = queue.send(near, links.second)
        both = queue.send(first, links.second)
        tiles, at = [], 0
        for own, wide in zip(owns, widths):
            tiles.append(Tiles((own, near, first, second, both), at))
            at += wide
        return tiles, column

    gains_own = jnp.concatenate([attn_gain, mlp_gain, query_gain, key_gain], 1)
    gain_width = gains_own.shape[1]
    weights = []
    for layer in range(layer_count):
        qkv, out, gate_up, down = own_chunks(layer)
        if layer == 0:
            tile_width = qkv.shape[1] // PLANE
            slots = 16 * tile_width
            extra = jnp.pad(gains_own.reshape(-1), (0, slots - gains_own.size))
            (t_qkv,), column = gather([qkv], extra.reshape(16, tile_width))
            gains = column[:, qkv.shape[0]:].reshape(groups, -1)[:, :gains_own.size]
            gains = gains.reshape(groups, layer_count, gain_width)
            (t_out, t_dn), _ = gather([out, down])
            (t_gu,), _ = gather([gate_up])
        else:
            (t_qkv, t_out), _ = gather([qkv, out])
            (t_gu,), _ = gather([gate_up])
            (t_dn,), _ = gather([down])
        weights.append((t_qkv, t_out, t_gu, t_dn))

    def gain_of(start, size, layer):
        return gains[:, layer, start:start + size].reshape(1, -1).astype(F32)

    def exchange(partial):
        return send(partial, links.pair)

    def own_rows(rows):
        return lax.dynamic_slice_in_dim(rows, core * row_count, row_count, 0)

    def shape(columns, kind):
        return jax.ShapeDtypeStruct((2 * row_count, columns), kind)

    qkv_columns = blocks * (q_width + 2 * head_width)
    mixed_columns = blocks * q_width
    hidden_columns = blocks * unit
    forms = (head_width, share)

    parts = [pair_rows(tokens)]
    kept = []
    ahead = len(nears) - 2 * layer_count + 1
    for layer in range(layer_count):
        t_qkv, t_out, t_gu, t_dn = weights[layer]
        attn_g = gain_of(0, part, layer)
        mlp_g = gain_of(part, part, layer)
        query_g = gain_of(2 * part, head_part, layer)
        key_g = gain_of(2 * part + head_part, head_part, layer)
        parts[0], _ = lax.optimization_barrier((parts[0], nears[min(ahead, len(nears) - 1)]))
        ahead += 1
        state, normed, proj, mixed, partial = call(
            functools.partial(attn_forward_kernel, len(parts), *forms, t_qkv.at, t_out.at),
            "attn_forward",
            [where, attn_g, query_g, key_g, cosine, sine, bias, *parts, *t_qkv.refs, *t_out.refs],
            [SMEM] + [VMEM] * (6 + len(parts)) + [ANY] * 10,
            [
                shape(width, F32),
                shape(width, BF16),
                shape(qkv_columns, F32),
                shape(mixed_columns, BF16),
                shape(width, BF16),
            ],
            tile_scratch(t_qkv) + tile_scratch(t_out),
            4 * row_count * width * (qkv_columns + mixed_columns),
        )
        came = exchange(partial)
        state, _ = lax.optimization_barrier((state, nears[min(ahead, len(nears) - 1)]))
        ahead += 1
        middle, mlp_in, gate_up, hidden = call(
            functools.partial(mlp_forward_kernel, unit, t_gu.at),
            "mlp_forward",
            [where, mlp_g, state, partial, came, *t_gu.refs],
            [SMEM] + [VMEM] * 4 + [ANY] * 5,
            [
                shape(width, F32),
                shape(width, BF16),
                shape(2 * hidden_columns, F32),
                shape(hidden_columns, BF16),
            ],
            tile_scratch(t_gu),
            8 * row_count * width * hidden_columns,
        )
        (partial,) = call(
            functools.partial(down_kernel, t_dn.at),
            "down",
            [where, hidden, *t_dn.refs],
            [SMEM, VMEM] + [ANY] * 5,
            [shape(width, BF16)],
            tile_scratch(t_dn),
            4 * row_count * width * hidden_columns,
        )
        came = exchange(partial)
        parts = [middle, partial, came]
        kept.append((state, normed, proj, mixed, middle, mlp_in, gate_up, hidden,
                     attn_g, mlp_g, query_g, key_g))
    result_tokens = own_rows(
        parts[0] + parts[1].astype(F32) + parts[2].astype(F32)
    ).astype(BF16)

    class Reduction:
        def __init__(self, rows, columns):
            self.count = columns.shape[1] // PLANE
            self.rows = rows
            self.picked = [
                lax.dynamic_slice_in_dim(columns, index * self.count, self.count, 1)
                for index in planes
            ]

        def first(self):
            pair = jnp.concatenate([self.picked[3], self.picked[1]], 1)
            self.came = queue.send(dot_tn(self.rows, pair).astype(BF16), links.first)

        def second(self):
            pair = jnp.concatenate([self.picked[2], self.picked[0]], 1)
            mine = dot_tn(self.rows, pair) + self.came.astype(F32)
            came = queue.send(mine[:, :self.count].astype(BF16), links.second)
            mine = mine[:, self.count:] + came.astype(F32)
            for perm in links.outer:
                mine = mine.astype(BF16)
                mine = mine.astype(F32) + send(mine, perm).astype(F32)
            self.tile = lax.psum_scatter(
                mine.astype(BF16), "group", scatter_dimension=0, tiled=True
            )

        def spread(self, after):
            first = queue.send(self.tile, links.first)
            second = queue.send(self.tile, links.second)
            both = queue.send(first, links.second)
            tiles = jnp.stack([self.tile, first, second, both])
            if after is not None:
                tiles, _ = lax.optimization_barrier((tiles, after[0]))
            return tiles, send(tiles, links.pair)

    gate_shape, down_shape = w_gate.shape, w_down.shape
    row_shape = jax.ShapeDtypeStruct((1, width), F32)
    head_shape = jax.ShapeDtypeStruct((1, head_width), F32)
    branch = pair_rows(cotangent)
    gradient = branch
    gain_terms = [None] * layer_count
    sums = [None] * layer_count
    for layer in reversed(range(layer_count)):
        t_qkv, t_out, t_gu, t_dn = weights[layer]
        (state, normed, proj, mixed, middle, mlp_in, gate_up, hidden,
         attn_g, mlp_g, query_g, key_g) = kept[layer]
        down_sum = Reduction(hidden, branch)
        down_sum.first()
        queue.depth = 1 if layer == layer_count - 1 else 2
        grad_gu, partial = call(
            functools.partial(mlp_back_kernel, unit, t_dn.at, t_gu.at),
            "mlp_back",
            [where, branch, gate_up, *t_dn.refs, *t_gu.refs],
            [SMEM] + [VMEM] * 2 + [ANY] * 10,
            [shape(2 * hidden_columns, BF16), shape(width, BF16)],
            tile_scratch(t_dn) + tile_scratch(t_gu),
            12 * row_count * width * hidden_columns,
        )
        came = exchange(partial)
        gu_sum = Reduction(mlp_in, grad_gu)
        gu_sum.first()
        queue.depth = 2
        down_sum.second()
        grad_middle, grad_out, mlp_term, grad_qkv, query_term, key_term, partial = call(
            functools.partial(attn_back_kernel, *forms, t_out.at, t_qkv.at),
            "attn_back",
            [where, mlp_g, query_g, key_g, cosine, sine, bias,
             middle, partial, came, gradient, proj, *t_out.refs, *t_qkv.refs],
            [SMEM] + [VMEM] * 11 + [ANY] * 10,
            [
                shape(width, F32),
                shape(width, BF16),
                row_shape,
                shape(qkv_columns, BF16),
                head_shape,
                head_shape,
                shape(width, BF16),
            ],
            tile_scratch(t_out) + tile_scratch(t_qkv)
            + [pltpu.VMEM((2 * row_count, mixed_columns), BF16)],
            4 * row_count * width * (qkv_columns + mixed_columns),
        )
        came = exchange(partial)
        gu_sum.second()
        qkv_sum = Reduction(normed, grad_qkv)
        out_sum = Reduction(mixed, grad_out)
        qkv_sum.first()
        out_sum.first()
        qkv_sum.second()
        out_sum.second()
        sums[layer] = (qkv_sum, out_sum, gu_sum, down_sum)
        gradient, branch, attn_term = call(
            norm_back_kernel,
            "norm_back",
            [attn_g, state, partial, came, grad_middle],
            [VMEM] * 5,
            [shape(width, F32), shape(width, BF16), row_shape],
            [],
        )
        gain_terms[layer] = jnp.concatenate([attn_term, mlp_term, query_term, key_term], 1)
    plans = [
        ([w_query.shape, w_key.shape, w_value.shape], [q_width, head_width, head_width], False),
        ([w_output.shape], [width // PLANE], True),
        ([gate_shape, gate_shape], [unit, unit], False),
        ([down_shape], [width // PLANE], True),
    ]
    outs = [None] * 4
    for layer in reversed(range(layer_count)):
        for k in (3, 2, 0, 1):
            outs[k] = finish(
                spot, *sums[layer][k].spread(outs[k]), layer, *plans[k], outs[k]
            )
    gain_sums = jnp.concatenate(gain_terms, 0)
    heads_term = gain_sums[:, 2 * width:]
    heads_term = heads_term + send(heads_term, links.pair)
    gain_sums = jnp.concatenate([gain_sums[:, :2 * width], heads_term], 1)
    for perm in links.turns + links.outer:
        gain_sums = gain_sums + send(gain_sums, perm)

    def own_gain(start, size):
        return lax.dynamic_slice_in_dim(gain_sums, start + z * size, size, 1)

    return (
        result_tokens,
        own_rows(gradient),
        own_gain(0, part),
        outs[0][0],
        outs[0][1],
        outs[0][2],
        own_gain(2 * width, head_part),
        own_gain(2 * width + head_width, head_part),
        outs[1][0],
        own_gain(width, part),
        outs[2][0],
        outs[2][1],
        outs[3][0],
    )


def solution(mesh):
    links = Links(mesh.shape["replica"], mesh.shape["group"])
    return jax.shard_map(
        functools.partial(body, links=links),
        mesh=mesh,
        in_specs=(
            P(AXES, None),
            P(AXES, None),
            P(AXES, None),
            P(None, "group"),
            P(None, "group", None),
            P(None, "group", None),
            P(None, "group", None),
            P(None, "group"),
            P(None, "group"),
            P(None, "group", None),
            P(None, "group"),
            P(None, "group", None),
            P(None, "group", None),
            P(None, "group", None),
        ),
        out_specs=(
            P(AXES, None),
            P(AXES, None),
            P(None, "group"),
            P(None, "group", None),
            P(None, "group", None),
            P(None, "group", None),
            P(None, "group"),
            P(None, "group"),
            P(None, "group", None),
            P(None, "group"),
            P(None, "group", None),
            P(None, "group", None),
            P(None, "group", None),
        ),
        check_vma=False,
    )
```

```python
import functools

import jax
import jax.numpy as jnp
from jax import lax
from jax.experimental import pallas as pl
from jax.experimental.pallas import tpu as pltpu
from jax.sharding import PartitionSpec as P

EPS = 1e-06
THETA = 1000000.0
MASKED = -1e30
AXES = ("replica", "group")
BF16 = jnp.bfloat16
F32 = jnp.float32
PLANE = 4
UNIT = 256


def dot(a, b):
    return jnp.dot(a, b, preferred_element_type=F32)


def dot_nt(a, b):
    return lax.dot_general(a, b, (((1,), (1,)), ((), ())), preferred_element_type=F32)


def dot_tn(a, b):
    return lax.dot_general(a, b, (((0,), (0,)), ((), ())), preferred_element_type=F32)


def rmsnorm(vector, gain_vec):
    return vector * lax.rsqrt(jnp.mean(vector * vector, -1, keepdims=True) + EPS) * gain_vec


class Queue:
    def __init__(self, depth):
        self.sent, self.depth = [], depth

    def send(self, x, perm):
        if len(self.sent) >= self.depth:
            x, _ = lax.optimization_barrier((x, self.sent[-self.depth]))
        x = Links.send(x, perm)
        self.sent.append(x)
        return x


class Tiles:
    def __init__(self, refs, at):
        self.refs, self.at = refs, at


class Links:
    def __init__(self, replicas, groups):
        self.replicas, self.groups = replicas, groups

        def pairs(move):
            return [
                (r * groups + g, move(r, g)[0] * groups + move(r, g)[1])
                for r in range(replicas)
                for g in range(groups)
            ]

        self.pair = pairs(lambda r, g: (r ^ 1, g))
        self.first = pairs(lambda r, g: (r ^ (4 if r & 1 else 2), g))
        self.second = pairs(lambda r, g: (r ^ (2 if r & 1 else 4), g))
        self.turns = [pairs(lambda r, g, b=b: (r ^ b, g)) for b in (2, 4)]
        bit = 1
        while bit < groups:
            self.turns.append(pairs(lambda r, g, b=bit: (r, g ^ b)))
            bit *= 2
        self.shift = [pairs(lambda r, g, d=d: (r, (g - d) % groups)) for d in range(groups)]
        self.outer = []
        bit = 8
        while bit < replicas:
            self.outer.append(pairs(lambda r, g, b=bit: (r ^ b, g)))
            bit *= 2

    @staticmethod
    def send(x, perm):
        return lax.ppermute(x, AXES, perm)


VMEM = pl.BlockSpec(memory_space=pltpu.VMEM)
SMEM = pl.BlockSpec(memory_space=pltpu.SMEM)
ANY = pl.BlockSpec(memory_space=pl.ANY)
STRIP = 64


def tile_copies(where, sources, weight, sems, offset=0):
    own, rest = sources[0], sources[1:]
    rows, columns = own.shape
    width = columns // PLANE
    others = weight.shape[0] // rows - 1

    def band(z):
        return pl.ds(pl.multiple_of(z * rows, rows), rows)

    copies = [pltpu.make_async_copy(own, weight.at[band(where[0])], sems.at[0])]
    for j, source in enumerate(rest):
        column = pl.multiple_of(where[1 + others + j] * width, 128)
        for d in range(others):
            for at_row, at_column, tall, wide, to_row, to_column in pieces(rows, width):
                top = pl.multiple_of(where[1 + d] * rows + to_row, 128)
                copies.append(
                    pltpu.make_async_copy(
                        source.at[d, pl.ds(at_row, tall), pl.ds(offset + at_column, wide)],
                        weight.at[pl.ds(top, tall), pl.ds(column + to_column, wide)],
                        sems.at[len(copies)],
                    )
                )
    return copies


def pieces(rows, width):
    if rows == UNIT:
        return [(0, 0, UNIT, width, 0, 0)]
    half, extra = width // 2, UNIT // 2
    return [
        (0, 0, UNIT, width, 0, 0),
        (0, width, extra, half, UNIT, 0),
        (extra, width, extra, half, UNIT, half),
    ]


def pack(tile):
    if tile.shape[0] == UNIT:
        return tile
    half = tile.shape[1] // 2
    return jnp.concatenate(
        [tile[:UNIT], jnp.concatenate([tile[UNIT:, :half], tile[UNIT:, half:]], 0)], 1
    )


def tile_scratch(tiles):
    own, near = tiles.refs[0], tiles.refs[1]
    groups = near.shape[0] + 1
    return [
        pltpu.VMEM((groups * own.shape[0], own.shape[1]), BF16),
        pltpu.SemaphoreType.DMA(
            (1 + PLANE * (groups - 1) * len(pieces(own.shape[0], own.shape[1] // PLANE)),)
        ),
    ]


def call(kernel, name, inputs, specs, outs, scratch, flops=0, vmem=52):
    moved = sum(x.size * x.dtype.itemsize for x in inputs)
    moved += sum(x.size * x.dtype.itemsize for x in outs)
    return pl.pallas_call(
        kernel,
        in_specs=specs,
        out_specs=[VMEM] * len(outs),
        out_shape=outs,
        scratch_shapes=scratch,
        compiler_params=pltpu.CompilerParams(vmem_limit_bytes=vmem << 20),
        cost_estimate=pl.CostEstimate(flops=flops, bytes_accessed=moved, transcendentals=0),
        name=name,
    )(*inputs)


def strips(rows, step):
    def run(i, carry):
        step(pl.ds(pl.multiple_of(i * STRIP, STRIP), STRIP))
        return carry

    lax.fori_loop(0, rows // STRIP, run, 0)


def head_forward(v, gain_vec, cosine, sine):
    r = lax.rsqrt(jnp.mean(v * v, -1, keepdims=True) + EPS)
    n = v * r * gain_vec
    return n * cosine + pltpu.roll(n, n.shape[-1] // 2, 1) * sine


def head_back(grad, v, gain_vec, cosine, sine):
    r = lax.rsqrt(jnp.mean(v * v, -1, keepdims=True) + EPS)
    grad = grad * cosine + pltpu.roll(grad * sine, grad.shape[-1] // 2, 1)
    unit_v = v * r
    gain_term = jnp.sum(grad * unit_v, 0, keepdims=True)
    inner = grad * gain_vec
    return r * (inner - unit_v * jnp.mean(unit_v * inner, -1, keepdims=True)), gain_term


def soft(queries, key_rows, bias):
    scores = dot_nt(queries, key_rows) * queries.shape[-1] ** (-0.5) + bias
    exponent = jnp.exp(scores - jnp.max(scores, -1, keepdims=True))
    return exponent / jnp.sum(exponent, -1, keepdims=True)


def attn_forward_kernel(count, head, share, qkv_at, out_at, *refs):
    where, gain, query_gain, key_gain, cosine, sine, bias = refs[:7]
    parts = refs[7:7 + count]
    qkv_tiles = refs[7 + count:12 + count]
    out_tiles = refs[12 + count:17 + count]
    state, normed, proj, mixed, partial = refs[17 + count:22 + count]
    w_qkv, sem_qkv, w_out, sem_out = refs[22 + count:]
    first_copies = tile_copies(where, qkv_tiles, w_qkv, sem_qkv, qkv_at)
    last_copies = tile_copies(where, out_tiles, w_out, sem_out, out_at)
    for copy in first_copies + last_copies:
        copy.start()

    def prepare(rows):
        total = parts[0][rows, :].astype(F32)
        for part in parts[1:]:
            total = total + part[rows, :].astype(F32)
        state[rows, :] = total
        normed[rows, :] = rmsnorm(total, gain[...]).astype(BF16)

    strips(state.shape[0], prepare)
    for copy in first_copies:
        copy.wait()
    span = (share + 2) * head
    packs, pack = bias.shape[0], bias.shape[1]

    def group(g, carry):
        columns = pl.ds(pl.multiple_of(g * span, span), span)
        proj[:, columns] = dot(normed[...], w_qkv[:, columns])
        base = g * span
        heads = [
            head_forward(
                proj[:, pl.ds(pl.multiple_of(base + h * head, head), head)],
                query_gain[...] if h < share else key_gain[...],
                cosine[...],
                sine[...],
            ).astype(BF16)
            for h in range(share + 1)
        ]
        value = proj[:, pl.ds(pl.multiple_of(base + (share + 1) * head, head), head)].astype(BF16)
        for b in range(packs):
            rows = slice(b * pack, (b + 1) * pack)
            for h in range(share):
                probs = soft(heads[h][rows], heads[share][rows], bias[b])
                at = pl.multiple_of((g * share + h) * head, head)
                mixed[rows, pl.ds(at, head)] = dot(probs.astype(BF16), value[rows]).astype(BF16)
        return carry

    lax.fori_loop(0, w_qkv.shape[1] // span, group, 0)
    for copy in last_copies:
        copy.wait()
    partial[...] = dot(mixed[...], w_out[...]).astype(BF16)


def mlp_forward_kernel(unit, at, *refs):
    where, gain, s_ref, p_ref, c_ref = refs[:5]
    tiles = refs[5:10]
    middle, mlp_in, gate_up, hidden = refs[10:14]
    weight, sems = refs[14:]
    copies = tile_copies(where, tiles, weight, sems, at)
    for copy in copies:
        copy.start()

    def prepare(rows):
        total = s_ref[rows, :] + p_ref[rows, :].astype(F32) + c_ref[rows, :].astype(F32)
        middle[rows, :] = total
        mlp_in[rows, :] = rmsnorm(total, gain[...]).astype(BF16)

    strips(middle.shape[0], prepare)
    for copy in copies:
        copy.wait()

    def block(j, carry):
        columns = pl.ds(pl.multiple_of(j * 2 * unit, 2 * unit), 2 * unit)
        gate_up[:, columns] = dot(mlp_in[...], weight[:, columns])
        gates = gate_up[:, pl.ds(pl.multiple_of(j * 2 * unit, unit), unit)]
        ups = gate_up[:, pl.ds(pl.multiple_of(j * 2 * unit + unit, unit), unit)]
        hidden[:, pl.ds(pl.multiple_of(j * unit, unit), unit)] = (
            gates / (1.0 + jnp.exp(-gates)) * ups
        ).astype(BF16)
        return carry

    lax.fori_loop(0, weight.shape[1] // (2 * unit), block, 0)


def down_kernel(at, where, hidden, *refs):
    tiles, partial, weight, sems = refs[:5], refs[5], refs[6], refs[7]
    copies = tile_copies(where, tiles, weight, sems, at)
    for copy in copies:
        copy.start()
    for copy in copies:
        copy.wait()
    partial[...] = dot(hidden[...], weight[...]).astype(BF16)


def mlp_back_kernel(unit, down_at, gu_at, *refs):
    where, branch, gate_up = refs[:3]
    down_tiles, gu_tiles = refs[3:8], refs[8:13]
    grad_gu, partial = refs[13:15]
    w_down, sem_down, w_gu, sem_gu = refs[15:]
    first_copies = tile_copies(where, down_tiles, w_down, sem_down, down_at)
    last_copies = tile_copies(where, gu_tiles, w_gu, sem_gu, gu_at)
    for copy in first_copies + last_copies:
        copy.start()
    for copy in first_copies:
        copy.wait()

    def block(j, carry):
        grad = dot_nt(branch[...], w_down[pl.ds(pl.multiple_of(j * unit, unit), unit), :])
        at = pl.ds(pl.multiple_of(j * 2 * unit, unit), unit)
        past = pl.ds(pl.multiple_of(j * 2 * unit + unit, unit), unit)
        gates = gate_up[:, at]
        sigma = 1.0 / (1.0 + jnp.exp(-gates))
        silu = gates * sigma
        grad_gu[:, at] = (grad * gate_up[:, past] * (sigma + silu * (1.0 - sigma))).astype(BF16)
        grad_gu[:, past] = (grad * silu).astype(BF16)
        return carry

    lax.fori_loop(0, w_down.shape[0] // unit, block, 0)
    for copy in last_copies:
        copy.wait()
    partial[...] = dot_nt(grad_gu[...], w_gu[...]).astype(BF16)


def norm_back(rows, v_ref, gain, p_ref, c_ref, residual, grad_ref, low_ref, term):
    v = v_ref[rows, :]
    r = lax.rsqrt(jnp.mean(v * v, -1, keepdims=True) + EPS)
    grad = p_ref[rows, :].astype(F32) + c_ref[rows, :].astype(F32)
    unit_v = v * r
    term[...] += jnp.sum(grad * unit_v, 0, keepdims=True)
    inner = grad * gain[...]
    total = residual[rows, :].astype(F32) + r * (
        inner - unit_v * jnp.mean(unit_v * inner, -1, keepdims=True)
    )
    grad_ref[rows, :] = total
    low_ref[rows, :] = total.astype(BF16)


def norm_back_kernel(gain, v_ref, p_ref, c_ref, residual, grad_ref, low_ref, term):
    term[...] = jnp.zeros_like(term)
    strips(
        v_ref.shape[0],
        lambda rows: norm_back(rows, v_ref, gain, p_ref, c_ref, residual, grad_ref, low_ref, term),
    )


def attn_back_kernel(head, share, out_at, qkv_at, *refs):
    where, gain, query_gain, key_gain, cosine, sine, bias = refs[:7]
    v_ref, p_ref, c_ref, residual, proj = refs[7:12]
    out_tiles, qkv_tiles = refs[12:17], refs[17:22]
    grad_ref, low_ref, term, grad_qkv, query_term, key_term, partial = refs[22:29]
    w_out, sem_out, w_qkv, sem_qkv, grad_mixed = refs[29:]
    first_copies = tile_copies(where, out_tiles, w_out, sem_out, out_at)
    last_copies = tile_copies(where, qkv_tiles, w_qkv, sem_qkv, qkv_at)
    for copy in first_copies + last_copies:
        copy.start()
    norm_back_kernel(gain, v_ref, p_ref, c_ref, residual, grad_ref, low_ref, term)
    for copy in first_copies:
        copy.wait()
    grad_mixed[...] = dot_nt(low_ref[...], w_out[...]).astype(BF16)
    span = (share + 2) * head
    packs, pack = bias.shape[0], bias.shape[1]
    query_term[...] = jnp.zeros_like(query_term)
    key_term[...] = jnp.zeros_like(key_term)
    scale = head ** (-0.5)

    def group(g, carry):
        def part(h):
            return pl.ds(pl.multiple_of(g * span + h * head, head), head)

        for b in range(packs):
            rows = slice(b * pack, (b + 1) * pack)
            cos_b, sin_b = cosine[rows, :], sine[rows, :]
            key_raw = proj[rows, part(share)]
            key_rows = head_forward(key_raw, key_gain[...], cos_b, sin_b).astype(BF16)
            value = proj[rows, part(share + 1)].astype(BF16)
            grad_key = jnp.zeros((pack, head), F32)
            grad_value = jnp.zeros((pack, head), F32)
            for h in range(share):
                query_raw = proj[rows, part(h)]
                query = head_forward(query_raw, query_gain[...], cos_b, sin_b).astype(BF16)
                probs = soft(query, key_rows, bias[b])
                at = pl.multiple_of((g * share + h) * head, head)
                upstream = grad_mixed[rows, pl.ds(at, head)]
                grad_value += dot_tn(probs.astype(BF16), upstream)
                grad_probs = dot_nt(upstream, value)
                grad_scores = probs * (
                    grad_probs - jnp.sum(probs * grad_probs, -1, keepdims=True)
                )
                grad_scores = grad_scores.astype(BF16)
                grad_key += dot_tn(grad_scores, query)
                grad_query, extra = head_back(
                    dot(grad_scores, key_rows) * scale, query_raw, query_gain[...], cos_b, sin_b
                )
                query_term[...] += extra
                grad_qkv[rows, part(h)] = grad_query.astype(BF16)
            grad_key, extra = head_back(grad_key * scale, key_raw, key_gain[...], cos_b, sin_b)
            key_term[...] += extra
            grad_qkv[rows, part(share)] = grad_key.astype(BF16)
            grad_qkv[rows, part(share + 1)] = grad_value.astype(BF16)
        return carry

    lax.fori_loop(0, w_qkv.shape[1] // span, group, 0)
    for copy in last_copies:
        copy.wait()
    partial[...] = dot_nt(grad_qkv[...], w_qkv[...]).astype(BF16)


SLOTS = 3


def finish_kernel(layer, items, spot, *refs):
    tiles = refs[:2 * PLANE]
    total = sum(len(widths) for _, widths, _ in items)
    outs, (narrow, wides, in_sems, sems) = refs[-4 - total:-4], refs[-4:]
    loads = [
        pltpu.make_async_copy(tile, narrow.at[n], in_sems.at[n]) for n, tile in enumerate(tiles)
    ]
    for load in loads:
        load.start()
    busy = [[] for _ in range(SLOTS)]
    for n, load in enumerate(loads):
        m, plane = divmod(n, PLANE)
        slot = n % SLOTS
        for copy in busy[slot]:
            copy.wait()
        load.wait()
        wides[slot] = narrow[n].astype(F32)
        busy[slot] = []
        at, k = 0, 0
        core, place = spot[m], spot[2 + PLANE * m + plane]
        for rows, widths, row_split in items:
            for width in widths:
                row, column = (core * rows, place * width) if row_split else (
                    0, (place * 2 + core) * width
                )
                for from_row, from_column, tall, wide, to_row, to_column in pieces(rows, width):
                    copy = pltpu.make_async_copy(
                        wides.at[slot, pl.ds(from_row, tall), pl.ds(at + from_column, wide)],
                        outs[k].at[
                            layer,
                            pl.ds(pl.multiple_of(row + to_row, 128), tall),
                            pl.ds(pl.multiple_of(column + to_column, 128), wide),
                        ],
                        sems.at[slot, len(busy[slot])],
                    )
                    copy.start()
                    busy[slot].append(copy)
                at += width * rows // UNIT
                k += 1
    for copies in busy:
        for copy in copies:
            copy.wait()


def finish(spot, tiles, layer, items, shapes, previous):
    extra = [] if previous is None else list(previous)
    width = tiles[0].shape[1]
    most = sum(len(pieces(rows, w)) for rows, widths, _ in items for w in widths)
    return pl.pallas_call(
        functools.partial(finish_kernel, layer, items),
        in_specs=[SMEM] + [ANY] * (2 * PLANE + len(extra)),
        out_specs=[ANY] * len(shapes),
        out_shape=[jax.ShapeDtypeStruct(s, F32) for s in shapes],
        scratch_shapes=[
            pltpu.VMEM((2 * PLANE, UNIT, width), BF16),
            pltpu.VMEM((SLOTS, UNIT, width), F32),
            pltpu.SemaphoreType.DMA((2 * PLANE,)),
            pltpu.SemaphoreType.DMA((SLOTS, most)),
        ],
        input_output_aliases={1 + 2 * PLANE + k: k for k in range(len(extra))},
        compiler_params=pltpu.CompilerParams(vmem_limit_bytes=24 << 20),
        cost_estimate=pl.CostEstimate(
            flops=0, bytes_accessed=48 * tiles[0].size, transcendentals=0
        ),
        name="finish",
    )(spot, *tiles, *extra)


def layout(lengths, row_count):
    seq_ends = jnp.cumsum(lengths, 1)
    starts = seq_ends - lengths
    indices = jnp.arange(row_count, dtype=jnp.int32)
    segment = jnp.sum((indices[None, :, None] >= seq_ends[:, None, :]).astype(jnp.int32), 2)
    owners = segment[:, :, None] == jnp.arange(lengths.shape[1], dtype=jnp.int32)[None, None, :]
    position = indices[None, :] - jnp.sum(jnp.where(owners, starts[:, None, :], 0), 2)
    visible = (segment[:, :, None] == segment[:, None, :]) & (
        indices[None, :, None] >= indices[None, None, :]
    )
    return position, jnp.where(visible, 0.0, MASKED).astype(F32)


def rope_tables(position, head_width):
    half_width = head_width // 2
    frequency = THETA ** (-jnp.arange(half_width, dtype=F32) * 2.0 / head_width)
    angles = position.reshape(-1).astype(F32)[:, None] * frequency
    cosine, sine = jnp.cos(angles), jnp.sin(angles)
    return jnp.concatenate([cosine, cosine], 1), jnp.concatenate([-sine, sine], 1)


def body(
    tokens,
    lengths,
    cotangent,
    attn_gain,
    w_query,
    w_key,
    w_value,
    query_gain,
    key_gain,
    w_output,
    mlp_gain,
    w_gate,
    w_up,
    w_down,
    links=None,
):
    send = links.send
    groups = links.groups
    row_count, width = tokens.shape
    layer_count = w_query.shape[0]
    head_width = query_gain.shape[1] * groups
    kv_heads = w_key.shape[2] // head_width
    share = w_query.shape[2] // w_key.shape[2]
    hidden_units = w_gate.shape[2]
    blocks = kv_heads // 2
    unit = hidden_units // (2 * blocks)
    q_width = share * head_width

    replica = lax.axis_index("replica")
    z = lax.axis_index("group")
    core = replica % 2
    plane = (replica // 2) % PLANE
    step_first = 1 + core
    step_second = 2 - core
    planes = [plane, plane ^ step_first, plane ^ step_second, plane ^ 3]
    where = jnp.stack(
        [z] + [(z + d) % groups for d in range(1, groups)] + planes
    ).astype(jnp.int32)
    partner_planes = [planes[0], planes[2], planes[1], planes[3]]
    spot = jnp.stack([core, 1 - core] + planes + partner_planes).astype(jnp.int32)

    part = attn_gain.shape[1]
    head_part = query_gain.shape[1]

    def pair_rows(rows):
        other = send(rows, links.pair)
        return jnp.concatenate(
            [jnp.where(core == 0, rows, other), jnp.where(core == 0, other, rows)], 0
        )

    position, bias = layout(pair_rows(lengths), row_count)
    cosine, sine = rope_tables(position, head_width)

    def half_columns(weight):
        shaped = weight.reshape(weight.shape[0], blocks, 2, -1)
        return lax.dynamic_index_in_dim(shaped, core, 2, keepdims=False)

    def half_rows(weight):
        shaped = weight.reshape(2, -1, weight.shape[1])
        return lax.dynamic_index_in_dim(shaped, core, 0, keepdims=False)

    def own_chunks(layer):
        rows = w_query.shape[1]
        qkv = jnp.concatenate(
            [half_columns(w_query[layer]), half_columns(w_key[layer]), half_columns(w_value[layer])],
            -1,
        ).reshape(rows, -1)
        gate_up = jnp.concatenate(
            [half_columns(w_gate[layer]), half_columns(w_up[layer])], -1
        ).reshape(rows, -1)
        return [qkv, half_rows(w_output[layer]), gate_up, half_rows(w_down[layer])]

    queue = Queue(3)

    nears = []

    def gather(owns, extra=None, direct=False):
        tile = []
        for own in owns:
            tile_width = own.shape[1] // PLANE
            tile.append(pack(lax.dynamic_slice_in_dim(own, plane * tile_width, tile_width, 1)))
        widths = [x.shape[1] for x in tile]
        least = max(0, 2 * UNIT - sum(widths))
        if least:
            tile.append(jnp.zeros((UNIT, least), BF16))
        tile = jnp.concatenate(tile, 1)
        if extra is not None:
            tile = jnp.concatenate([tile, extra], 0)
        if direct:
            column = None
            near = jnp.stack([send(tile, links.shift[d]) for d in range(1, groups)])
        else:
            column = lax.all_gather(tile, "group", axis=0)
            if nears:
                column, _ = lax.optimization_barrier((column, queue.sent[-3]))
            near = jnp.stack(
                [
                    lax.dynamic_index_in_dim(
                        column[:, :UNIT, :sum(widths)], (z + d) % groups, 0, keepdims=False
                    )
                    for d in range(1, groups)
                ]
            )
        nears.append(near)
        first = queue.send(near, links.first)
        second = queue.send(near, links.second)
        both = queue.send(first, links.second)
        tiles, at = [], 0
        for own, wide in zip(owns, widths):
            tiles.append(Tiles((own, near, first, second, both), at))
            at += wide
        return tiles, column

    gains_own = jnp.concatenate([attn_gain, mlp_gain, query_gain, key_gain], 1)
    gain_width = gains_own.shape[1]
    weights = []
    for layer in range(layer_count):
        qkv, out, gate_up, down = own_chunks(layer)
        if layer == 0:
            (t_qkv,), _ = gather([qkv], direct=True)
            tile_width = (out.shape[1] + down.shape[1] * down.shape[0] // UNIT) // PLANE
            extra = jnp.pad(gains_own.reshape(-1), (0, 16 * tile_width - gains_own.size))
            (t_out, t_dn), column = gather([out, down], extra.reshape(16, tile_width))
            gains = column[:, UNIT:].reshape(groups, -1)[:, :gains_own.size]
            gains = gains.reshape(groups, layer_count, gain_width)
            (t_gu,), _ = gather([gate_up])
        else:
            (t_qkv, t_out), _ = gather([qkv, out])
            (t_gu,), _ = gather([gate_up])
            (t_dn,), _ = gather([down])
        weights.append((t_qkv, t_out, t_gu, t_dn))

    def gain_of(start, size, layer):
        return gains[:, layer, start:start + size].reshape(1, -1).astype(F32)

    def exchange(partial):
        return send(partial, links.pair)

    def own_rows(rows):
        return lax.dynamic_slice_in_dim(rows, core * row_count, row_count, 0)

    def shape(columns, kind):
        return jax.ShapeDtypeStruct((2 * row_count, columns), kind)

    qkv_columns = blocks * (q_width + 2 * head_width)
    mixed_columns = blocks * q_width
    hidden_columns = blocks * unit
    forms = (head_width, share)

    parts = [pair_rows(tokens)]
    kept = []
    ahead = len(nears) - 2 * layer_count + 1
    for layer in range(layer_count):
        t_qkv, t_out, t_gu, t_dn = weights[layer]
        attn_g = gain_of(0, part, layer)
        mlp_g = gain_of(part, part, layer)
        query_g = gain_of(2 * part, head_part, layer)
        key_g = gain_of(2 * part + head_part, head_part, layer)
        parts[0], _ = lax.optimization_barrier((parts[0], nears[min(ahead, len(nears) - 1)]))
        ahead += 1
        state, normed, proj, mixed, partial = call(
            functools.partial(attn_forward_kernel, len(parts), *forms, t_qkv.at, t_out.at),
            "attn_forward",
            [where, attn_g, query_g, key_g, cosine, sine, bias, *parts, *t_qkv.refs, *t_out.refs],
            [SMEM] + [VMEM] * (6 + len(parts)) + [ANY] * 10,
            [
                shape(width, F32),
                shape(width, BF16),
                shape(qkv_columns, F32),
                shape(mixed_columns, BF16),
                shape(width, BF16),
            ],
            tile_scratch(t_qkv) + tile_scratch(t_out),
            4 * row_count * width * (qkv_columns + mixed_columns),
        )
        came = exchange(partial)
        state, _ = lax.optimization_barrier((state, nears[min(ahead, len(nears) - 1)]))
        ahead += 1
        middle, mlp_in, gate_up, hidden = call(
            functools.partial(mlp_forward_kernel, unit, t_gu.at),
            "mlp_forward",
            [where, mlp_g, state, partial, came, *t_gu.refs],
            [SMEM] + [VMEM] * 4 + [ANY] * 5,
            [
                shape(width, F32),
                shape(width, BF16),
                shape(2 * hidden_columns, F32),
                shape(hidden_columns, BF16),
            ],
            tile_scratch(t_gu),
            8 * row_count * width * hidden_columns,
        )
        (partial,) = call(
            functools.partial(down_kernel, t_dn.at),
            "down",
            [where, hidden, *t_dn.refs],
            [SMEM, VMEM] + [ANY] * 5,
            [shape(width, BF16)],
            tile_scratch(t_dn),
            4 * row_count * width * hidden_columns,
        )
        came = exchange(partial)
        parts = [middle, partial, came]
        kept.append((state, normed, proj, mixed, middle, mlp_in, gate_up, hidden,
                     attn_g, mlp_g, query_g, key_g))
    result_tokens = own_rows(
        parts[0] + parts[1].astype(F32) + parts[2].astype(F32)
    ).astype(BF16)

    class Reduction:
        def __init__(self, rows, columns, early=False):
            self.count = columns.shape[1] // PLANE
            self.rows, self.early = rows, early
            self.picked = [
                lax.dynamic_slice_in_dim(columns, index * self.count, self.count, 1)
                for index in planes
            ]
            if early:
                every = jnp.concatenate([self.picked[j] for j in (3, 1, 2, 0)], 1)
                self.band = self.scatter(dot_tn(rows, every))

        @staticmethod
        def scatter(x):
            return lax.psum_scatter(x.astype(BF16), "group", scatter_dimension=0, tiled=True)

        def part(self, j):
            if self.early:
                return self.band[:, j * 2 * self.count:(j + 1) * 2 * self.count]
            pair = (3, 1) if j == 0 else (2, 0)
            return dot_tn(self.rows, jnp.concatenate([self.picked[k] for k in pair], 1))

        def first(self):
            self.came = queue.send(self.part(0).astype(BF16), links.first)

        def second(self, after=None):
            if after is not None:
                self.came, _ = lax.optimization_barrier((self.came, after))
            mine = self.part(1).astype(F32) + self.came.astype(F32)
            came = queue.send(mine[:, :self.count].astype(BF16), links.second)
            mine = mine[:, self.count:] + came.astype(F32)
            for perm in links.outer:
                mine = mine.astype(BF16)
                mine = mine.astype(F32) + send(mine, perm).astype(F32)
            self.tile = mine.astype(BF16) if self.early else self.scatter(mine)

    def spread(sums, after):
        tile = jnp.concatenate([pack(x.tile) for x in sums], 1)
        first = queue.send(tile, links.first)
        second = queue.send(tile, links.second)
        both = queue.send(first, links.second)
        mine = [tile, first, second, both]
        held = mine
        if after is not None:
            held = lax.optimization_barrier((*mine, after))[:4]
        return mine + [send(x, links.pair) for x in held]

    row_shape = jax.ShapeDtypeStruct((1, width), F32)
    head_shape = jax.ShapeDtypeStruct((1, head_width), F32)
    branch = pair_rows(cotangent)
    gradient = branch
    gain_terms = [None] * layer_count
    sums = []
    for layer in reversed(range(layer_count)):
        t_qkv, t_out, t_gu, t_dn = weights[layer]
        (state, normed, proj, mixed, middle, mlp_in, gate_up, hidden,
         attn_g, mlp_g, query_g, key_g) = kept[layer]
        down_sum = Reduction(hidden, branch, early=bool(sums))
        if not sums:
            down_sum.first()
            queue.depth = 1
        grad_gu, partial = call(
            functools.partial(mlp_back_kernel, unit, t_dn.at, t_gu.at),
            "mlp_back",
            [where, branch, gate_up, *t_dn.refs, *t_gu.refs],
            [SMEM] + [VMEM] * 2 + [ANY] * 10,
            [shape(2 * hidden_columns, BF16), shape(width, BF16)],
            tile_scratch(t_dn) + tile_scratch(t_gu),
            12 * row_count * width * hidden_columns,
        )
        came = exchange(partial)
        gu_sum = Reduction(mlp_in, grad_gu)
        if not sums:
            gu_sum.first()
            queue.depth = 3
            down_sum.second()
        grad_middle, grad_out, mlp_term, grad_qkv, query_term, key_term, partial = call(
            functools.partial(attn_back_kernel, *forms, t_out.at, t_qkv.at),
            "attn_back",
            [where, mlp_g, query_g, key_g, cosine, sine, bias,
             middle, partial, came, gradient, proj, *t_out.refs, *t_qkv.refs],
            [SMEM] + [VMEM] * 11 + [ANY] * 10,
            [
                shape(width, F32),
                shape(width, BF16),
                row_shape,
                shape(qkv_columns, BF16),
                head_shape,
                head_shape,
                shape(width, BF16),
            ],
            tile_scratch(t_out) + tile_scratch(t_qkv)
            + [pltpu.VMEM((2 * row_count, mixed_columns), BF16)],
            4 * row_count * width * (qkv_columns + mixed_columns),
        )
        came = exchange(partial)
        if sums:
            above = sums[-1]
            above[0].second(query_term)
            above[1].second()
            gu_sum.first()
            down_sum.first()
            down_sum.second(result_tokens)
            gu_sum.second()
        else:
            gu_sum.second(query_term)
        qkv_sum = Reduction(normed, grad_qkv)
        out_sum = Reduction(mixed, grad_out)
        qkv_sum.first()
        out_sum.first()
        sums.append((qkv_sum, out_sum, gu_sum, down_sum))
        gradient, branch, attn_term = call(
            norm_back_kernel,
            "norm_back",
            [attn_g, state, partial, came, grad_middle],
            [VMEM] * 5,
            [shape(width, F32), shape(width, BF16), row_shape],
            [],
        )
        gain_terms[layer] = jnp.concatenate([attn_term, mlp_term, query_term, key_term], 1)
    sums[-1][0].second(attn_term)
    sums[-1][1].second()

    gain_sums = jnp.concatenate(gain_terms, 0)
    heads_term = gain_sums[:, 2 * width:]
    heads_term = heads_term + send(heads_term, links.pair)
    gain_sums = jnp.concatenate([gain_sums[:, :2 * width], heads_term], 1)
    for perm in links.turns + links.outer:
        gain_sums = gain_sums + send(gain_sums, perm)

    quarter = width // PLANE
    head_items = [
        (UNIT, (q_width, head_width, head_width), False),
        (w_output.shape[1] // 2, (quarter,), True),
    ]
    unit_items = [(UNIT, (unit, unit), False), (w_down.shape[1] // 2, (quarter,), True)]
    head_shapes = [w_query.shape, w_key.shape, w_value.shape, w_output.shape]
    unit_shapes = [w_gate.shape, w_up.shape, w_down.shape]
    outs = None
    for layer, layer_sums in zip(reversed(range(layer_count)), sums):
        if layer > 0:
            outs = finish(
                spot, spread(layer_sums, outs and outs[0]), layer,
                head_items + unit_items, head_shapes + unit_shapes, outs,
            )
        else:
            held = outs and outs[0]
            unit_outs = finish(
                spot, spread(layer_sums[2:], held), layer,
                unit_items, unit_shapes, outs and outs[len(head_shapes):],
            )
            head_outs = finish(
                spot, spread(layer_sums[:2], unit_outs[0]), layer,
                head_items, head_shapes, outs and outs[:len(head_shapes)],
            )
            outs = list(head_outs) + list(unit_outs)

    def own_gain(start, size):
        return lax.dynamic_slice_in_dim(gain_sums, start + z * size, size, 1)

    return (
        result_tokens,
        own_rows(gradient),
        own_gain(0, part),
        outs[0],
        outs[1],
        outs[2],
        own_gain(2 * width, head_part),
        own_gain(2 * width + head_width, head_part),
        outs[3],
        own_gain(width, part),
        outs[4],
        outs[5],
        outs[6],
    )


def solution(mesh):
    links = Links(mesh.shape["replica"], mesh.shape["group"])
    return jax.shard_map(
        functools.partial(body, links=links),
        mesh=mesh,
        in_specs=(
            P(AXES, None),
            P(AXES, None),
            P(AXES, None),
            P(None, "group"),
            P(None, "group", None),
            P(None, "group", None),
            P(None, "group", None),
            P(None, "group"),
            P(None, "group"),
            P(None, "group", None),
            P(None, "group"),
            P(None, "group", None),
            P(None, "group", None),
            P(None, "group", None),
        ),
        out_specs=(
            P(AXES, None),
            P(AXES, None),
            P(None, "group"),
            P(None, "group", None),
            P(None, "group", None),
            P(None, "group", None),
            P(None, "group"),
            P(None, "group"),
            P(None, "group", None),
            P(None, "group"),
            P(None, "group", None),
            P(None, "group", None),
            P(None, "group", None),
        ),
        check_vma=False,
    )
```

```python
import functools

import jax
import jax.numpy as jnp
from jax import lax
from jax.experimental import pallas as pl
from jax.experimental.pallas import tpu as pltpu
from jax.sharding import PartitionSpec as P

EPS = 1e-06
THETA = 1000000.0
MASKED = -1e30
AXES = ("replica", "group")
BF16 = jnp.bfloat16
F32 = jnp.float32
PLANE = 4
UNIT = 256


def dot(a, b):
    return jnp.dot(a, b, preferred_element_type=F32)


def dot_nt(a, b):
    return lax.dot_general(a, b, (((1,), (1,)), ((), ())), preferred_element_type=F32)


def dot_tn(a, b):
    return lax.dot_general(a, b, (((0,), (0,)), ((), ())), preferred_element_type=F32)


def rmsnorm(vector, gain_vec):
    return vector * lax.rsqrt(jnp.mean(vector * vector, -1, keepdims=True) + EPS) * gain_vec


class Queue:
    def __init__(self, depth):
        self.sent, self.depth = [], depth

    def send(self, x, perm):
        if len(self.sent) >= self.depth:
            x, _ = lax.optimization_barrier((x, self.sent[-self.depth]))
        x = Links.send(x, perm)
        self.sent.append(x)
        return x


class Tiles:
    def __init__(self, own, layer, sent, at, by_rows):
        self.own, self.layer, self.at, self.by_rows = own, layer, at, by_rows
        self.refs = [*own, *sent]
        self.rows = own[0].shape[1] // (2 if by_rows else 1)
        self.widths = [x.shape[2] // (PLANE if by_rows else 2 * PLANE) for x in own]
        self.width = sum(self.widths)
        self.groups = sent[0].shape[0] + 1
        self.count = len(self.refs)

    def scratch(self):
        own = 1 if self.by_rows else PLANE * len(self.own)
        rest = PLANE * (self.groups - 1) * len(pieces(self.rows, self.width))
        return [
            pltpu.VMEM((self.groups * self.rows, PLANE * self.width), BF16),
            pltpu.SemaphoreType.DMA((own + rest,)),
        ]

    def copies(self, where, refs, weight, sems):
        own, rest = refs[:len(self.own)], refs[len(self.own):]
        others, rows, core = self.groups - 1, self.rows, where[self.groups + PLANE]
        band = pl.ds(pl.multiple_of(where[0] * rows, 128), rows)
        moves = []
        if self.by_rows:
            half = pl.ds(pl.multiple_of(core * rows, 128), rows)
            moves.append((own[0].at[self.layer, half], weight.at[band]))
        else:
            for p in range(PLANE):
                column = p * self.width
                for ref, width in zip(own, self.widths):
                    part = pl.ds(pl.multiple_of((2 * p + core) * width, 128), width)
                    moves.append(
                        (ref.at[self.layer, :, part], weight.at[band, pl.ds(column, width)])
                    )
                    column += width
        for j, source in enumerate(rest):
            column = pl.multiple_of(where[1 + others + j] * self.width, 128)
            for d in range(others):
                for row, left, tall, wide, to_row, to_column in pieces(rows, self.width):
                    top = pl.multiple_of(where[1 + d] * rows + to_row, 128)
                    moves.append(
                        (
                            source.at[d, pl.ds(row, tall), pl.ds(self.at + left, wide)],
                            weight.at[pl.ds(top, tall), pl.ds(column + to_column, wide)],
                        )
                    )
        return [
            pltpu.make_async_copy(source, target, sems.at[n])
            for n, (source, target) in enumerate(moves)
        ]


class Links:
    def __init__(self, replicas, groups):
        self.replicas, self.groups = replicas, groups

        def pairs(move):
            return [
                (r * groups + g, move(r, g)[0] * groups + move(r, g)[1])
                for r in range(replicas)
                for g in range(groups)
            ]

        self.pair = pairs(lambda r, g: (r ^ 1, g))
        self.first = pairs(lambda r, g: (r ^ (4 if r & 1 else 2), g))
        self.second = pairs(lambda r, g: (r ^ (2 if r & 1 else 4), g))
        self.turns = [pairs(lambda r, g, b=b: (r ^ b, g)) for b in (2, 4)]
        bit = 1
        while bit < groups:
            self.turns.append(pairs(lambda r, g, b=bit: (r, g ^ b)))
            bit *= 2
        self.shift = [pairs(lambda r, g, d=d: (r, (g - d) % groups)) for d in range(groups)]
        self.outer = []
        bit = 8
        while bit < replicas:
            self.outer.append(pairs(lambda r, g, b=bit: (r ^ b, g)))
            bit *= 2

    @staticmethod
    def send(x, perm):
        return lax.ppermute(x, AXES, perm)


VMEM = pl.BlockSpec(memory_space=pltpu.VMEM)
SMEM = pl.BlockSpec(memory_space=pltpu.SMEM)
ANY = pl.BlockSpec(memory_space=pl.ANY)
STRIP = 64


def pieces(rows, width):
    if rows == UNIT:
        return [(0, 0, UNIT, width, 0, 0)]
    half, extra = width // 2, UNIT // 2
    return [
        (0, 0, UNIT, width, 0, 0),
        (0, width, extra, half, UNIT, 0),
        (extra, width, extra, half, UNIT, half),
    ]


def pack(tile):
    if tile.shape[0] == UNIT:
        return tile
    half = tile.shape[1] // 2
    return jnp.concatenate(
        [tile[:UNIT], jnp.concatenate([tile[UNIT:, :half], tile[UNIT:, half:]], 0)], 1
    )


def take(refs, *counts):
    runs, at = [], 0
    for count in counts:
        runs.append(refs[at:at + count])
        at += count
    return [*runs, refs[at:]]


def call(kernel, name, inputs, specs, outs, scratch, vmem=52):
    return pl.pallas_call(
        kernel,
        in_specs=specs,
        out_specs=[VMEM] * len(outs),
        out_shape=outs,
        scratch_shapes=scratch,
        compiler_params=pltpu.CompilerParams(vmem_limit_bytes=vmem << 20),
        cost_estimate=pl.CostEstimate(flops=0, bytes_accessed=1 << 20, transcendentals=0),
        name=name,
    )(*inputs)


def strips(rows, step):
    def run(i, carry):
        step(pl.ds(pl.multiple_of(i * STRIP, STRIP), STRIP))
        return carry

    lax.fori_loop(0, rows // STRIP, run, 0)


def head_forward(v, gain_vec, cosine, sine):
    r = lax.rsqrt(jnp.mean(v * v, -1, keepdims=True) + EPS)
    n = v * r * gain_vec
    return n * cosine + pltpu.roll(n, n.shape[-1] // 2, 1) * sine


def head_back(grad, v, gain_vec, cosine, sine):
    r = lax.rsqrt(jnp.mean(v * v, -1, keepdims=True) + EPS)
    grad = grad * cosine + pltpu.roll(grad * sine, grad.shape[-1] // 2, 1)
    unit_v = v * r
    gain_term = jnp.sum(grad * unit_v, 0, keepdims=True)
    inner = grad * gain_vec
    return r * (inner - unit_v * jnp.mean(unit_v * inner, -1, keepdims=True)), gain_term


def soft(queries, key_rows, bias):
    scores = dot_nt(queries, key_rows) * queries.shape[-1] ** (-0.5) + bias
    exponent = jnp.exp(scores - jnp.max(scores, -1, keepdims=True))
    return exponent / jnp.sum(exponent, -1, keepdims=True)


def attn_forward_kernel(count, head, share, t_qkv, t_out, *refs):
    small, parts, qkv_refs, out_refs, made, scratch = take(
        refs, 7, count, t_qkv.count, t_out.count, 5
    )
    where, gain, query_gain, key_gain, cosine, sine, bias = small
    state, normed, proj, mixed, partial = made
    w_qkv, sem_qkv, w_out, sem_out = scratch
    first_copies = t_qkv.copies(where, qkv_refs, w_qkv, sem_qkv)
    last_copies = t_out.copies(where, out_refs, w_out, sem_out)
    for copy in first_copies + last_copies:
        copy.start()

    def prepare(rows):
        total = parts[0][rows, :].astype(F32)
        for part in parts[1:]:
            total = total + part[rows, :].astype(F32)
        state[rows, :] = total
        normed[rows, :] = rmsnorm(total, gain[...]).astype(BF16)

    strips(state.shape[0], prepare)
    for copy in first_copies:
        copy.wait()
    span = (share + 2) * head
    packs, pack = bias.shape[0], bias.shape[1]

    def group(g, carry):
        columns = pl.ds(pl.multiple_of(g * span, span), span)
        proj[:, columns] = dot(normed[...], w_qkv[:, columns])
        base = g * span
        heads = [
            head_forward(
                proj[:, pl.ds(pl.multiple_of(base + h * head, head), head)],
                query_gain[...] if h < share else key_gain[...],
                cosine[...],
                sine[...],
            ).astype(BF16)
            for h in range(share + 1)
        ]
        value = proj[:, pl.ds(pl.multiple_of(base + (share + 1) * head, head), head)].astype(BF16)
        for b in range(packs):
            rows = slice(b * pack, (b + 1) * pack)
            for h in range(share):
                probs = soft(heads[h][rows], heads[share][rows], bias[b])
                at = pl.multiple_of((g * share + h) * head, head)
                mixed[rows, pl.ds(at, head)] = dot(probs.astype(BF16), value[rows]).astype(BF16)
        return carry

    lax.fori_loop(0, w_qkv.shape[1] // span, group, 0)
    for copy in last_copies:
        copy.wait()
    partial[...] = dot(mixed[...], w_out[...]).astype(BF16)


def mlp_forward_kernel(unit, t_gu, *refs):
    small, gu_refs, made, (weight, sems) = take(refs, 5, t_gu.count, 4)
    where, gain, s_ref, p_ref, c_ref = small
    middle, mlp_in, gate_up, hidden = made
    copies = t_gu.copies(where, gu_refs, weight, sems)
    for copy in copies:
        copy.start()

    def prepare(rows):
        total = s_ref[rows, :] + p_ref[rows, :].astype(F32) + c_ref[rows, :].astype(F32)
        middle[rows, :] = total
        mlp_in[rows, :] = rmsnorm(total, gain[...]).astype(BF16)

    strips(middle.shape[0], prepare)
    for copy in copies:
        copy.wait()

    def block(j, carry):
        columns = pl.ds(pl.multiple_of(j * 2 * unit, 2 * unit), 2 * unit)
        gate_up[:, columns] = dot(mlp_in[...], weight[:, columns])
        gates = gate_up[:, pl.ds(pl.multiple_of(j * 2 * unit, unit), unit)]
        ups = gate_up[:, pl.ds(pl.multiple_of(j * 2 * unit + unit, unit), unit)]
        hidden[:, pl.ds(pl.multiple_of(j * unit, unit), unit)] = (
            gates / (1.0 + jnp.exp(-gates)) * ups
        ).astype(BF16)
        return carry

    lax.fori_loop(0, weight.shape[1] // (2 * unit), block, 0)


def down_kernel(t_dn, where, hidden, *refs):
    dn_refs, (partial,), (weight, sems) = take(refs, t_dn.count, 1)
    copies = t_dn.copies(where, dn_refs, weight, sems)
    for copy in copies:
        copy.start()
    for copy in copies:
        copy.wait()
    partial[...] = dot(hidden[...], weight[...]).astype(BF16)


def mlp_back_kernel(unit, t_dn, t_gu, *refs):
    (where, branch, gate_up), dn_refs, gu_refs, (grad_gu, partial), scratch = take(
        refs, 3, t_dn.count, t_gu.count, 2
    )
    w_down, sem_down, w_gu, sem_gu = scratch
    first_copies = t_dn.copies(where, dn_refs, w_down, sem_down)
    last_copies = t_gu.copies(where, gu_refs, w_gu, sem_gu)
    for copy in first_copies + last_copies:
        copy.start()
    for copy in first_copies:
        copy.wait()

    def block(j, carry):
        grad = dot_nt(branch[...], w_down[pl.ds(pl.multiple_of(j * unit, unit), unit), :])
        at = pl.ds(pl.multiple_of(j * 2 * unit, unit), unit)
        past = pl.ds(pl.multiple_of(j * 2 * unit + unit, unit), unit)
        gates = gate_up[:, at]
        sigma = 1.0 / (1.0 + jnp.exp(-gates))
        silu = gates * sigma
        grad_gu[:, at] = (grad * gate_up[:, past] * (sigma + silu * (1.0 - sigma))).astype(BF16)
        grad_gu[:, past] = (grad * silu).astype(BF16)
        return carry

    lax.fori_loop(0, w_down.shape[0] // unit, block, 0)
    for copy in last_copies:
        copy.wait()
    partial[...] = dot_nt(grad_gu[...], w_gu[...]).astype(BF16)


def norm_back(rows, v_ref, gain, p_ref, c_ref, residual, grad_ref, low_ref, term):
    v = v_ref[rows, :]
    r = lax.rsqrt(jnp.mean(v * v, -1, keepdims=True) + EPS)
    grad = p_ref[rows, :].astype(F32) + c_ref[rows, :].astype(F32)
    unit_v = v * r
    term[...] += jnp.sum(grad * unit_v, 0, keepdims=True)
    inner = grad * gain[...]
    total = residual[rows, :].astype(F32) + r * (
        inner - unit_v * jnp.mean(unit_v * inner, -1, keepdims=True)
    )
    grad_ref[rows, :] = total
    low_ref[rows, :] = total.astype(BF16)


def norm_back_kernel(gain, v_ref, p_ref, c_ref, residual, grad_ref, low_ref, term):
    term[...] = jnp.zeros_like(term)
    strips(
        v_ref.shape[0],
        lambda rows: norm_back(rows, v_ref, gain, p_ref, c_ref, residual, grad_ref, low_ref, term),
    )


def attn_back_kernel(head, share, t_out, t_qkv, *refs):
    small, large, out_refs, qkv_refs, made, scratch = take(
        refs, 7, 5, t_out.count, t_qkv.count, 7
    )
    where, gain, query_gain, key_gain, cosine, sine, bias = small
    v_ref, p_ref, c_ref, residual, proj = large
    grad_ref, low_ref, term, grad_qkv, query_term, key_term, partial = made
    w_out, sem_out, w_qkv, sem_qkv, grad_mixed = scratch
    first_copies = t_out.copies(where, out_refs, w_out, sem_out)
    last_copies = t_qkv.copies(where, qkv_refs, w_qkv, sem_qkv)
    for copy in first_copies + last_copies:
        copy.start()
    norm_back_kernel(gain, v_ref, p_ref, c_ref, residual, grad_ref, low_ref, term)
    for copy in first_copies:
        copy.wait()
    grad_mixed[...] = dot_nt(low_ref[...], w_out[...]).astype(BF16)
    span = (share + 2) * head
    packs, pack = bias.shape[0], bias.shape[1]
    query_term[...] = jnp.zeros_like(query_term)
    key_term[...] = jnp.zeros_like(key_term)
    scale = head ** (-0.5)

    def group(g, carry):
        def part(h):
            return pl.ds(pl.multiple_of(g * span + h * head, head), head)

        for b in range(packs):
            rows = slice(b * pack, (b + 1) * pack)
            cos_b, sin_b = cosine[rows, :], sine[rows, :]
            key_raw = proj[rows, part(share)]
            key_rows = head_forward(key_raw, key_gain[...], cos_b, sin_b).astype(BF16)
            value = proj[rows, part(share + 1)].astype(BF16)
            grad_key = jnp.zeros((pack, head), F32)
            grad_value = jnp.zeros((pack, head), F32)
            for h in range(share):
                query_raw = proj[rows, part(h)]
                query = head_forward(query_raw, query_gain[...], cos_b, sin_b).astype(BF16)
                probs = soft(query, key_rows, bias[b])
                at = pl.multiple_of((g * share + h) * head, head)
                upstream = grad_mixed[rows, pl.ds(at, head)]
                grad_value += dot_tn(probs.astype(BF16), upstream)
                grad_probs = dot_nt(upstream, value)
                grad_scores = probs * (
                    grad_probs - jnp.sum(probs * grad_probs, -1, keepdims=True)
                )
                grad_scores = grad_scores.astype(BF16)
                grad_key += dot_tn(grad_scores, query)
                grad_query, extra = head_back(
                    dot(grad_scores, key_rows) * scale, query_raw, query_gain[...], cos_b, sin_b
                )
                query_term[...] += extra
                grad_qkv[rows, part(h)] = grad_query.astype(BF16)
            grad_key, extra = head_back(grad_key * scale, key_raw, key_gain[...], cos_b, sin_b)
            key_term[...] += extra
            grad_qkv[rows, part(share)] = grad_key.astype(BF16)
            grad_qkv[rows, part(share + 1)] = grad_value.astype(BF16)
        return carry

    lax.fori_loop(0, w_qkv.shape[1] // span, group, 0)
    for copy in last_copies:
        copy.wait()
    partial[...] = dot_nt(grad_qkv[...], w_qkv[...]).astype(BF16)


SLOTS = 3


def finish_kernel(layer, items, spot, *refs):
    tiles = refs[:2 * PLANE]
    total = sum(len(widths) for _, widths, _ in items)
    outs, (narrow, wides, in_sems, sems) = refs[-4 - total:-4], refs[-4:]
    loads = [
        pltpu.make_async_copy(tile, narrow.at[n], in_sems.at[n]) for n, tile in enumerate(tiles)
    ]
    for load in loads:
        load.start()
    busy = [[] for _ in range(SLOTS)]
    for n, load in enumerate(loads):
        m, plane = divmod(n, PLANE)
        slot = n % SLOTS
        for copy in busy[slot]:
            copy.wait()
        load.wait()
        wides[slot] = narrow[n].astype(F32)
        busy[slot] = []
        at, k = 0, 0
        core, place = spot[m], spot[2 + PLANE * m + plane]
        for rows, widths, row_split in items:
            for width in widths:
                row, column = (core * rows, place * width) if row_split else (
                    0, (place * 2 + core) * width
                )
                for from_row, from_column, tall, wide, to_row, to_column in pieces(rows, width):
                    copy = pltpu.make_async_copy(
                        wides.at[slot, pl.ds(from_row, tall), pl.ds(at + from_column, wide)],
                        outs[k].at[
                            layer,
                            pl.ds(pl.multiple_of(row + to_row, 128), tall),
                            pl.ds(pl.multiple_of(column + to_column, 128), wide),
                        ],
                        sems.at[slot, len(busy[slot])],
                    )
                    copy.start()
                    busy[slot].append(copy)
                at += width * rows // UNIT
                k += 1
    for copies in busy:
        for copy in copies:
            copy.wait()


def finish(spot, tiles, layer, items, shapes, previous):
    extra = [] if previous is None else list(previous)
    width = tiles[0].shape[1]
    most = sum(len(pieces(rows, w)) for rows, widths, _ in items for w in widths)
    return pl.pallas_call(
        functools.partial(finish_kernel, layer, items),
        in_specs=[SMEM] + [ANY] * (2 * PLANE + len(extra)),
        out_specs=[ANY] * len(shapes),
        out_shape=[jax.ShapeDtypeStruct(s, F32) for s in shapes],
        scratch_shapes=[
            pltpu.VMEM((2 * PLANE, UNIT, width), BF16),
            pltpu.VMEM((SLOTS, UNIT, width), F32),
            pltpu.SemaphoreType.DMA((2 * PLANE,)),
            pltpu.SemaphoreType.DMA((SLOTS, most)),
        ],
        input_output_aliases={1 + 2 * PLANE + k: k for k in range(len(extra))},
        compiler_params=pltpu.CompilerParams(vmem_limit_bytes=24 << 20),
        cost_estimate=pl.CostEstimate(
            flops=0, bytes_accessed=48 * tiles[0].size, transcendentals=0
        ),
        name="finish",
    )(spot, *tiles, *extra)


def layout(lengths, row_count):
    seq_ends = jnp.cumsum(lengths, 1)
    starts = seq_ends - lengths
    indices = jnp.arange(row_count, dtype=jnp.int32)
    segment = jnp.sum((indices[None, :, None] >= seq_ends[:, None, :]).astype(jnp.int32), 2)
    owners = segment[:, :, None] == jnp.arange(lengths.shape[1], dtype=jnp.int32)[None, None, :]
    position = indices[None, :] - jnp.sum(jnp.where(owners, starts[:, None, :], 0), 2)
    visible = (segment[:, :, None] == segment[:, None, :]) & (
        indices[None, :, None] >= indices[None, None, :]
    )
    return position, jnp.where(visible, 0.0, MASKED).astype(F32)


def rope_tables(position, head_width):
    half_width = head_width // 2
    frequency = THETA ** (-jnp.arange(half_width, dtype=F32) * 2.0 / head_width)
    angles = position.reshape(-1).astype(F32)[:, None] * frequency
    cosine, sine = jnp.cos(angles), jnp.sin(angles)
    return jnp.concatenate([cosine, cosine], 1), jnp.concatenate([-sine, sine], 1)


def body(
    tokens,
    lengths,
    cotangent,
    attn_gain,
    w_query,
    w_key,
    w_value,
    query_gain,
    key_gain,
    w_output,
    mlp_gain,
    w_gate,
    w_up,
    w_down,
    links=None,
):
    send = links.send
    groups = links.groups
    row_count, width = tokens.shape
    layer_count = w_query.shape[0]
    head_width = query_gain.shape[1] * groups
    kv_heads = w_key.shape[2] // head_width
    share = w_query.shape[2] // w_key.shape[2]
    hidden_units = w_gate.shape[2]
    blocks = kv_heads // 2
    unit = hidden_units // (2 * blocks)
    q_width = share * head_width

    replica = lax.axis_index("replica")
    z = lax.axis_index("group")
    core = replica % 2
    plane = (replica // 2) % PLANE
    step_first = 1 + core
    step_second = 2 - core
    planes = [plane, plane ^ step_first, plane ^ step_second, plane ^ 3]
    where = jnp.stack(
        [z] + [(z + d) % groups for d in range(1, groups)] + planes + [core]
    ).astype(jnp.int32)
    partner_planes = [planes[0], planes[2], planes[1], planes[3]]
    spot = jnp.stack([core, 1 - core] + planes + partner_planes).astype(jnp.int32)

    part = attn_gain.shape[1]
    head_part = query_gain.shape[1]

    def pair_rows(rows):
        other = send(rows, links.pair)
        return jnp.concatenate(
            [jnp.where(core == 0, rows, other), jnp.where(core == 0, other, rows)], 0
        )

    position, bias = layout(pair_rows(lengths), row_count)
    cosine, sine = rope_tables(position, head_width)

    def tile_of(own, layer, by_rows):
        sides = []
        for weight in own:
            if by_rows:
                tall, wide = weight.shape[1] // 2, weight.shape[2] // PLANE
                at = (core * tall, plane * wide)
            else:
                tall, wide = weight.shape[1], weight.shape[2] // (2 * PLANE)
                at = (0, (2 * plane + core) * wide)
            sides.append(lax.dynamic_slice(weight, (layer, *at), (1, tall, wide))[0])
        return pack(jnp.concatenate(sides, 1))

    queue = Queue(3)
    nears = []

    def gather(owns, layer, extra=None, direct=False):
        tile = [tile_of(own, layer, by_rows) for own, by_rows in owns]
        widths = [x.shape[1] for x in tile]
        least = max(0, 2 * UNIT - sum(widths))
        if least:
            tile.append(jnp.zeros((UNIT, least), BF16))
        tile = jnp.concatenate(tile, 1)
        if extra is not None:
            extra = jnp.pad(extra, (0, 16 * tile.shape[1] - extra.size))
            tile = jnp.concatenate([tile, extra.reshape(16, -1)], 0)
        if direct:
            column = None
            near = jnp.stack([send(tile, links.shift[d]) for d in range(1, groups)])
        else:
            column = lax.all_gather(tile, "group", axis=0)
            if nears:
                column, _ = lax.optimization_barrier((column, queue.sent[-3]))
            near = jnp.stack(
                [
                    lax.dynamic_index_in_dim(
                        column[:, :UNIT, :sum(widths)], (z + d) % groups, 0, keepdims=False
                    )
                    for d in range(1, groups)
                ]
            )
        nears.append(near)
        first = queue.send(near, links.first)
        second = queue.send(near, links.second)
        both = queue.send(first, links.second)
        tiles, at = [], 0
        for (own, by_rows), wide in zip(owns, widths):
            tiles.append(Tiles(own, layer, (near, first, second, both), at, by_rows))
            at += wide
        return tiles, column

    gains_own = jnp.concatenate([attn_gain, mlp_gain, query_gain, key_gain], 1)
    gain_width = gains_own.shape[1]
    qkv, out = ((w_query, w_key, w_value), False), ((w_output,), True)
    gate_up, down = ((w_gate, w_up), False), ((w_down,), True)
    weights = []
    for layer in range(layer_count):
        if layer == 0:
            (t_qkv,), _ = gather([qkv], layer, direct=True)
            (t_out, t_dn), column = gather([out, down], layer, gains_own.reshape(-1))
            gains = column[:, UNIT:].reshape(groups, -1)[:, :gains_own.size]
            gains = gains.reshape(groups, layer_count, gain_width)
            (t_gu,), _ = gather([gate_up], layer)
        else:
            (t_qkv, t_out), _ = gather([qkv, out], layer)
            (t_gu,), _ = gather([gate_up], layer)
            (t_dn,), _ = gather([down], layer)
        weights.append((t_qkv, t_out, t_gu, t_dn))

    def gain_of(start, size, layer):
        return gains[:, layer, start:start + size].reshape(1, -1).astype(F32)

    def exchange(partial):
        return send(partial, links.pair)

    def own_rows(rows):
        return lax.dynamic_slice_in_dim(rows, core * row_count, row_count, 0)

    def shape(columns, kind):
        return jax.ShapeDtypeStruct((2 * row_count, columns), kind)

    qkv_columns = blocks * (q_width + 2 * head_width)
    mixed_columns = blocks * q_width
    hidden_columns = blocks * unit
    forms = (head_width, share)

    parts = [pair_rows(tokens)]
    kept = []
    ahead = len(nears) - 2 * layer_count + 1
    for layer in range(layer_count):
        t_qkv, t_out, t_gu, t_dn = weights[layer]
        attn_g = gain_of(0, part, layer)
        mlp_g = gain_of(part, part, layer)
        query_g = gain_of(2 * part, head_part, layer)
        key_g = gain_of(2 * part + head_part, head_part, layer)
        parts[0], _ = lax.optimization_barrier((parts[0], nears[min(ahead, len(nears) - 1)]))
        ahead += 1
        state, normed, proj, mixed, partial = call(
            functools.partial(attn_forward_kernel, len(parts), *forms, t_qkv, t_out),
            "attn_forward",
            [where, attn_g, query_g, key_g, cosine, sine, bias, *parts, *t_qkv.refs, *t_out.refs],
            [SMEM] + [VMEM] * (6 + len(parts)) + [ANY] * (t_qkv.count + t_out.count),
            [
                shape(width, F32),
                shape(width, BF16),
                shape(qkv_columns, F32),
                shape(mixed_columns, BF16),
                shape(width, BF16),
            ],
            t_qkv.scratch() + t_out.scratch(),
        )
        came = exchange(partial)
        state, _ = lax.optimization_barrier((state, nears[min(ahead, len(nears) - 1)]))
        ahead += 1
        middle, mlp_in, gate_up, hidden = call(
            functools.partial(mlp_forward_kernel, unit, t_gu),
            "mlp_forward",
            [where, mlp_g, state, partial, came, *t_gu.refs],
            [SMEM] + [VMEM] * 4 + [ANY] * t_gu.count,
            [
                shape(width, F32),
                shape(width, BF16),
                shape(2 * hidden_columns, F32),
                shape(hidden_columns, BF16),
            ],
            t_gu.scratch(),
        )
        (partial,) = call(
            functools.partial(down_kernel, t_dn),
            "down",
            [where, hidden, *t_dn.refs],
            [SMEM, VMEM] + [ANY] * t_dn.count,
            [shape(width, BF16)],
            t_dn.scratch(),
        )
        came = exchange(partial)
        parts = [middle, partial, came]
        kept.append((state, normed, proj, mixed, middle, mlp_in, gate_up, hidden,
                     attn_g, mlp_g, query_g, key_g))
    result_tokens = own_rows(
        parts[0] + parts[1].astype(F32) + parts[2].astype(F32)
    ).astype(BF16)

    class Reduction:
        def __init__(self, rows, columns, early=False):
            self.count = columns.shape[1] // PLANE
            self.rows, self.early = rows, early
            self.picked = [
                lax.dynamic_slice_in_dim(columns, index * self.count, self.count, 1)
                for index in planes
            ]
            if early:
                every = jnp.concatenate([self.picked[j] for j in (3, 1, 2, 0)], 1)
                self.band = self.scatter(dot_tn(rows, every))

        @staticmethod
        def scatter(x):
            return lax.psum_scatter(x.astype(BF16), "group", scatter_dimension=0, tiled=True)

        def part(self, j):
            if self.early:
                return self.band[:, j * 2 * self.count:(j + 1) * 2 * self.count]
            pair = (3, 1) if j == 0 else (2, 0)
            return dot_tn(self.rows, jnp.concatenate([self.picked[k] for k in pair], 1))

        def first(self):
            self.came = queue.send(self.part(0).astype(BF16), links.first)

        def second(self, after=None, alone=True):
            if after is not None:
                self.came, _ = lax.optimization_barrier((self.came, after))
            mine = self.part(1).astype(F32) + self.came.astype(F32)
            self.last = queue.send(mine[:, :self.count].astype(BF16), links.second)
            mine = mine[:, self.count:] + self.last.astype(F32)
            for perm in links.outer:
                mine = mine.astype(BF16)
                mine = mine.astype(F32) + send(mine, perm).astype(F32)
            self.mine = mine.astype(BF16)
            if alone:
                self.tile = pack(self.mine if self.early else self.scatter(self.mine))

    def spread(tiles, after):
        tile = jnp.concatenate(tiles, 1)
        first = queue.send(tile, links.first)
        second = queue.send(tile, links.second)
        both = queue.send(first, links.second)
        mine = [tile, first, second, both]
        held = mine
        if after is not None:
            held = lax.optimization_barrier((*mine, after))[:4]
        return mine + [send(x, links.pair) for x in held]

    row_shape = jax.ShapeDtypeStruct((1, width), F32)
    head_shape = jax.ShapeDtypeStruct((1, head_width), F32)
    branch = pair_rows(cotangent)
    gradient = branch
    gain_terms = [None] * layer_count
    sums = []
    for layer in reversed(range(layer_count)):
        t_qkv, t_out, t_gu, t_dn = weights[layer]
        (state, normed, proj, mixed, middle, mlp_in, gate_up, hidden,
         attn_g, mlp_g, query_g, key_g) = kept[layer]
        down_sum = Reduction(hidden, branch, early=bool(sums))
        if not sums:
            down_sum.first()
        grad_gu, partial = call(
            functools.partial(mlp_back_kernel, unit, t_dn, t_gu),
            "mlp_back",
            [where, branch, gate_up, *t_dn.refs, *t_gu.refs],
            [SMEM] + [VMEM] * 2 + [ANY] * (t_dn.count + t_gu.count),
            [shape(2 * hidden_columns, BF16), shape(width, BF16)],
            t_dn.scratch() + t_gu.scratch(),
        )
        grad_gu, partial, _ = lax.optimization_barrier(
            (grad_gu, partial, sums[-1][2].last if sums else down_sum.came)
        )
        came = exchange(partial)
        gu_sum = Reduction(mlp_in, grad_gu)
        gu_sum.first()
        grad_middle, grad_out, mlp_term, grad_qkv, query_term, key_term, partial = call(
            functools.partial(attn_back_kernel, *forms, t_out, t_qkv),
            "attn_back",
            [where, mlp_g, query_g, key_g, cosine, sine, bias,
             middle, partial, came, gradient, proj, *t_out.refs, *t_qkv.refs],
            [SMEM] + [VMEM] * 11 + [ANY] * (t_out.count + t_qkv.count),
            [
                shape(width, F32),
                shape(width, BF16),
                row_shape,
                shape(qkv_columns, BF16),
                head_shape,
                head_shape,
                shape(width, BF16),
            ],
            t_out.scratch() + t_qkv.scratch()
            + [pltpu.VMEM((2 * row_count, mixed_columns), BF16)],
        )
        grad_middle, grad_out, grad_qkv, partial, _ = lax.optimization_barrier(
            (grad_middle, grad_out, grad_qkv, partial, (sums[-1][0] if sums else gu_sum).came)
        )
        came = exchange(partial)
        qkv_sum = Reduction(normed, grad_qkv)
        out_sum = Reduction(mixed, grad_out, early=not sums)
        if not sums:
            down_sum.second(query_term)
            gu_sum.second()
            qkv_sum.first()
        else:
            above = sums[-1]
            above[0].second(query_term)
            above[1].first()
            above[1].second()
            qkv_sum.first()
            out_sum.first()
            gu_sum.second(result_tokens)
        sums.append((qkv_sum, out_sum, gu_sum, down_sum))
        gradient, branch, attn_term = call(
            norm_back_kernel,
            "norm_back",
            [attn_g, state, partial, came, grad_middle],
            [VMEM] * 5,
            [shape(width, F32), shape(width, BF16), row_shape],
            [],
        )
        gain_terms[layer] = jnp.concatenate([attn_term, mlp_term, query_term, key_term], 1)
    sums[-1][0].second(attn_term, alone=False)
    sums[-1][1].second(alone=False)
    sums[-1][3].first()
    sums[-1][3].second()
    head_tile = Reduction.scatter(jnp.concatenate([x.mine for x in sums[-1][:2]], 1))

    gain_sums = jnp.concatenate(gain_terms, 0)
    heads_term = gain_sums[:, 2 * width:]
    heads_term = heads_term + send(heads_term, links.pair)
    gain_sums = jnp.concatenate([gain_sums[:, :2 * width], heads_term], 1)
    for perm in links.turns + links.outer:
        gain_sums = gain_sums + send(gain_sums, perm)

    quarter = width // PLANE
    head_items = [
        (UNIT, (q_width, head_width, head_width), False),
        (w_output.shape[1] // 2, (quarter,), True),
    ]
    unit_items = [(UNIT, (unit, unit), False), (w_down.shape[1] // 2, (quarter,), True)]
    head_shapes = [w_query.shape, w_key.shape, w_value.shape, w_output.shape]
    unit_shapes = [w_gate.shape, w_up.shape, w_down.shape]
    outs = None
    for layer, layer_sums in zip(reversed(range(layer_count)), sums):
        if layer > 0:
            outs = finish(
                spot, spread([x.tile for x in layer_sums], outs and outs[0]), layer,
                head_items + unit_items, head_shapes + unit_shapes, outs,
            )
        else:
            held = outs and outs[0]
            unit_outs = finish(
                spot, spread([x.tile for x in layer_sums[2:]], held), layer,
                unit_items, unit_shapes, outs and outs[len(head_shapes):],
            )
            head_outs = finish(
                spot, spread([head_tile], unit_outs[0]), layer,
                head_items, head_shapes, outs and outs[:len(head_shapes)],
            )
            outs = list(head_outs) + list(unit_outs)

    def own_gain(start, size):
        return lax.dynamic_slice_in_dim(gain_sums, start + z * size, size, 1)

    return (
        result_tokens,
        own_rows(gradient),
        own_gain(0, part),
        outs[0],
        outs[1],
        outs[2],
        own_gain(2 * width, head_part),
        own_gain(2 * width + head_width, head_part),
        outs[3],
        own_gain(width, part),
        outs[4],
        outs[5],
        outs[6],
    )


def solution(mesh):
    links = Links(mesh.shape["replica"], mesh.shape["group"])
    return jax.shard_map(
        functools.partial(body, links=links),
        mesh=mesh,
        in_specs=(
            P(AXES, None),
            P(AXES, None),
            P(AXES, None),
            P(None, "group"),
            P(None, "group", None),
            P(None, "group", None),
            P(None, "group", None),
            P(None, "group"),
            P(None, "group"),
            P(None, "group", None),
            P(None, "group"),
            P(None, "group", None),
            P(None, "group", None),
            P(None, "group", None),
        ),
        out_specs=(
            P(AXES, None),
            P(AXES, None),
            P(None, "group"),
            P(None, "group", None),
            P(None, "group", None),
            P(None, "group", None),
            P(None, "group"),
            P(None, "group"),
            P(None, "group", None),
            P(None, "group"),
            P(None, "group", None),
            P(None, "group", None),
            P(None, "group", None),
        ),
        check_vma=False,
    )
```

```python
import functools

import jax
import jax.numpy as jnp
from jax import lax
from jax.experimental import pallas as pl
from jax.experimental.pallas import tpu as pltpu
from jax.sharding import PartitionSpec as P

EPS = 1e-06
THETA = 1000000.0
MASKED = -1e30
AXES = ("replica", "group")
BF16 = jnp.bfloat16
F32 = jnp.float32
PLANE = 4
UNIT = 256


def dot(a, b):
    return jnp.dot(a, b, preferred_element_type=F32)


def dot_nt(a, b):
    return lax.dot_general(a, b, (((1,), (1,)), ((), ())), preferred_element_type=F32)


def dot_tn(a, b):
    return lax.dot_general(a, b, (((0,), (0,)), ((), ())), preferred_element_type=F32)


def rmsnorm(vector, gain_vec):
    return vector * lax.rsqrt(jnp.mean(vector * vector, -1, keepdims=True) + EPS) * gain_vec


class Queue:
    def __init__(self, depth):
        self.sent, self.depth = [], depth

    def send(self, x, perm):
        if len(self.sent) >= self.depth:
            x, _ = lax.optimization_barrier((x, self.sent[-self.depth]))
        x = Links.send(x, perm)
        self.sent.append(x)
        return x


class Tiles:
    def __init__(self, own, layer, sent, at, by_rows):
        self.own, self.layer, self.at, self.by_rows = own, layer, at, by_rows
        self.refs = [*own, *sent]
        self.rows = own[0].shape[1] // (2 if by_rows else 1)
        self.widths = [x.shape[2] // (PLANE if by_rows else 2 * PLANE) for x in own]
        self.width = sum(self.widths)
        self.groups = sent[0].shape[0] + 1
        self.count = len(self.refs)

    def scratch(self):
        own = 1 if self.by_rows else PLANE * len(self.own)
        rest = PLANE * (self.groups - 1) * len(pieces(self.rows, self.width))
        return [
            pltpu.VMEM((self.groups * self.rows, PLANE * self.width), BF16),
            pltpu.SemaphoreType.DMA((own + rest,)),
        ]

    def copies(self, where, refs, weight, sems):
        own, rest = refs[:len(self.own)], refs[len(self.own):]
        others, rows, core = self.groups - 1, self.rows, where[self.groups + PLANE]
        band = pl.ds(pl.multiple_of(where[0] * rows, 128), rows)
        moves = []
        if self.by_rows:
            half = pl.ds(pl.multiple_of(core * rows, 128), rows)
            moves.append((own[0].at[self.layer, half], weight.at[band]))
        else:
            for p in range(PLANE):
                column = p * self.width
                for ref, width in zip(own, self.widths):
                    part = pl.ds(pl.multiple_of((2 * p + core) * width, 128), width)
                    moves.append(
                        (ref.at[self.layer, :, part], weight.at[band, pl.ds(column, width)])
                    )
                    column += width
        for j, source in enumerate(rest):
            column = pl.multiple_of(where[1 + others + j] * self.width, 128)
            for d in range(others):
                for row, left, tall, wide, to_row, to_column in pieces(rows, self.width):
                    top = pl.multiple_of(where[1 + d] * rows + to_row, 128)
                    moves.append(
                        (
                            source.at[d, pl.ds(row, tall), pl.ds(self.at + left, wide)],
                            weight.at[pl.ds(top, tall), pl.ds(column + to_column, wide)],
                        )
                    )
        return [
            pltpu.make_async_copy(source, target, sems.at[n])
            for n, (source, target) in enumerate(moves)
        ]


class Links:
    def __init__(self, replicas, groups):
        self.replicas, self.groups = replicas, groups

        def pairs(move):
            return [
                (r * groups + g, move(r, g)[0] * groups + move(r, g)[1])
                for r in range(replicas)
                for g in range(groups)
            ]

        self.pair = pairs(lambda r, g: (r ^ 1, g))
        self.first = pairs(lambda r, g: (r ^ (4 if r & 1 else 2), g))
        self.second = pairs(lambda r, g: (r ^ (2 if r & 1 else 4), g))
        self.turns = [pairs(lambda r, g, b=b: (r ^ b, g)) for b in (2, 4)]
        bit = 1
        while bit < groups:
            self.turns.append(pairs(lambda r, g, b=bit: (r, g ^ b)))
            bit *= 2
        self.shift = [pairs(lambda r, g, d=d: (r, (g - d) % groups)) for d in range(groups)]
        self.outer = []
        bit = 8
        while bit < replicas:
            self.outer.append(pairs(lambda r, g, b=bit: (r ^ b, g)))
            bit *= 2

    @staticmethod
    def send(x, perm):
        return lax.ppermute(x, AXES, perm)


VMEM = pl.BlockSpec(memory_space=pltpu.VMEM)
SMEM = pl.BlockSpec(memory_space=pltpu.SMEM)
ANY = pl.BlockSpec(memory_space=pl.ANY)
STRIP = 64


def pieces(rows, width):
    if rows == UNIT:
        return [(0, 0, UNIT, width, 0, 0)]
    half, extra = width // 2, UNIT // 2
    return [
        (0, 0, UNIT, width, 0, 0),
        (0, width, extra, half, UNIT, 0),
        (extra, width, extra, half, UNIT, half),
    ]


def pack(tile):
    if tile.shape[0] == UNIT:
        return tile
    half = tile.shape[1] // 2
    return jnp.concatenate(
        [tile[:UNIT], jnp.concatenate([tile[UNIT:, :half], tile[UNIT:, half:]], 0)], 1
    )


def take(refs, *counts):
    runs, at = [], 0
    for count in counts:
        runs.append(refs[at:at + count])
        at += count
    return [*runs, refs[at:]]


def call(kernel, name, inputs, specs, outs, scratch, vmem=52):
    return pl.pallas_call(
        kernel,
        in_specs=specs,
        out_specs=[VMEM] * len(outs),
        out_shape=outs,
        scratch_shapes=scratch,
        compiler_params=pltpu.CompilerParams(vmem_limit_bytes=vmem << 20),
        cost_estimate=pl.CostEstimate(flops=0, bytes_accessed=1 << 20, transcendentals=0),
        name=name,
    )(*inputs)


def strips(rows, step):
    def run(i, carry):
        step(pl.ds(pl.multiple_of(i * STRIP, STRIP), STRIP))
        return carry

    lax.fori_loop(0, rows // STRIP, run, 0)


def head_forward(v, gain_vec, cosine, sine):
    r = lax.rsqrt(jnp.mean(v * v, -1, keepdims=True) + EPS)
    n = v * r * gain_vec
    return n * cosine + pltpu.roll(n, n.shape[-1] // 2, 1) * sine


def head_back(grad, v, gain_vec, cosine, sine):
    r = lax.rsqrt(jnp.mean(v * v, -1, keepdims=True) + EPS)
    grad = grad * cosine + pltpu.roll(grad * sine, grad.shape[-1] // 2, 1)
    unit_v = v * r
    gain_term = jnp.sum(grad * unit_v, 0, keepdims=True)
    inner = grad * gain_vec
    return r * (inner - unit_v * jnp.mean(unit_v * inner, -1, keepdims=True)), gain_term


def soft(queries, key_rows, bias):
    scores = dot_nt(queries, key_rows) * queries.shape[-1] ** (-0.5) + bias
    exponent = jnp.exp(scores - jnp.max(scores, -1, keepdims=True))
    return exponent / jnp.sum(exponent, -1, keepdims=True)


def attn_forward_kernel(count, head, share, t_qkv, t_out, *refs):
    small, parts, qkv_refs, out_refs, made, scratch = take(
        refs, 7, count, t_qkv.count, t_out.count, 5
    )
    where, gain, query_gain, key_gain, cosine, sine, bias = small
    state, normed, proj, mixed, partial = made
    w_qkv, sem_qkv, w_out, sem_out = scratch
    first_copies = t_qkv.copies(where, qkv_refs, w_qkv, sem_qkv)
    last_copies = t_out.copies(where, out_refs, w_out, sem_out)
    for copy in first_copies + last_copies:
        copy.start()

    def prepare(rows):
        total = parts[0][rows, :].astype(F32)
        for part in parts[1:]:
            total = total + part[rows, :].astype(F32)
        state[rows, :] = total
        normed[rows, :] = rmsnorm(total, gain[...]).astype(BF16)

    strips(state.shape[0], prepare)
    for copy in first_copies:
        copy.wait()
    span = (share + 2) * head
    packs, pack = bias.shape[0], bias.shape[1]

    def group(g, carry):
        columns = pl.ds(pl.multiple_of(g * span, span), span)
        proj[:, columns] = dot(normed[...], w_qkv[:, columns])
        base = g * span
        heads = [
            head_forward(
                proj[:, pl.ds(pl.multiple_of(base + h * head, head), head)],
                query_gain[...] if h < share else key_gain[...],
                cosine[...],
                sine[...],
            ).astype(BF16)
            for h in range(share + 1)
        ]
        value = proj[:, pl.ds(pl.multiple_of(base + (share + 1) * head, head), head)].astype(BF16)
        for b in range(packs):
            rows = slice(b * pack, (b + 1) * pack)
            for h in range(share):
                probs = soft(heads[h][rows], heads[share][rows], bias[b])
                at = pl.multiple_of((g * share + h) * head, head)
                mixed[rows, pl.ds(at, head)] = dot(probs.astype(BF16), value[rows]).astype(BF16)
        return carry

    lax.fori_loop(0, w_qkv.shape[1] // span, group, 0)
    for copy in last_copies:
        copy.wait()
    partial[...] = dot(mixed[...], w_out[...]).astype(BF16)


def mlp_forward_kernel(unit, t_gu, *refs):
    small, gu_refs, made, (weight, sems) = take(refs, 5, t_gu.count, 4)
    where, gain, s_ref, p_ref, c_ref = small
    middle, mlp_in, gate_up, hidden = made
    copies = t_gu.copies(where, gu_refs, weight, sems)
    for copy in copies:
        copy.start()

    def prepare(rows):
        total = s_ref[rows, :] + p_ref[rows, :].astype(F32) + c_ref[rows, :].astype(F32)
        middle[rows, :] = total
        mlp_in[rows, :] = rmsnorm(total, gain[...]).astype(BF16)

    strips(middle.shape[0], prepare)
    for copy in copies:
        copy.wait()

    def block(j, carry):
        columns = pl.ds(pl.multiple_of(j * 2 * unit, 2 * unit), 2 * unit)
        gate_up[:, columns] = dot(mlp_in[...], weight[:, columns])
        gates = gate_up[:, pl.ds(pl.multiple_of(j * 2 * unit, unit), unit)]
        ups = gate_up[:, pl.ds(pl.multiple_of(j * 2 * unit + unit, unit), unit)]
        hidden[:, pl.ds(pl.multiple_of(j * unit, unit), unit)] = (
            gates / (1.0 + jnp.exp(-gates)) * ups
        ).astype(BF16)
        return carry

    lax.fori_loop(0, weight.shape[1] // (2 * unit), block, 0)


def down_kernel(t_dn, where, hidden, *refs):
    dn_refs, (partial,), (weight, sems) = take(refs, t_dn.count, 1)
    copies = t_dn.copies(where, dn_refs, weight, sems)
    for copy in copies:
        copy.start()
    for copy in copies:
        copy.wait()
    partial[...] = dot(hidden[...], weight[...]).astype(BF16)


def mlp_back_kernel(unit, t_dn, t_gu, *refs):
    (where, branch, gate_up), dn_refs, gu_refs, (grad_gu, partial), scratch = take(
        refs, 3, t_dn.count, t_gu.count, 2
    )
    w_down, sem_down, w_gu, sem_gu = scratch
    first_copies = t_dn.copies(where, dn_refs, w_down, sem_down)
    last_copies = t_gu.copies(where, gu_refs, w_gu, sem_gu)
    for copy in first_copies + last_copies:
        copy.start()
    for copy in first_copies:
        copy.wait()

    def block(j, carry):
        grad = dot_nt(branch[...], w_down[pl.ds(pl.multiple_of(j * unit, unit), unit), :])
        at = pl.ds(pl.multiple_of(j * 2 * unit, unit), unit)
        past = pl.ds(pl.multiple_of(j * 2 * unit + unit, unit), unit)
        gates = gate_up[:, at]
        sigma = 1.0 / (1.0 + jnp.exp(-gates))
        silu = gates * sigma
        grad_gu[:, at] = (grad * gate_up[:, past] * (sigma + silu * (1.0 - sigma))).astype(BF16)
        grad_gu[:, past] = (grad * silu).astype(BF16)
        return carry

    lax.fori_loop(0, w_down.shape[0] // unit, block, 0)
    for copy in last_copies:
        copy.wait()
    partial[...] = dot_nt(grad_gu[...], w_gu[...]).astype(BF16)


def norm_back(rows, v_ref, gain, p_ref, c_ref, residual, grad_ref, low_ref, term):
    v = v_ref[rows, :]
    r = lax.rsqrt(jnp.mean(v * v, -1, keepdims=True) + EPS)
    grad = p_ref[rows, :].astype(F32) + c_ref[rows, :].astype(F32)
    unit_v = v * r
    term[...] += jnp.sum(grad * unit_v, 0, keepdims=True)
    inner = grad * gain[...]
    total = residual[rows, :].astype(F32) + r * (
        inner - unit_v * jnp.mean(unit_v * inner, -1, keepdims=True)
    )
    grad_ref[rows, :] = total
    low_ref[rows, :] = total.astype(BF16)


def norm_back_kernel(gain, v_ref, p_ref, c_ref, residual, grad_ref, low_ref, term):
    term[...] = jnp.zeros_like(term)
    strips(
        v_ref.shape[0],
        lambda rows: norm_back(rows, v_ref, gain, p_ref, c_ref, residual, grad_ref, low_ref, term),
    )


def attn_back_kernel(head, share, t_out, t_qkv, *refs):
    small, large, out_refs, qkv_refs, made, scratch = take(
        refs, 7, 5, t_out.count, t_qkv.count, 7
    )
    where, gain, query_gain, key_gain, cosine, sine, bias = small
    v_ref, p_ref, c_ref, residual, proj = large
    grad_ref, low_ref, term, grad_qkv, query_term, key_term, partial = made
    w_out, sem_out, w_qkv, sem_qkv, grad_mixed = scratch
    first_copies = t_out.copies(where, out_refs, w_out, sem_out)
    last_copies = t_qkv.copies(where, qkv_refs, w_qkv, sem_qkv)
    for copy in first_copies + last_copies:
        copy.start()
    norm_back_kernel(gain, v_ref, p_ref, c_ref, residual, grad_ref, low_ref, term)
    for copy in first_copies:
        copy.wait()
    grad_mixed[...] = dot_nt(low_ref[...], w_out[...]).astype(BF16)
    span = (share + 2) * head
    packs, pack = bias.shape[0], bias.shape[1]
    query_term[...] = jnp.zeros_like(query_term)
    key_term[...] = jnp.zeros_like(key_term)
    scale = head ** (-0.5)

    def group(g, carry):
        def part(h):
            return pl.ds(pl.multiple_of(g * span + h * head, head), head)

        for b in range(packs):
            rows = slice(b * pack, (b + 1) * pack)
            cos_b, sin_b = cosine[rows, :], sine[rows, :]
            key_raw = proj[rows, part(share)]
            key_rows = head_forward(key_raw, key_gain[...], cos_b, sin_b).astype(BF16)
            value = proj[rows, part(share + 1)].astype(BF16)
            grad_key = jnp.zeros((pack, head), F32)
            grad_value = jnp.zeros((pack, head), F32)
            for h in range(share):
                query_raw = proj[rows, part(h)]
                query = head_forward(query_raw, query_gain[...], cos_b, sin_b).astype(BF16)
                probs = soft(query, key_rows, bias[b])
                at = pl.multiple_of((g * share + h) * head, head)
                upstream = grad_mixed[rows, pl.ds(at, head)]
                grad_value += dot_tn(probs.astype(BF16), upstream)
                grad_probs = dot_nt(upstream, value)
                grad_scores = probs * (
                    grad_probs - jnp.sum(probs * grad_probs, -1, keepdims=True)
                )
                grad_scores = grad_scores.astype(BF16)
                grad_key += dot_tn(grad_scores, query)
                grad_query, extra = head_back(
                    dot(grad_scores, key_rows) * scale, query_raw, query_gain[...], cos_b, sin_b
                )
                query_term[...] += extra
                grad_qkv[rows, part(h)] = grad_query.astype(BF16)
            grad_key, extra = head_back(grad_key * scale, key_raw, key_gain[...], cos_b, sin_b)
            key_term[...] += extra
            grad_qkv[rows, part(share)] = grad_key.astype(BF16)
            grad_qkv[rows, part(share + 1)] = grad_value.astype(BF16)
        return carry

    lax.fori_loop(0, w_qkv.shape[1] // span, group, 0)
    for copy in last_copies:
        copy.wait()
    partial[...] = dot_nt(grad_qkv[...], w_qkv[...]).astype(BF16)


SLOTS = 3


def finish_kernel(layer, items, spot, *refs):
    tiles = refs[:2 * PLANE]
    total = sum(len(widths) for _, widths, _ in items)
    outs, (narrow, wides, in_sems, sems) = refs[-4 - total:-4], refs[-4:]
    loads = [
        pltpu.make_async_copy(tile, narrow.at[n], in_sems.at[n]) for n, tile in enumerate(tiles)
    ]
    for load in loads:
        load.start()
    busy = [[] for _ in range(SLOTS)]
    for n, load in enumerate(loads):
        m, plane = divmod(n, PLANE)
        slot = n % SLOTS
        for copy in busy[slot]:
            copy.wait()
        load.wait()
        wides[slot] = narrow[n].astype(F32)
        busy[slot] = []
        at, k = 0, 0
        core, place = spot[m], spot[2 + PLANE * m + plane]
        for rows, widths, row_split in items:
            for width in widths:
                row, column = (core * rows, place * width) if row_split else (
                    0, (place * 2 + core) * width
                )
                for from_row, from_column, tall, wide, to_row, to_column in pieces(rows, width):
                    copy = pltpu.make_async_copy(
                        wides.at[slot, pl.ds(from_row, tall), pl.ds(at + from_column, wide)],
                        outs[k].at[
                            layer,
                            pl.ds(pl.multiple_of(row + to_row, 128), tall),
                            pl.ds(pl.multiple_of(column + to_column, 128), wide),
                        ],
                        sems.at[slot, len(busy[slot])],
                    )
                    copy.start()
                    busy[slot].append(copy)
                at += width * rows // UNIT
                k += 1
    for copies in busy:
        for copy in copies:
            copy.wait()


def finish(spot, tiles, layer, items, shapes, previous):
    extra = [] if previous is None else list(previous)
    width = tiles[0].shape[1]
    most = sum(len(pieces(rows, w)) for rows, widths, _ in items for w in widths)
    return pl.pallas_call(
        functools.partial(finish_kernel, layer, items),
        in_specs=[SMEM] + [ANY] * (2 * PLANE + len(extra)),
        out_specs=[ANY] * len(shapes),
        out_shape=[jax.ShapeDtypeStruct(s, F32) for s in shapes],
        scratch_shapes=[
            pltpu.VMEM((2 * PLANE, UNIT, width), BF16),
            pltpu.VMEM((SLOTS, UNIT, width), F32),
            pltpu.SemaphoreType.DMA((2 * PLANE,)),
            pltpu.SemaphoreType.DMA((SLOTS, most)),
        ],
        input_output_aliases={1 + 2 * PLANE + k: k for k in range(len(extra))},
        compiler_params=pltpu.CompilerParams(vmem_limit_bytes=24 << 20),
        cost_estimate=pl.CostEstimate(
            flops=0, bytes_accessed=48 * tiles[0].size, transcendentals=0
        ),
        name="finish",
    )(spot, *tiles, *extra)


def layout(lengths, row_count):
    seq_ends = jnp.cumsum(lengths, 1)
    starts = seq_ends - lengths
    indices = jnp.arange(row_count, dtype=jnp.int32)
    segment = jnp.sum((indices[None, :, None] >= seq_ends[:, None, :]).astype(jnp.int32), 2)
    owners = segment[:, :, None] == jnp.arange(lengths.shape[1], dtype=jnp.int32)[None, None, :]
    position = indices[None, :] - jnp.sum(jnp.where(owners, starts[:, None, :], 0), 2)
    visible = (segment[:, :, None] == segment[:, None, :]) & (
        indices[None, :, None] >= indices[None, None, :]
    )
    return position, jnp.where(visible, 0.0, MASKED).astype(F32)


def rope_tables(position, head_width):
    half_width = head_width // 2
    frequency = THETA ** (-jnp.arange(half_width, dtype=F32) * 2.0 / head_width)
    angles = position.reshape(-1).astype(F32)[:, None] * frequency
    cosine, sine = jnp.cos(angles), jnp.sin(angles)
    return jnp.concatenate([cosine, cosine], 1), jnp.concatenate([-sine, sine], 1)


def body(
    tokens,
    lengths,
    cotangent,
    attn_gain,
    w_query,
    w_key,
    w_value,
    query_gain,
    key_gain,
    w_output,
    mlp_gain,
    w_gate,
    w_up,
    w_down,
    links=None,
):
    send = links.send
    groups = links.groups
    row_count, width = tokens.shape
    layer_count = w_query.shape[0]
    head_width = query_gain.shape[1] * groups
    kv_heads = w_key.shape[2] // head_width
    share = w_query.shape[2] // w_key.shape[2]
    hidden_units = w_gate.shape[2]
    blocks = kv_heads // 2
    unit = hidden_units // (2 * blocks)
    q_width = share * head_width

    replica = lax.axis_index("replica")
    z = lax.axis_index("group")
    core = replica % 2
    plane = (replica // 2) % PLANE
    step_first = 1 + core
    step_second = 2 - core
    planes = [plane, plane ^ step_first, plane ^ step_second, plane ^ 3]
    where = jnp.stack(
        [z] + [(z + d) % groups for d in range(1, groups)] + planes + [core]
    ).astype(jnp.int32)
    partner_planes = [planes[0], planes[2], planes[1], planes[3]]
    spot = jnp.stack([core, 1 - core] + planes + partner_planes).astype(jnp.int32)

    part = attn_gain.shape[1]
    head_part = query_gain.shape[1]

    def pair_rows(rows):
        other = send(rows, links.pair)
        return jnp.concatenate(
            [jnp.where(core == 0, rows, other), jnp.where(core == 0, other, rows)], 0
        )

    position, bias = layout(pair_rows(lengths), row_count)
    cosine, sine = rope_tables(position, head_width)

    def tile_of(own, layer, by_rows):
        sides = []
        for weight in own:
            if by_rows:
                tall, wide = weight.shape[1] // 2, weight.shape[2] // PLANE
                at = (core * tall, plane * wide)
            else:
                tall, wide = weight.shape[1], weight.shape[2] // (2 * PLANE)
                at = (0, (2 * plane + core) * wide)
            sides.append(lax.dynamic_slice(weight, (layer, *at), (1, tall, wide))[0])
        return pack(jnp.concatenate(sides, 1))

    queue = Queue(3)
    nears = []

    def gather(owns, layer, extra=None, direct=False):
        tile = [tile_of(own, layer, by_rows) for own, by_rows in owns]
        widths = [x.shape[1] for x in tile]
        least = max(0, 2 * UNIT - sum(widths))
        if least:
            tile.append(jnp.zeros((UNIT, least), BF16))
        tile = jnp.concatenate(tile, 1)
        if extra is not None:
            extra = jnp.pad(extra, (0, 16 * tile.shape[1] - extra.size))
            tile = jnp.concatenate([tile, extra.reshape(16, -1)], 0)
        if direct:
            column = None
            near = jnp.stack([send(tile, links.shift[d]) for d in range(1, groups)])
        else:
            column = lax.all_gather(tile, "group", axis=0)
            if nears:
                past = queue.sent[-2 if len(nears) == 1 else -3]
                column, _ = lax.optimization_barrier((column, past))
            near = jnp.stack(
                [
                    lax.dynamic_index_in_dim(
                        column[:, :UNIT, :sum(widths)], (z + d) % groups, 0, keepdims=False
                    )
                    for d in range(1, groups)
                ]
            )
        nears.append(near)
        first = queue.send(near, links.first)
        second = queue.send(near, links.second)
        both = queue.send(first, links.second)
        tiles, at = [], 0
        for (own, by_rows), wide in zip(owns, widths):
            tiles.append(Tiles(own, layer, (near, first, second, both), at, by_rows))
            at += wide
        return tiles, column

    gains_own = jnp.concatenate([attn_gain, mlp_gain, query_gain, key_gain], 1)
    gain_width = gains_own.shape[1]
    qkv, out = ((w_query, w_key, w_value), False), ((w_output,), True)
    gate_up, down = ((w_gate, w_up), False), ((w_down,), True)
    weights = []
    for layer in range(layer_count):
        if layer == 0:
            (t_qkv,), _ = gather([qkv], layer, direct=True)
            (t_out, t_dn), column = gather([out, down], layer, gains_own.reshape(-1))
            gains = column[:, UNIT:].reshape(groups, -1)[:, :gains_own.size]
            gains = gains.reshape(groups, layer_count, gain_width)
            (t_gu,), _ = gather([gate_up], layer)
        else:
            (t_qkv, t_out), _ = gather([qkv, out], layer)
            (t_gu,), _ = gather([gate_up], layer)
            (t_dn,), _ = gather([down], layer)
        weights.append((t_qkv, t_out, t_gu, t_dn))

    def gain_of(start, size, layer):
        return gains[:, layer, start:start + size].reshape(1, -1).astype(F32)

    def exchange(partial):
        return send(partial, links.pair)

    def own_rows(rows):
        return lax.dynamic_slice_in_dim(rows, core * row_count, row_count, 0)

    def shape(columns, kind):
        return jax.ShapeDtypeStruct((2 * row_count, columns), kind)

    qkv_columns = blocks * (q_width + 2 * head_width)
    mixed_columns = blocks * q_width
    hidden_columns = blocks * unit
    forms = (head_width, share)

    parts = [pair_rows(tokens)]
    kept = []
    ahead = len(nears) - 2 * layer_count + 1
    for layer in range(layer_count):
        t_qkv, t_out, t_gu, t_dn = weights[layer]
        attn_g = gain_of(0, part, layer)
        mlp_g = gain_of(part, part, layer)
        query_g = gain_of(2 * part, head_part, layer)
        key_g = gain_of(2 * part + head_part, head_part, layer)
        parts[0], _ = lax.optimization_barrier((parts[0], nears[min(ahead, len(nears) - 1)]))
        ahead += 1
        state, normed, proj, mixed, partial = call(
            functools.partial(attn_forward_kernel, len(parts), *forms, t_qkv, t_out),
            "attn_forward",
            [where, attn_g, query_g, key_g, cosine, sine, bias, *parts, *t_qkv.refs, *t_out.refs],
            [SMEM] + [VMEM] * (6 + len(parts)) + [ANY] * (t_qkv.count + t_out.count),
            [
                shape(width, F32),
                shape(width, BF16),
                shape(qkv_columns, F32),
                shape(mixed_columns, BF16),
                shape(width, BF16),
            ],
            t_qkv.scratch() + t_out.scratch(),
        )
        if layer == layer_count - 1:
            partial, _, _ = lax.optimization_barrier((partial, *queue.sent[-3:-1]))
        came = exchange(partial)
        state, _ = lax.optimization_barrier((state, nears[min(ahead, len(nears) - 1)]))
        ahead += 1
        middle, mlp_in, gate_up, hidden = call(
            functools.partial(mlp_forward_kernel, unit, t_gu),
            "mlp_forward",
            [where, mlp_g, state, partial, came, *t_gu.refs],
            [SMEM] + [VMEM] * 4 + [ANY] * t_gu.count,
            [
                shape(width, F32),
                shape(width, BF16),
                shape(2 * hidden_columns, F32),
                shape(hidden_columns, BF16),
            ],
            t_gu.scratch(),
        )
        (partial,) = call(
            functools.partial(down_kernel, t_dn),
            "down",
            [where, hidden, *t_dn.refs],
            [SMEM, VMEM] + [ANY] * t_dn.count,
            [shape(width, BF16)],
            t_dn.scratch(),
        )
        came = exchange(partial)
        parts = [middle, partial, came]
        kept.append((state, normed, proj, mixed, middle, mlp_in, gate_up, hidden,
                     attn_g, mlp_g, query_g, key_g))
    result_tokens = own_rows(
        parts[0] + parts[1].astype(F32) + parts[2].astype(F32)
    ).astype(BF16)

    class Reduction:
        def __init__(self, rows, columns, early=False):
            self.count = columns.shape[1] // PLANE
            self.rows, self.early, self.kept = rows, early, None
            self.picked = [
                lax.dynamic_slice_in_dim(columns, index * self.count, self.count, 1)
                for index in planes
            ]
            if early:
                every = jnp.concatenate([self.picked[j] for j in (3, 1, 2, 0)], 1)
                self.band = self.scatter(dot_tn(rows, every))

        @staticmethod
        def scatter(x):
            return lax.psum_scatter(x.astype(BF16), "group", scatter_dimension=0, tiled=True)

        def part(self, j):
            if self.early:
                return self.band[:, j * 2 * self.count:(j + 1) * 2 * self.count]
            pair = (3, 1) if j == 0 else (2, 0)
            return dot_tn(self.rows, jnp.concatenate([self.picked[k] for k in pair], 1))

        def first(self):
            self.came = queue.send(self.part(0).astype(BF16), links.first)

        def second(self, after=None, alone=True):
            if after is not None:
                self.came, _ = lax.optimization_barrier((self.came, after))
            kept = self.part(1) if self.kept is None else self.kept
            mine = kept.astype(F32) + self.came.astype(F32)
            self.last = queue.send(mine[:, :self.count].astype(BF16), links.second)
            mine = mine[:, self.count:] + self.last.astype(F32)
            for perm in links.outer:
                mine = mine.astype(BF16)
                mine = mine.astype(F32) + send(mine, perm).astype(F32)
            self.mine = mine.astype(BF16)
            if alone:
                self.tile = pack(self.mine if self.early else self.scatter(self.mine))

    def spread(tiles, after):
        tile, _ = lax.optimization_barrier((jnp.concatenate(tiles, 1), gain_step()))
        first = queue.send(tile, links.first)
        held, _ = lax.optimization_barrier((tile, gain_step()))
        second = queue.send(held, links.second)
        both = queue.send(first, links.second)
        mine = [tile, first, second, both]
        held = both
        if after is not None:
            held, _ = lax.optimization_barrier((both, after))
        return mine + [send(x, links.pair) for x in (*mine[:3], held)]

    row_shape = jax.ShapeDtypeStruct((1, width), F32)
    head_shape = jax.ShapeDtypeStruct((1, head_width), F32)
    branch = pair_rows(cotangent)
    gradient = branch
    gain_terms = [None] * layer_count
    sums = []
    for layer in reversed(range(layer_count)):
        t_qkv, t_out, t_gu, t_dn = weights[layer]
        (state, normed, proj, mixed, middle, mlp_in, gate_up, hidden,
         attn_g, mlp_g, query_g, key_g) = kept[layer]
        down_sum = Reduction(hidden, branch, early=bool(sums))
        if not sums:
            down_sum.first()
            down_sum.second()
        grad_gu, partial = call(
            functools.partial(mlp_back_kernel, unit, t_dn, t_gu),
            "mlp_back",
            [where, branch, gate_up, *t_dn.refs, *t_gu.refs],
            [SMEM] + [VMEM] * 2 + [ANY] * (t_dn.count + t_gu.count),
            [shape(2 * hidden_columns, BF16), shape(width, BF16)],
            t_dn.scratch() + t_gu.scratch(),
        )
        grad_gu, partial, _ = lax.optimization_barrier(
            (grad_gu, partial, (sums[-1][2] if sums else down_sum).last)
        )
        came = exchange(partial)
        gu_sum = Reduction(mlp_in, grad_gu)
        gu_sum.first()
        came, gu_sum.kept = lax.optimization_barrier((came, gu_sum.part(1).astype(BF16)))
        grad_middle, grad_out, mlp_term, grad_qkv, query_term, key_term, partial = call(
            functools.partial(attn_back_kernel, *forms, t_out, t_qkv),
            "attn_back",
            [where, mlp_g, query_g, key_g, cosine, sine, bias,
             middle, partial, came, gradient, proj, *t_out.refs, *t_qkv.refs],
            [SMEM] + [VMEM] * 11 + [ANY] * (t_out.count + t_qkv.count),
            [
                shape(width, F32),
                shape(width, BF16),
                row_shape,
                shape(qkv_columns, BF16),
                head_shape,
                head_shape,
                shape(width, BF16),
            ],
            t_out.scratch() + t_qkv.scratch()
            + [pltpu.VMEM((2 * row_count, mixed_columns), BF16)],
        )
        grad_middle, grad_out, grad_qkv, partial, _ = lax.optimization_barrier(
            (grad_middle, grad_out, grad_qkv, partial, gu_sum.came)
        )
        came = exchange(partial)
        qkv_sum = Reduction(normed, grad_qkv)
        out_sum = Reduction(mixed, grad_out, early=not sums)
        if not sums:
            gu_sum.second(query_term)
            qkv_sum.first()
        else:
            above = sums[-1]
            above[0].second(query_term)
            above[1].first()
            above[1].second()
            qkv_sum.first()
            out_sum.first()
            gu_sum.second(result_tokens)
        sums.append((qkv_sum, out_sum, gu_sum, down_sum))
        gradient, branch, attn_term = call(
            norm_back_kernel,
            "norm_back",
            [attn_g, state, partial, came, grad_middle],
            [VMEM] * 5,
            [shape(width, F32), shape(width, BF16), row_shape],
            [],
        )
        gain_terms[layer] = jnp.concatenate([attn_term, mlp_term, query_term, key_term], 1)
    sums[-1][0].second(attn_term, alone=False)
    sums[-1][1].second(alone=False)
    sums[-1][3].first()
    sums[-1][3].second()
    head_tile = Reduction.scatter(jnp.concatenate([x.mine for x in sums[-1][:2]], 1))

    gain_sums = jnp.concatenate(gain_terms, 0)
    gain_sums = jnp.concatenate([gain_sums[:, :2 * width] * 0.5, gain_sums[:, 2 * width:]], 1)
    gain_turns = [links.pair, *links.turns, *links.outer]

    def gain_step():
        nonlocal gain_sums
        if gain_turns:
            gain_sums = gain_sums + send(gain_sums, gain_turns.pop(0))
        return gain_sums

    quarter = width // PLANE
    head_items = [
        (UNIT, (q_width, head_width, head_width), False),
        (w_output.shape[1] // 2, (quarter,), True),
    ]
    unit_items = [(UNIT, (unit, unit), False), (w_down.shape[1] // 2, (quarter,), True)]
    head_shapes = [w_query.shape, w_key.shape, w_value.shape, w_output.shape]
    unit_shapes = [w_gate.shape, w_up.shape, w_down.shape]
    outs = None
    for layer, layer_sums in zip(reversed(range(layer_count)), sums):
        if layer > 0:
            outs = finish(
                spot, spread([x.tile for x in layer_sums], outs and outs[0]), layer,
                head_items + unit_items, head_shapes + unit_shapes, outs,
            )
        else:
            held = outs and outs[0]
            unit_outs = finish(
                spot, spread([x.tile for x in layer_sums[2:]], held), layer,
                unit_items, unit_shapes, outs and outs[len(head_shapes):],
            )
            head_outs = finish(
                spot, spread([head_tile], unit_outs[0]), layer,
                head_items, head_shapes, outs and outs[:len(head_shapes)],
            )
            outs = list(head_outs) + list(unit_outs)

    while gain_turns:
        gain_step()

    def own_gain(start, size):
        return lax.dynamic_slice_in_dim(gain_sums, start + z * size, size, 1)

    return (
        result_tokens,
        own_rows(gradient),
        own_gain(0, part),
        outs[0],
        outs[1],
        outs[2],
        own_gain(2 * width, head_part),
        own_gain(2 * width + head_width, head_part),
        outs[3],
        own_gain(width, part),
        outs[4],
        outs[5],
        outs[6],
    )


def solution(mesh):
    links = Links(mesh.shape["replica"], mesh.shape["group"])
    return jax.shard_map(
        functools.partial(body, links=links),
        mesh=mesh,
        in_specs=(
            P(AXES, None),
            P(AXES, None),
            P(AXES, None),
            P(None, "group"),
            P(None, "group", None),
            P(None, "group", None),
            P(None, "group", None),
            P(None, "group"),
            P(None, "group"),
            P(None, "group", None),
            P(None, "group"),
            P(None, "group", None),
            P(None, "group", None),
            P(None, "group", None),
        ),
        out_specs=(
            P(AXES, None),
            P(AXES, None),
            P(None, "group"),
            P(None, "group", None),
            P(None, "group", None),
            P(None, "group", None),
            P(None, "group"),
            P(None, "group"),
            P(None, "group", None),
            P(None, "group"),
            P(None, "group", None),
            P(None, "group", None),
            P(None, "group", None),
        ),
        check_vma=False,
    )
```

```python
import functools

import jax
import jax.numpy as jnp
from jax import lax
from jax.experimental import pallas as pl
from jax.experimental.pallas import tpu as pltpu
from jax.sharding import PartitionSpec as P

EPS = 1e-06
THETA = 1000000.0
MASKED = -1e30
AXES = ("replica", "group")
BF16 = jnp.bfloat16
F32 = jnp.float32
PLANE = 4
UNIT = 256


def dot(a, b):
    return jnp.dot(a, b, preferred_element_type=F32)


def dot_nt(a, b):
    return lax.dot_general(a, b, (((1,), (1,)), ((), ())), preferred_element_type=F32)


def dot_tn(a, b):
    return lax.dot_general(a, b, (((0,), (0,)), ((), ())), preferred_element_type=F32)


def rmsnorm(vector, gain_vec):
    return vector * lax.rsqrt(jnp.mean(vector * vector, -1, keepdims=True) + EPS) * gain_vec


class Queue:
    def __init__(self, depth):
        self.sent, self.depth = [], depth

    def send(self, x, perm):
        if len(self.sent) >= self.depth:
            x, _ = lax.optimization_barrier((x, self.sent[-self.depth]))
        x = Links.send(x, perm)
        self.sent.append(x)
        return x


class Tiles:
    def __init__(self, own, layer, sent, at, by_rows):
        self.own, self.layer, self.at, self.by_rows = own, layer, at, by_rows
        self.refs = [*own, *sent]
        self.rows = own[0].shape[1] // (2 if by_rows else 1)
        self.widths = [x.shape[2] // (PLANE if by_rows else 2 * PLANE) for x in own]
        self.width = sum(self.widths)
        self.groups = sent[0].shape[0] + 1
        self.count = len(self.refs)

    def scratch(self):
        own = 1 if self.by_rows else PLANE * len(self.own)
        rest = PLANE * (self.groups - 1) * len(pieces(self.rows, self.width))
        return [
            pltpu.VMEM((self.groups * self.rows, PLANE * self.width), BF16),
            pltpu.SemaphoreType.DMA((own + rest,)),
        ]

    def copies(self, where, refs, weight, sems):
        own, rest = refs[:len(self.own)], refs[len(self.own):]
        others, rows, core = self.groups - 1, self.rows, where[self.groups + PLANE]
        band = pl.ds(pl.multiple_of(where[0] * rows, 128), rows)
        moves = []
        if self.by_rows:
            half = pl.ds(pl.multiple_of(core * rows, 128), rows)
            moves.append((own[0].at[self.layer, half], weight.at[band]))
        else:
            for p in range(PLANE):
                column = p * self.width
                for ref, width in zip(own, self.widths):
                    part = pl.ds(pl.multiple_of((2 * p + core) * width, 128), width)
                    moves.append(
                        (ref.at[self.layer, :, part], weight.at[band, pl.ds(column, width)])
                    )
                    column += width
        for j, source in enumerate(rest):
            column = pl.multiple_of(where[1 + others + j] * self.width, 128)
            for d in range(others):
                for row, left, tall, wide, to_row, to_column in pieces(rows, self.width):
                    top = pl.multiple_of(where[1 + d] * rows + to_row, 128)
                    moves.append(
                        (
                            source.at[d, pl.ds(row, tall), pl.ds(self.at + left, wide)],
                            weight.at[pl.ds(top, tall), pl.ds(column + to_column, wide)],
                        )
                    )
        return [
            pltpu.make_async_copy(source, target, sems.at[n])
            for n, (source, target) in enumerate(moves)
        ]


class Links:
    def __init__(self, replicas, groups):
        self.replicas, self.groups = replicas, groups

        def pairs(move):
            return [
                (r * groups + g, move(r, g)[0] * groups + move(r, g)[1])
                for r in range(replicas)
                for g in range(groups)
            ]

        self.pair = pairs(lambda r, g: (r ^ 1, g))
        self.first = pairs(lambda r, g: (r ^ (4 if r & 1 else 2), g))
        self.second = pairs(lambda r, g: (r ^ (2 if r & 1 else 4), g))
        self.turns = [pairs(lambda r, g, b=b: (r ^ b, g)) for b in (2, 4)]
        bit = 1
        while bit < groups:
            self.turns.append(pairs(lambda r, g, b=bit: (r, g ^ b)))
            bit *= 2
        self.shift = [pairs(lambda r, g, d=d: (r, (g - d) % groups)) for d in range(groups)]
        self.outer = []
        bit = 8
        while bit < replicas:
            self.outer.append(pairs(lambda r, g, b=bit: (r ^ b, g)))
            bit *= 2

    @staticmethod
    def send(x, perm):
        return lax.ppermute(x, AXES, perm)


VMEM = pl.BlockSpec(memory_space=pltpu.VMEM)
SMEM = pl.BlockSpec(memory_space=pltpu.SMEM)
ANY = pl.BlockSpec(memory_space=pl.ANY)
STRIP = 64


def pieces(rows, width):
    if rows == UNIT:
        return [(0, 0, UNIT, width, 0, 0)]
    half, extra = width // 2, UNIT // 2
    return [
        (0, 0, UNIT, width, 0, 0),
        (0, width, extra, half, UNIT, 0),
        (extra, width, extra, half, UNIT, half),
    ]


def pack(tile):
    if tile.shape[0] == UNIT:
        return tile
    half = tile.shape[1] // 2
    return jnp.concatenate(
        [tile[:UNIT], jnp.concatenate([tile[UNIT:, :half], tile[UNIT:, half:]], 0)], 1
    )


def take(refs, *counts):
    runs, at = [], 0
    for count in counts:
        runs.append(refs[at:at + count])
        at += count
    return [*runs, refs[at:]]


def call(kernel, name, inputs, specs, outs, scratch, vmem=52):
    return pl.pallas_call(
        kernel,
        in_specs=specs,
        out_specs=[VMEM] * len(outs),
        out_shape=outs,
        scratch_shapes=scratch,
        compiler_params=pltpu.CompilerParams(vmem_limit_bytes=vmem << 20),
        cost_estimate=pl.CostEstimate(flops=0, bytes_accessed=1 << 20, transcendentals=0),
        name=name,
    )(*inputs)


def strips(rows, step):
    def run(i, carry):
        step(pl.ds(pl.multiple_of(i * STRIP, STRIP), STRIP))
        return carry

    lax.fori_loop(0, rows // STRIP, run, 0)


def head_forward(v, gain_vec, cosine, sine):
    r = lax.rsqrt(jnp.mean(v * v, -1, keepdims=True) + EPS)
    n = v * r * gain_vec
    return n * cosine + pltpu.roll(n, n.shape[-1] // 2, 1) * sine


def head_back(grad, v, gain_vec, cosine, sine):
    r = lax.rsqrt(jnp.mean(v * v, -1, keepdims=True) + EPS)
    grad = grad * cosine + pltpu.roll(grad * sine, grad.shape[-1] // 2, 1)
    unit_v = v * r
    gain_term = jnp.sum(grad * unit_v, 0, keepdims=True)
    inner = grad * gain_vec
    return r * (inner - unit_v * jnp.mean(unit_v * inner, -1, keepdims=True)), gain_term


def soft(queries, key_rows, bias):
    scores = dot_nt(queries, key_rows) * queries.shape[-1] ** (-0.5) + bias
    exponent = jnp.exp(scores - jnp.max(scores, -1, keepdims=True))
    return exponent / jnp.sum(exponent, -1, keepdims=True)


def weight_grad(where, planes_at, turned, columns, outs):
    width = columns.shape[1] // PLANE
    each = PLANE // len(outs)
    for n, j in enumerate((3, 1, 2, 0)):
        block = columns[:, pl.ds(pl.multiple_of(where[planes_at + j] * width, 128), width)]
        at = (n % each) * width
        outs[n // each][:, at:at + width] = dot(turned, block).astype(BF16)


def attn_forward_kernel(count, head, share, t_qkv, t_out, *refs):
    small, parts, qkv_refs, out_refs, made, scratch = take(
        refs, 7, count, t_qkv.count, t_out.count, 5
    )
    where, gain, query_gain, key_gain, cosine, sine, bias = small
    state, normed, proj, mixed, partial = made
    w_qkv, sem_qkv, w_out, sem_out = scratch
    first_copies = t_qkv.copies(where, qkv_refs, w_qkv, sem_qkv)
    last_copies = t_out.copies(where, out_refs, w_out, sem_out)
    for copy in first_copies + last_copies:
        copy.start()

    def prepare(rows):
        total = parts[0][rows, :].astype(F32)
        for part in parts[1:]:
            total = total + part[rows, :].astype(F32)
        state[rows, :] = total
        normed[rows, :] = rmsnorm(total, gain[...]).astype(BF16)

    strips(state.shape[0], prepare)
    for copy in first_copies:
        copy.wait()
    span = (share + 2) * head
    packs, pack = bias.shape[0], bias.shape[1]

    def group(g, carry):
        columns = pl.ds(pl.multiple_of(g * span, span), span)
        proj[:, columns] = dot(normed[...], w_qkv[:, columns])
        base = g * span
        heads = [
            head_forward(
                proj[:, pl.ds(pl.multiple_of(base + h * head, head), head)],
                query_gain[...] if h < share else key_gain[...],
                cosine[...],
                sine[...],
            ).astype(BF16)
            for h in range(share + 1)
        ]
        value = proj[:, pl.ds(pl.multiple_of(base + (share + 1) * head, head), head)].astype(BF16)
        for b in range(packs):
            rows = slice(b * pack, (b + 1) * pack)
            for h in range(share):
                probs = soft(heads[h][rows], heads[share][rows], bias[b])
                at = pl.multiple_of((g * share + h) * head, head)
                mixed[rows, pl.ds(at, head)] = dot(probs.astype(BF16), value[rows]).astype(BF16)
        return carry

    lax.fori_loop(0, w_qkv.shape[1] // span, group, 0)
    for copy in last_copies:
        copy.wait()
    partial[...] = dot(mixed[...], w_out[...]).astype(BF16)


def mlp_forward_kernel(unit, t_gu, last, *refs):
    small, branch, gu_refs, made, grads, (weight, sems) = take(
        refs, 5, int(last), t_gu.count, 4, 2 * int(last)
    )
    where, gain, s_ref, p_ref, c_ref = small
    middle, mlp_in, gate_up, hidden = made
    copies = t_gu.copies(where, gu_refs, weight, sems)
    for copy in copies:
        copy.start()

    def prepare(rows):
        total = s_ref[rows, :] + p_ref[rows, :].astype(F32) + c_ref[rows, :].astype(F32)
        middle[rows, :] = total
        mlp_in[rows, :] = rmsnorm(total, gain[...]).astype(BF16)

    strips(middle.shape[0], prepare)
    for copy in copies:
        copy.wait()

    def block(j, carry):
        columns = pl.ds(pl.multiple_of(j * 2 * unit, 2 * unit), 2 * unit)
        gate_up[:, columns] = dot(mlp_in[...], weight[:, columns])
        gates = gate_up[:, pl.ds(pl.multiple_of(j * 2 * unit, unit), unit)]
        ups = gate_up[:, pl.ds(pl.multiple_of(j * 2 * unit + unit, unit), unit)]
        hidden[:, pl.ds(pl.multiple_of(j * unit, unit), unit)] = (
            gates / (1.0 + jnp.exp(-gates)) * ups
        ).astype(BF16)
        return carry

    lax.fori_loop(0, weight.shape[1] // (2 * unit), block, 0)
    if last:
        weight_grad(where, t_gu.groups, hidden[...].T, branch[0], grads)


def down_kernel(t_dn, where, hidden, *refs):
    dn_refs, (partial,), (weight, sems) = take(refs, t_dn.count, 1)
    copies = t_dn.copies(where, dn_refs, weight, sems)
    for copy in copies:
        copy.start()
    for copy in copies:
        copy.wait()
    partial[...] = dot(hidden[...], weight[...]).astype(BF16)


def mlp_back_kernel(unit, t_dn, t_gu, more, *refs):
    small, hidden, dn_refs, gu_refs, (partial,), gu_grads, dn_grads, scratch = take(
        refs, 4, int(more), t_dn.count, t_gu.count, 1, 2, int(more)
    )
    where, branch, gate_up, mlp_in = small
    w_down, sem_down, w_gu, sem_gu, grad_gu = scratch
    first_copies = t_dn.copies(where, dn_refs, w_down, sem_down)
    last_copies = t_gu.copies(where, gu_refs, w_gu, sem_gu)
    for copy in first_copies + last_copies:
        copy.start()
    for copy in first_copies:
        copy.wait()

    def block(j, carry):
        grad = dot_nt(branch[...], w_down[pl.ds(pl.multiple_of(j * unit, unit), unit), :])
        at = pl.ds(pl.multiple_of(j * 2 * unit, unit), unit)
        past = pl.ds(pl.multiple_of(j * 2 * unit + unit, unit), unit)
        gates = gate_up[:, at]
        sigma = 1.0 / (1.0 + jnp.exp(-gates))
        silu = gates * sigma
        grad_gu[:, at] = (grad * gate_up[:, past] * (sigma + silu * (1.0 - sigma))).astype(BF16)
        grad_gu[:, past] = (grad * silu).astype(BF16)
        return carry

    lax.fori_loop(0, w_down.shape[0] // unit, block, 0)
    for copy in last_copies:
        copy.wait()
    partial[...] = dot_nt(grad_gu[...], w_gu[...]).astype(BF16)
    weight_grad(where, t_gu.groups, mlp_in[...].T, grad_gu, gu_grads)
    if more:
        weight_grad(where, t_gu.groups, hidden[0][...].T, branch, dn_grads)


def norm_back(rows, v_ref, gain, p_ref, c_ref, residual, grad_ref, low_ref, term):
    v = v_ref[rows, :]
    r = lax.rsqrt(jnp.mean(v * v, -1, keepdims=True) + EPS)
    grad = p_ref[rows, :].astype(F32) + c_ref[rows, :].astype(F32)
    unit_v = v * r
    term[...] += jnp.sum(grad * unit_v, 0, keepdims=True)
    inner = grad * gain[...]
    total = residual[rows, :].astype(F32) + r * (
        inner - unit_v * jnp.mean(unit_v * inner, -1, keepdims=True)
    )
    grad_ref[rows, :] = total
    low_ref[rows, :] = total.astype(BF16)


def norm_back_kernel(gain, v_ref, p_ref, c_ref, residual, grad_ref, low_ref, term):
    term[...] = jnp.zeros_like(term)
    strips(
        v_ref.shape[0],
        lambda rows: norm_back(rows, v_ref, gain, p_ref, c_ref, residual, grad_ref, low_ref, term),
    )


def attn_back_kernel(head, share, t_out, t_qkv, out_count, *refs):
    small, large, out_refs, qkv_refs, made, qkv_grads, out_grads, scratch = take(
        refs, 7, 7, t_out.count, t_qkv.count, 6, 2, out_count
    )
    where, gain, query_gain, key_gain, cosine, sine, bias = small
    v_ref, p_ref, c_ref, residual, proj, normed, mixed = large
    grad_ref, low_ref, term, query_term, key_term, partial = made
    w_out, sem_out, w_qkv, sem_qkv, grad_mixed, grad_qkv = scratch
    first_copies = t_out.copies(where, out_refs, w_out, sem_out)
    last_copies = t_qkv.copies(where, qkv_refs, w_qkv, sem_qkv)
    for copy in first_copies + last_copies:
        copy.start()
    norm_back_kernel(gain, v_ref, p_ref, c_ref, residual, grad_ref, low_ref, term)
    for copy in first_copies:
        copy.wait()
    grad_mixed[...] = dot_nt(low_ref[...], w_out[...]).astype(BF16)
    span = (share + 2) * head
    packs, pack = bias.shape[0], bias.shape[1]
    query_term[...] = jnp.zeros_like(query_term)
    key_term[...] = jnp.zeros_like(key_term)
    scale = head ** (-0.5)

    def group(g, carry):
        def part(h):
            return pl.ds(pl.multiple_of(g * span + h * head, head), head)

        for b in range(packs):
            rows = slice(b * pack, (b + 1) * pack)
            cos_b, sin_b = cosine[rows, :], sine[rows, :]
            key_raw = proj[rows, part(share)]
            key_rows = head_forward(key_raw, key_gain[...], cos_b, sin_b).astype(BF16)
            value = proj[rows, part(share + 1)].astype(BF16)
            grad_key = jnp.zeros((pack, head), F32)
            grad_value = jnp.zeros((pack, head), F32)
            for h in range(share):
                query_raw = proj[rows, part(h)]
                query = head_forward(query_raw, query_gain[...], cos_b, sin_b).astype(BF16)
                probs = soft(query, key_rows, bias[b])
                at = pl.multiple_of((g * share + h) * head, head)
                upstream = grad_mixed[rows, pl.ds(at, head)]
                grad_value += dot_tn(probs.astype(BF16), upstream)
                grad_probs = dot_nt(upstream, value)
                grad_scores = probs * (
                    grad_probs - jnp.sum(probs * grad_probs, -1, keepdims=True)
                )
                grad_scores = grad_scores.astype(BF16)
                grad_key += dot_tn(grad_scores, query)
                grad_query, extra = head_back(
                    dot(grad_scores, key_rows) * scale, query_raw, query_gain[...], cos_b, sin_b
                )
                query_term[...] += extra
                grad_qkv[rows, part(h)] = grad_query.astype(BF16)
            grad_key, extra = head_back(grad_key * scale, key_raw, key_gain[...], cos_b, sin_b)
            key_term[...] += extra
            grad_qkv[rows, part(share)] = grad_key.astype(BF16)
            grad_qkv[rows, part(share + 1)] = grad_value.astype(BF16)
        return carry

    lax.fori_loop(0, w_qkv.shape[1] // span, group, 0)
    for copy in last_copies:
        copy.wait()
    partial[...] = dot_nt(grad_qkv[...], w_qkv[...]).astype(BF16)
    weight_grad(where, t_qkv.groups, normed[...].T, grad_qkv, qkv_grads)
    weight_grad(where, t_qkv.groups, mixed[...].T, low_ref, out_grads)


SLOTS = 3


def finish_kernel(layer, items, spot, *refs):
    tiles = refs[:2 * PLANE]
    total = sum(len(widths) for _, widths, _ in items)
    outs, (narrow, wides, in_sems, sems) = refs[-4 - total:-4], refs[-4:]
    loads = [
        pltpu.make_async_copy(tile, narrow.at[n], in_sems.at[n]) for n, tile in enumerate(tiles)
    ]
    for load in loads:
        load.start()
    busy = [[] for _ in range(SLOTS)]
    for n, load in enumerate(loads):
        m, plane = divmod(n, PLANE)
        slot = n % SLOTS
        for copy in busy[slot]:
            copy.wait()
        load.wait()
        wides[slot] = narrow[n].astype(F32)
        busy[slot] = []
        at, k = 0, 0
        core, place = spot[m], spot[2 + PLANE * m + plane]
        for rows, widths, row_split in items:
            for width in widths:
                row, column = (core * rows, place * width) if row_split else (
                    0, (place * 2 + core) * width
                )
                for from_row, from_column, tall, wide, to_row, to_column in pieces(rows, width):
                    copy = pltpu.make_async_copy(
                        wides.at[slot, pl.ds(from_row, tall), pl.ds(at + from_column, wide)],
                        outs[k].at[
                            layer,
                            pl.ds(pl.multiple_of(row + to_row, 128), tall),
                            pl.ds(pl.multiple_of(column + to_column, 128), wide),
                        ],
                        sems.at[slot, len(busy[slot])],
                    )
                    copy.start()
                    busy[slot].append(copy)
                at += width * rows // UNIT
                k += 1
    for copies in busy:
        for copy in copies:
            copy.wait()


def finish(spot, tiles, layer, items, shapes, previous):
    extra = [] if previous is None else list(previous)
    width = tiles[0].shape[1]
    most = sum(len(pieces(rows, w)) for rows, widths, _ in items for w in widths)
    return pl.pallas_call(
        functools.partial(finish_kernel, layer, items),
        in_specs=[SMEM] + [ANY] * (2 * PLANE + len(extra)),
        out_specs=[ANY] * len(shapes),
        out_shape=[jax.ShapeDtypeStruct(s, F32) for s in shapes],
        scratch_shapes=[
            pltpu.VMEM((2 * PLANE, UNIT, width), BF16),
            pltpu.VMEM((SLOTS, UNIT, width), F32),
            pltpu.SemaphoreType.DMA((2 * PLANE,)),
            pltpu.SemaphoreType.DMA((SLOTS, most)),
        ],
        input_output_aliases={1 + 2 * PLANE + k: k for k in range(len(extra))},
        compiler_params=pltpu.CompilerParams(vmem_limit_bytes=24 << 20),
        cost_estimate=pl.CostEstimate(
            flops=0, bytes_accessed=48 * tiles[0].size, transcendentals=0
        ),
        name="finish",
    )(spot, *tiles, *extra)


def layout(lengths, row_count):
    seq_ends = jnp.cumsum(lengths, 1)
    starts = seq_ends - lengths
    indices = jnp.arange(row_count, dtype=jnp.int32)
    segment = jnp.sum((indices[None, :, None] >= seq_ends[:, None, :]).astype(jnp.int32), 2)
    owners = segment[:, :, None] == jnp.arange(lengths.shape[1], dtype=jnp.int32)[None, None, :]
    position = indices[None, :] - jnp.sum(jnp.where(owners, starts[:, None, :], 0), 2)
    visible = (segment[:, :, None] == segment[:, None, :]) & (
        indices[None, :, None] >= indices[None, None, :]
    )
    return position, jnp.where(visible, 0.0, MASKED).astype(F32)


def rope_tables(position, head_width):
    half_width = head_width // 2
    frequency = THETA ** (-jnp.arange(half_width, dtype=F32) * 2.0 / head_width)
    angles = position.reshape(-1).astype(F32)[:, None] * frequency
    cosine, sine = jnp.cos(angles), jnp.sin(angles)
    return jnp.concatenate([cosine, cosine], 1), jnp.concatenate([-sine, sine], 1)


def body(
    tokens,
    lengths,
    cotangent,
    attn_gain,
    w_query,
    w_key,
    w_value,
    query_gain,
    key_gain,
    w_output,
    mlp_gain,
    w_gate,
    w_up,
    w_down,
    links=None,
):
    send = links.send
    groups = links.groups
    row_count, width = tokens.shape
    layer_count = w_query.shape[0]
    head_width = query_gain.shape[1] * groups
    kv_heads = w_key.shape[2] // head_width
    share = w_query.shape[2] // w_key.shape[2]
    hidden_units = w_gate.shape[2]
    blocks = kv_heads // 2
    unit = hidden_units // (2 * blocks)
    q_width = share * head_width

    replica = lax.axis_index("replica")
    z = lax.axis_index("group")
    core = replica % 2
    plane = (replica // 2) % PLANE
    step_first = 1 + core
    step_second = 2 - core
    planes = [plane, plane ^ step_first, plane ^ step_second, plane ^ 3]
    where = jnp.stack(
        [z] + [(z + d) % groups for d in range(1, groups)] + planes + [core]
    ).astype(jnp.int32)
    partner_planes = [planes[0], planes[2], planes[1], planes[3]]
    spot = jnp.stack([core, 1 - core] + planes + partner_planes).astype(jnp.int32)

    part = attn_gain.shape[1]
    head_part = query_gain.shape[1]

    def pair_rows(rows):
        other = send(rows, links.pair)
        return jnp.concatenate(
            [jnp.where(core == 0, rows, other), jnp.where(core == 0, other, rows)], 0
        )

    position, bias = layout(pair_rows(lengths), row_count)
    cosine, sine = rope_tables(position, head_width)

    def tile_of(own, layer, by_rows):
        sides = []
        for weight in own:
            if by_rows:
                tall, wide = weight.shape[1] // 2, weight.shape[2] // PLANE
                at = (core * tall, plane * wide)
            else:
                tall, wide = weight.shape[1], weight.shape[2] // (2 * PLANE)
                at = (0, (2 * plane + core) * wide)
            sides.append(lax.dynamic_slice(weight, (layer, *at), (1, tall, wide))[0])
        return pack(jnp.concatenate(sides, 1))

    queue = Queue(3)
    nears = []

    def gather(owns, layer, extra=None, direct=False):
        tile = [tile_of(own, layer, by_rows) for own, by_rows in owns]
        widths = [x.shape[1] for x in tile]
        least = max(0, 2 * UNIT - sum(widths))
        if least:
            tile.append(jnp.zeros((UNIT, least), BF16))
        tile = jnp.concatenate(tile, 1)
        if extra is not None:
            extra = jnp.pad(extra, (0, 16 * tile.shape[1] - extra.size))
            tile = jnp.concatenate([tile, extra.reshape(16, -1)], 0)
        if direct:
            column = None
            near = jnp.stack([send(tile, links.shift[d]) for d in range(1, groups)])
        else:
            column = lax.all_gather(tile, "group", axis=0)
            if nears:
                column, _ = lax.optimization_barrier((column, queue.sent[-3]))
            near = jnp.stack(
                [
                    lax.dynamic_index_in_dim(
                        column[:, :UNIT, :sum(widths)], (z + d) % groups, 0, keepdims=False
                    )
                    for d in range(1, groups)
                ]
            )
        nears.append(near)
        first = queue.send(near, links.first)
        second = queue.send(near, links.second)
        both = queue.send(first, links.second)
        tiles, at = [], 0
        for (own, by_rows), wide in zip(owns, widths):
            tiles.append(Tiles(own, layer, (near, first, second, both), at, by_rows))
            at += wide
        return tiles, column

    gains_own = jnp.concatenate([attn_gain, mlp_gain, query_gain, key_gain], 1)
    gain_width = gains_own.shape[1]
    qkv, out = ((w_query, w_key, w_value), False), ((w_output,), True)
    gate_up, down = ((w_gate, w_up), False), ((w_down,), True)
    weights = []
    for layer in range(layer_count):
        if layer == 0:
            (t_qkv,), _ = gather([qkv], layer, direct=True)
            (t_out, t_dn), column = gather([out, down], layer, gains_own.reshape(-1))
            gains = column[:, UNIT:].reshape(groups, -1)[:, :gains_own.size]
            gains = gains.reshape(groups, layer_count, gain_width)
            (t_gu,), _ = gather([gate_up], layer)
        else:
            (t_qkv, t_out), _ = gather([qkv, out], layer)
            (t_gu,), _ = gather([gate_up], layer)
            (t_dn,), _ = gather([down], layer)
        weights.append((t_qkv, t_out, t_gu, t_dn))

    def gain_of(start, size, layer):
        return gains[:, layer, start:start + size].reshape(1, -1).astype(F32)

    def exchange(partial):
        return send(partial, links.pair)

    def own_rows(rows):
        return lax.dynamic_slice_in_dim(rows, core * row_count, row_count, 0)

    def shape(columns, kind):
        return jax.ShapeDtypeStruct((2 * row_count, columns), kind)

    def grad_shape(rows, columns):
        return jax.ShapeDtypeStruct((rows, columns), BF16)

    branch = pair_rows(cotangent)
    qkv_columns = blocks * (q_width + 2 * head_width)
    mixed_columns = blocks * q_width
    hidden_columns = blocks * unit
    forms = (head_width, share)

    parts = [pair_rows(tokens)]
    kept = []
    ahead = len(nears) - 2 * layer_count + 1
    for layer in range(layer_count):
        t_qkv, t_out, t_gu, t_dn = weights[layer]
        attn_g = gain_of(0, part, layer)
        mlp_g = gain_of(part, part, layer)
        query_g = gain_of(2 * part, head_part, layer)
        key_g = gain_of(2 * part + head_part, head_part, layer)
        parts[0], _ = lax.optimization_barrier((parts[0], nears[min(ahead, len(nears) - 1)]))
        ahead += 1
        state, normed, proj, mixed, partial = call(
            functools.partial(attn_forward_kernel, len(parts), *forms, t_qkv, t_out),
            "attn_forward",
            [where, attn_g, query_g, key_g, cosine, sine, bias, *parts, *t_qkv.refs, *t_out.refs],
            [SMEM] + [VMEM] * (6 + len(parts)) + [ANY] * (t_qkv.count + t_out.count),
            [
                shape(width, F32),
                shape(width, BF16),
                shape(qkv_columns, F32),
                shape(mixed_columns, BF16),
                shape(width, BF16),
            ],
            t_qkv.scratch() + t_out.scratch(),
        )
        came = exchange(partial)
        state, _ = lax.optimization_barrier((state, nears[min(ahead, len(nears) - 1)]))
        ahead += 1
        last = int(layer == layer_count - 1)
        middle, mlp_in, gate_up, hidden, *down_grads = call(
            functools.partial(mlp_forward_kernel, unit, t_gu, last),
            "mlp_forward",
            [where, mlp_g, state, partial, came, *[branch] * last, *t_gu.refs],
            [SMEM] + [VMEM] * (4 + last) + [ANY] * t_gu.count,
            [
                shape(width, F32),
                shape(width, BF16),
                shape(2 * hidden_columns, F32),
                shape(hidden_columns, BF16),
            ]
            + [grad_shape(hidden_columns, width // 2)] * (2 * last),
            t_gu.scratch(),
        )
        if last:
            down_grads = lax.optimization_barrier((*down_grads, *queue.sent[-2:]))[:2]
        (partial,) = call(
            functools.partial(down_kernel, t_dn),
            "down",
            [where, hidden, *t_dn.refs],
            [SMEM, VMEM] + [ANY] * t_dn.count,
            [shape(width, BF16)],
            t_dn.scratch(),
        )
        came = exchange(partial)
        parts = [middle, partial, came]
        kept.append((state, normed, proj, mixed, middle, mlp_in, gate_up, hidden,
                     attn_g, mlp_g, query_g, key_g))
    result_tokens = own_rows(
        parts[0] + parts[1].astype(F32) + parts[2].astype(F32)
    ).astype(BF16)

    class Reduction:
        def __init__(self, grads):
            self.early = len(grads) == 1
            if self.early:
                band = self.scatter(grads[0])
                half = band.shape[1] // 2
                grads = (band[:, :half], band[:, half:])
            self.leaving, self.kept = grads
            self.count = self.kept.shape[1] // 2

        @staticmethod
        def scatter(x):
            return lax.psum_scatter(x.astype(BF16), "group", scatter_dimension=0, tiled=True)

        def first(self):
            self.came = queue.send(self.leaving, links.first)

        def second(self, after=None, alone=True):
            if after is not None:
                self.came, _ = lax.optimization_barrier((self.came, after))
            mine = self.kept.astype(F32) + self.came.astype(F32)
            self.last = queue.send(mine[:, :self.count].astype(BF16), links.second)
            mine = mine[:, self.count:] + self.last.astype(F32)
            for perm in links.outer:
                mine = mine.astype(BF16)
                mine = mine.astype(F32) + send(mine, perm).astype(F32)
            self.mine = mine.astype(BF16)
            if alone:
                self.tile = pack(self.mine if self.early else self.scatter(self.mine))

    def spread(tiles, after):
        tile, _ = lax.optimization_barrier((jnp.concatenate(tiles, 1), gain_step()))
        first = queue.send(tile, links.first)
        held, _ = lax.optimization_barrier((tile, gain_step()))
        second = queue.send(held, links.second)
        both = queue.send(first, links.second)
        mine = [tile, first, second, both]
        held = both
        if after is not None:
            held, _ = lax.optimization_barrier((both, after))
        return mine + [send(x, links.pair) for x in (*mine[:3], held)]

    row_shape = jax.ShapeDtypeStruct((1, width), F32)
    head_shape = jax.ShapeDtypeStruct((1, head_width), F32)
    gradient = branch
    gain_terms = [None] * layer_count
    sums = []
    for layer in reversed(range(layer_count)):
        t_qkv, t_out, t_gu, t_dn = weights[layer]
        (state, normed, proj, mixed, middle, mlp_in, gate_up, hidden,
         attn_g, mlp_g, query_g, key_g) = kept[layer]
        if not sums:
            down_sum = Reduction(down_grads)
            down_sum.first()
        else:
            branch, _ = lax.optimization_barrier((branch, result_tokens))
        more = len(sums)
        partial, *grads = call(
            functools.partial(mlp_back_kernel, unit, t_dn, t_gu, more),
            "mlp_back",
            [where, branch, gate_up, mlp_in, *[hidden] * more, *t_dn.refs, *t_gu.refs],
            [SMEM] + [VMEM] * (3 + more) + [ANY] * (t_dn.count + t_gu.count),
            [shape(width, BF16)]
            + [grad_shape(width, hidden_columns)] * 2
            + [grad_shape(hidden_columns, width)] * more,
            t_dn.scratch() + t_gu.scratch() + [pltpu.VMEM((2 * row_count, 2 * hidden_columns), BF16)],
        )
        partial, *grads = lax.optimization_barrier(
            (partial, *grads, sums[-1][2].last if sums else down_sum.came)
        )[:-1]
        came = exchange(partial)
        gu_sum = Reduction(grads[:2])
        gu_sum.first()
        if sums:
            down_sum = Reduction(grads[2:])
        out_count = 2 if sums else 1
        grad_middle, _, mlp_term, query_term, key_term, partial, *grads = call(
            functools.partial(attn_back_kernel, *forms, t_out, t_qkv, out_count),
            "attn_back",
            [where, mlp_g, query_g, key_g, cosine, sine, bias,
             middle, partial, came, gradient, proj, normed, mixed, *t_out.refs, *t_qkv.refs],
            [SMEM] + [VMEM] * 13 + [ANY] * (t_out.count + t_qkv.count),
            [
                shape(width, F32),
                shape(width, BF16),
                row_shape,
                head_shape,
                head_shape,
                shape(width, BF16),
            ]
            + [grad_shape(width, qkv_columns // 2)] * 2
            + [grad_shape(mixed_columns, width // out_count)] * out_count,
            t_out.scratch() + t_qkv.scratch()
            + [
                pltpu.VMEM((2 * row_count, mixed_columns), BF16),
                pltpu.VMEM((2 * row_count, qkv_columns), BF16),
            ],
        )
        grad_middle, partial, *grads = lax.optimization_barrier(
            (grad_middle, partial, *grads, gu_sum.came)
        )[:-1]
        came = exchange(partial)
        qkv_sum = Reduction(grads[:2])
        out_sum = Reduction(grads[2:])
        if not sums:
            gu_sum.second(query_term)
            down_sum.second()
            qkv_sum.first()
        else:
            above = sums[-1]
            above[0].second(query_term)
            above[1].first()
            above[1].second()
            qkv_sum.first()
            out_sum.first()
            gu_sum.second()
        sums.append((qkv_sum, out_sum, gu_sum, down_sum))
        gradient, branch, attn_term = call(
            norm_back_kernel,
            "norm_back",
            [attn_g, state, partial, came, grad_middle],
            [VMEM] * 5,
            [shape(width, F32), shape(width, BF16), row_shape],
            [],
        )
        gain_terms[layer] = jnp.concatenate([attn_term, mlp_term, query_term, key_term], 1)
    sums[-1][0].second(attn_term, alone=False)
    sums[-1][1].second(alone=False)
    sums[-1][3].first()
    sums[-1][3].second()
    head_tile = Reduction.scatter(jnp.concatenate([x.mine for x in sums[-1][:2]], 1))

    gain_sums = jnp.concatenate(gain_terms, 0)
    gain_sums = jnp.concatenate([gain_sums[:, :2 * width] * 0.5, gain_sums[:, 2 * width:]], 1)
    gain_turns = [links.pair, *links.turns, *links.outer]

    def gain_step():
        nonlocal gain_sums
        if gain_turns:
            gain_sums = gain_sums + send(gain_sums, gain_turns.pop(0))
        return gain_sums

    quarter = width // PLANE
    head_items = [
        (UNIT, (q_width, head_width, head_width), False),
        (w_output.shape[1] // 2, (quarter,), True),
    ]
    unit_items = [(UNIT, (unit, unit), False), (w_down.shape[1] // 2, (quarter,), True)]
    head_shapes = [w_query.shape, w_key.shape, w_value.shape, w_output.shape]
    unit_shapes = [w_gate.shape, w_up.shape, w_down.shape]
    outs = None
    for layer, layer_sums in zip(reversed(range(layer_count)), sums):
        if layer > 0:
            outs = finish(
                spot, spread([x.tile for x in layer_sums], outs and outs[0]), layer,
                head_items + unit_items, head_shapes + unit_shapes, outs,
            )
        else:
            held = outs and outs[0]
            unit_outs = finish(
                spot, spread([x.tile for x in layer_sums[2:]], held), layer,
                unit_items, unit_shapes, outs and outs[len(head_shapes):],
            )
            head_outs = finish(
                spot, spread([head_tile], unit_outs[0]), layer,
                head_items, head_shapes, outs and outs[:len(head_shapes)],
            )
            outs = list(head_outs) + list(unit_outs)

    while gain_turns:
        gain_step()

    def own_gain(start, size):
        return lax.dynamic_slice_in_dim(gain_sums, start + z * size, size, 1)

    return (
        result_tokens,
        own_rows(gradient),
        own_gain(0, part),
        outs[0],
        outs[1],
        outs[2],
        own_gain(2 * width, head_part),
        own_gain(2 * width + head_width, head_part),
        outs[3],
        own_gain(width, part),
        outs[4],
        outs[5],
        outs[6],
    )


def solution(mesh):
    links = Links(mesh.shape["replica"], mesh.shape["group"])
    return jax.shard_map(
        functools.partial(body, links=links),
        mesh=mesh,
        in_specs=(
            P(AXES, None),
            P(AXES, None),
            P(AXES, None),
            P(None, "group"),
            P(None, "group", None),
            P(None, "group", None),
            P(None, "group", None),
            P(None, "group"),
            P(None, "group"),
            P(None, "group", None),
            P(None, "group"),
            P(None, "group", None),
            P(None, "group", None),
            P(None, "group", None),
        ),
        out_specs=(
            P(AXES, None),
            P(AXES, None),
            P(None, "group"),
            P(None, "group", None),
            P(None, "group", None),
            P(None, "group", None),
            P(None, "group"),
            P(None, "group"),
            P(None, "group", None),
            P(None, "group"),
            P(None, "group", None),
            P(None, "group", None),
            P(None, "group", None),
        ),
        check_vma=False,
    )
```

```python
import functools

import jax
import jax.numpy as jnp
from jax import lax
from jax.experimental import pallas as pl
from jax.experimental.pallas import tpu as pltpu
from jax.sharding import PartitionSpec as P

EPS = 1e-06
THETA = 1000000.0
MASKED = -1e30
AXES = ("replica", "group")
BF16 = jnp.bfloat16
F32 = jnp.float32
PLANE = 4
UNIT = 256


def dot(a, b):
    return jnp.dot(a, b, preferred_element_type=F32)


def dot_nt(a, b):
    return lax.dot_general(a, b, (((1,), (1,)), ((), ())), preferred_element_type=F32)


def dot_tn(a, b):
    return lax.dot_general(a, b, (((0,), (0,)), ((), ())), preferred_element_type=F32)


def rmsnorm(vector, gain_vec):
    return vector * lax.rsqrt(jnp.mean(vector * vector, -1, keepdims=True) + EPS) * gain_vec


class Queue:
    def __init__(self, depth):
        self.sent, self.depth = [], depth

    def send(self, x, perm):
        if len(self.sent) >= self.depth:
            x, _ = lax.optimization_barrier((x, self.sent[-self.depth]))
        x = Links.send(x, perm)
        self.sent.append(x)
        return x


class Tiles:
    def __init__(self, own, layer, sent, at, by_rows):
        self.own, self.layer, self.at, self.by_rows = own, layer, at, by_rows
        self.refs = [*own, *sent]
        self.rows = own[0].shape[1] // (2 if by_rows else 1)
        self.widths = [x.shape[2] // (PLANE if by_rows else 2 * PLANE) for x in own]
        self.width = sum(self.widths)
        self.groups = sent[0].shape[0] + 1
        self.count = len(self.refs)

    def scratch(self):
        own = 1 if self.by_rows else PLANE * len(self.own)
        rest = PLANE * (self.groups - 1) * len(pieces(self.rows, self.width))
        return [
            pltpu.VMEM((self.groups * self.rows, PLANE * self.width), BF16),
            pltpu.SemaphoreType.DMA((own + rest,)),
        ]

    def copies(self, where, refs, weight, sems):
        own, rest = refs[:len(self.own)], refs[len(self.own):]
        others, rows, core = self.groups - 1, self.rows, where[self.groups + PLANE]
        band = pl.ds(pl.multiple_of(where[0] * rows, 128), rows)
        moves = []
        if self.by_rows:
            half = pl.ds(pl.multiple_of(core * rows, 128), rows)
            moves.append((own[0].at[self.layer, half], weight.at[band]))
        else:
            for p in range(PLANE):
                column = p * self.width
                for ref, width in zip(own, self.widths):
                    part = pl.ds(pl.multiple_of((2 * p + core) * width, 128), width)
                    moves.append(
                        (ref.at[self.layer, :, part], weight.at[band, pl.ds(column, width)])
                    )
                    column += width
        for j, source in enumerate(rest):
            column = pl.multiple_of(where[1 + others + j] * self.width, 128)
            for d in range(others):
                for row, left, tall, wide, to_row, to_column in pieces(rows, self.width):
                    top = pl.multiple_of(where[1 + d] * rows + to_row, 128)
                    moves.append(
                        (
                            source.at[d, pl.ds(row, tall), pl.ds(self.at + left, wide)],
                            weight.at[pl.ds(top, tall), pl.ds(column + to_column, wide)],
                        )
                    )
        return [
            pltpu.make_async_copy(source, target, sems.at[n])
            for n, (source, target) in enumerate(moves)
        ]


class Links:
    def __init__(self, replicas, groups):
        self.replicas, self.groups = replicas, groups

        def pairs(move):
            return [
                (r * groups + g, move(r, g)[0] * groups + move(r, g)[1])
                for r in range(replicas)
                for g in range(groups)
            ]

        self.pair = pairs(lambda r, g: (r ^ 1, g))
        self.first = pairs(lambda r, g: (r ^ (4 if r & 1 else 2), g))
        self.second = pairs(lambda r, g: (r ^ (2 if r & 1 else 4), g))
        self.turns = [pairs(lambda r, g, b=b: (r ^ b, g)) for b in (2, 4)]
        bit = 1
        while bit < groups:
            self.turns.append(pairs(lambda r, g, b=bit: (r, g ^ b)))
            bit *= 2
        self.shift = [pairs(lambda r, g, d=d: (r, (g - d) % groups)) for d in range(groups)]
        self.outer = []
        bit = 8
        while bit < replicas:
            self.outer.append(pairs(lambda r, g, b=bit: (r ^ b, g)))
            bit *= 2

    @staticmethod
    def send(x, perm):
        return lax.ppermute(x, AXES, perm)


VMEM = pl.BlockSpec(memory_space=pltpu.VMEM)
SMEM = pl.BlockSpec(memory_space=pltpu.SMEM)
ANY = pl.BlockSpec(memory_space=pl.ANY)
STRIP = 64


def pieces(rows, width):
    if rows == UNIT:
        return [(0, 0, UNIT, width, 0, 0)]
    half, extra = width // 2, UNIT // 2
    return [
        (0, 0, UNIT, width, 0, 0),
        (0, width, extra, half, UNIT, 0),
        (extra, width, extra, half, UNIT, half),
    ]


def pack(tile):
    if tile.shape[0] == UNIT:
        return tile
    half = tile.shape[1] // 2
    return jnp.concatenate(
        [tile[:UNIT], jnp.concatenate([tile[UNIT:, :half], tile[UNIT:, half:]], 0)], 1
    )


def take(refs, *counts):
    runs, at = [], 0
    for count in counts:
        runs.append(refs[at:at + count])
        at += count
    return [*runs, refs[at:]]


def call(kernel, name, inputs, specs, outs, scratch, vmem=52):
    return pl.pallas_call(
        kernel,
        in_specs=specs,
        out_specs=[VMEM] * len(outs),
        out_shape=outs,
        scratch_shapes=scratch,
        compiler_params=pltpu.CompilerParams(vmem_limit_bytes=vmem << 20),
        cost_estimate=pl.CostEstimate(flops=0, bytes_accessed=1 << 20, transcendentals=0),
        name=name,
    )(*inputs)


def strips(rows, step):
    def run(i, carry):
        step(pl.ds(pl.multiple_of(i * STRIP, STRIP), STRIP))
        return carry

    lax.fori_loop(0, rows // STRIP, run, 0)


def head_forward(v, gain_vec, cosine, sine):
    r = lax.rsqrt(jnp.mean(v * v, -1, keepdims=True) + EPS)
    n = v * r * gain_vec
    return n * cosine + pltpu.roll(n, n.shape[-1] // 2, 1) * sine


def head_back(grad, v, gain_vec, cosine, sine):
    r = lax.rsqrt(jnp.mean(v * v, -1, keepdims=True) + EPS)
    grad = grad * cosine + pltpu.roll(grad * sine, grad.shape[-1] // 2, 1)
    unit_v = v * r
    gain_term = jnp.sum(grad * unit_v, 0, keepdims=True)
    inner = grad * gain_vec
    return r * (inner - unit_v * jnp.mean(unit_v * inner, -1, keepdims=True)), gain_term


def soft(queries, key_rows, bias):
    scores = dot_nt(queries, key_rows) * queries.shape[-1] ** (-0.5) + bias
    exponent = jnp.exp(scores - jnp.max(scores, -1, keepdims=True))
    return exponent / jnp.sum(exponent, -1, keepdims=True)


def weight_grad(where, planes_at, turned, columns, outs):
    width = columns.shape[1] // PLANE
    each = PLANE // len(outs)
    for n, j in enumerate((3, 1, 2, 0)):
        block = columns[:, pl.ds(pl.multiple_of(where[planes_at + j] * width, 128), width)]
        at = (n % each) * width
        outs[n // each][:, at:at + width] = dot(turned, block).astype(BF16)


def attn_forward_kernel(count, head, share, t_qkv, t_out, *refs):
    small, parts, qkv_refs, out_refs, made, scratch = take(
        refs, 7, count, t_qkv.count, t_out.count, 5
    )
    where, gain, query_gain, key_gain, cosine, sine, bias = small
    state, normed, proj, mixed, partial = made
    w_qkv, sem_qkv, w_out, sem_out = scratch
    first_copies = t_qkv.copies(where, qkv_refs, w_qkv, sem_qkv)
    last_copies = t_out.copies(where, out_refs, w_out, sem_out)
    for copy in first_copies + last_copies:
        copy.start()

    def prepare(rows):
        total = parts[0][rows, :].astype(F32)
        for part in parts[1:]:
            total = total + part[rows, :].astype(F32)
        state[rows, :] = total
        normed[rows, :] = rmsnorm(total, gain[...]).astype(BF16)

    strips(state.shape[0], prepare)
    for copy in first_copies:
        copy.wait()
    span = (share + 2) * head
    packs, pack = bias.shape[0], bias.shape[1]

    def group(g, carry):
        columns = pl.ds(pl.multiple_of(g * span, span), span)
        proj[:, columns] = dot(normed[...], w_qkv[:, columns])
        base = g * span
        heads = [
            head_forward(
                proj[:, pl.ds(pl.multiple_of(base + h * head, head), head)],
                query_gain[...] if h < share else key_gain[...],
                cosine[...],
                sine[...],
            ).astype(BF16)
            for h in range(share + 1)
        ]
        value = proj[:, pl.ds(pl.multiple_of(base + (share + 1) * head, head), head)].astype(BF16)
        for b in range(packs):
            rows = slice(b * pack, (b + 1) * pack)
            for h in range(share):
                probs = soft(heads[h][rows], heads[share][rows], bias[b])
                at = pl.multiple_of((g * share + h) * head, head)
                mixed[rows, pl.ds(at, head)] = dot(probs.astype(BF16), value[rows]).astype(BF16)
        return carry

    lax.fori_loop(0, w_qkv.shape[1] // span, group, 0)
    for copy in last_copies:
        copy.wait()
    partial[...] = dot(mixed[...], w_out[...]).astype(BF16)


def mlp_forward_kernel(unit, t_gu, last, *refs):
    small, branch, gu_refs, made, grads, (weight, sems) = take(
        refs, 5, int(last), t_gu.count, 4, int(last)
    )
    where, gain, s_ref, p_ref, c_ref = small
    middle, mlp_in, gate_up, hidden = made
    copies = t_gu.copies(where, gu_refs, weight, sems)
    for copy in copies:
        copy.start()

    def prepare(rows):
        total = s_ref[rows, :] + p_ref[rows, :].astype(F32) + c_ref[rows, :].astype(F32)
        middle[rows, :] = total
        mlp_in[rows, :] = rmsnorm(total, gain[...]).astype(BF16)

    strips(middle.shape[0], prepare)
    for copy in copies:
        copy.wait()

    def block(j, carry):
        columns = pl.ds(pl.multiple_of(j * 2 * unit, 2 * unit), 2 * unit)
        gate_up[:, columns] = dot(mlp_in[...], weight[:, columns])
        gates = gate_up[:, pl.ds(pl.multiple_of(j * 2 * unit, unit), unit)]
        ups = gate_up[:, pl.ds(pl.multiple_of(j * 2 * unit + unit, unit), unit)]
        hidden[:, pl.ds(pl.multiple_of(j * unit, unit), unit)] = (
            gates / (1.0 + jnp.exp(-gates)) * ups
        ).astype(BF16)
        return carry

    lax.fori_loop(0, weight.shape[1] // (2 * unit), block, 0)
    if last:
        weight_grad(where, t_gu.groups, hidden[...].T, branch[0], grads)


def down_kernel(t_dn, where, hidden, *refs):
    dn_refs, (partial,), (weight, sems) = take(refs, t_dn.count, 1)
    copies = t_dn.copies(where, dn_refs, weight, sems)
    for copy in copies:
        copy.start()
    for copy in copies:
        copy.wait()
    partial[...] = dot(hidden[...], weight[...]).astype(BF16)


def mlp_back_kernel(unit, t_dn, t_gu, more, *refs):
    small, hidden, dn_refs, gu_refs, (partial,), gu_grads, dn_grads, scratch = take(
        refs, 4, int(more), t_dn.count, t_gu.count, 1, 2, int(more)
    )
    where, branch, gate_up, mlp_in = small
    w_down, sem_down, w_gu, sem_gu, grad_gu = scratch
    first_copies = t_dn.copies(where, dn_refs, w_down, sem_down)
    last_copies = t_gu.copies(where, gu_refs, w_gu, sem_gu)
    for copy in first_copies + last_copies:
        copy.start()
    for copy in first_copies:
        copy.wait()

    def block(j, carry):
        grad = dot_nt(branch[...], w_down[pl.ds(pl.multiple_of(j * unit, unit), unit), :])
        at = pl.ds(pl.multiple_of(j * 2 * unit, unit), unit)
        past = pl.ds(pl.multiple_of(j * 2 * unit + unit, unit), unit)
        gates = gate_up[:, at]
        sigma = 1.0 / (1.0 + jnp.exp(-gates))
        silu = gates * sigma
        grad_gu[:, at] = (grad * gate_up[:, past] * (sigma + silu * (1.0 - sigma))).astype(BF16)
        grad_gu[:, past] = (grad * silu).astype(BF16)
        return carry

    lax.fori_loop(0, w_down.shape[0] // unit, block, 0)
    for copy in last_copies:
        copy.wait()
    partial[...] = dot_nt(grad_gu[...], w_gu[...]).astype(BF16)
    weight_grad(where, t_gu.groups, mlp_in[...].T, grad_gu, gu_grads)
    if more:
        weight_grad(where, t_gu.groups, hidden[0][...].T, branch, dn_grads)


def norm_back(rows, v_ref, gain, p_ref, c_ref, residual, grad_ref, low_ref, term):
    v = v_ref[rows, :]
    r = lax.rsqrt(jnp.mean(v * v, -1, keepdims=True) + EPS)
    grad = p_ref[rows, :].astype(F32) + c_ref[rows, :].astype(F32)
    unit_v = v * r
    term[...] += jnp.sum(grad * unit_v, 0, keepdims=True)
    inner = grad * gain[...]
    total = residual[rows, :].astype(F32) + r * (
        inner - unit_v * jnp.mean(unit_v * inner, -1, keepdims=True)
    )
    grad_ref[rows, :] = total
    low_ref[rows, :] = total.astype(BF16)


def norm_back_kernel(gain, v_ref, p_ref, c_ref, residual, grad_ref, low_ref, term):
    term[...] = jnp.zeros_like(term)
    strips(
        v_ref.shape[0],
        lambda rows: norm_back(rows, v_ref, gain, p_ref, c_ref, residual, grad_ref, low_ref, term),
    )


def attn_back_kernel(head, share, t_out, t_qkv, out_count, *refs):
    small, large, out_refs, qkv_refs, made, qkv_grads, out_grads, scratch = take(
        refs, 7, 7, t_out.count, t_qkv.count, 6, 2, out_count
    )
    where, gain, query_gain, key_gain, cosine, sine, bias = small
    v_ref, p_ref, c_ref, residual, proj, normed, mixed = large
    grad_ref, low_ref, term, query_term, key_term, partial = made
    w_out, sem_out, w_qkv, sem_qkv, grad_mixed, grad_qkv = scratch
    first_copies = t_out.copies(where, out_refs, w_out, sem_out)
    last_copies = t_qkv.copies(where, qkv_refs, w_qkv, sem_qkv)
    for copy in first_copies + last_copies:
        copy.start()
    norm_back_kernel(gain, v_ref, p_ref, c_ref, residual, grad_ref, low_ref, term)
    for copy in first_copies:
        copy.wait()
    grad_mixed[...] = dot_nt(low_ref[...], w_out[...]).astype(BF16)
    span = (share + 2) * head
    packs, pack = bias.shape[0], bias.shape[1]
    query_term[...] = jnp.zeros_like(query_term)
    key_term[...] = jnp.zeros_like(key_term)
    scale = head ** (-0.5)

    def group(g, carry):
        def part(h):
            return pl.ds(pl.multiple_of(g * span + h * head, head), head)

        for b in range(packs):
            rows = slice(b * pack, (b + 1) * pack)
            cos_b, sin_b = cosine[rows, :], sine[rows, :]
            key_raw = proj[rows, part(share)]
            key_rows = head_forward(key_raw, key_gain[...], cos_b, sin_b).astype(BF16)
            value = proj[rows, part(share + 1)].astype(BF16)
            grad_key = jnp.zeros((pack, head), F32)
            grad_value = jnp.zeros((pack, head), F32)
            for h in range(share):
                query_raw = proj[rows, part(h)]
                query = head_forward(query_raw, query_gain[...], cos_b, sin_b).astype(BF16)
                probs = soft(query, key_rows, bias[b])
                at = pl.multiple_of((g * share + h) * head, head)
                upstream = grad_mixed[rows, pl.ds(at, head)]
                grad_value += dot_tn(probs.astype(BF16), upstream)
                grad_probs = dot_nt(upstream, value)
                grad_scores = probs * (
                    grad_probs - jnp.sum(probs * grad_probs, -1, keepdims=True)
                )
                grad_scores = grad_scores.astype(BF16)
                grad_key += dot_tn(grad_scores, query)
                grad_query, extra = head_back(
                    dot(grad_scores, key_rows) * scale, query_raw, query_gain[...], cos_b, sin_b
                )
                query_term[...] += extra
                grad_qkv[rows, part(h)] = grad_query.astype(BF16)
            grad_key, extra = head_back(grad_key * scale, key_raw, key_gain[...], cos_b, sin_b)
            key_term[...] += extra
            grad_qkv[rows, part(share)] = grad_key.astype(BF16)
            grad_qkv[rows, part(share + 1)] = grad_value.astype(BF16)
        return carry

    lax.fori_loop(0, w_qkv.shape[1] // span, group, 0)
    for copy in last_copies:
        copy.wait()
    partial[...] = dot_nt(grad_qkv[...], w_qkv[...]).astype(BF16)
    weight_grad(where, t_qkv.groups, normed[...].T, grad_qkv, qkv_grads)
    weight_grad(where, t_qkv.groups, mixed[...].T, low_ref, out_grads)


SLOTS = 3


def finish_kernel(layer, items, spot, *refs):
    tiles = refs[:2 * PLANE]
    total = sum(len(widths) for _, widths, _ in items)
    outs, (narrow, wides, in_sems, sems) = refs[-4 - total:-4], refs[-4:]
    loads = [
        pltpu.make_async_copy(tile, narrow.at[n], in_sems.at[n]) for n, tile in enumerate(tiles)
    ]
    for load in loads:
        load.start()
    busy = [[] for _ in range(SLOTS)]
    for n, load in enumerate(loads):
        m, plane = divmod(n, PLANE)
        slot = n % SLOTS
        for copy in busy[slot]:
            copy.wait()
        load.wait()
        wides[slot] = narrow[n].astype(F32)
        busy[slot] = []
        at, k = 0, 0
        core, place = spot[m], spot[2 + PLANE * m + plane]
        for rows, widths, row_split in items:
            for width in widths:
                row, column = (core * rows, place * width) if row_split else (
                    0, (place * 2 + core) * width
                )
                for from_row, from_column, tall, wide, to_row, to_column in pieces(rows, width):
                    copy = pltpu.make_async_copy(
                        wides.at[slot, pl.ds(from_row, tall), pl.ds(at + from_column, wide)],
                        outs[k].at[
                            layer,
                            pl.ds(pl.multiple_of(row + to_row, 128), tall),
                            pl.ds(pl.multiple_of(column + to_column, 128), wide),
                        ],
                        sems.at[slot, len(busy[slot])],
                    )
                    copy.start()
                    busy[slot].append(copy)
                at += width * rows // UNIT
                k += 1
    for copies in busy:
        for copy in copies:
            copy.wait()


def finish(spot, tiles, layer, items, shapes, previous):
    extra = [] if previous is None else list(previous)
    width = tiles[0].shape[1]
    most = sum(len(pieces(rows, w)) for rows, widths, _ in items for w in widths)
    return pl.pallas_call(
        functools.partial(finish_kernel, layer, items),
        in_specs=[SMEM] + [ANY] * (2 * PLANE + len(extra)),
        out_specs=[ANY] * len(shapes),
        out_shape=[jax.ShapeDtypeStruct(s, F32) for s in shapes],
        scratch_shapes=[
            pltpu.VMEM((2 * PLANE, UNIT, width), BF16),
            pltpu.VMEM((SLOTS, UNIT, width), F32),
            pltpu.SemaphoreType.DMA((2 * PLANE,)),
            pltpu.SemaphoreType.DMA((SLOTS, most)),
        ],
        input_output_aliases={1 + 2 * PLANE + k: k for k in range(len(extra))},
        compiler_params=pltpu.CompilerParams(vmem_limit_bytes=24 << 20),
        cost_estimate=pl.CostEstimate(
            flops=0, bytes_accessed=48 * tiles[0].size, transcendentals=0
        ),
        name="finish",
    )(spot, *tiles, *extra)


def layout(lengths, row_count):
    seq_ends = jnp.cumsum(lengths, 1)
    starts = seq_ends - lengths
    indices = jnp.arange(row_count, dtype=jnp.int32)
    segment = jnp.sum((indices[None, :, None] >= seq_ends[:, None, :]).astype(jnp.int32), 2)
    owners = segment[:, :, None] == jnp.arange(lengths.shape[1], dtype=jnp.int32)[None, None, :]
    position = indices[None, :] - jnp.sum(jnp.where(owners, starts[:, None, :], 0), 2)
    visible = (segment[:, :, None] == segment[:, None, :]) & (
        indices[None, :, None] >= indices[None, None, :]
    )
    return position, jnp.where(visible, 0.0, MASKED).astype(F32)


def rope_tables(position, head_width):
    half_width = head_width // 2
    frequency = THETA ** (-jnp.arange(half_width, dtype=F32) * 2.0 / head_width)
    angles = position.reshape(-1).astype(F32)[:, None] * frequency
    cosine, sine = jnp.cos(angles), jnp.sin(angles)
    return jnp.concatenate([cosine, cosine], 1), jnp.concatenate([-sine, sine], 1)


def body(
    tokens,
    lengths,
    cotangent,
    attn_gain,
    w_query,
    w_key,
    w_value,
    query_gain,
    key_gain,
    w_output,
    mlp_gain,
    w_gate,
    w_up,
    w_down,
    links=None,
):
    send = links.send
    groups = links.groups
    row_count, width = tokens.shape
    layer_count = w_query.shape[0]
    head_width = query_gain.shape[1] * groups
    kv_heads = w_key.shape[2] // head_width
    share = w_query.shape[2] // w_key.shape[2]
    hidden_units = w_gate.shape[2]
    blocks = kv_heads // 2
    unit = hidden_units // (2 * blocks)
    q_width = share * head_width

    replica = lax.axis_index("replica")
    z = lax.axis_index("group")
    core = replica % 2
    plane = (replica // 2) % PLANE
    step_first = 1 + core
    step_second = 2 - core
    planes = [plane, plane ^ step_first, plane ^ step_second, plane ^ 3]
    where = jnp.stack(
        [z] + [(z + d) % groups for d in range(1, groups)] + planes + [core]
    ).astype(jnp.int32)
    partner_planes = [planes[0], planes[2], planes[1], planes[3]]
    spot = jnp.stack([core, 1 - core] + planes + partner_planes).astype(jnp.int32)

    part = attn_gain.shape[1]
    head_part = query_gain.shape[1]

    def pair_rows(rows):
        other = send(rows, links.pair)
        return jnp.concatenate(
            [jnp.where(core == 0, rows, other), jnp.where(core == 0, other, rows)], 0
        )

    position, bias = layout(pair_rows(lengths), row_count)
    cosine, sine = rope_tables(position, head_width)

    def tile_of(own, layer, by_rows):
        sides = []
        for weight in own:
            if by_rows:
                tall, wide = weight.shape[1] // 2, weight.shape[2] // PLANE
                at = (core * tall, plane * wide)
            else:
                tall, wide = weight.shape[1], weight.shape[2] // (2 * PLANE)
                at = (0, (2 * plane + core) * wide)
            sides.append(lax.dynamic_slice(weight, (layer, *at), (1, tall, wide))[0])
        return pack(jnp.concatenate(sides, 1))

    queue = Queue(3)
    nears = []

    def gather(owns, layer, extra=None, direct=False):
        tile = [tile_of(own, layer, by_rows) for own, by_rows in owns]
        widths = [x.shape[1] for x in tile]
        least = max(0, 2 * UNIT - sum(widths))
        if least:
            tile.append(jnp.zeros((UNIT, least), BF16))
        tile = jnp.concatenate(tile, 1)
        if extra is not None:
            extra = jnp.pad(extra, (0, 16 * tile.shape[1] - extra.size))
            tile = jnp.concatenate([tile, extra.reshape(16, -1)], 0)
        if direct:
            column = None
            near = jnp.stack([send(tile, links.shift[d]) for d in range(1, groups)])
        else:
            column = lax.all_gather(tile, "group", axis=0)
            if nears:
                column, _ = lax.optimization_barrier((column, queue.sent[-3]))
            near = jnp.stack(
                [
                    lax.dynamic_index_in_dim(
                        column[:, :UNIT, :sum(widths)], (z + d) % groups, 0, keepdims=False
                    )
                    for d in range(1, groups)
                ]
            )
        nears.append(near)
        first = queue.send(near, links.first)
        second = queue.send(near, links.second)
        both = queue.send(first, links.second)
        tiles, at = [], 0
        for (own, by_rows), wide in zip(owns, widths):
            tiles.append(Tiles(own, layer, (near, first, second, both), at, by_rows))
            at += wide
        return tiles, column

    gains_own = jnp.concatenate([attn_gain, mlp_gain, query_gain, key_gain], 1)
    gain_width = gains_own.shape[1]
    qkv, out = ((w_query, w_key, w_value), False), ((w_output,), True)
    gate_up, down = ((w_gate, w_up), False), ((w_down,), True)
    weights = []
    for layer in range(layer_count):
        if layer == 0:
            (t_qkv,), _ = gather([qkv], layer, direct=True)
            (t_out, t_dn), column = gather([out, down], layer, gains_own.reshape(-1))
            gains = column[:, UNIT:].reshape(groups, -1)[:, :gains_own.size]
            gains = gains.reshape(groups, layer_count, gain_width)
            (t_gu,), _ = gather([gate_up], layer)
        else:
            (t_qkv, t_out), _ = gather([qkv, out], layer)
            (t_gu,), _ = gather([gate_up], layer)
            (t_dn,), _ = gather([down], layer)
        weights.append((t_qkv, t_out, t_gu, t_dn))

    def gain_of(start, size, layer):
        return gains[:, layer, start:start + size].reshape(1, -1).astype(F32)

    def exchange(partial):
        return send(partial, links.pair)

    def own_rows(rows):
        return lax.dynamic_slice_in_dim(rows, core * row_count, row_count, 0)

    def shape(columns, kind):
        return jax.ShapeDtypeStruct((2 * row_count, columns), kind)

    def grad_shape(rows, columns):
        return jax.ShapeDtypeStruct((rows, columns), BF16)

    branch = pair_rows(cotangent)
    qkv_columns = blocks * (q_width + 2 * head_width)
    mixed_columns = blocks * q_width
    hidden_columns = blocks * unit
    forms = (head_width, share)

    parts = [pair_rows(tokens)]
    kept = []
    ahead = len(nears) - 2 * layer_count + 1
    for layer in range(layer_count):
        t_qkv, t_out, t_gu, t_dn = weights[layer]
        attn_g = gain_of(0, part, layer)
        mlp_g = gain_of(part, part, layer)
        query_g = gain_of(2 * part, head_part, layer)
        key_g = gain_of(2 * part + head_part, head_part, layer)
        parts[0], _ = lax.optimization_barrier((parts[0], nears[min(ahead, len(nears) - 1)]))
        ahead += 1
        state, normed, proj, mixed, partial = call(
            functools.partial(attn_forward_kernel, len(parts), *forms, t_qkv, t_out),
            "attn_forward",
            [where, attn_g, query_g, key_g, cosine, sine, bias, *parts, *t_qkv.refs, *t_out.refs],
            [SMEM] + [VMEM] * (6 + len(parts)) + [ANY] * (t_qkv.count + t_out.count),
            [
                shape(width, F32),
                shape(width, BF16),
                shape(qkv_columns, F32),
                shape(mixed_columns, BF16),
                shape(width, BF16),
            ],
            t_qkv.scratch() + t_out.scratch(),
        )
        came = exchange(partial)
        state, _ = lax.optimization_barrier((state, nears[min(ahead, len(nears) - 1)]))
        ahead += 1
        last = int(layer == layer_count - 1)
        middle, mlp_in, gate_up, hidden, *down_grads = call(
            functools.partial(mlp_forward_kernel, unit, t_gu, last),
            "mlp_forward",
            [where, mlp_g, state, partial, came, *[branch] * last, *t_gu.refs],
            [SMEM] + [VMEM] * (4 + last) + [ANY] * t_gu.count,
            [
                shape(width, F32),
                shape(width, BF16),
                shape(2 * hidden_columns, F32),
                shape(hidden_columns, BF16),
            ]
            + [grad_shape(hidden_columns, width)] * last,
            t_gu.scratch(),
        )
        if last:
            down_grads = lax.optimization_barrier((*down_grads, *queue.sent[-2:]))[:1]
        (partial,) = call(
            functools.partial(down_kernel, t_dn),
            "down",
            [where, hidden, *t_dn.refs],
            [SMEM, VMEM] + [ANY] * t_dn.count,
            [shape(width, BF16)],
            t_dn.scratch(),
        )
        came = exchange(partial)
        parts = [middle, partial, came]
        kept.append((state, normed, proj, mixed, middle, mlp_in, gate_up, hidden,
                     attn_g, mlp_g, query_g, key_g))
    result_tokens = own_rows(
        parts[0] + parts[1].astype(F32) + parts[2].astype(F32)
    ).astype(BF16)

    bands = []

    class Reduction:
        def __init__(self, grads):
            self.early = len(grads) == 1
            if self.early:
                band = self.scatter(grads[0])
                half = band.shape[1] // 2
                grads = (band[:, :half], band[:, half:])
            self.leaving, self.kept = grads
            self.count = self.kept.shape[1] // 2

        @staticmethod
        def scatter(x):
            if bands:
                x, _ = lax.optimization_barrier((x, bands[-1]))
            bands.append(lax.psum_scatter(x, "group", scatter_dimension=0, tiled=True))
            return bands[-1]

        def first(self):
            self.came = queue.send(self.leaving, links.first)

        def second(self, after=None, alone=True):
            if after is not None:
                self.came, _ = lax.optimization_barrier((self.came, after))
            mine = self.kept.astype(F32) + self.came.astype(F32)
            self.last = queue.send(mine[:, :self.count].astype(BF16), links.second)
            mine = mine[:, self.count:] + self.last.astype(F32)
            for perm in links.outer:
                mine = mine.astype(BF16)
                mine = mine.astype(F32) + send(mine, perm).astype(F32)
            self.mine = mine.astype(BF16)
            if alone:
                self.tile = pack(self.mine if self.early else self.scatter(self.mine))

    def spread(tiles, after):
        tile, _ = lax.optimization_barrier((jnp.concatenate(tiles, 1), gain_step()))
        first = queue.send(tile, links.first)
        held, _ = lax.optimization_barrier((tile, gain_step()))
        second = queue.send(held, links.second)
        both = queue.send(first, links.second)
        mine = [tile, first, second, both]
        held = both
        if after is not None:
            held, _ = lax.optimization_barrier((both, after))
        return mine + [send(x, links.pair) for x in (*mine[:3], held)]

    row_shape = jax.ShapeDtypeStruct((1, width), F32)
    head_shape = jax.ShapeDtypeStruct((1, head_width), F32)
    gradient = branch
    gain_terms = [None] * layer_count
    sums = []
    for layer in reversed(range(layer_count)):
        t_qkv, t_out, t_gu, t_dn = weights[layer]
        (state, normed, proj, mixed, middle, mlp_in, gate_up, hidden,
         attn_g, mlp_g, query_g, key_g) = kept[layer]
        if not sums:
            down_sum = Reduction(down_grads)
        else:
            branch, _ = lax.optimization_barrier((branch, result_tokens))
        more = len(sums)
        partial, *grads = call(
            functools.partial(mlp_back_kernel, unit, t_dn, t_gu, more),
            "mlp_back",
            [where, branch, gate_up, mlp_in, *[hidden] * more, *t_dn.refs, *t_gu.refs],
            [SMEM] + [VMEM] * (3 + more) + [ANY] * (t_dn.count + t_gu.count),
            [shape(width, BF16)]
            + [grad_shape(width, hidden_columns)] * 2
            + [grad_shape(hidden_columns, width)] * more,
            t_dn.scratch() + t_gu.scratch() + [pltpu.VMEM((2 * row_count, 2 * hidden_columns), BF16)],
        )
        if sums:
            partial, *grads = lax.optimization_barrier((partial, *grads, sums[-1][0].came))[:-1]
        came = exchange(partial)
        gu_sum = Reduction(grads[:2])
        gu_sum.first()
        if sums:
            down_sum = Reduction(grads[2:])
        out_count = 2 if sums else 1
        grad_middle, _, mlp_term, query_term, key_term, partial, *grads = call(
            functools.partial(attn_back_kernel, *forms, t_out, t_qkv, out_count),
            "attn_back",
            [where, mlp_g, query_g, key_g, cosine, sine, bias,
             middle, partial, came, gradient, proj, normed, mixed, *t_out.refs, *t_qkv.refs],
            [SMEM] + [VMEM] * 13 + [ANY] * (t_out.count + t_qkv.count),
            [
                shape(width, F32),
                shape(width, BF16),
                row_shape,
                head_shape,
                head_shape,
                shape(width, BF16),
            ]
            + [grad_shape(width, qkv_columns // 2)] * 2
            + [grad_shape(mixed_columns, width // out_count)] * out_count,
            t_out.scratch() + t_qkv.scratch()
            + [
                pltpu.VMEM((2 * row_count, mixed_columns), BF16),
                pltpu.VMEM((2 * row_count, qkv_columns), BF16),
            ],
        )
        grad_middle, query_term, partial, *grads = lax.optimization_barrier(
            (grad_middle, query_term, partial, *grads, gu_sum.came)
        )[:-1]
        came = exchange(partial)
        qkv_sum = Reduction(grads[:2])
        out_sum = Reduction(grads[2:])
        if not sums:
            gu_sum.second(query_term)
            qkv_sum.first()
        else:
            above = sums[-1]
            above[0].second(query_term)
            for x in (above[1], above[3]):
                x.leaving, _ = lax.optimization_barrier((x.leaving, query_term))
                x.first()
                x.second()
            qkv_sum.first()
            out_sum.first()
            gu_sum.second()
        sums.append((qkv_sum, out_sum, gu_sum, down_sum))
        gradient, branch, attn_term = call(
            norm_back_kernel,
            "norm_back",
            [attn_g, state, partial, came, grad_middle],
            [VMEM] * 5,
            [shape(width, F32), shape(width, BF16), row_shape],
            [],
        )
        gain_terms[layer] = jnp.concatenate([attn_term, mlp_term, query_term, key_term], 1)
    sums[-1][0].second(attn_term, alone=False)
    sums[-1][1].second(alone=False)
    sums[-1][3].first()
    sums[-1][3].second()
    head_tile = Reduction.scatter(jnp.concatenate([x.mine for x in sums[-1][:2]], 1))

    gain_sums = jnp.concatenate(gain_terms, 0)
    gain_sums = jnp.concatenate([gain_sums[:, :2 * width] * 0.5, gain_sums[:, 2 * width:]], 1)
    gain_turns = [links.pair, *links.turns, *links.outer]

    def gain_step():
        nonlocal gain_sums
        if gain_turns:
            gain_sums = gain_sums + send(gain_sums, gain_turns.pop(0))
        return gain_sums

    quarter = width // PLANE
    head_items = [
        (UNIT, (q_width, head_width, head_width), False),
        (w_output.shape[1] // 2, (quarter,), True),
    ]
    unit_items = [(UNIT, (unit, unit), False), (w_down.shape[1] // 2, (quarter,), True)]
    head_shapes = [w_query.shape, w_key.shape, w_value.shape, w_output.shape]
    unit_shapes = [w_gate.shape, w_up.shape, w_down.shape]
    outs = None
    for layer, layer_sums in zip(reversed(range(layer_count)), sums):
        if layer > 0:
            outs = finish(
                spot, spread([x.tile for x in layer_sums], outs and outs[0]), layer,
                head_items + unit_items, head_shapes + unit_shapes, outs,
            )
        else:
            held = outs and outs[0]
            unit_outs = finish(
                spot, spread([x.tile for x in layer_sums[2:]], held), layer,
                unit_items, unit_shapes, outs and outs[len(head_shapes):],
            )
            head_outs = finish(
                spot, spread([head_tile], unit_outs[0]), layer,
                head_items, head_shapes, outs and outs[:len(head_shapes)],
            )
            outs = list(head_outs) + list(unit_outs)

    while gain_turns:
        gain_step()

    def own_gain(start, size):
        return lax.dynamic_slice_in_dim(gain_sums, start + z * size, size, 1)

    return (
        result_tokens,
        own_rows(gradient),
        own_gain(0, part),
        outs[0],
        outs[1],
        outs[2],
        own_gain(2 * width, head_part),
        own_gain(2 * width + head_width, head_part),
        outs[3],
        own_gain(width, part),
        outs[4],
        outs[5],
        outs[6],
    )


def solution(mesh):
    links = Links(mesh.shape["replica"], mesh.shape["group"])
    return jax.shard_map(
        functools.partial(body, links=links),
        mesh=mesh,
        in_specs=(
            P(AXES, None),
            P(AXES, None),
            P(AXES, None),
            P(None, "group"),
            P(None, "group", None),
            P(None, "group", None),
            P(None, "group", None),
            P(None, "group"),
            P(None, "group"),
            P(None, "group", None),
            P(None, "group"),
            P(None, "group", None),
            P(None, "group", None),
            P(None, "group", None),
        ),
        out_specs=(
            P(AXES, None),
            P(AXES, None),
            P(None, "group"),
            P(None, "group", None),
            P(None, "group", None),
            P(None, "group", None),
            P(None, "group"),
            P(None, "group"),
            P(None, "group", None),
            P(None, "group"),
            P(None, "group", None),
            P(None, "group", None),
            P(None, "group", None),
        ),
        check_vma=False,
    )
```

```python
import functools

import jax
import jax.numpy as jnp
from jax import lax
from jax.experimental import pallas as pl
from jax.experimental.pallas import tpu as pltpu
from jax.sharding import PartitionSpec as P

EPS = 1e-06
THETA = 1000000.0
MASKED = -1e30
AXES = ("replica", "group")
BF16 = jnp.bfloat16
F32 = jnp.float32
PLANE = 4
UNIT = 256


def dot(a, b):
    return jnp.dot(a, b, preferred_element_type=F32)


def dot_nt(a, b):
    return lax.dot_general(a, b, (((1,), (1,)), ((), ())), preferred_element_type=F32)


def dot_tn(a, b):
    return lax.dot_general(a, b, (((0,), (0,)), ((), ())), preferred_element_type=F32)


def rmsnorm(vector, gain_vec):
    return vector * lax.rsqrt(jnp.mean(vector * vector, -1, keepdims=True) + EPS) * gain_vec


class Queue:
    def __init__(self, depth):
        self.sent, self.depth = [], depth

    def send(self, x, perm):
        if len(self.sent) >= self.depth:
            x, _ = lax.optimization_barrier((x, self.sent[-self.depth]))
        x = Links.send(x, perm)
        self.sent.append(x)
        return x


class Tiles:
    def __init__(self, own, layer, sent, at, by_rows):
        self.own, self.layer, self.at, self.by_rows = own, layer, at, by_rows
        self.refs = [*own, *sent]
        self.rows = own[0].shape[1] // (2 if by_rows else 1)
        self.widths = [x.shape[2] // (PLANE if by_rows else 2 * PLANE) for x in own]
        self.width = sum(self.widths)
        self.groups = sent[0].shape[0] + 1
        self.count = len(self.refs)

    def scratch(self):
        own = 1 if self.by_rows else PLANE * len(self.own)
        rest = PLANE * (self.groups - 1) * len(pieces(self.rows, self.width))
        return [
            pltpu.VMEM((self.groups * self.rows, PLANE * self.width), BF16),
            pltpu.SemaphoreType.DMA((own + rest,)),
        ]

    def copies(self, where, refs, weight, sems):
        own, rest = refs[:len(self.own)], refs[len(self.own):]
        others, rows, core = self.groups - 1, self.rows, where[self.groups + PLANE]
        band = pl.ds(pl.multiple_of(where[0] * rows, 128), rows)
        moves = []
        if self.by_rows:
            half = pl.ds(pl.multiple_of(core * rows, 128), rows)
            moves.append((own[0].at[self.layer, half], weight.at[band]))
        else:
            for p in range(PLANE):
                column = p * self.width
                for ref, width in zip(own, self.widths):
                    part = pl.ds(pl.multiple_of((2 * p + core) * width, 128), width)
                    moves.append(
                        (ref.at[self.layer, :, part], weight.at[band, pl.ds(column, width)])
                    )
                    column += width
        for j, source in enumerate(rest):
            column = pl.multiple_of(where[1 + others + j] * self.width, 128)
            for d in range(others):
                for row, left, tall, wide, to_row, to_column in pieces(rows, self.width):
                    top = pl.multiple_of(where[1 + d] * rows + to_row, 128)
                    moves.append(
                        (
                            source.at[d, pl.ds(row, tall), pl.ds(self.at + left, wide)],
                            weight.at[pl.ds(top, tall), pl.ds(column + to_column, wide)],
                        )
                    )
        return [
            pltpu.make_async_copy(source, target, sems.at[n])
            for n, (source, target) in enumerate(moves)
        ]


class Links:
    def __init__(self, replicas, groups):
        self.replicas, self.groups = replicas, groups

        def pairs(move):
            return [
                (r * groups + g, move(r, g)[0] * groups + move(r, g)[1])
                for r in range(replicas)
                for g in range(groups)
            ]

        self.pair = pairs(lambda r, g: (r ^ 1, g))
        self.first = pairs(lambda r, g: (r ^ (4 if r & 1 else 2), g))
        self.second = pairs(lambda r, g: (r ^ (2 if r & 1 else 4), g))
        self.turns = [pairs(lambda r, g, b=b: (r ^ b, g)) for b in (2, 4)]
        bit = 1
        while bit < groups:
            self.turns.append(pairs(lambda r, g, b=bit: (r, g ^ b)))
            bit *= 2
        self.shift = [pairs(lambda r, g, d=d: (r, (g - d) % groups)) for d in range(groups)]
        self.outer = []
        bit = 8
        while bit < replicas:
            self.outer.append(pairs(lambda r, g, b=bit: (r ^ b, g)))
            bit *= 2

    @staticmethod
    def send(x, perm):
        return lax.ppermute(x, AXES, perm)


VMEM = pl.BlockSpec(memory_space=pltpu.VMEM)
SMEM = pl.BlockSpec(memory_space=pltpu.SMEM)
ANY = pl.BlockSpec(memory_space=pl.ANY)
STRIP = 64


def pieces(rows, width):
    if rows == UNIT:
        return [(0, 0, UNIT, width, 0, 0)]
    half, extra = width // 2, UNIT // 2
    return [
        (0, 0, UNIT, width, 0, 0),
        (0, width, extra, half, UNIT, 0),
        (extra, width, extra, half, UNIT, half),
    ]


def pack(tile):
    if tile.shape[0] == UNIT:
        return tile
    half = tile.shape[1] // 2
    return jnp.concatenate(
        [tile[:UNIT], jnp.concatenate([tile[UNIT:, :half], tile[UNIT:, half:]], 0)], 1
    )


def take(refs, *counts):
    runs, at = [], 0
    for count in counts:
        runs.append(refs[at:at + count])
        at += count
    return [*runs, refs[at:]]


def call(kernel, name, inputs, specs, outs, scratch, vmem=52):
    return pl.pallas_call(
        kernel,
        in_specs=specs,
        out_specs=[VMEM] * len(outs),
        out_shape=outs,
        scratch_shapes=scratch,
        compiler_params=pltpu.CompilerParams(vmem_limit_bytes=vmem << 20),
        cost_estimate=pl.CostEstimate(flops=0, bytes_accessed=1 << 20, transcendentals=0),
        name=name,
    )(*inputs)


def strips(rows, step):
    def run(i, carry):
        step(pl.ds(pl.multiple_of(i * STRIP, STRIP), STRIP))
        return carry

    lax.fori_loop(0, rows // STRIP, run, 0)


def head_forward(v, gain_vec, cosine, sine):
    r = lax.rsqrt(jnp.mean(v * v, -1, keepdims=True) + EPS)
    n = v * r * gain_vec
    return n * cosine + pltpu.roll(n, n.shape[-1] // 2, 1) * sine


def head_back(grad, v, gain_vec, cosine, sine):
    r = lax.rsqrt(jnp.mean(v * v, -1, keepdims=True) + EPS)
    grad = grad * cosine + pltpu.roll(grad * sine, grad.shape[-1] // 2, 1)
    unit_v = v * r
    gain_term = jnp.sum(grad * unit_v, 0, keepdims=True)
    inner = grad * gain_vec
    return r * (inner - unit_v * jnp.mean(unit_v * inner, -1, keepdims=True)), gain_term


def soft(queries, key_rows, bias):
    scores = dot_nt(queries, key_rows) * queries.shape[-1] ** (-0.5) + bias
    exponent = jnp.exp(scores - jnp.max(scores, -1, keepdims=True))
    return exponent / jnp.sum(exponent, -1, keepdims=True)


def weight_grad(where, planes_at, turned, columns, outs):
    width = columns.shape[1] // PLANE
    each = PLANE // len(outs)
    for n, j in enumerate((3, 1, 2, 0)):
        block = columns[:, pl.ds(pl.multiple_of(where[planes_at + j] * width, 128), width)]
        at = (n % each) * width
        outs[n // each][:, at:at + width] = dot(turned, block).astype(BF16)


def attn_forward_kernel(count, head, share, t_qkv, t_out, *refs):
    small, parts, qkv_refs, out_refs, made, scratch = take(
        refs, 7, count, t_qkv.count, t_out.count, 5
    )
    where, gain, query_gain, key_gain, cosine, sine, bias = small
    state, normed, proj, mixed, partial = made
    w_qkv, sem_qkv, w_out, sem_out = scratch
    first_copies = t_qkv.copies(where, qkv_refs, w_qkv, sem_qkv)
    last_copies = t_out.copies(where, out_refs, w_out, sem_out)
    for copy in first_copies + last_copies:
        copy.start()

    def prepare(rows):
        total = parts[0][rows, :].astype(F32)
        for part in parts[1:]:
            total = total + part[rows, :].astype(F32)
        state[rows, :] = total
        normed[rows, :] = rmsnorm(total, gain[...]).astype(BF16)

    strips(state.shape[0], prepare)
    for copy in first_copies:
        copy.wait()
    span = (share + 2) * head
    packs, pack = bias.shape[0], bias.shape[1]

    def group(g, carry):
        columns = pl.ds(pl.multiple_of(g * span, span), span)
        proj[:, columns] = dot(normed[...], w_qkv[:, columns])
        base = g * span
        heads = [
            head_forward(
                proj[:, pl.ds(pl.multiple_of(base + h * head, head), head)],
                query_gain[...] if h < share else key_gain[...],
                cosine[...],
                sine[...],
            ).astype(BF16)
            for h in range(share + 1)
        ]
        value = proj[:, pl.ds(pl.multiple_of(base + (share + 1) * head, head), head)].astype(BF16)
        for b in range(packs):
            rows = slice(b * pack, (b + 1) * pack)
            for h in range(share):
                probs = soft(heads[h][rows], heads[share][rows], bias[b])
                at = pl.multiple_of((g * share + h) * head, head)
                mixed[rows, pl.ds(at, head)] = dot(probs.astype(BF16), value[rows]).astype(BF16)
        return carry

    lax.fori_loop(0, w_qkv.shape[1] // span, group, 0)
    for copy in last_copies:
        copy.wait()
    partial[...] = dot(mixed[...], w_out[...]).astype(BF16)


def mlp_forward_kernel(unit, t_gu, last, *refs):
    small, branch, gu_refs, made, grads, (weight, sems) = take(
        refs, 5, int(last), t_gu.count, 4, int(last)
    )
    where, gain, s_ref, p_ref, c_ref = small
    middle, mlp_in, gate_up, hidden = made
    copies = t_gu.copies(where, gu_refs, weight, sems)
    for copy in copies:
        copy.start()

    def prepare(rows):
        total = s_ref[rows, :] + p_ref[rows, :].astype(F32) + c_ref[rows, :].astype(F32)
        middle[rows, :] = total
        mlp_in[rows, :] = rmsnorm(total, gain[...]).astype(BF16)

    strips(middle.shape[0], prepare)
    for copy in copies:
        copy.wait()

    def block(j, carry):
        columns = pl.ds(pl.multiple_of(j * 2 * unit, 2 * unit), 2 * unit)
        gate_up[:, columns] = dot(mlp_in[...], weight[:, columns])
        gates = gate_up[:, pl.ds(pl.multiple_of(j * 2 * unit, unit), unit)]
        ups = gate_up[:, pl.ds(pl.multiple_of(j * 2 * unit + unit, unit), unit)]
        hidden[:, pl.ds(pl.multiple_of(j * unit, unit), unit)] = (
            gates / (1.0 + jnp.exp(-gates)) * ups
        ).astype(BF16)
        return carry

    lax.fori_loop(0, weight.shape[1] // (2 * unit), block, 0)
    if last:
        weight_grad(where, t_gu.groups, hidden[...].T, branch[0], grads)


def down_kernel(t_dn, where, hidden, *refs):
    dn_refs, (partial,), (weight, sems) = take(refs, t_dn.count, 1)
    copies = t_dn.copies(where, dn_refs, weight, sems)
    for copy in copies:
        copy.start()
    for copy in copies:
        copy.wait()
    partial[...] = dot(hidden[...], weight[...]).astype(BF16)


def mlp_back_kernel(unit, t_dn, t_gu, more, *refs):
    small, hidden, dn_refs, gu_refs, (partial,), gu_grads, dn_grads, scratch = take(
        refs, 4, int(more), t_dn.count, t_gu.count, 1, 2, 2 * int(more)
    )
    where, branch, gate_up, mlp_in = small
    w_down, sem_down, w_gu, sem_gu, grad_gu = scratch
    first_copies = t_dn.copies(where, dn_refs, w_down, sem_down)
    last_copies = t_gu.copies(where, gu_refs, w_gu, sem_gu)
    for copy in first_copies + last_copies:
        copy.start()
    for copy in first_copies:
        copy.wait()

    def block(j, carry):
        grad = dot_nt(branch[...], w_down[pl.ds(pl.multiple_of(j * unit, unit), unit), :])
        at = pl.ds(pl.multiple_of(j * 2 * unit, unit), unit)
        past = pl.ds(pl.multiple_of(j * 2 * unit + unit, unit), unit)
        gates = gate_up[:, at]
        sigma = 1.0 / (1.0 + jnp.exp(-gates))
        silu = gates * sigma
        grad_gu[:, at] = (grad * gate_up[:, past] * (sigma + silu * (1.0 - sigma))).astype(BF16)
        grad_gu[:, past] = (grad * silu).astype(BF16)
        return carry

    lax.fori_loop(0, w_down.shape[0] // unit, block, 0)
    for copy in last_copies:
        copy.wait()
    partial[...] = dot_nt(grad_gu[...], w_gu[...]).astype(BF16)
    weight_grad(where, t_gu.groups, mlp_in[...].T, grad_gu, gu_grads)
    if more:
        weight_grad(where, t_gu.groups, hidden[0][...].T, branch, dn_grads)


def norm_back(rows, v_ref, gain, p_ref, c_ref, residual, grad_ref, low_ref, term):
    v = v_ref[rows, :]
    r = lax.rsqrt(jnp.mean(v * v, -1, keepdims=True) + EPS)
    grad = p_ref[rows, :].astype(F32) + c_ref[rows, :].astype(F32)
    unit_v = v * r
    term[...] += jnp.sum(grad * unit_v, 0, keepdims=True)
    inner = grad * gain[...]
    total = residual[rows, :].astype(F32) + r * (
        inner - unit_v * jnp.mean(unit_v * inner, -1, keepdims=True)
    )
    grad_ref[rows, :] = total
    low_ref[rows, :] = total.astype(BF16)


def norm_back_kernel(gain, v_ref, p_ref, c_ref, residual, grad_ref, low_ref, term):
    term[...] = jnp.zeros_like(term)
    strips(
        v_ref.shape[0],
        lambda rows: norm_back(rows, v_ref, gain, p_ref, c_ref, residual, grad_ref, low_ref, term),
    )


def attn_back_kernel(head, share, t_out, t_qkv, out_count, *refs):
    small, large, out_refs, qkv_refs, made, qkv_grads, out_grads, scratch = take(
        refs, 7, 7, t_out.count, t_qkv.count, 6, 2, out_count
    )
    where, gain, query_gain, key_gain, cosine, sine, bias = small
    v_ref, p_ref, c_ref, residual, proj, normed, mixed = large
    grad_ref, low_ref, term, query_term, key_term, partial = made
    w_out, sem_out, w_qkv, sem_qkv, grad_mixed, grad_qkv = scratch
    first_copies = t_out.copies(where, out_refs, w_out, sem_out)
    last_copies = t_qkv.copies(where, qkv_refs, w_qkv, sem_qkv)
    for copy in first_copies + last_copies:
        copy.start()
    norm_back_kernel(gain, v_ref, p_ref, c_ref, residual, grad_ref, low_ref, term)
    for copy in first_copies:
        copy.wait()
    grad_mixed[...] = dot_nt(low_ref[...], w_out[...]).astype(BF16)
    span = (share + 2) * head
    packs, pack = bias.shape[0], bias.shape[1]
    query_term[...] = jnp.zeros_like(query_term)
    key_term[...] = jnp.zeros_like(key_term)
    scale = head ** (-0.5)

    def group(g, carry):
        def part(h):
            return pl.ds(pl.multiple_of(g * span + h * head, head), head)

        for b in range(packs):
            rows = slice(b * pack, (b + 1) * pack)
            cos_b, sin_b = cosine[rows, :], sine[rows, :]
            key_raw = proj[rows, part(share)]
            key_rows = head_forward(key_raw, key_gain[...], cos_b, sin_b).astype(BF16)
            value = proj[rows, part(share + 1)].astype(BF16)
            grad_key = jnp.zeros((pack, head), F32)
            grad_value = jnp.zeros((pack, head), F32)
            for h in range(share):
                query_raw = proj[rows, part(h)]
                query = head_forward(query_raw, query_gain[...], cos_b, sin_b).astype(BF16)
                probs = soft(query, key_rows, bias[b])
                at = pl.multiple_of((g * share + h) * head, head)
                upstream = grad_mixed[rows, pl.ds(at, head)]
                grad_value += dot_tn(probs.astype(BF16), upstream)
                grad_probs = dot_nt(upstream, value)
                grad_scores = probs * (
                    grad_probs - jnp.sum(probs * grad_probs, -1, keepdims=True)
                )
                grad_scores = grad_scores.astype(BF16)
                grad_key += dot_tn(grad_scores, query)
                grad_query, extra = head_back(
                    dot(grad_scores, key_rows) * scale, query_raw, query_gain[...], cos_b, sin_b
                )
                query_term[...] += extra
                grad_qkv[rows, part(h)] = grad_query.astype(BF16)
            grad_key, extra = head_back(grad_key * scale, key_raw, key_gain[...], cos_b, sin_b)
            key_term[...] += extra
            grad_qkv[rows, part(share)] = grad_key.astype(BF16)
            grad_qkv[rows, part(share + 1)] = grad_value.astype(BF16)
        return carry

    lax.fori_loop(0, w_qkv.shape[1] // span, group, 0)
    for copy in last_copies:
        copy.wait()
    partial[...] = dot_nt(grad_qkv[...], w_qkv[...]).astype(BF16)
    weight_grad(where, t_qkv.groups, normed[...].T, grad_qkv, qkv_grads)
    weight_grad(where, t_qkv.groups, mixed[...].T, low_ref, out_grads)


SLOTS = 3


def finish_kernel(layer, items, spot, *refs):
    tiles = refs[:2 * PLANE]
    total = sum(len(widths) for _, widths, _ in items)
    outs, (narrow, wides, in_sems, sems) = refs[-4 - total:-4], refs[-4:]
    loads = [
        pltpu.make_async_copy(tile, narrow.at[n], in_sems.at[n]) for n, tile in enumerate(tiles)
    ]
    for load in loads:
        load.start()
    busy = [[] for _ in range(SLOTS)]
    for n, load in enumerate(loads):
        m, plane = divmod(n, PLANE)
        slot = n % SLOTS
        for copy in busy[slot]:
            copy.wait()
        load.wait()
        wides[slot] = narrow[n].astype(F32)
        busy[slot] = []
        at, k = 0, 0
        core, place = spot[m], spot[2 + PLANE * m + plane]
        for rows, widths, row_split in items:
            for width in widths:
                row, column = (core * rows, place * width) if row_split else (
                    0, (place * 2 + core) * width
                )
                for from_row, from_column, tall, wide, to_row, to_column in pieces(rows, width):
                    copy = pltpu.make_async_copy(
                        wides.at[slot, pl.ds(from_row, tall), pl.ds(at + from_column, wide)],
                        outs[k].at[
                            layer,
                            pl.ds(pl.multiple_of(row + to_row, 128), tall),
                            pl.ds(pl.multiple_of(column + to_column, 128), wide),
                        ],
                        sems.at[slot, len(busy[slot])],
                    )
                    copy.start()
                    busy[slot].append(copy)
                at += width * rows // UNIT
                k += 1
    for copies in busy:
        for copy in copies:
            copy.wait()


def finish(spot, tiles, layer, items, shapes, previous):
    extra = [] if previous is None else list(previous)
    width = tiles[0].shape[1]
    most = sum(len(pieces(rows, w)) for rows, widths, _ in items for w in widths)
    return pl.pallas_call(
        functools.partial(finish_kernel, layer, items),
        in_specs=[SMEM] + [ANY] * (2 * PLANE + len(extra)),
        out_specs=[ANY] * len(shapes),
        out_shape=[jax.ShapeDtypeStruct(s, F32) for s in shapes],
        scratch_shapes=[
            pltpu.VMEM((2 * PLANE, UNIT, width), BF16),
            pltpu.VMEM((SLOTS, UNIT, width), F32),
            pltpu.SemaphoreType.DMA((2 * PLANE,)),
            pltpu.SemaphoreType.DMA((SLOTS, most)),
        ],
        input_output_aliases={1 + 2 * PLANE + k: k for k in range(len(extra))},
        compiler_params=pltpu.CompilerParams(vmem_limit_bytes=24 << 20),
        cost_estimate=pl.CostEstimate(
            flops=0, bytes_accessed=48 * tiles[0].size, transcendentals=0
        ),
        name="finish",
    )(spot, *tiles, *extra)


def layout(lengths, row_count):
    seq_ends = jnp.cumsum(lengths, 1)
    starts = seq_ends - lengths
    indices = jnp.arange(row_count, dtype=jnp.int32)
    segment = jnp.sum((indices[None, :, None] >= seq_ends[:, None, :]).astype(jnp.int32), 2)
    owners = segment[:, :, None] == jnp.arange(lengths.shape[1], dtype=jnp.int32)[None, None, :]
    position = indices[None, :] - jnp.sum(jnp.where(owners, starts[:, None, :], 0), 2)
    visible = (segment[:, :, None] == segment[:, None, :]) & (
        indices[None, :, None] >= indices[None, None, :]
    )
    return position, jnp.where(visible, 0.0, MASKED).astype(F32)


def rope_tables(position, head_width):
    half_width = head_width // 2
    frequency = THETA ** (-jnp.arange(half_width, dtype=F32) * 2.0 / head_width)
    angles = position.reshape(-1).astype(F32)[:, None] * frequency
    cosine, sine = jnp.cos(angles), jnp.sin(angles)
    return jnp.concatenate([cosine, cosine], 1), jnp.concatenate([-sine, sine], 1)


def body(
    tokens,
    lengths,
    cotangent,
    attn_gain,
    w_query,
    w_key,
    w_value,
    query_gain,
    key_gain,
    w_output,
    mlp_gain,
    w_gate,
    w_up,
    w_down,
    links=None,
):
    send = links.send
    groups = links.groups
    row_count, width = tokens.shape
    layer_count = w_query.shape[0]
    head_width = query_gain.shape[1] * groups
    kv_heads = w_key.shape[2] // head_width
    share = w_query.shape[2] // w_key.shape[2]
    hidden_units = w_gate.shape[2]
    blocks = kv_heads // 2
    unit = hidden_units // (2 * blocks)
    q_width = share * head_width

    replica = lax.axis_index("replica")
    z = lax.axis_index("group")
    core = replica % 2
    plane = (replica // 2) % PLANE
    step_first = 1 + core
    step_second = 2 - core
    planes = [plane, plane ^ step_first, plane ^ step_second, plane ^ 3]
    where = jnp.stack(
        [z] + [(z + d) % groups for d in range(1, groups)] + planes + [core]
    ).astype(jnp.int32)
    partner_planes = [planes[0], planes[2], planes[1], planes[3]]
    spot = jnp.stack([core, 1 - core] + planes + partner_planes).astype(jnp.int32)

    part = attn_gain.shape[1]
    head_part = query_gain.shape[1]

    def pair_rows(rows):
        other = send(rows, links.pair)
        return jnp.concatenate(
            [jnp.where(core == 0, rows, other), jnp.where(core == 0, other, rows)], 0
        )

    position, bias = layout(pair_rows(lengths), row_count)
    cosine, sine = rope_tables(position, head_width)

    def tile_of(own, layer, by_rows):
        sides = []
        for weight in own:
            if by_rows:
                tall, wide = weight.shape[1] // 2, weight.shape[2] // PLANE
                at = (core * tall, plane * wide)
            else:
                tall, wide = weight.shape[1], weight.shape[2] // (2 * PLANE)
                at = (0, (2 * plane + core) * wide)
            sides.append(lax.dynamic_slice(weight, (layer, *at), (1, tall, wide))[0])
        return pack(jnp.concatenate(sides, 1))

    queue = Queue(3)
    nears = []

    def gather(owns, layer, extra=None, direct=False):
        tile = [tile_of(own, layer, by_rows) for own, by_rows in owns]
        widths = [x.shape[1] for x in tile]
        least = max(0, 2 * UNIT - sum(widths))
        if least:
            tile.append(jnp.zeros((UNIT, least), BF16))
        tile = jnp.concatenate(tile, 1)
        if extra is not None:
            extra = jnp.pad(extra, (0, 16 * tile.shape[1] - extra.size))
            tile = jnp.concatenate([tile, extra.reshape(16, -1)], 0)
        if direct:
            column = None
            near = jnp.stack([send(tile, links.shift[d]) for d in range(1, groups)])
        else:
            column = lax.all_gather(tile, "group", axis=0)
            if nears:
                column, _ = lax.optimization_barrier((column, queue.sent[-3]))
            near = jnp.stack(
                [
                    lax.dynamic_index_in_dim(
                        column[:, :UNIT, :sum(widths)], (z + d) % groups, 0, keepdims=False
                    )
                    for d in range(1, groups)
                ]
            )
        nears.append(near)
        first = queue.send(near, links.first)
        second = queue.send(near, links.second)
        both = queue.send(first, links.second)
        tiles, at = [], 0
        for (own, by_rows), wide in zip(owns, widths):
            tiles.append(Tiles(own, layer, (near, first, second, both), at, by_rows))
            at += wide
        return tiles, column

    gains_own = jnp.concatenate([attn_gain, mlp_gain, query_gain, key_gain], 1)
    gain_width = gains_own.shape[1]
    qkv, out = ((w_query, w_key, w_value), False), ((w_output,), True)
    gate_up, down = ((w_gate, w_up), False), ((w_down,), True)
    weights = []
    for layer in range(layer_count):
        if layer == 0:
            (t_qkv,), _ = gather([qkv], layer, direct=True)
            (t_out, t_dn), column = gather([out, down], layer, gains_own.reshape(-1))
            gains = column[:, UNIT:].reshape(groups, -1)[:, :gains_own.size]
            gains = gains.reshape(groups, layer_count, gain_width)
            (t_gu,), _ = gather([gate_up], layer)
        else:
            (t_qkv, t_out), _ = gather([qkv, out], layer)
            (t_gu,), _ = gather([gate_up], layer)
            (t_dn,), _ = gather([down], layer)
        weights.append((t_qkv, t_out, t_gu, t_dn))

    def gain_of(start, size, layer):
        return gains[:, layer, start:start + size].reshape(1, -1).astype(F32)

    def exchange(partial):
        return send(partial, links.pair)

    def own_rows(rows):
        return lax.dynamic_slice_in_dim(rows, core * row_count, row_count, 0)

    def shape(columns, kind):
        return jax.ShapeDtypeStruct((2 * row_count, columns), kind)

    def grad_shape(rows, columns):
        return jax.ShapeDtypeStruct((rows, columns), BF16)

    branch = pair_rows(cotangent)
    qkv_columns = blocks * (q_width + 2 * head_width)
    mixed_columns = blocks * q_width
    hidden_columns = blocks * unit
    forms = (head_width, share)

    parts = [pair_rows(tokens)]
    kept = []
    ahead = len(nears) - 2 * layer_count + 1
    for layer in range(layer_count):
        t_qkv, t_out, t_gu, t_dn = weights[layer]
        attn_g = gain_of(0, part, layer)
        mlp_g = gain_of(part, part, layer)
        query_g = gain_of(2 * part, head_part, layer)
        key_g = gain_of(2 * part + head_part, head_part, layer)
        parts[0], _ = lax.optimization_barrier((parts[0], nears[min(ahead, len(nears) - 1)]))
        ahead += 1
        state, normed, proj, mixed, partial = call(
            functools.partial(attn_forward_kernel, len(parts), *forms, t_qkv, t_out),
            "attn_forward",
            [where, attn_g, query_g, key_g, cosine, sine, bias, *parts, *t_qkv.refs, *t_out.refs],
            [SMEM] + [VMEM] * (6 + len(parts)) + [ANY] * (t_qkv.count + t_out.count),
            [
                shape(width, F32),
                shape(width, BF16),
                shape(qkv_columns, F32),
                shape(mixed_columns, BF16),
                shape(width, BF16),
            ],
            t_qkv.scratch() + t_out.scratch(),
        )
        came = exchange(partial)
        state, _ = lax.optimization_barrier((state, nears[min(ahead, len(nears) - 1)]))
        ahead += 1
        last = int(layer == layer_count - 1)
        middle, mlp_in, gate_up, hidden, *down_grads = call(
            functools.partial(mlp_forward_kernel, unit, t_gu, last),
            "mlp_forward",
            [where, mlp_g, state, partial, came, *[branch] * last, *t_gu.refs],
            [SMEM] + [VMEM] * (4 + last) + [ANY] * t_gu.count,
            [
                shape(width, F32),
                shape(width, BF16),
                shape(2 * hidden_columns, F32),
                shape(hidden_columns, BF16),
            ]
            + [grad_shape(hidden_columns, width)] * last,
            t_gu.scratch(),
        )
        if last:
            down_grads = lax.optimization_barrier((*down_grads, *queue.sent[-2:]))[:1]
        (partial,) = call(
            functools.partial(down_kernel, t_dn),
            "down",
            [where, hidden, *t_dn.refs],
            [SMEM, VMEM] + [ANY] * t_dn.count,
            [shape(width, BF16)],
            t_dn.scratch(),
        )
        came = exchange(partial)
        parts = [middle, partial, came]
        kept.append((state, normed, proj, mixed, middle, mlp_in, gate_up, hidden,
                     attn_g, mlp_g, query_g, key_g))
    result_tokens = own_rows(
        parts[0] + parts[1].astype(F32) + parts[2].astype(F32)
    ).astype(BF16)

    class Reduction:
        def __init__(self, grads):
            self.early = len(grads) == 1
            if self.early:
                band = self.scatter(grads[0])
                half = band.shape[1] // 2
                grads = (band[:, :half], band[:, half:])
            self.leaving, self.kept = grads
            self.count = self.kept.shape[1] // 2

        @staticmethod
        def scatter(x):
            return lax.psum_scatter(x, "group", scatter_dimension=0, tiled=True)

        def first(self):
            self.came = queue.send(self.leaving, links.first)

        def second(self, after=None, alone=True, settle=True):
            if after is not None:
                self.came, _ = lax.optimization_barrier((self.came, after))
            mine = self.kept.astype(F32) + self.came.astype(F32)
            self.last = queue.send(mine[:, :self.count].astype(BF16), links.second)
            self.mine = mine[:, self.count:]
            if settle:
                self.settle(alone=alone)

        def settle(self, after=None, alone=True):
            last = self.last
            if after is not None:
                last, _ = lax.optimization_barrier((last, after))
            mine = self.mine + last.astype(F32)
            for perm in links.outer:
                mine = mine.astype(BF16)
                mine = mine.astype(F32) + send(mine, perm).astype(F32)
            self.mine = mine.astype(BF16)
            if alone:
                self.tile = pack(self.mine if self.early else self.scatter(self.mine))

    def spread(tiles, after):
        tile, _ = lax.optimization_barrier((jnp.concatenate(tiles, 1), gain_step()))
        first = queue.send(tile, links.first)
        held, _ = lax.optimization_barrier((tile, gain_step()))
        second = queue.send(held, links.second)
        both = queue.send(first, links.second)
        mine = [tile, first, second, both]
        held = both
        if after is not None:
            held, _ = lax.optimization_barrier((both, after))
        return mine + [send(x, links.pair) for x in (*mine[:3], held)]

    row_shape = jax.ShapeDtypeStruct((1, width), F32)
    head_shape = jax.ShapeDtypeStruct((1, head_width), F32)
    gradient = branch
    gain_terms = [None] * layer_count
    sums = []
    for layer in reversed(range(layer_count)):
        t_qkv, t_out, t_gu, t_dn = weights[layer]
        (state, normed, proj, mixed, middle, mlp_in, gate_up, hidden,
         attn_g, mlp_g, query_g, key_g) = kept[layer]
        if not sums:
            down_sum = Reduction(down_grads)
        else:
            branch, _ = lax.optimization_barrier((branch, result_tokens))
        more = len(sums)
        partial, *grads = call(
            functools.partial(mlp_back_kernel, unit, t_dn, t_gu, more),
            "mlp_back",
            [where, branch, gate_up, mlp_in, *[hidden] * more, *t_dn.refs, *t_gu.refs],
            [SMEM] + [VMEM] * (3 + more) + [ANY] * (t_dn.count + t_gu.count),
            [shape(width, BF16)]
            + [grad_shape(width, hidden_columns)] * 2
            + [grad_shape(hidden_columns, width // 2)] * (2 * more),
            t_dn.scratch() + t_gu.scratch() + [pltpu.VMEM((2 * row_count, 2 * hidden_columns), BF16)],
        )
        if sums:
            sums[-1][2].settle(partial)
            partial, *grads = lax.optimization_barrier(
                (partial, *grads, sums[-1][0].came, sums[-1][1].leaving)
            )[:-2]
        came = exchange(partial)
        gu_sum = Reduction(grads[:2])
        gu_sum.first()
        if sums:
            down_sum = Reduction(grads[2:])
            down_sum.first()
        out_count = 2 if sums else 1
        grad_middle, _, mlp_term, query_term, key_term, partial, *grads = call(
            functools.partial(attn_back_kernel, *forms, t_out, t_qkv, out_count),
            "attn_back",
            [where, mlp_g, query_g, key_g, cosine, sine, bias,
             middle, partial, came, gradient, proj, normed, mixed, *t_out.refs, *t_qkv.refs],
            [SMEM] + [VMEM] * 13 + [ANY] * (t_out.count + t_qkv.count),
            [
                shape(width, F32),
                shape(width, BF16),
                row_shape,
                head_shape,
                head_shape,
                shape(width, BF16),
            ]
            + [grad_shape(width, qkv_columns // 2)] * 2
            + [grad_shape(mixed_columns, width // out_count)] * out_count,
            t_out.scratch() + t_qkv.scratch()
            + [
                pltpu.VMEM((2 * row_count, mixed_columns), BF16),
                pltpu.VMEM((2 * row_count, qkv_columns), BF16),
            ],
        )
        under_way = [gu_sum.came, sums[-1][2].tile if sums else down_sum.leaving]
        grad_middle, query_term, partial, *grads = lax.optimization_barrier(
            (grad_middle, query_term, partial, *grads, *under_way)
        )[:-len(under_way)]
        came = exchange(partial)
        qkv_sum = Reduction(grads[:2])
        out_sum = Reduction(grads[2:])
        if not sums:
            gu_sum.second(query_term, settle=False)
            qkv_sum.first()
        else:
            above = sums[-1]
            above[0].second(query_term)
            gu_sum.second(query_term)
            down_sum.second(query_term)
            qkv_sum.first()
            out_sum.first()
            for x in (above[1], above[3]):
                x.leaving, _ = lax.optimization_barrier((x.leaving, query_term))
                x.first()
                x.second()
        sums.append((qkv_sum, out_sum, gu_sum, down_sum))
        gradient, branch, attn_term = call(
            norm_back_kernel,
            "norm_back",
            [attn_g, state, partial, came, grad_middle],
            [VMEM] * 5,
            [shape(width, F32), shape(width, BF16), row_shape],
            [],
        )
        gain_terms[layer] = jnp.concatenate([attn_term, mlp_term, query_term, key_term], 1)
    sums[-1][0].second(attn_term, alone=False)
    sums[-1][1].second(alone=False)
    head_tile = Reduction.scatter(jnp.concatenate([x.mine for x in sums[-1][:2]], 1))

    gain_sums = jnp.concatenate(gain_terms, 0)
    gain_sums = jnp.concatenate([gain_sums[:, :2 * width] * 0.5, gain_sums[:, 2 * width:]], 1)
    gain_turns = [links.pair, *reversed(links.turns), *links.outer]

    def gain_step():
        nonlocal gain_sums
        if gain_turns:
            gain_sums = gain_sums + send(gain_sums, gain_turns.pop(0))
        return gain_sums

    quarter = width // PLANE
    head_items = [
        (UNIT, (q_width, head_width, head_width), False),
        (w_output.shape[1] // 2, (quarter,), True),
    ]
    unit_items = [(UNIT, (unit, unit), False), (w_down.shape[1] // 2, (quarter,), True)]
    head_shapes = [w_query.shape, w_key.shape, w_value.shape, w_output.shape]
    unit_shapes = [w_gate.shape, w_up.shape, w_down.shape]
    outs = None
    for layer, layer_sums in zip(reversed(range(layer_count)), sums):
        if layer > 0:
            outs = finish(
                spot, spread([x.tile for x in layer_sums], outs and outs[0]), layer,
                head_items + unit_items, head_shapes + unit_shapes, outs,
            )
        else:
            held = outs and outs[0]
            unit_outs = finish(
                spot, spread([x.tile for x in layer_sums[2:]], held), layer,
                unit_items, unit_shapes, outs and outs[len(head_shapes):],
            )
            head_outs = finish(
                spot, spread([head_tile], unit_outs[0]), layer,
                head_items, head_shapes, outs and outs[:len(head_shapes)],
            )
            outs = list(head_outs) + list(unit_outs)

    while gain_turns:
        gain_step()

    def own_gain(start, size):
        return lax.dynamic_slice_in_dim(gain_sums, start + z * size, size, 1)

    return (
        result_tokens,
        own_rows(gradient),
        own_gain(0, part),
        outs[0],
        outs[1],
        outs[2],
        own_gain(2 * width, head_part),
        own_gain(2 * width + head_width, head_part),
        outs[3],
        own_gain(width, part),
        outs[4],
        outs[5],
        outs[6],
    )


def solution(mesh):
    links = Links(mesh.shape["replica"], mesh.shape["group"])
    return jax.shard_map(
        functools.partial(body, links=links),
        mesh=mesh,
        in_specs=(
            P(AXES, None),
            P(AXES, None),
            P(AXES, None),
            P(None, "group"),
            P(None, "group", None),
            P(None, "group", None),
            P(None, "group", None),
            P(None, "group"),
            P(None, "group"),
            P(None, "group", None),
            P(None, "group"),
            P(None, "group", None),
            P(None, "group", None),
            P(None, "group", None),
        ),
        out_specs=(
            P(AXES, None),
            P(AXES, None),
            P(None, "group"),
            P(None, "group", None),
            P(None, "group", None),
            P(None, "group", None),
            P(None, "group"),
            P(None, "group"),
            P(None, "group", None),
            P(None, "group"),
            P(None, "group", None),
            P(None, "group", None),
            P(None, "group", None),
        ),
        check_vma=False,
    )
```

```python
import functools

import jax
import jax.numpy as jnp
from jax import lax
from jax.experimental import pallas as pl
from jax.experimental.pallas import tpu as pltpu
from jax.sharding import PartitionSpec as P

EPS = 1e-06
THETA = 1000000.0
MASKED = -1e30
AXES = ("replica", "group")
BF16 = jnp.bfloat16
F32 = jnp.float32
PLANE = 4
UNIT = 256


def dot(a, b):
    return jnp.dot(a, b, preferred_element_type=F32)


def dot_nt(a, b):
    return lax.dot_general(a, b, (((1,), (1,)), ((), ())), preferred_element_type=F32)


def dot_tn(a, b):
    return lax.dot_general(a, b, (((0,), (0,)), ((), ())), preferred_element_type=F32)


def rmsnorm(vector, gain_vec):
    return vector * lax.rsqrt(jnp.mean(vector * vector, -1, keepdims=True) + EPS) * gain_vec


class Queue:
    def __init__(self, depth):
        self.sent, self.depth = [], depth

    def send(self, x, perm):
        if len(self.sent) >= self.depth:
            x, _ = lax.optimization_barrier((x, self.sent[-self.depth]))
        x = Links.send(x, perm)
        self.sent.append(x)
        return x


class Tiles:
    def __init__(self, own, layer, sent, at, by_rows):
        self.own, self.layer, self.at, self.by_rows = own, layer, at, by_rows
        self.refs = [*own, *sent]
        self.rows = own[0].shape[1] // (2 if by_rows else 1)
        self.widths = [x.shape[2] // (PLANE if by_rows else 2 * PLANE) for x in own]
        self.width = sum(self.widths)
        self.groups = sent[0].shape[0] + 1
        self.count = len(self.refs)

    def scratch(self):
        own = 1 if self.by_rows else PLANE * len(self.own)
        rest = PLANE * (self.groups - 1) * len(pieces(self.rows, self.width))
        return [
            pltpu.VMEM((self.groups * self.rows, PLANE * self.width), BF16),
            pltpu.SemaphoreType.DMA((own + rest,)),
        ]

    def copies(self, where, refs, weight, sems):
        own, rest = refs[:len(self.own)], refs[len(self.own):]
        others, rows, core = self.groups - 1, self.rows, where[self.groups + PLANE]
        band = pl.ds(pl.multiple_of(where[0] * rows, 128), rows)
        moves = []
        if self.by_rows:
            half = pl.ds(pl.multiple_of(core * rows, 128), rows)
            moves.append((own[0].at[self.layer, half], weight.at[band]))
        else:
            for p in range(PLANE):
                column = p * self.width
                for ref, width in zip(own, self.widths):
                    part = pl.ds(pl.multiple_of((2 * p + core) * width, 128), width)
                    moves.append(
                        (ref.at[self.layer, :, part], weight.at[band, pl.ds(column, width)])
                    )
                    column += width
        for j, source in enumerate(rest):
            column = pl.multiple_of(where[1 + others + j] * self.width, 128)
            for d in range(others):
                for row, left, tall, wide, to_row, to_column in pieces(rows, self.width):
                    top = pl.multiple_of(where[1 + d] * rows + to_row, 128)
                    moves.append(
                        (
                            source.at[d, pl.ds(row, tall), pl.ds(self.at + left, wide)],
                            weight.at[pl.ds(top, tall), pl.ds(column + to_column, wide)],
                        )
                    )
        return [
            pltpu.make_async_copy(source, target, sems.at[n])
            for n, (source, target) in enumerate(moves)
        ]


class Links:
    def __init__(self, replicas, groups):
        self.replicas, self.groups = replicas, groups

        def pairs(move):
            return [
                (r * groups + g, move(r, g)[0] * groups + move(r, g)[1])
                for r in range(replicas)
                for g in range(groups)
            ]

        self.pair = pairs(lambda r, g: (r ^ 1, g))
        self.first = pairs(lambda r, g: (r ^ (4 if r & 1 else 2), g))
        self.second = pairs(lambda r, g: (r ^ (2 if r & 1 else 4), g))
        self.turns = [pairs(lambda r, g, b=b: (r ^ b, g)) for b in (2, 4)]
        bit = 1
        while bit < groups:
            self.turns.append(pairs(lambda r, g, b=bit: (r, g ^ b)))
            bit *= 2
        self.shift = [pairs(lambda r, g, d=d: (r, (g - d) % groups)) for d in range(groups)]
        self.outer = []
        bit = 8
        while bit < replicas:
            self.outer.append(pairs(lambda r, g, b=bit: (r ^ b, g)))
            bit *= 2

    @staticmethod
    def send(x, perm):
        return lax.ppermute(x, AXES, perm)


VMEM = pl.BlockSpec(memory_space=pltpu.VMEM)
SMEM = pl.BlockSpec(memory_space=pltpu.SMEM)
ANY = pl.BlockSpec(memory_space=pl.ANY)
STRIP = 64


def pieces(rows, width):
    if rows == UNIT:
        return [(0, 0, UNIT, width, 0, 0)]
    half, extra = width // 2, UNIT // 2
    return [
        (0, 0, UNIT, width, 0, 0),
        (0, width, extra, half, UNIT, 0),
        (extra, width, extra, half, UNIT, half),
    ]


def pack(tile):
    if tile.shape[0] == UNIT:
        return tile
    half = tile.shape[1] // 2
    return jnp.concatenate(
        [tile[:UNIT], jnp.concatenate([tile[UNIT:, :half], tile[UNIT:, half:]], 0)], 1
    )


def take(refs, *counts):
    runs, at = [], 0
    for count in counts:
        runs.append(refs[at:at + count])
        at += count
    return [*runs, refs[at:]]


def call(kernel, name, inputs, specs, outs, scratch, vmem=52):
    return pl.pallas_call(
        kernel,
        in_specs=specs,
        out_specs=[VMEM] * len(outs),
        out_shape=outs,
        scratch_shapes=scratch,
        compiler_params=pltpu.CompilerParams(vmem_limit_bytes=vmem << 20),
        cost_estimate=pl.CostEstimate(flops=0, bytes_accessed=1 << 20, transcendentals=0),
        name=name,
    )(*inputs)


def strips(rows, step):
    def run(i, carry):
        step(pl.ds(pl.multiple_of(i * STRIP, STRIP), STRIP))
        return carry

    lax.fori_loop(0, rows // STRIP, run, 0)


def head_forward(v, gain_vec, cosine, sine):
    r = lax.rsqrt(jnp.mean(v * v, -1, keepdims=True) + EPS)
    n = v * r * gain_vec
    return n * cosine + pltpu.roll(n, n.shape[-1] // 2, 1) * sine


def head_back(grad, v, gain_vec, cosine, sine):
    r = lax.rsqrt(jnp.mean(v * v, -1, keepdims=True) + EPS)
    grad = grad * cosine + pltpu.roll(grad * sine, grad.shape[-1] // 2, 1)
    unit_v = v * r
    gain_term = jnp.sum(grad * unit_v, 0, keepdims=True)
    inner = grad * gain_vec
    return r * (inner - unit_v * jnp.mean(unit_v * inner, -1, keepdims=True)), gain_term


def soft(queries, key_rows, bias):
    scores = dot_nt(queries, key_rows) * queries.shape[-1] ** (-0.5) + bias
    exponent = jnp.exp(scores - jnp.max(scores, -1, keepdims=True))
    return exponent / jnp.sum(exponent, -1, keepdims=True)


def weight_grad(where, planes_at, turned, columns, outs):
    width = columns.shape[1] // PLANE
    each = PLANE // len(outs)
    for n, j in enumerate((3, 1, 2, 0)):
        block = columns[:, pl.ds(pl.multiple_of(where[planes_at + j] * width, 128), width)]
        at = (n % each) * width
        outs[n // each][:, at:at + width] = dot(turned, block).astype(BF16)


def attn_forward_kernel(count, head, share, t_qkv, t_out, *refs):
    small, parts, qkv_refs, out_refs, made, scratch = take(
        refs, 7, count, t_qkv.count, t_out.count, 5
    )
    where, gain, query_gain, key_gain, cosine, sine, bias = small
    state, normed, proj, mixed, partial = made
    w_qkv, sem_qkv, w_out, sem_out = scratch
    first_copies = t_qkv.copies(where, qkv_refs, w_qkv, sem_qkv)
    last_copies = t_out.copies(where, out_refs, w_out, sem_out)
    for copy in first_copies + last_copies:
        copy.start()

    def prepare(rows):
        total = parts[0][rows, :].astype(F32)
        for part in parts[1:]:
            total = total + part[rows, :].astype(F32)
        state[rows, :] = total
        normed[rows, :] = rmsnorm(total, gain[...]).astype(BF16)

    strips(state.shape[0], prepare)
    for copy in first_copies:
        copy.wait()
    span = (share + 2) * head
    packs, pack = bias.shape[0], bias.shape[1]

    def group(g, carry):
        columns = pl.ds(pl.multiple_of(g * span, span), span)
        proj[:, columns] = dot(normed[...], w_qkv[:, columns])
        base = g * span
        heads = [
            head_forward(
                proj[:, pl.ds(pl.multiple_of(base + h * head, head), head)],
                query_gain[...] if h < share else key_gain[...],
                cosine[...],
                sine[...],
            ).astype(BF16)
            for h in range(share + 1)
        ]
        value = proj[:, pl.ds(pl.multiple_of(base + (share + 1) * head, head), head)].astype(BF16)
        for b in range(packs):
            rows = slice(b * pack, (b + 1) * pack)
            for h in range(share):
                probs = soft(heads[h][rows], heads[share][rows], bias[b])
                at = pl.multiple_of((g * share + h) * head, head)
                mixed[rows, pl.ds(at, head)] = dot(probs.astype(BF16), value[rows]).astype(BF16)
        return carry

    lax.fori_loop(0, w_qkv.shape[1] // span, group, 0)
    for copy in last_copies:
        copy.wait()
    partial[...] = dot(mixed[...], w_out[...]).astype(BF16)


def mlp_forward_kernel(unit, t_gu, last, *refs):
    small, branch, gu_refs, made, grads, (weight, sems) = take(
        refs, 5, int(last), t_gu.count, 4, int(last)
    )
    where, gain, s_ref, p_ref, c_ref = small
    middle, mlp_in, gate_up, hidden = made
    copies = t_gu.copies(where, gu_refs, weight, sems)
    for copy in copies:
        copy.start()

    def prepare(rows):
        total = s_ref[rows, :] + p_ref[rows, :].astype(F32) + c_ref[rows, :].astype(F32)
        middle[rows, :] = total
        mlp_in[rows, :] = rmsnorm(total, gain[...]).astype(BF16)

    strips(middle.shape[0], prepare)
    for copy in copies:
        copy.wait()

    def block(j, carry):
        columns = pl.ds(pl.multiple_of(j * 2 * unit, 2 * unit), 2 * unit)
        gate_up[:, columns] = dot(mlp_in[...], weight[:, columns])
        gates = gate_up[:, pl.ds(pl.multiple_of(j * 2 * unit, unit), unit)]
        ups = gate_up[:, pl.ds(pl.multiple_of(j * 2 * unit + unit, unit), unit)]
        hidden[:, pl.ds(pl.multiple_of(j * unit, unit), unit)] = (
            gates / (1.0 + jnp.exp(-gates)) * ups
        ).astype(BF16)
        return carry

    lax.fori_loop(0, weight.shape[1] // (2 * unit), block, 0)
    if last:
        weight_grad(where, t_gu.groups, hidden[...].T, branch[0], grads)


def down_kernel(t_dn, where, hidden, *refs):
    dn_refs, (partial,), (weight, sems) = take(refs, t_dn.count, 1)
    copies = t_dn.copies(where, dn_refs, weight, sems)
    for copy in copies:
        copy.start()
    for copy in copies:
        copy.wait()
    partial[...] = dot(hidden[...], weight[...]).astype(BF16)


def mlp_back_kernel(unit, t_dn, t_gu, more, *refs):
    small, hidden, dn_refs, gu_refs, (partial,), gu_grads, dn_grads, scratch = take(
        refs, 4, int(more), t_dn.count, t_gu.count, 1, 2, 2 * int(more)
    )
    where, branch, gate_up, mlp_in = small
    w_down, sem_down, w_gu, sem_gu, grad_gu = scratch
    first_copies = t_dn.copies(where, dn_refs, w_down, sem_down)
    last_copies = t_gu.copies(where, gu_refs, w_gu, sem_gu)
    for copy in first_copies + last_copies:
        copy.start()
    for copy in first_copies:
        copy.wait()

    def block(j, carry):
        grad = dot_nt(branch[...], w_down[pl.ds(pl.multiple_of(j * unit, unit), unit), :])
        at = pl.ds(pl.multiple_of(j * 2 * unit, unit), unit)
        past = pl.ds(pl.multiple_of(j * 2 * unit + unit, unit), unit)
        gates = gate_up[:, at]
        sigma = 1.0 / (1.0 + jnp.exp(-gates))
        silu = gates * sigma
        grad_gu[:, at] = (grad * gate_up[:, past] * (sigma + silu * (1.0 - sigma))).astype(BF16)
        grad_gu[:, past] = (grad * silu).astype(BF16)
        return carry

    lax.fori_loop(0, w_down.shape[0] // unit, block, 0)
    for copy in last_copies:
        copy.wait()
    partial[...] = dot_nt(grad_gu[...], w_gu[...]).astype(BF16)
    weight_grad(where, t_gu.groups, mlp_in[...].T, grad_gu, gu_grads)
    if more:
        weight_grad(where, t_gu.groups, hidden[0][...].T, branch, dn_grads)


def norm_back(rows, v_ref, gain, p_ref, c_ref, residual, grad_ref, low_ref, term):
    v = v_ref[rows, :]
    r = lax.rsqrt(jnp.mean(v * v, -1, keepdims=True) + EPS)
    grad = p_ref[rows, :].astype(F32) + c_ref[rows, :].astype(F32)
    unit_v = v * r
    term[...] += jnp.sum(grad * unit_v, 0, keepdims=True)
    inner = grad * gain[...]
    total = residual[rows, :].astype(F32) + r * (
        inner - unit_v * jnp.mean(unit_v * inner, -1, keepdims=True)
    )
    grad_ref[rows, :] = total
    low_ref[rows, :] = total.astype(BF16)


def norm_back_kernel(gain, v_ref, p_ref, c_ref, residual, grad_ref, low_ref, term):
    term[...] = jnp.zeros_like(term)
    strips(
        v_ref.shape[0],
        lambda rows: norm_back(rows, v_ref, gain, p_ref, c_ref, residual, grad_ref, low_ref, term),
    )


def attn_back_kernel(head, share, t_out, t_qkv, out_count, *refs):
    small, large, out_refs, qkv_refs, made, qkv_grads, out_grads, scratch = take(
        refs, 7, 7, t_out.count, t_qkv.count, 6, 2, out_count
    )
    where, gain, query_gain, key_gain, cosine, sine, bias = small
    v_ref, p_ref, c_ref, residual, proj, normed, mixed = large
    grad_ref, low_ref, term, query_term, key_term, partial = made
    w_out, sem_out, w_qkv, sem_qkv, grad_mixed, grad_qkv = scratch
    first_copies = t_out.copies(where, out_refs, w_out, sem_out)
    last_copies = t_qkv.copies(where, qkv_refs, w_qkv, sem_qkv)
    for copy in first_copies + last_copies:
        copy.start()
    norm_back_kernel(gain, v_ref, p_ref, c_ref, residual, grad_ref, low_ref, term)
    for copy in first_copies:
        copy.wait()
    grad_mixed[...] = dot_nt(low_ref[...], w_out[...]).astype(BF16)
    span = (share + 2) * head
    packs, pack = bias.shape[0], bias.shape[1]
    query_term[...] = jnp.zeros_like(query_term)
    key_term[...] = jnp.zeros_like(key_term)
    scale = head ** (-0.5)

    def group(g, carry):
        def part(h):
            return pl.ds(pl.multiple_of(g * span + h * head, head), head)

        for b in range(packs):
            rows = slice(b * pack, (b + 1) * pack)
            cos_b, sin_b = cosine[rows, :], sine[rows, :]
            key_raw = proj[rows, part(share)]
            key_rows = head_forward(key_raw, key_gain[...], cos_b, sin_b).astype(BF16)
            value = proj[rows, part(share + 1)].astype(BF16)
            grad_key = jnp.zeros((pack, head), F32)
            grad_value = jnp.zeros((pack, head), F32)
            for h in range(share):
                query_raw = proj[rows, part(h)]
                query = head_forward(query_raw, query_gain[...], cos_b, sin_b).astype(BF16)
                probs = soft(query, key_rows, bias[b])
                at = pl.multiple_of((g * share + h) * head, head)
                upstream = grad_mixed[rows, pl.ds(at, head)]
                grad_value += dot_tn(probs.astype(BF16), upstream)
                grad_probs = dot_nt(upstream, value)
                grad_scores = probs * (
                    grad_probs - jnp.sum(probs * grad_probs, -1, keepdims=True)
                )
                grad_scores = grad_scores.astype(BF16)
                grad_key += dot_tn(grad_scores, query)
                grad_query, extra = head_back(
                    dot(grad_scores, key_rows) * scale, query_raw, query_gain[...], cos_b, sin_b
                )
                query_term[...] += extra
                grad_qkv[rows, part(h)] = grad_query.astype(BF16)
            grad_key, extra = head_back(grad_key * scale, key_raw, key_gain[...], cos_b, sin_b)
            key_term[...] += extra
            grad_qkv[rows, part(share)] = grad_key.astype(BF16)
            grad_qkv[rows, part(share + 1)] = grad_value.astype(BF16)
        return carry

    lax.fori_loop(0, w_qkv.shape[1] // span, group, 0)
    for copy in last_copies:
        copy.wait()
    partial[...] = dot_nt(grad_qkv[...], w_qkv[...]).astype(BF16)
    weight_grad(where, t_qkv.groups, normed[...].T, grad_qkv, qkv_grads)
    weight_grad(where, t_qkv.groups, mixed[...].T, low_ref, out_grads)


SLOTS = 3


def finish_kernel(layer, items, spot, *refs):
    tiles = refs[:2 * PLANE]
    total = sum(len(widths) for _, widths, _ in items)
    outs, (narrow, wides, in_sems, sems) = refs[-4 - total:-4], refs[-4:]
    loads = [
        pltpu.make_async_copy(tile, narrow.at[n], in_sems.at[n]) for n, tile in enumerate(tiles)
    ]
    for load in loads:
        load.start()
    busy = [[] for _ in range(SLOTS)]
    for n, load in enumerate(loads):
        m, plane = divmod(n, PLANE)
        slot = n % SLOTS
        for copy in busy[slot]:
            copy.wait()
        load.wait()
        wides[slot] = narrow[n].astype(F32)
        busy[slot] = []
        at, k = 0, 0
        core, place = spot[m], spot[2 + PLANE * m + plane]
        for rows, widths, row_split in items:
            for width in widths:
                row, column = (core * rows, place * width) if row_split else (
                    0, (place * 2 + core) * width
                )
                for from_row, from_column, tall, wide, to_row, to_column in pieces(rows, width):
                    copy = pltpu.make_async_copy(
                        wides.at[slot, pl.ds(from_row, tall), pl.ds(at + from_column, wide)],
                        outs[k].at[
                            layer,
                            pl.ds(pl.multiple_of(row + to_row, 128), tall),
                            pl.ds(pl.multiple_of(column + to_column, 128), wide),
                        ],
                        sems.at[slot, len(busy[slot])],
                    )
                    copy.start()
                    busy[slot].append(copy)
                at += width * rows // UNIT
                k += 1
    for copies in busy:
        for copy in copies:
            copy.wait()


def finish(spot, tiles, layer, items, shapes, previous):
    extra = [] if previous is None else list(previous)
    width = tiles[0].shape[1]
    most = sum(len(pieces(rows, w)) for rows, widths, _ in items for w in widths)
    return pl.pallas_call(
        functools.partial(finish_kernel, layer, items),
        in_specs=[SMEM] + [ANY] * (2 * PLANE + len(extra)),
        out_specs=[ANY] * len(shapes),
        out_shape=[jax.ShapeDtypeStruct(s, F32) for s in shapes],
        scratch_shapes=[
            pltpu.VMEM((2 * PLANE, UNIT, width), BF16),
            pltpu.VMEM((SLOTS, UNIT, width), F32),
            pltpu.SemaphoreType.DMA((2 * PLANE,)),
            pltpu.SemaphoreType.DMA((SLOTS, most)),
        ],
        input_output_aliases={1 + 2 * PLANE + k: k for k in range(len(extra))},
        compiler_params=pltpu.CompilerParams(vmem_limit_bytes=24 << 20),
        cost_estimate=pl.CostEstimate(
            flops=0, bytes_accessed=48 * tiles[0].size, transcendentals=0
        ),
        name="finish",
    )(spot, *tiles, *extra)


def layout(lengths, row_count):
    seq_ends = jnp.cumsum(lengths, 1)
    starts = seq_ends - lengths
    indices = jnp.arange(row_count, dtype=jnp.int32)
    segment = jnp.sum((indices[None, :, None] >= seq_ends[:, None, :]).astype(jnp.int32), 2)
    owners = segment[:, :, None] == jnp.arange(lengths.shape[1], dtype=jnp.int32)[None, None, :]
    position = indices[None, :] - jnp.sum(jnp.where(owners, starts[:, None, :], 0), 2)
    visible = (segment[:, :, None] == segment[:, None, :]) & (
        indices[None, :, None] >= indices[None, None, :]
    )
    return position, jnp.where(visible, 0.0, MASKED).astype(F32)


def rope_tables(position, head_width):
    half_width = head_width // 2
    frequency = THETA ** (-jnp.arange(half_width, dtype=F32) * 2.0 / head_width)
    angles = position.reshape(-1).astype(F32)[:, None] * frequency
    cosine, sine = jnp.cos(angles), jnp.sin(angles)
    return jnp.concatenate([cosine, cosine], 1), jnp.concatenate([-sine, sine], 1)


def body(
    tokens,
    lengths,
    cotangent,
    attn_gain,
    w_query,
    w_key,
    w_value,
    query_gain,
    key_gain,
    w_output,
    mlp_gain,
    w_gate,
    w_up,
    w_down,
    links=None,
):
    send = links.send
    groups = links.groups
    row_count, width = tokens.shape
    layer_count = w_query.shape[0]
    head_width = query_gain.shape[1] * groups
    kv_heads = w_key.shape[2] // head_width
    share = w_query.shape[2] // w_key.shape[2]
    hidden_units = w_gate.shape[2]
    blocks = kv_heads // 2
    unit = hidden_units // (2 * blocks)
    q_width = share * head_width

    replica = lax.axis_index("replica")
    z = lax.axis_index("group")
    core = replica % 2
    plane = (replica // 2) % PLANE
    step_first = 1 + core
    step_second = 2 - core
    planes = [plane, plane ^ step_first, plane ^ step_second, plane ^ 3]
    where = jnp.stack(
        [z] + [(z + d) % groups for d in range(1, groups)] + planes + [core]
    ).astype(jnp.int32)
    partner_planes = [planes[0], planes[2], planes[1], planes[3]]
    spot = jnp.stack([core, 1 - core] + planes + partner_planes).astype(jnp.int32)

    part = attn_gain.shape[1]
    head_part = query_gain.shape[1]

    def pair_rows(rows):
        other = send(rows, links.pair)
        return jnp.concatenate(
            [jnp.where(core == 0, rows, other), jnp.where(core == 0, other, rows)], 0
        )

    position, bias = layout(pair_rows(lengths), row_count)
    cosine, sine = rope_tables(position, head_width)

    def tile_of(own, layer, by_rows):
        sides = []
        for weight in own:
            if by_rows:
                tall, wide = weight.shape[1] // 2, weight.shape[2] // PLANE
                at = (core * tall, plane * wide)
            else:
                tall, wide = weight.shape[1], weight.shape[2] // (2 * PLANE)
                at = (0, (2 * plane + core) * wide)
            sides.append(lax.dynamic_slice(weight, (layer, *at), (1, tall, wide))[0])
        return pack(jnp.concatenate(sides, 1))

    queue = Queue(3)
    nears = []

    def gather(owns, layer, extra=None, direct=False):
        tile = [tile_of(own, layer, by_rows) for own, by_rows in owns]
        widths = [x.shape[1] for x in tile]
        least = max(0, 2 * UNIT - sum(widths))
        if least:
            tile.append(jnp.zeros((UNIT, least), BF16))
        tile = jnp.concatenate(tile, 1)
        if extra is not None:
            extra = jnp.pad(extra, (0, 16 * tile.shape[1] - extra.size))
            tile = jnp.concatenate([tile, extra.reshape(16, -1)], 0)
        if direct:
            column = None
            near = jnp.stack([send(tile, links.shift[d]) for d in range(1, groups)])
        else:
            column = lax.all_gather(tile, "group", axis=0)
            if nears:
                column, _ = lax.optimization_barrier((column, queue.sent[-3]))
            near = jnp.stack(
                [
                    lax.dynamic_index_in_dim(
                        column[:, :UNIT, :sum(widths)], (z + d) % groups, 0, keepdims=False
                    )
                    for d in range(1, groups)
                ]
            )
        nears.append(near)
        first = queue.send(near, links.first)
        second = queue.send(near, links.second)
        both = queue.send(first, links.second)
        tiles, at = [], 0
        for (own, by_rows), wide in zip(owns, widths):
            tiles.append(Tiles(own, layer, (near, first, second, both), at, by_rows))
            at += wide
        return tiles, column

    gains_own = jnp.concatenate([attn_gain, mlp_gain, query_gain, key_gain], 1)
    gain_width = gains_own.shape[1]
    qkv, out = ((w_query, w_key, w_value), False), ((w_output,), True)
    gate_up, down = ((w_gate, w_up), False), ((w_down,), True)
    weights = []
    for layer in range(layer_count):
        if layer == 0:
            (t_qkv,), _ = gather([qkv], layer, direct=True)
            (t_out, t_dn), column = gather([out, down], layer, gains_own.reshape(-1))
            gains = column[:, UNIT:].reshape(groups, -1)[:, :gains_own.size]
            gains = gains.reshape(groups, layer_count, gain_width)
            (t_gu,), _ = gather([gate_up], layer)
        else:
            (t_qkv, t_out), _ = gather([qkv, out], layer)
            (t_gu,), _ = gather([gate_up], layer)
            (t_dn,), _ = gather([down], layer)
        weights.append((t_qkv, t_out, t_gu, t_dn))

    def gain_of(start, size, layer):
        return gains[:, layer, start:start + size].reshape(1, -1).astype(F32)

    def exchange(partial):
        return send(partial, links.pair)

    def own_rows(rows):
        return lax.dynamic_slice_in_dim(rows, core * row_count, row_count, 0)

    def shape(columns, kind):
        return jax.ShapeDtypeStruct((2 * row_count, columns), kind)

    def grad_shape(rows, columns):
        return jax.ShapeDtypeStruct((rows, columns), BF16)

    branch = pair_rows(cotangent)
    qkv_columns = blocks * (q_width + 2 * head_width)
    mixed_columns = blocks * q_width
    hidden_columns = blocks * unit
    forms = (head_width, share)

    parts = [pair_rows(tokens)]
    kept = []
    ahead = len(nears) - 2 * layer_count + 1
    for layer in range(layer_count):
        t_qkv, t_out, t_gu, t_dn = weights[layer]
        attn_g = gain_of(0, part, layer)
        mlp_g = gain_of(part, part, layer)
        query_g = gain_of(2 * part, head_part, layer)
        key_g = gain_of(2 * part + head_part, head_part, layer)
        parts[0], _ = lax.optimization_barrier((parts[0], nears[min(ahead, len(nears) - 1)]))
        ahead += 1
        state, normed, proj, mixed, partial = call(
            functools.partial(attn_forward_kernel, len(parts), *forms, t_qkv, t_out),
            "attn_forward",
            [where, attn_g, query_g, key_g, cosine, sine, bias, *parts, *t_qkv.refs, *t_out.refs],
            [SMEM] + [VMEM] * (6 + len(parts)) + [ANY] * (t_qkv.count + t_out.count),
            [
                shape(width, F32),
                shape(width, BF16),
                shape(qkv_columns, F32),
                shape(mixed_columns, BF16),
                shape(width, BF16),
            ],
            t_qkv.scratch() + t_out.scratch(),
        )
        came = exchange(partial)
        state, _ = lax.optimization_barrier((state, nears[min(ahead, len(nears) - 1)]))
        ahead += 1
        last = int(layer == layer_count - 1)
        middle, mlp_in, gate_up, hidden, *down_grads = call(
            functools.partial(mlp_forward_kernel, unit, t_gu, last),
            "mlp_forward",
            [where, mlp_g, state, partial, came, *[branch] * last, *t_gu.refs],
            [SMEM] + [VMEM] * (4 + last) + [ANY] * t_gu.count,
            [
                shape(width, F32),
                shape(width, BF16),
                shape(2 * hidden_columns, F32),
                shape(hidden_columns, BF16),
            ]
            + [grad_shape(hidden_columns, width)] * last,
            t_gu.scratch(),
        )
        if last:
            down_grads = lax.optimization_barrier((*down_grads, *queue.sent[-2:]))[:1]
        (partial,) = call(
            functools.partial(down_kernel, t_dn),
            "down",
            [where, hidden, *t_dn.refs],
            [SMEM, VMEM] + [ANY] * t_dn.count,
            [shape(width, BF16)],
            t_dn.scratch(),
        )
        came = exchange(partial)
        parts = [middle, partial, came]
        kept.append((state, normed, proj, mixed, middle, mlp_in, gate_up, hidden,
                     attn_g, mlp_g, query_g, key_g))
    result_tokens = own_rows(
        parts[0] + parts[1].astype(F32) + parts[2].astype(F32)
    ).astype(BF16)

    class Reduction:
        def __init__(self, grads):
            self.early = len(grads) == 1
            if self.early:
                band = self.scatter(grads[0])
                half = band.shape[1] // 2
                grads = (band[:, :half], band[:, half:])
            self.leaving, self.kept = grads
            self.count = self.kept.shape[1] // 2

        @staticmethod
        def scatter(x):
            return lax.psum_scatter(x, "group", scatter_dimension=0, tiled=True)

        def join(self, other):
            def side(x, n):
                return pack(x[:, n * x.shape[1] // 2:(n + 1) * x.shape[1] // 2])

            self.leaving, self.kept = (
                jnp.concatenate([side(x, n) for n in range(2) for x in both], 1)
                for both in ((self.leaving, other.leaving), (self.kept, other.kept))
            )
            self.count = self.kept.shape[1] // 2

        def first(self):
            self.came = queue.send(self.leaving, links.first)

        def second(self, after=None, alone=True, settle=True):
            if after is not None:
                self.came, _ = lax.optimization_barrier((self.came, after))
            mine = self.kept.astype(F32) + self.came.astype(F32)
            self.last = queue.send(mine[:, :self.count].astype(BF16), links.second)
            self.mine = mine[:, self.count:]
            if settle:
                self.settle(alone=alone)

        def settle(self, after=None, alone=True):
            last = self.last
            if after is not None:
                last, _ = lax.optimization_barrier((last, after))
            mine = self.mine + last.astype(F32)
            for perm in links.outer:
                mine = mine.astype(BF16)
                mine = mine.astype(F32) + send(mine, perm).astype(F32)
            self.mine = mine.astype(BF16)
            if alone:
                self.tile = pack(self.mine if self.early else self.scatter(self.mine))

    def spread(tiles, after):
        tile = jnp.concatenate(tiles, 1)
        first = queue.send(tile, links.first)
        second = queue.send(tile, links.second)
        held, _ = lax.optimization_barrier((first, gain_step()))
        both = queue.send(held, links.second)
        mine = [tile, first, second, both]
        held = both
        if after is not None:
            held, _, _ = lax.optimization_barrier((both, after, gain_step()))
        return mine + [send(x, links.pair) for x in (*mine[:3], held)]

    row_shape = jax.ShapeDtypeStruct((1, width), F32)
    head_shape = jax.ShapeDtypeStruct((1, head_width), F32)
    gradient = branch
    gain_terms = [None] * layer_count
    sums = []
    for layer in reversed(range(layer_count)):
        t_qkv, t_out, t_gu, t_dn = weights[layer]
        (state, normed, proj, mixed, middle, mlp_in, gate_up, hidden,
         attn_g, mlp_g, query_g, key_g) = kept[layer]
        if not sums:
            down_sum = Reduction(down_grads)
        else:
            branch, _ = lax.optimization_barrier((branch, result_tokens))
        more = len(sums)
        partial, *grads = call(
            functools.partial(mlp_back_kernel, unit, t_dn, t_gu, more),
            "mlp_back",
            [where, branch, gate_up, mlp_in, *[hidden] * more, *t_dn.refs, *t_gu.refs],
            [SMEM] + [VMEM] * (3 + more) + [ANY] * (t_dn.count + t_gu.count),
            [shape(width, BF16)]
            + [grad_shape(width, hidden_columns)] * 2
            + [grad_shape(hidden_columns, width // 2)] * (2 * more),
            t_dn.scratch() + t_gu.scratch() + [pltpu.VMEM((2 * row_count, 2 * hidden_columns), BF16)],
        )
        if sums:
            sums[-1][2].settle(partial)
            partial, *grads = lax.optimization_barrier(
                (partial, *grads, sums[-1][0].came, sums[-1][1].leaving)
            )[:-2]
        came = exchange(partial)
        gu_sum = Reduction(grads[:2])
        gu_sum.first()
        if sums:
            down_sum = Reduction(grads[2:])
            down_sum.first()
        out_count = 2 if sums else 1
        grad_middle, _, mlp_term, query_term, key_term, partial, *grads = call(
            functools.partial(attn_back_kernel, *forms, t_out, t_qkv, out_count),
            "attn_back",
            [where, mlp_g, query_g, key_g, cosine, sine, bias,
             middle, partial, came, gradient, proj, normed, mixed, *t_out.refs, *t_qkv.refs],
            [SMEM] + [VMEM] * 13 + [ANY] * (t_out.count + t_qkv.count),
            [
                shape(width, F32),
                shape(width, BF16),
                row_shape,
                head_shape,
                head_shape,
                shape(width, BF16),
            ]
            + [grad_shape(width, qkv_columns // 2)] * 2
            + [grad_shape(mixed_columns, width // out_count)] * out_count,
            t_out.scratch() + t_qkv.scratch()
            + [
                pltpu.VMEM((2 * row_count, mixed_columns), BF16),
                pltpu.VMEM((2 * row_count, qkv_columns), BF16),
            ],
        )
        under_way = [gu_sum.came, sums[-1][2].tile if sums else down_sum.leaving]
        grad_middle, query_term, partial, *grads = lax.optimization_barrier(
            (grad_middle, query_term, partial, *grads, *under_way)
        )[:-len(under_way)]
        came = exchange(partial)
        qkv_sum = Reduction(grads[:2])
        out_sum = Reduction(grads[2:])
        if not sums:
            gu_sum.second(query_term, settle=False)
            qkv_sum.first()
        else:
            above = sums[-1]
            above[0].second(query_term)
            gu_sum.second(query_term)
            down_sum.second(query_term)
            qkv_sum.first()
            out_sum.first()
            above[1].join(above[3])
            above[1].leaving, _ = lax.optimization_barrier((above[1].leaving, query_term))
            above[1].first()
            above[1].second()
        sums.append((qkv_sum, out_sum, gu_sum, down_sum))
        gradient, branch, attn_term = call(
            norm_back_kernel,
            "norm_back",
            [attn_g, state, partial, came, grad_middle],
            [VMEM] * 5,
            [shape(width, F32), shape(width, BF16), row_shape],
            [],
        )
        gain_terms[layer] = jnp.concatenate([attn_term, mlp_term, query_term, key_term], 1)
    gain_sums = jnp.concatenate(gain_terms, 0)
    gain_sums = jnp.concatenate([gain_sums[:, :2 * width] * 0.5, gain_sums[:, 2 * width:]], 1)
    gain_turns = [links.pair, *links.turns, *links.outer]

    def gain_step():
        nonlocal gain_sums
        if gain_turns:
            gain_sums = gain_sums + send(gain_sums, gain_turns.pop(0))
        return gain_sums

    sums[-1][0].second(gain_step(), alone=False)
    sums[-1][1].second(gain_step(), alone=False)
    head_tile = Reduction.scatter(jnp.concatenate([x.mine for x in sums[-1][:2]], 1))

    quarter = width // PLANE
    head_items = [
        (UNIT, (q_width, head_width, head_width), False),
        (w_output.shape[1] // 2, (quarter,), True),
    ]
    unit_items = [(UNIT, (unit, unit), False), (w_down.shape[1] // 2, (quarter,), True)]
    head_shapes = [w_query.shape, w_key.shape, w_value.shape, w_output.shape]
    unit_shapes = [w_gate.shape, w_up.shape, w_down.shape]
    outs = None
    for layer, layer_sums in zip(reversed(range(layer_count)), sums):
        if layer > 0:
            qkv_sum, both_sum, gu_sum, _ = layer_sums
            *outs, grad_dn, grad_gate, grad_up = finish(
                spot, spread([x.tile for x in (qkv_sum, both_sum, gu_sum)], outs and outs[0]),
                layer,
                [*head_items, unit_items[1], unit_items[0]],
                [*head_shapes, w_down.shape, w_gate.shape, w_up.shape],
                outs and [*outs[:4], outs[6], outs[4], outs[5]],
            )
            outs = [*outs, grad_gate, grad_up, grad_dn]
        else:
            held = outs and outs[0]
            unit_outs = finish(
                spot, spread([x.tile for x in layer_sums[2:]], held), layer,
                unit_items, unit_shapes, outs and outs[len(head_shapes):],
            )
            head_outs = finish(
                spot, spread([head_tile], unit_outs[0]), layer,
                head_items, head_shapes, outs and outs[:len(head_shapes)],
            )
            outs = list(head_outs) + list(unit_outs)

    while gain_turns:
        gain_step()

    def own_gain(start, size):
        return lax.dynamic_slice_in_dim(gain_sums, start + z * size, size, 1)

    return (
        result_tokens,
        own_rows(gradient),
        own_gain(0, part),
        outs[0],
        outs[1],
        outs[2],
        own_gain(2 * width, head_part),
        own_gain(2 * width + head_width, head_part),
        outs[3],
        own_gain(width, part),
        outs[4],
        outs[5],
        outs[6],
    )


def solution(mesh):
    links = Links(mesh.shape["replica"], mesh.shape["group"])
    return jax.shard_map(
        functools.partial(body, links=links),
        mesh=mesh,
        in_specs=(
            P(AXES, None),
            P(AXES, None),
            P(AXES, None),
            P(None, "group"),
            P(None, "group", None),
            P(None, "group", None),
            P(None, "group", None),
            P(None, "group"),
            P(None, "group"),
            P(None, "group", None),
            P(None, "group"),
            P(None, "group", None),
            P(None, "group", None),
            P(None, "group", None),
        ),
        out_specs=(
            P(AXES, None),
            P(AXES, None),
            P(None, "group"),
            P(None, "group", None),
            P(None, "group", None),
            P(None, "group", None),
            P(None, "group"),
            P(None, "group"),
            P(None, "group", None),
            P(None, "group"),
            P(None, "group", None),
            P(None, "group", None),
            P(None, "group", None),
        ),
        check_vma=False,
    )
```
